32 devices in a mesh: rows: 16 (over z, x, core), cols: 2 (over y).
Axes of the slice: x: 2, y: 2, z: 4, core: 2. Of those that a mesh axis runs over, the one named last changes fastest.
Arguments:
- fact_cells: bfloat16 [768, 8, 512], P('rows', 'cols'), may hold values from -6 to 6
- gain_col: float32 [512], replicated, may hold values from 0.1 to 1.9
- w_qkv: bfloat16 [512, 1536], replicated, may hold values from -0.25 to 0.25
- w_col_out: bfloat16 [512, 512], replicated, may hold values from -0.25 to 0.25
- gain_tile: float32 [512], replicated, may hold values from 0.1 to 1.9
- w_query: bfloat16 [512, 512], replicated, may hold values from -0.25 to 0.25
- w_tile_out: bfloat16 [512, 512], replicated, may hold values from -0.25 to 0.25
- tile_kv: bfloat16 [64, 128, 8, 128], P('rows', None, 'cols'), may hold values from -70 to 70
- tile_ids: int32 [16, 12], P('rows'), may hold values from -1 to 63, as said below
- key_mask: int32 [768, 12], P('rows'), may hold values from 0 to 1, as said below
Outputs:
- layer_out: bfloat16 [768, 8, 512], P('rows', 'cols')
The draws below stay inside these ranges and needn't reach their ends.
Inputs may be any that keep to these rules, and one draw needn't show every extreme that they name: `tile_ids`: tile t is held by index t // 4 of rows. In every block the first slots, 9 of them or more, hold distinct tile ids and the rest hold -1; some block fills all 12 slots. The listed tiles of one block are held by distinct indices of rows. `key_mask`: 0 wherever the row's block holds -1 in that slot; 1 in slot 0 of every row.
All inputs are finite; a program needn't handle non-finite values.
Results may differ from the reference program's by a relative error of at most 0.023.
The reference program's roundings to bfloat16 on the way (of `normed`, `packed`, `col_weights`, `mixed_col`, `normed2`, `asked_q`, `tile_weights` and `answer`) count: a program that leaves them out, or rounds other values in their place, can miss the bound.
Values may be sent and summed in bfloat16 or wider, within the bound.
No kernel may reach another device: no remote copies, remote signals or barrier semaphores. Data moves between devices by JAX's collectives and lax.ppermute only.
A program may use at most 64 MiB of HBM per device.

```python
import jax
import jax.numpy as jnp
from jax import lax

D = 512
HEADS = 8
HD = 64
COLUMNS = 8
R_DEV = 48
ROWS = 768
BLOCKS = 16
KEYS = 128
TILE_DEV = 4
NTILES = 64
CAP = 1
MAXT = 12


def count_draw(key):
    base_key = jax.random.fold_in(key, 11)
    key_first, key_second = jax.random.split(base_key)
    block_counts = jax.random.randint(key_first, (BLOCKS,), 3 * MAXT // 4, MAXT + 1)
    full_block = jax.random.randint(key_second, (), 0, BLOCKS)
    return jnp.where(jnp.arange(BLOCKS) == full_block, MAXT, block_counts).astype(jnp.int32)


def ids_block(block_key, block_count):
    key_perm, key_offs, key_order = jax.random.split(block_key, 3)
    slot_total = BLOCKS * CAP
    perm_order = jax.random.permutation(key_perm, slot_total)
    partner = (perm_order[0] + BLOCKS) % slot_total
    where_partner = jnp.argmax(perm_order == partner)
    second_val = perm_order[1]
    perm_order = perm_order.at[1].set(partner)
    perm_order = perm_order.at[where_partner].set(second_val)
    picked = perm_order[:MAXT]
    owners = picked % BLOCKS
    copies = picked // BLOCKS
    offsets = jax.random.randint(key_offs, (BLOCKS,), 0, TILE_DEV)
    local_idx = (offsets[owners] + copies) % TILE_DEV
    tile_list = owners * TILE_DEV + local_idx
    slot_pos = jnp.arange(MAXT)
    order_scores = jnp.where(slot_pos < block_count, jax.random.permutation(key_order, MAXT), MAXT + slot_pos)
    shuffle_idx = jnp.argsort(order_scores)
    return jnp.where(slot_pos < block_count, tile_list[shuffle_idx], -1).astype(jnp.int32)


def draw_tile_ids(key, part):
    block_counts = count_draw(key)
    block_keys = jax.random.split(jax.random.fold_in(key, 23), BLOCKS)
    return jax.vmap(ids_block)(block_keys, block_counts)


def draw_key_mask(key, part):
    block_counts = count_draw(key)
    mask_bits = jax.random.randint(jax.random.fold_in(key, 37), (ROWS, MAXT), 0, 2)
    slot_pos = jnp.arange(MAXT)[None, :]
    row_count = jnp.repeat(block_counts, R_DEV)[:, None]
    live_slot = (slot_pos < row_count).astype(jnp.int32)
    return (jnp.where(slot_pos == 0, 1, mask_bits) * live_slot).astype(jnp.int32)


def draw_tile_kv(key, part):
    key_a, key_b = jax.random.split(key, 2)
    arr_shape = (NTILES, KEYS, HEADS, HD)
    key_part = 2.0 * jax.random.normal(key_a, arr_shape, jnp.float32)
    val_part = 3.0 * jax.random.normal(key_b, arr_shape, jnp.float32)
    return jnp.concatenate([key_part, val_part], axis=-1).astype(jnp.bfloat16)


def steps_of(own_key, extent, shards, least, high):
    gain = 1.0
    for dim, parts in shards:
        draws = jax.random.uniform(jax.random.fold_in(jax.random.fold_in(own_key, 6), dim), (parts,), jnp.float32, least / len(shards), high / len(shards))
        gain = gain * jnp.repeat(jnp.exp(draws), extent[dim] // parts).reshape((-1,) + (1,) * (len(extent) - 1 - dim))
    return gain


def normal_values(key, dims, scale, bound, cuts=(), held_as=jnp.bfloat16):
    level = steps_of(key, dims, cuts, -0.22, 0.18) if cuts else 1.0
    entries = jax.random.normal(key, dims, jnp.float32) * scale * level
    return jnp.minimum(jnp.maximum(entries, -bound), bound).astype(held_as)


def setup_inputs(seed: int = 0) -> dict:
    seeds = jax.random.split(jax.random.key(seed), 11)
    return {
        "fact_cells": normal_values(seeds[0], (ROWS, COLUMNS, D), 1.0, 6.0, ((0, 16), (1, 2))),
        "gain_col": jnp.clip(1.0 + 0.18 * jax.random.normal(seeds[1], (D,), jnp.float32), 0.1, 1.9),
        "w_qkv": normal_values(seeds[2], (D, 3 * D), D ** -0.5, 0.25),
        "w_col_out": normal_values(seeds[3], (D, D), D ** -0.5, 0.25),
        "gain_tile": jnp.clip(1.0 + 0.18 * jax.random.normal(seeds[4], (D,), jnp.float32), 0.1, 1.9),
        "w_query": normal_values(seeds[5], (D, D), D ** -0.5, 0.25),
        "w_tile_out": normal_values(seeds[6], (D, D), D ** -0.5, 0.25),
        "tile_kv": draw_tile_kv(jax.random.fold_in(seeds[10], 71), 0),
        "tile_ids": draw_tile_ids(jax.random.fold_in(seeds[10], 71), 0),
        "key_mask": draw_key_mask(jax.random.fold_in(seeds[10], 71), 0),
    }


def rms_scale(values, gain_vec):
    mean_sq = lax.optimization_barrier(jnp.mean(values * values, axis=-1, keepdims=True))
    return values * lax.rsqrt(mean_sq + 1e-05) * gain_vec

def soft_weights(scores, axes):
    row_top = lax.optimization_barrier(jnp.max(scores, axis=axes, keepdims=True))
    expo_vals = jnp.exp(scores - row_top)
    return expo_vals / lax.optimization_barrier(jnp.sum(expo_vals, axis=axes, keepdims=True))

def rounded(values):
    return lax.optimization_barrier(values.astype(jnp.bfloat16)).astype(jnp.float32)

def reference(fact_cells, gain_col, w_qkv, w_col_out, gain_tile, w_query, w_tile_out, tile_kv, tile_ids, key_mask):
    row_total, col_total, model_width = fact_cells.shape
    head_size = model_width // HEADS
    scale = head_size ** (-0.5)
    residual = fact_cells.astype(jnp.float32)
    normed = rms_scale(residual, gain_col).astype(jnp.bfloat16)
    packed = jnp.dot(normed.reshape(-1, model_width), w_qkv, preferred_element_type=jnp.float32)
    packed = rounded(packed).reshape(row_total, col_total, 3, HEADS, head_size)
    queries = packed[:, :, 0]
    key_part = packed[:, :, 1]
    val_part = packed[:, :, 2]
    scores = jnp.einsum('rchd,rkhd->rhck', queries, key_part) * scale
    col_weights = rounded(soft_weights(scores, (3,)))
    mixed_col = jnp.einsum('rhck,rkhd->rchd', col_weights, val_part).astype(jnp.bfloat16)
    residual2 = residual + jnp.dot(mixed_col.reshape(-1, model_width), w_col_out, preferred_element_type=jnp.float32).reshape(residual.shape)
    normed2 = rms_scale(residual2, gain_tile).astype(jnp.bfloat16)
    asked_q = jnp.dot(normed2.reshape(-1, model_width), w_query, preferred_element_type=jnp.float32)
    asked_q = rounded(asked_q).reshape(row_total, col_total, HEADS, head_size)

    def one_block(block_idx):
        start = block_idx * 4
        block_q = lax.dynamic_slice_in_dim(asked_q, start, 4, 0)
        block_m = lax.dynamic_slice_in_dim(key_mask, start, 4, 0)
        slot_ids = lax.dynamic_index_in_dim(tile_ids, start // R_DEV, 0, keepdims=False)
        chosen = jnp.take(tile_kv, jnp.maximum(slot_ids, 0).astype(jnp.int32), axis=0).astype(jnp.float32)
        tile_keys = chosen[..., :head_size]
        tile_vals = chosen[..., head_size:]
        block_scores = jnp.einsum('rchd,tkhd->rchtk', block_q, tile_keys) * scale
        live_keys = (block_m > 0)[:, None, None, :, None]
        block_scores = jnp.where(live_keys, block_scores, -1e+30)
        tile_weights = rounded(soft_weights(block_scores, (3, 4)))
        return jnp.einsum('rchtk,tkhd->rchd', tile_weights, tile_vals).astype(jnp.bfloat16)
    answer = lax.map(one_block, jnp.arange(row_total // 4, dtype=jnp.int32))
    answer = answer.reshape(row_total * col_total, model_width)
    layer_out = residual2 + jnp.dot(answer, w_tile_out, preferred_element_type=jnp.float32).reshape(residual.shape)
    return layer_out.astype(jnp.bfloat16)
```

```python
import jax
import jax.numpy as jnp
from jax import lax
from jax.sharding import PartitionSpec as P


def rms_scale(values, gain_vec):
    mean_sq = jnp.mean(values * values, axis=-1, keepdims=True)
    return values * lax.rsqrt(mean_sq + 1e-05) * gain_vec


def soft_weights(scores, axes):
    row_top = jnp.max(scores, axis=axes, keepdims=True)
    expo_vals = jnp.exp(scores - row_top)
    return (expo_vals / jnp.sum(expo_vals, axis=axes, keepdims=True)).astype(jnp.bfloat16)


def project(values, weight):
    return jnp.dot(values, weight, preferred_element_type=jnp.float32)


def turn(size, step):
    return [(src, (src + step) % size) for src in range(size)]


def from_ahead(value, axis, size, step):
    return lax.ppermute(value, axis, turn(size, -step))


def fetch_tiles(tile_kv, tile_ids, row_size):
    tiles_here = tile_kv.shape[0]
    me = lax.axis_index("rows")
    all_ids = lax.all_gather(tile_ids[0], "rows", axis=0)
    mine = (all_ids >= 0) & (all_ids // tiles_here == me)
    wanted = jnp.sum(jnp.where(mine, all_ids % tiles_here, 0), axis=1)
    heads_first = jnp.transpose(tile_kv, (0, 2, 1, 3))
    outgoing = jnp.take(heads_first, wanted, axis=0)
    return lax.all_to_all(outgoing, "rows", split_axis=0, concat_axis=0, tiled=True)


def shards(row_size, col_size, fact_cells, gain_col, w_qkv, w_col_out, gain_tile, w_query, w_tile_out,
           tile_kv, tile_ids, key_mask):
    width = fact_cells.shape[2]
    head_size = tile_kv.shape[3] // 2
    heads_here = tile_kv.shape[2]
    heads_all = width // head_size
    rows, cols = fact_cells.shape[:2]
    tiles_here = tile_kv.shape[0]
    scale = head_size ** (-0.5)
    col_me = lax.axis_index("cols")

    others = [from_ahead(fact_cells, "cols", col_size, step) for step in range(1, col_size)]
    fetched = fetch_tiles(tile_kv, tile_ids, row_size)

    cells = jnp.concatenate([fact_cells] + others, axis=1)
    cols_all = cells.shape[1]
    residual = cells.astype(jnp.float32).reshape(-1, width)
    normed = rms_scale(residual, gain_col).astype(jnp.bfloat16)
    packed = project(normed, w_qkv).astype(jnp.bfloat16).reshape(rows, cols_all, 3, heads_all, head_size)
    scores = jnp.einsum("rchd,rkhd->rhck", packed[:, :, 0], packed[:, :, 1], preferred_element_type=jnp.float32) * scale
    mixed_col = jnp.einsum("rhck,rkhd->rchd", soft_weights(scores, (3,)), packed[:, :, 2],
                           preferred_element_type=jnp.float32).astype(jnp.bfloat16)
    residual = residual + project(mixed_col.reshape(-1, width), w_col_out)
    normed2 = rms_scale(residual, gain_tile).astype(jnp.bfloat16)
    group = heads_here * head_size
    query_here = lax.dynamic_slice_in_dim(w_query, col_me * group, group, 1)
    asked = project(normed2, query_here).astype(jnp.bfloat16).reshape(rows, cols_all, heads_here, head_size)

    holder = jnp.where(tile_ids[0] >= 0, tile_ids[0] // tiles_here, -1)
    slot_of = (holder[:, None] == jnp.arange(row_size)[None, :]) & (key_mask[:, :, None] > 0)
    live = jnp.any(slot_of, axis=1)

    key_part = fetched[..., :head_size]
    val_part = fetched[..., head_size:]
    scores = jnp.einsum("rchd,thkd->hrctk", asked, key_part, preferred_element_type=jnp.float32) * scale
    scores = jnp.where(live[None, :, None, :, None], scores, -1e30)
    weights = soft_weights(scores, (3, 4))
    answer = jnp.einsum("hrctk,thkd->rchd", weights, val_part, preferred_element_type=jnp.float32)
    answer = answer.astype(jnp.bfloat16).reshape(rows, cols_all, group)

    final = residual.reshape(rows, cols_all, width)[:, :cols].reshape(-1, width)
    for step in range(col_size):
        part = answer[:, step * cols:(step + 1) * cols].reshape(-1, group)
        if step:
            part = lax.ppermute(part, "cols", turn(col_size, step))
        start = (col_me - step) % col_size * group
        final = final + project(part, lax.dynamic_slice_in_dim(w_tile_out, start, group, 0))
    return final.astype(jnp.bfloat16).reshape(rows, cols, width)


def solution(mesh):
    row_size, col_size = mesh.shape["rows"], mesh.shape["cols"]
    placed = (P("rows", "cols", None), P(), P(), P(), P(), P(), P(), P("rows", None, "cols", None),
              P("rows", None), P("rows", None))

    def body(*arrays):
        return shards(row_size, col_size, *arrays)

    return jax.shard_map(body, mesh=mesh, in_specs=placed, out_specs=P("rows", "cols", None), check_vma=False)
```

```python
import functools

import jax
import jax.numpy as jnp
from jax import lax
from jax.experimental import pallas as pl
from jax.experimental.pallas import tpu as pltpu
from jax.sharding import PartitionSpec as P

ROW_GROUP = 16
BIG = -1e30
VMEM_BYTES = 48 * 1024 * 1024


def params():
    return pltpu.CompilerParams(vmem_limit_bytes=VMEM_BYTES)


def dot_rows(left, right):
    return lax.dot_general(left, right, (((1,), (0,)), ((), ())), preferred_element_type=jnp.float32)


def dot_lanes(left, right):
    return lax.dot_general(left, right, (((1,), (1,)), ((), ())), preferred_element_type=jnp.float32)


def rms_scale(values, gain_vec):
    mean_sq = jnp.mean(values * values, axis=-1, keepdims=True)
    return values * lax.rsqrt(mean_sq + 1e-05) * gain_vec


def pick_kernel(count, wanted_ref, tiles_ref, out_ref):
    for peer in range(count):
        out_ref[peer] = tiles_ref[wanted_ref[peer]]


def pick(tiles, wanted):
    count = wanted.shape[0]
    return pl.pallas_call(
        functools.partial(pick_kernel, count),
        out_shape=jax.ShapeDtypeStruct((count,) + tiles.shape[1:], tiles.dtype),
        in_specs=[pl.BlockSpec(memory_space=pltpu.SMEM), pl.BlockSpec(memory_space=pltpu.VMEM)],
        out_specs=pl.BlockSpec(memory_space=pltpu.VMEM),
        compiler_params=params(),
        cost_estimate=pl.CostEstimate(flops=0, bytes_accessed=tiles.size * 2 + count * tiles[0].size * 2, transcendentals=0),
        name="pick",
    )(wanted, tiles)


def front_kernel(groups, heads, head_size, chunk, cols, *refs):
    cell_refs, refs = refs[:groups], refs[groups:]
    (gain_col_ref, w_qkv_ref, w_out_ref, gain_tile_ref, w_query_ref,
     resid_ref, asked_ref, normed_ref, packed_ref) = refs
    own_rows, width = cell_refs[0].shape
    steps = own_rows // chunk
    span = groups * chunk
    for step in range(steps):
        for group in range(groups):
            cells = cell_refs[group][pl.ds(step * chunk, chunk), :].astype(jnp.float32)
            normed_ref[pl.ds(step * span + group * chunk, chunk), :] = rms_scale(cells, gain_col_ref[...]).astype(jnp.bfloat16)
    for part in range(3):
        packed_ref[part] = dot_rows(normed_ref[...], w_qkv_ref[:, pl.ds(part * width, width)]).astype(jnp.bfloat16)
    row_of = lax.broadcasted_iota(jnp.int32, (span, span), 0) % chunk // cols
    col_of = lax.broadcasted_iota(jnp.int32, (span, span), 1) % chunk // cols
    same_row = row_of == col_of
    lane_low = lax.broadcasted_iota(jnp.int32, (span, 2 * head_size), 1) < head_size
    scale = head_size ** (-0.5)
    for step in range(steps):
        rows = pl.ds(step * span, span)
        for pair in range(heads // 2):
            lanes = pl.ds(pair * 2 * head_size, 2 * head_size)
            query, keys, vals = packed_ref[0, rows, lanes], packed_ref[1, rows, lanes], packed_ref[2, rows, lanes]
            mixed = []
            for low in (True, False):
                query_one = jnp.where(lane_low == low, query, jnp.zeros_like(query))
                scores = jnp.where(same_row, dot_lanes(query_one, keys) * scale, BIG)
                expo = jnp.exp(scores - jnp.max(scores, axis=1, keepdims=True))
                weights = (expo / jnp.sum(expo, axis=1, keepdims=True)).astype(jnp.bfloat16)
                mixed.append(dot_rows(weights, vals))
            normed_ref[rows, lanes] = jnp.where(lane_low, mixed[0], mixed[1]).astype(jnp.bfloat16)
    delta = dot_rows(normed_ref[...], w_out_ref[...])
    for step in range(steps):
        for group in range(groups):
            start = step * span + group * chunk
            resid = cell_refs[group][pl.ds(step * chunk, chunk), :].astype(jnp.float32) + delta[start:start + chunk]
            if group == 0:
                resid_ref[pl.ds(step * chunk, chunk), :] = resid
            normed_ref[pl.ds(start, chunk), :] = rms_scale(resid, gain_tile_ref[...]).astype(jnp.bfloat16)
    asked = dot_rows(normed_ref[...], w_query_ref[...]).astype(jnp.bfloat16)
    asked_ref[...] = asked * jnp.bfloat16(scale)


def front(cells, gain_col, w_qkv, w_out, gain_tile, w_query, heads, head_size, cols):
    groups = len(cells)
    own_rows, width = cells[0].shape
    total = groups * own_rows
    asked_width = w_query.shape[1]
    vmem = pl.BlockSpec(memory_space=pltpu.VMEM)
    return pl.pallas_call(
        functools.partial(front_kernel, groups, heads, head_size, ROW_GROUP * cols, cols),
        out_shape=(jax.ShapeDtypeStruct((own_rows, width), jnp.float32),
                   jax.ShapeDtypeStruct((total, asked_width), jnp.bfloat16)),
        in_specs=[vmem] * (groups + 5),
        out_specs=(vmem, vmem),
        scratch_shapes=[pltpu.VMEM((total, width), jnp.bfloat16), pltpu.VMEM((3, total, width), jnp.bfloat16)],
        compiler_params=params(),
        cost_estimate=pl.CostEstimate(flops=2 * total * width * (4 * width + asked_width), bytes_accessed=4 * 1024 * 1024,
                                      transcendentals=total * heads * 128),
        name="front",
    )(*cells, gain_col.reshape(1, width), w_qkv, w_out, gain_tile.reshape(1, width), w_query)


def weigh(query, bias, tiles):
    slots, keys, lanes = tiles.shape
    scores = dot_lanes(query, tiles.reshape(slots * keys, lanes))
    parts = [scores[:, s * keys:(s + 1) * keys] + bias[:, s:s + 1] for s in range(slots)]
    top = parts[0]
    for part in parts[1:]:
        top = jnp.maximum(top, part)
    top = jnp.max(top, axis=1, keepdims=True)
    expo = [jnp.exp(part - top) for part in parts]
    total = expo[0]
    for part in expo[1:]:
        total = total + part
    total = jnp.sum(total, axis=1, keepdims=True)
    probs = jnp.concatenate([part.astype(jnp.bfloat16) for part in expo], axis=1)
    return top, total, dot_rows(probs, tiles.reshape(slots * keys, lanes))


def first_kernel(heads, chunk, asked_ref, bias_ref, tiles_ref, state_ref):
    rows_all, lanes = asked_ref.shape[0], tiles_ref.shape[3]
    lane = lax.broadcasted_iota(jnp.int32, (chunk, lanes), 1)
    for step in range(rows_all // chunk):
        rows = pl.ds(step * chunk, chunk)
        for head in range(heads):
            top, total, summed = weigh(asked_ref[rows, pl.ds(head * lanes, lanes)], bias_ref[rows, :], tiles_ref[:, head])
            state_ref[head, rows, :] = jnp.where(lane < lanes // 4, top, jnp.where(lane < lanes // 2, total, summed))


def first_tiles(asked, bias, tiles):
    slots, heads, keys, lanes = tiles.shape
    rows = asked.shape[0]
    vmem = pl.BlockSpec(memory_space=pltpu.VMEM)
    return pl.pallas_call(
        functools.partial(first_kernel, heads, 128),
        out_shape=jax.ShapeDtypeStruct((heads, rows, lanes), jnp.float32),
        in_specs=[vmem] * 3,
        out_specs=vmem,
        compiler_params=params(),
        cost_estimate=pl.CostEstimate(flops=4 * rows * heads * slots * keys * lanes, bytes_accessed=4 * 1024 * 1024,
                                      transcendentals=rows * heads * slots * keys),
        name="first_tiles",
    )(asked, bias, tiles)


def last_kernel(groups, first_head, heads, chunk, asked_ref, bias_ref, tiles_ref, state_ref, *out_refs):
    rows_all, lanes = asked_ref.shape[0], tiles_ref.shape[3]
    half = lanes // 2
    span = groups * chunk
    lane_low = lax.broadcasted_iota(jnp.int32, (span, lanes), 1) < half
    for step in range(rows_all // span):
        rows = pl.ds(step * span, span)
        answers = []
        for head in range(heads):
            query = asked_ref[rows, pl.ds((first_head + head) * lanes, lanes)]
            top, total, summed = weigh(query, bias_ref[rows, :], tiles_ref[:, head])
            state = state_ref[first_head + head, rows, :]
            old_top, old_total = state[:, 0:1], state[:, lanes // 4:lanes // 4 + 1]
            new_top = jnp.maximum(top, old_top)
            keep, add = jnp.exp(old_top - new_top), jnp.exp(top - new_top)
            whole = old_total * keep + total * add
            answers.append((state * keep + summed * add) / whole)
        if heads % 2 == 0:
            for pair in range(heads // 2):
                low = pltpu.roll(answers[2 * pair], half, 1)
                both = jnp.where(lane_low, low, answers[2 * pair + 1]).astype(jnp.bfloat16)
                for group in range(groups):
                    out_refs[group][pl.ds(step * chunk, chunk), pl.ds(pair * lanes, lanes)] = both[group * chunk:(group + 1) * chunk]
        else:
            for head in range(heads):
                one = answers[head][:, half:].astype(jnp.bfloat16)
                for group in range(groups):
                    out_refs[group][pl.ds(step * chunk, chunk), pl.ds(head * half, half)] = one[group * chunk:(group + 1) * chunk]


def last_tiles(asked, bias, tiles, state, first_head, groups, cols):
    slots, heads, keys, lanes = tiles.shape
    rows = asked.shape[0]
    vmem = pl.BlockSpec(memory_space=pltpu.VMEM)
    out = jax.ShapeDtypeStruct((rows // groups, heads * lanes // 2), jnp.bfloat16)
    return pl.pallas_call(
        functools.partial(last_kernel, groups, first_head, heads, ROW_GROUP * cols),
        out_shape=(out,) * groups,
        in_specs=[vmem] * 4,
        out_specs=(vmem,) * groups,
        compiler_params=params(),
        cost_estimate=pl.CostEstimate(flops=4 * rows * heads * slots * keys * lanes, bytes_accessed=4 * 1024 * 1024,
                                      transcendentals=rows * heads * slots * keys),
        name="last_tiles",
    )(asked, bias, tiles, state)


def turn(size, step):
    return [(src, (src + step) % size) for src in range(size)]


def shards(row_size, col_size, fact_cells, gain_col, w_qkv, w_col_out, gain_tile, w_query, w_tile_out,
           tile_kv, tile_ids, key_mask):
    rows, cols, width = fact_cells.shape
    tiles_here, keys, heads_here, lanes = tile_kv.shape
    head_size = lanes // 2
    heads_all = width // head_size
    group_width = heads_here * head_size
    half = row_size // 2
    parts = 2 if heads_here % 2 == 0 else 1
    part_heads = heads_here // parts
    col_me = lax.axis_index("cols")
    my_half = lax.axis_index("rows") // half
    halves = [list(range(half)), list(range(half, row_size))]

    def swap(value):
        return lax.all_to_all(value, "rows", split_axis=0, concat_axis=0, tiled=True, axis_index_groups=halves)

    listed = tile_ids[0] >= 0
    holder = jnp.where(listed, tile_ids[0] // tiles_here, -1)
    match = holder[:, None] == jnp.arange(row_size)[None, :]
    wanted = jnp.sum(jnp.where(match, (tile_ids[0] % tiles_here)[:, None], 0), axis=0).astype(jnp.int32)
    wanted = jnp.roll(wanted, -my_half * half).reshape(2, half)
    asked_of = jnp.broadcast_to(wanted.T[:, :, None], (half, 2, 128))
    asked_by = swap(asked_of)[:, :, 0]

    cells = [fact_cells.reshape(rows * cols, width)]
    for step in range(1, col_size):
        cells.append(lax.ppermute(cells[0], "cols", turn(col_size, -step)))

    heads_first = jnp.transpose(tile_kv, (0, 2, 1, 3))
    mirrored = [lax.ppermute(heads_first[:, part * part_heads:(part + 1) * part_heads], "rows", turn(row_size, half))
                for part in range(parts)]
    near = swap(pick(heads_first, asked_by[:, 0]))

    query_here = lax.dynamic_slice_in_dim(w_query, col_me * group_width, group_width, 1)
    query_here = jnp.pad(query_here.reshape(width, heads_here, head_size), ((0, 0), (0, 0), (0, head_size)))
    residual, asked = front(cells, gain_col, w_qkv, w_col_out, gain_tile, query_here.reshape(width, heads_here * lanes),
                            heads_all, head_size, cols)

    live = jnp.any(match[None, :, :] & (key_mask[:, :, None] > 0), axis=1)
    bias = jnp.where(live, 0.0, BIG).astype(jnp.float32)
    bias = jnp.roll(bias, -my_half * half, axis=1)
    bias = jnp.broadcast_to(bias.reshape(rows // ROW_GROUP, 1, ROW_GROUP, 1, row_size),
                            (rows // ROW_GROUP, col_size, ROW_GROUP, cols, row_size)).reshape(-1, row_size)
    state = first_tiles(asked, bias[:, :half], near)

    final = residual
    for part in range(parts):
        far = swap(pick(mirrored[part], asked_by[:, 1]))
        answers = last_tiles(asked, bias[:, half:], far, state, part * part_heads, col_size, cols)
        for step in range(col_size):
            answer = lax.ppermute(answers[step], "cols", turn(col_size, step)) if step else answers[0]
            start = (col_me - step) % col_size * group_width + part * part_heads * head_size
            weight = lax.dynamic_slice_in_dim(w_tile_out, start, part_heads * head_size, 0)
            final = final + dot_rows(answer, weight)
    return final.astype(jnp.bfloat16).reshape(rows, cols, width)


def solution(mesh):
    row_size, col_size = mesh.shape["rows"], mesh.shape["cols"]
    placed = (P("rows", "cols", None), P(), P(), P(), P(), P(), P(), P("rows", None, "cols", None),
              P("rows", None), P("rows", None))

    def body(*arrays):
        return shards(row_size, col_size, *arrays)

    return jax.shard_map(body, mesh=mesh, in_specs=placed, out_specs=P("rows", "cols", None), check_vma=False)
```

```python
import functools

import jax
import jax.numpy as jnp
from jax import lax
from jax.experimental import pallas as pl
from jax.experimental.pallas import tpu as pltpu
from jax.sharding import PartitionSpec as P

ROW_GROUP = 16
BIG = -1e30
VMEM_BYTES = 48 * 1024 * 1024


def params():
    return pltpu.CompilerParams(vmem_limit_bytes=VMEM_BYTES)


def dot_rows(left, right):
    return lax.dot_general(left, right, (((1,), (0,)), ((), ())), preferred_element_type=jnp.float32)


def dot_lanes(left, right):
    return lax.dot_general(left, right, (((1,), (1,)), ((), ())), preferred_element_type=jnp.float32)


def rms_scale(values, gain_vec):
    mean_sq = jnp.mean(values * values, axis=-1, keepdims=True)
    return values * lax.rsqrt(mean_sq + 1e-05) * gain_vec


def pick_kernel(count, wanted_ref, tiles_ref, out_ref):
    for peer in range(count):
        out_ref[peer] = tiles_ref[wanted_ref[peer]]


def pick(tiles, wanted):
    count = wanted.shape[0]
    return pl.pallas_call(
        functools.partial(pick_kernel, count),
        out_shape=jax.ShapeDtypeStruct((count,) + tiles.shape[1:], tiles.dtype),
        in_specs=[pl.BlockSpec(memory_space=pltpu.SMEM), pl.BlockSpec(memory_space=pltpu.VMEM)],
        out_specs=pl.BlockSpec(memory_space=pltpu.VMEM),
        compiler_params=params(),
        cost_estimate=pl.CostEstimate(flops=0, bytes_accessed=tiles.size * 2 + count * tiles[0].size * 2, transcendentals=0),
        name="pick",
    )(wanted, tiles)


def front_kernel(groups, heads, head_size, chunk, cols, *refs):
    cell_refs, refs = refs[:groups], refs[groups:]
    (gain_col_ref, w_qkv_ref, w_out_ref, gain_tile_ref, w_query_ref,
     resid_ref, asked_ref, normed_ref, packed_ref) = refs
    own_rows, width = cell_refs[0].shape
    steps = own_rows // chunk
    span = groups * chunk
    for step in range(steps):
        for group in range(groups):
            cells = cell_refs[group][pl.ds(step * chunk, chunk), :].astype(jnp.float32)
            normed_ref[pl.ds(step * span + group * chunk, chunk), :] = rms_scale(cells, gain_col_ref[...]).astype(jnp.bfloat16)
    for part in range(3):
        packed_ref[part] = dot_rows(normed_ref[...], w_qkv_ref[:, pl.ds(part * width, width)]).astype(jnp.bfloat16)
    stacked = heads * span
    row_of = lax.broadcasted_iota(jnp.int32, (stacked, span), 0) % chunk // cols
    col_of = lax.broadcasted_iota(jnp.int32, (stacked, span), 1) % chunk // cols
    same_row = row_of == col_of
    lane_low = lax.broadcasted_iota(jnp.int32, (span, 2 * head_size), 1) < head_size
    scale = head_size ** (-0.5)
    for step in range(steps):
        rows = pl.ds(step * span, span)
        scores = []
        for head in range(heads):
            lanes = pl.ds(head // 2 * 2 * head_size, 2 * head_size)
            query = packed_ref[0, rows, lanes]
            query = jnp.where(lane_low == (head % 2 == 0), query, jnp.zeros_like(query))
            scores.append(dot_lanes(query, packed_ref[1, rows, lanes]))
        scores = jnp.where(same_row, jnp.concatenate(scores, axis=0) * scale, BIG)
        expo = jnp.exp(scores - jnp.max(scores, axis=1, keepdims=True))
        weights = (expo / jnp.sum(expo, axis=1, keepdims=True)).astype(jnp.bfloat16)
        for pair in range(heads // 2):
            lanes = pl.ds(pair * 2 * head_size, 2 * head_size)
            start = 2 * pair * span
            mixed = dot_rows(weights[start:start + 2 * span], packed_ref[2, rows, lanes])
            normed_ref[rows, lanes] = jnp.where(lane_low, mixed[:span], mixed[span:]).astype(jnp.bfloat16)
    delta = dot_rows(normed_ref[...], w_out_ref[...])
    for step in range(steps):
        for group in range(groups):
            start = step * span + group * chunk
            resid = cell_refs[group][pl.ds(step * chunk, chunk), :].astype(jnp.float32) + delta[start:start + chunk]
            if group == 0:
                resid_ref[pl.ds(step * chunk, chunk), :] = resid
            normed_ref[pl.ds(start, chunk), :] = rms_scale(resid, gain_tile_ref[...]).astype(jnp.bfloat16)
    asked = dot_rows(normed_ref[...], w_query_ref[...]).astype(jnp.bfloat16)
    asked_ref[...] = asked * jnp.bfloat16(scale)


def front(cells, gain_col, w_qkv, w_out, gain_tile, w_query, heads, head_size, cols):
    groups = len(cells)
    own_rows, width = cells[0].shape
    total = groups * own_rows
    asked_width = w_query.shape[1]
    vmem = pl.BlockSpec(memory_space=pltpu.VMEM)
    return pl.pallas_call(
        functools.partial(front_kernel, groups, heads, head_size, ROW_GROUP * cols, cols),
        out_shape=(jax.ShapeDtypeStruct((own_rows, width), jnp.float32),
                   jax.ShapeDtypeStruct((total, asked_width), jnp.bfloat16)),
        in_specs=[vmem] * (groups + 5),
        out_specs=(vmem, vmem),
        scratch_shapes=[pltpu.VMEM((total, width), jnp.bfloat16), pltpu.VMEM((3, total, width), jnp.bfloat16)],
        compiler_params=params(),
        cost_estimate=pl.CostEstimate(flops=2 * total * width * (4 * width + asked_width), bytes_accessed=4 * 1024 * 1024,
                                      transcendentals=total * heads * 128),
        name="front",
    )(*cells, gain_col.reshape(1, width), w_qkv, w_out, gain_tile.reshape(1, width), w_query)


def weigh(query, bias, tiles):
    slots, keys, lanes = tiles.shape
    scores = dot_lanes(query, tiles.reshape(slots * keys, lanes))
    parts = [scores[:, s * keys:(s + 1) * keys] + bias[:, s:s + 1] for s in range(slots)]
    top = parts[0]
    for part in parts[1:]:
        top = jnp.maximum(top, part)
    top = jnp.max(top, axis=1, keepdims=True)
    expo = [jnp.exp(part - top) for part in parts]
    total = expo[0]
    for part in expo[1:]:
        total = total + part
    total = jnp.sum(total, axis=1, keepdims=True)
    probs = jnp.concatenate([part.astype(jnp.bfloat16) for part in expo], axis=1)
    return top, total, dot_rows(probs, tiles.reshape(slots * keys, lanes))


def first_kernel(heads, chunk, asked_ref, bias_ref, tiles_ref, state_ref):
    rows_all, lanes = asked_ref.shape[0], tiles_ref.shape[3]
    lane = lax.broadcasted_iota(jnp.int32, (chunk, lanes), 1)
    for step in range(rows_all // chunk):
        rows = pl.ds(step * chunk, chunk)
        for head in range(heads):
            top, total, summed = weigh(asked_ref[rows, pl.ds(head * lanes, lanes)], bias_ref[rows, :], tiles_ref[:, head])
            state_ref[head, rows, :] = jnp.where(lane < lanes // 4, top, jnp.where(lane < lanes // 2, total, summed))


def first_tiles(asked, bias, tiles):
    slots, heads, keys, lanes = tiles.shape
    rows = asked.shape[0]
    vmem = pl.BlockSpec(memory_space=pltpu.VMEM)
    return pl.pallas_call(
        functools.partial(first_kernel, heads, rows if rows <= 512 else 128),
        out_shape=jax.ShapeDtypeStruct((heads, rows, lanes), jnp.float32),
        in_specs=[vmem] * 3,
        out_specs=vmem,
        compiler_params=params(),
        cost_estimate=pl.CostEstimate(flops=4 * rows * heads * slots * keys * lanes, bytes_accessed=4 * 1024 * 1024,
                                      transcendentals=rows * heads * slots * keys),
        name="first_tiles",
    )(asked, bias, tiles)


def last_kernel(groups, first_head, heads, chunk, asked_ref, bias_ref, tiles_ref, state_ref, *out_refs):
    rows_all, lanes = asked_ref.shape[0], tiles_ref.shape[3]
    half = lanes // 2
    span = groups * chunk
    block = rows_all if rows_all <= 512 else span
    lane_low = lax.broadcasted_iota(jnp.int32, (block, lanes), 1) < half

    def put(step, values, lane, lane_count):
        for part in range(block // span):
            for group in range(groups):
                start = part * span + group * chunk
                place = pl.ds(step * (block // groups) + part * chunk, chunk)
                out_refs[group][place, pl.ds(lane, lane_count)] = values[start:start + chunk]

    for step in range(rows_all // block):
        rows = pl.ds(step * block, block)
        answers = []
        for head in range(heads):
            query = asked_ref[rows, pl.ds((first_head + head) * lanes, lanes)]
            top, total, summed = weigh(query, bias_ref[rows, :], tiles_ref[:, head])
            state = state_ref[first_head + head, rows, :]
            old_top, old_total = state[:, 0:1], state[:, lanes // 4:lanes // 4 + 1]
            new_top = jnp.maximum(top, old_top)
            keep, add = jnp.exp(old_top - new_top), jnp.exp(top - new_top)
            inverse = 1.0 / (old_total * keep + total * add)
            answers.append(state * (keep * inverse) + summed * (add * inverse))
        if heads % 2 == 0:
            for pair in range(heads // 2):
                low = pltpu.roll(answers[2 * pair], half, 1)
                put(step, jnp.where(lane_low, low, answers[2 * pair + 1]).astype(jnp.bfloat16), pair * lanes, lanes)
        else:
            for head in range(heads):
                put(step, answers[head][:, half:].astype(jnp.bfloat16), head * half, half)


def last_tiles(asked, bias, tiles, state, first_head, groups, cols):
    slots, heads, keys, lanes = tiles.shape
    rows = asked.shape[0]
    vmem = pl.BlockSpec(memory_space=pltpu.VMEM)
    out = jax.ShapeDtypeStruct((rows // groups, heads * lanes // 2), jnp.bfloat16)
    return pl.pallas_call(
        functools.partial(last_kernel, groups, first_head, heads, ROW_GROUP * cols),
        out_shape=(out,) * groups,
        in_specs=[vmem] * 4,
        out_specs=(vmem,) * groups,
        compiler_params=params(),
        cost_estimate=pl.CostEstimate(flops=4 * rows * heads * slots * keys * lanes, bytes_accessed=4 * 1024 * 1024,
                                      transcendentals=rows * heads * slots * keys),
        name="last_tiles",
    )(asked, bias, tiles, state)


def turn(size, step):
    return [(src, (src + step) % size) for src in range(size)]


def shards(row_size, col_size, fact_cells, gain_col, w_qkv, w_col_out, gain_tile, w_query, w_tile_out,
           tile_kv, tile_ids, key_mask):
    rows, cols, width = fact_cells.shape
    tiles_here, keys, heads_here, lanes = tile_kv.shape
    head_size = lanes // 2
    heads_all = width // head_size
    group_width = heads_here * head_size
    half = row_size // 2
    col_me = lax.axis_index("cols")
    my_half = lax.axis_index("rows") // half
    halves = [list(range(half)), list(range(half, row_size))]

    def swap(value):
        return lax.all_to_all(value, "rows", split_axis=0, concat_axis=0, tiled=True, axis_index_groups=halves)

    listed = tile_ids[0] >= 0
    holder = jnp.where(listed, tile_ids[0] // tiles_here, -1)
    match = holder[:, None] == jnp.arange(row_size)[None, :]
    wanted = jnp.sum(jnp.where(match, (tile_ids[0] % tiles_here)[:, None], 0), axis=0).astype(jnp.int32)
    wanted = jnp.roll(wanted, -my_half * half).reshape(2, half)
    asked_of = jnp.broadcast_to(wanted.T[:, :, None], (half, 2, 128))
    asked_by = swap(asked_of)[:, :, 0]

    cells = [fact_cells.reshape(rows * cols, width)]
    for step in range(1, col_size):
        cells.append(lax.ppermute(cells[0], "cols", turn(col_size, -step)))

    heads_first = jnp.transpose(tile_kv, (0, 2, 1, 3))
    mirrored = lax.ppermute(heads_first, "rows", turn(row_size, half))
    near = swap(pick(heads_first, asked_by[:, 0]))

    query_here = lax.dynamic_slice_in_dim(w_query, col_me * group_width, group_width, 1)
    query_here = jnp.pad(query_here.reshape(width, heads_here, head_size), ((0, 0), (0, 0), (0, head_size)))
    residual, asked = front(cells, gain_col, w_qkv, w_col_out, gain_tile, query_here.reshape(width, heads_here * lanes),
                            heads_all, head_size, cols)

    live = jnp.any(match[None, :, :] & (key_mask[:, :, None] > 0), axis=1)
    bias = jnp.where(live, 0.0, BIG).astype(jnp.float32)
    bias = jnp.roll(bias, -my_half * half, axis=1)
    bias = jnp.broadcast_to(bias.reshape(rows // ROW_GROUP, 1, ROW_GROUP, 1, row_size),
                            (rows // ROW_GROUP, col_size, ROW_GROUP, cols, row_size)).reshape(-1, row_size)
    near_bias, far_bias = bias[:, :half], bias[:, half:]

    asked, residual, near, far_by, near_bias, far_bias = lax.optimization_barrier(
        (asked, residual, near, asked_by[:, 1], near_bias, far_bias))
    far = swap(pick(mirrored, far_by))
    state = first_tiles(asked, near_bias, near)
    answers = last_tiles(asked, far_bias, far, state, 0, col_size, cols)

    final = residual
    for step in range(col_size):
        answer = lax.ppermute(answers[step], "cols", turn(col_size, step)) if step else answers[0]
        start = (col_me - step) % col_size * group_width
        final = final + dot_rows(answer, lax.dynamic_slice_in_dim(w_tile_out, start, group_width, 0))
    return final.astype(jnp.bfloat16).reshape(rows, cols, width)


def solution(mesh):
    row_size, col_size = mesh.shape["rows"], mesh.shape["cols"]
    placed = (P("rows", "cols", None), P(), P(), P(), P(), P(), P(), P("rows", None, "cols", None),
              P("rows", None), P("rows", None))

    def body(*arrays):
        return shards(row_size, col_size, *arrays)

    return jax.shard_map(body, mesh=mesh, in_specs=placed, out_specs=P("rows", "cols", None), check_vma=False)
```

```python
import functools

import jax
import jax.numpy as jnp
from jax import lax
from jax.experimental import pallas as pl
from jax.experimental.pallas import tpu as pltpu
from jax.sharding import PartitionSpec as P

ROW_GROUP = 16
BIG = -1e30
MIB = 1024 * 1024
VMEM = pl.BlockSpec(memory_space=pltpu.VMEM)


def params(rows):
    return pltpu.CompilerParams(vmem_limit_bytes=(14 if rows <= 512 else 48) * MIB)


def dot_rows(left, right):
    return lax.dot_general(left, right, (((1,), (0,)), ((), ())), preferred_element_type=jnp.float32)


def dot_lanes(left, right):
    return lax.dot_general(left, right, (((1,), (1,)), ((), ())), preferred_element_type=jnp.float32)


def rms_scale(values, gain_vec):
    mean_sq = jnp.mean(values * values, axis=-1, keepdims=True)
    return values * lax.rsqrt(mean_sq + 1e-05) * gain_vec


def iota(shape, dim):
    return lax.broadcasted_iota(jnp.int32, shape, dim)


def pick_kernel(count, wanted_ref, tiles_ref, out_ref):
    for peer in range(count):
        out_ref[peer] = tiles_ref[wanted_ref[peer]]


def pick(tiles, wanted):
    count = wanted.shape[0]
    return pl.pallas_call(
        functools.partial(pick_kernel, count),
        out_shape=jax.ShapeDtypeStruct((count,) + tiles.shape[1:], tiles.dtype),
        in_specs=[pl.BlockSpec(memory_space=pltpu.SMEM), VMEM],
        out_specs=VMEM,
        compiler_params=params(0),
        cost_estimate=pl.CostEstimate(flops=0, bytes_accessed=2 * MIB, transcendentals=0),
        name="pick",
    )(wanted, tiles)


def front_kernel(groups, heads, head_size, chunk, cols, row_size, *refs):
    cell_refs, refs = refs[:groups], refs[groups:]
    (holder_ref, mask_ref, gain_col_ref, w_qkv_ref, w_out_ref, gain_tile_ref, w_query_ref,
     resid_ref, asked_ref, normed_ref, packed_ref) = refs
    own_rows, width = cell_refs[0].shape
    steps = own_rows // chunk
    span = groups * chunk
    lanes_two = 2 * head_size
    for step in range(steps):
        for group in range(groups):
            cells = cell_refs[group][pl.ds(step * chunk, chunk), :].astype(jnp.float32)
            normed_ref[pl.ds(step * span + group * chunk, chunk), :] = rms_scale(cells, gain_col_ref[...]).astype(jnp.bfloat16)
    for part in range(3):
        packed_ref[part] = dot_rows(normed_ref[...], w_qkv_ref[:, pl.ds(part * width, width)]).astype(jnp.bfloat16)
    stacked = heads * span
    same_row = iota((stacked, span), 0) % chunk // cols == iota((stacked, span), 1) % chunk // cols
    lane_low = iota((span, lanes_two), 1) < head_size
    scale = head_size ** (-0.5)
    for step in range(steps):
        rows = pl.ds(step * span, span)
        scores = []
        for head in range(heads):
            lanes = pl.ds(head // 2 * lanes_two, lanes_two)
            query = packed_ref[0, rows, lanes]
            query = jnp.where(lane_low == (head % 2 == 0), query, jnp.zeros_like(query))
            scores.append(dot_lanes(query, packed_ref[1, rows, lanes]))
        scores = jnp.where(same_row, jnp.concatenate(scores, axis=0) * scale, BIG)
        expo = jnp.exp(scores - jnp.max(scores, axis=1, keepdims=True))
        weights = (expo / jnp.sum(expo, axis=1, keepdims=True)).astype(jnp.bfloat16)
        for pair in range(heads // 2):
            lanes = pl.ds(pair * lanes_two, lanes_two)
            start = 2 * pair * span
            mixed = dot_rows(weights[start:start + 2 * span], packed_ref[2, rows, lanes])
            normed_ref[rows, lanes] = jnp.where(lane_low, mixed[:span], mixed[span:]).astype(jnp.bfloat16)
    delta = dot_rows(normed_ref[...], w_out_ref[...])
    for step in range(steps):
        for group in range(groups):
            start = step * span + group * chunk
            resid = cell_refs[group][pl.ds(step * chunk, chunk), :].astype(jnp.float32) + delta[start:start + chunk]
            if group == 0:
                resid_ref[pl.ds(step * chunk, chunk), :] = resid
            normed_ref[pl.ds(start, chunk), :] = rms_scale(resid, gain_tile_ref[...]).astype(jnp.bfloat16)
    slots = mask_ref.shape[1]
    place = (holder_ref[...] + head_size == iota((slots, lanes_two), 1)).astype(jnp.bfloat16)
    live = dot_rows((mask_ref[...] > 0).astype(jnp.bfloat16), place)
    lane = iota(live.shape, 1)
    shut = jnp.where((lane >= head_size) & (lane < head_size + row_size) & (live < 0.5), 1.0, 0.0).astype(jnp.bfloat16)
    total = steps * span
    cell = iota((total, shut.shape[0]), 0)
    row_of = cell // span * (chunk // cols) + cell % chunk // cols
    spread = (row_of == iota((total, shut.shape[0]), 1)).astype(jnp.bfloat16)
    bias = dot_rows(spread, shut) * BIG
    asked = dot_rows(normed_ref[...], w_query_ref[...]).astype(jnp.bfloat16).astype(jnp.float32) * scale
    heads_here = asked.shape[1] // head_size
    low = iota((total, lanes_two), 1) < head_size
    for head in range(heads_here):
        if heads_here % 2 == 0:
            two = asked[:, head // 2 * lanes_two:(head // 2 + 1) * lanes_two]
            one = two if head % 2 == 0 else pltpu.roll(two, head_size, 1)
            query = jnp.where(low, one, bias)
        else:
            one = asked[:, head * head_size:(head + 1) * head_size]
            query = jnp.concatenate([one, bias[:, head_size:]], axis=1)
        asked_ref[:, pl.ds(head * lanes_two, lanes_two)] = query.astype(jnp.bfloat16)


def front(cells, holder, key_mask, gain_col, w_qkv, w_out, gain_tile, w_query, heads, head_size, cols, row_size):
    groups = len(cells)
    own_rows, width = cells[0].shape
    total = groups * own_rows
    asked_width = 2 * w_query.shape[1]
    return pl.pallas_call(
        functools.partial(front_kernel, groups, heads, head_size, ROW_GROUP * cols, cols, row_size),
        out_shape=(jax.ShapeDtypeStruct((own_rows, width), jnp.float32),
                   jax.ShapeDtypeStruct((total, asked_width), jnp.bfloat16)),
        in_specs=[VMEM] * (groups + 7),
        out_specs=(VMEM, VMEM),
        scratch_shapes=[pltpu.VMEM((total, width), jnp.bfloat16), pltpu.VMEM((3, total, width), jnp.bfloat16)],
        compiler_params=params(total),
        cost_estimate=pl.CostEstimate(flops=2 * total * width * (4 * width + asked_width), bytes_accessed=4 * MIB,
                                      transcendentals=total * heads * 128),
        name="front",
    )(*cells, holder, key_mask, gain_col.reshape(1, width), w_qkv, w_out, gain_tile.reshape(1, width), w_query)


def weigh(query, tiles, first_holder):
    slots, keys, lanes = tiles.shape
    half = lanes // 2
    lane = iota(tiles.shape, 2)
    slot = iota(tiles.shape, 0)
    marks = (lane == slot + (half + first_holder)).astype(tiles.dtype)
    key_part = jnp.where(lane < half, tiles, marks).reshape(slots * keys, lanes)
    val_part = jnp.where(lane < half, jnp.ones_like(tiles), tiles).reshape(slots * keys, lanes)
    scores = dot_lanes(query, key_part)
    top = jnp.max(scores, axis=1, keepdims=True)
    return top, dot_rows(jnp.exp(scores - top).astype(jnp.bfloat16), val_part)


def first_kernel(heads, block, asked_ref, tiles_ref, sums_ref, tops_ref):
    rows_all, lanes = asked_ref.shape[0], tiles_ref.shape[3]
    lane = iota((block, lanes), 1)
    for step in range(rows_all // block):
        rows = pl.ds(step * block, block)
        tops = jnp.zeros((block, lanes), jnp.float32)
        for head in range(heads):
            top, sums_ref[head, rows, :] = weigh(asked_ref[rows, pl.ds(head * lanes, lanes)], tiles_ref[:, head], 0)
            tops = jnp.where(lane == head, top, tops)
        tops_ref[rows, :] = tops


def first_tiles(asked, tiles):
    slots, heads, keys, lanes = tiles.shape
    rows = asked.shape[0]
    return pl.pallas_call(
        functools.partial(first_kernel, heads, rows if rows <= 512 else 128),
        out_shape=(jax.ShapeDtypeStruct((heads, rows, lanes), jnp.float32), jax.ShapeDtypeStruct((rows, lanes), jnp.float32)),
        in_specs=[VMEM] * 2,
        out_specs=(VMEM, VMEM),
        compiler_params=params(rows),
        cost_estimate=pl.CostEstimate(flops=4 * rows * heads * slots * keys * lanes, bytes_accessed=4 * MIB,
                                      transcendentals=rows * heads * slots * keys),
        name="first_tiles",
    )(asked, tiles)


def last_kernel(groups, first_holder, first_head, heads, chunk, asked_ref, tiles_ref, sums_ref, tops_ref, *out_refs):
    rows_all, lanes = asked_ref.shape[0], tiles_ref.shape[3]
    half = lanes // 2
    span = groups * chunk
    block = rows_all if rows_all <= 512 else span
    lane_low = iota((block, lanes), 1) < half

    def put(step, values, lane, lane_count):
        for part in range(block // span):
            for group in range(groups):
                start = part * span + group * chunk
                place = pl.ds(step * (block // groups) + part * chunk, chunk)
                out_refs[group][place, pl.ds(lane, lane_count)] = values[start:start + chunk]

    for step in range(rows_all // block):
        rows = pl.ds(step * block, block)
        low = None
        for head in range(heads):
            here = first_head + head
            top, sums = weigh(asked_ref[rows, pl.ds(here * lanes, lanes)], tiles_ref[:, head], first_holder)
            old_top = tops_ref[rows, here:here + 1]
            new_top = jnp.maximum(top, old_top)
            sums = sums_ref[here, rows, :] * jnp.exp(old_top - new_top) + sums * jnp.exp(top - new_top)
            turned = pltpu.roll(sums, half, 1)
            if heads % 2:
                put(step, (sums / turned)[:, half:].astype(jnp.bfloat16), head * half, half)
            elif head % 2 == 0:
                low = turned / sums
            else:
                put(step, jnp.where(lane_low, low, sums / turned).astype(jnp.bfloat16), head // 2 * lanes, lanes)


def last_tiles(asked, tiles, sums, tops, first_holder, first_head, groups, cols):
    slots, heads, keys, lanes = tiles.shape
    rows = asked.shape[0]
    out = jax.ShapeDtypeStruct((rows // groups, heads * lanes // 2), jnp.bfloat16)
    return pl.pallas_call(
        functools.partial(last_kernel, groups, first_holder, first_head, heads, ROW_GROUP * cols),
        out_shape=(out,) * groups,
        in_specs=[VMEM] * 4,
        out_specs=(VMEM,) * groups,
        compiler_params=params(rows),
        cost_estimate=pl.CostEstimate(flops=4 * rows * heads * slots * keys * lanes, bytes_accessed=4 * MIB,
                                      transcendentals=rows * heads * slots * keys),
        name="last_tiles",
    )(asked, tiles, sums, tops)


def turn(size, step):
    return [(src, (src + step) % size) for src in range(size)]


def shards(row_size, col_size, fact_cells, gain_col, w_qkv, w_col_out, gain_tile, w_query, w_tile_out,
           tile_kv, tile_ids, key_mask):
    rows, cols, width = fact_cells.shape
    tiles_here, keys, heads_here, lanes = tile_kv.shape
    head_size = lanes // 2
    heads_all = width // head_size
    group_width = heads_here * head_size
    half = row_size // 2
    col_me = lax.axis_index("cols")
    my_half = lax.axis_index("rows") // half
    halves = [list(range(half)), list(range(half, row_size))]
    assert row_size <= head_size and row_size % 2 == 0

    def swap(value):
        return lax.all_to_all(value, "rows", split_axis=0, concat_axis=0, tiled=True, axis_index_groups=halves)

    heads_first = jnp.transpose(tile_kv, (0, 2, 1, 3))
    mirrored = lax.ppermute(heads_first, "rows", turn(row_size, half))

    listed = tile_ids[0] >= 0
    holder = jnp.where(listed, (tile_ids[0] // tiles_here + my_half * half) % row_size, -1)
    wanted = jnp.sum(jnp.where(holder[:, None] == jnp.arange(row_size)[None, :], (tile_ids[0] % tiles_here)[:, None], 0), axis=0)
    asked_of = jnp.broadcast_to(wanted.astype(jnp.int32).reshape(2, half).T[:, :, None], (half, 2, 128))
    asked_by = swap(asked_of)[:, :, 0]

    cells = [fact_cells.reshape(rows * cols, width)]
    for step in range(1, col_size):
        cells.append(lax.ppermute(cells[0], "cols", turn(col_size, -step)))

    near = swap(pick(heads_first, asked_by[:, 0]))
    mirrored, near = lax.optimization_barrier((mirrored, near))
    far_sent = pick(mirrored, asked_by[:, 1])

    cells, far_sent = lax.optimization_barrier((cells, far_sent))
    far = swap(far_sent)
    query_here = lax.dynamic_slice_in_dim(w_query, col_me * group_width, group_width, 1)
    residual, asked = front(cells, holder[:, None], key_mask, gain_col, w_qkv, w_col_out, gain_tile, query_here,
                            heads_all, head_size, cols, row_size)
    sums, tops = first_tiles(asked, near)
    answers = last_tiles(asked, far, sums, tops, half, 0, col_size, cols)

    final = residual
    for step in range(col_size):
        answer = lax.ppermute(answers[step], "cols", turn(col_size, step)) if step else answers[0]
        start = (col_me - step) % col_size * group_width
        final = final + dot_rows(answer, lax.dynamic_slice_in_dim(w_tile_out, start, group_width, 0))
    return final.astype(jnp.bfloat16).reshape(rows, cols, width)


def solution(mesh):
    row_size, col_size = mesh.shape["rows"], mesh.shape["cols"]
    placed = (P("rows", "cols", None), P(), P(), P(), P(), P(), P(), P("rows", None, "cols", None),
              P("rows", None), P("rows", None))

    def body(*arrays):
        return shards(row_size, col_size, *arrays)

    return jax.shard_map(body, mesh=mesh, in_specs=placed, out_specs=P("rows", "cols", None), check_vma=False)
```

```python
import functools

import jax
import jax.numpy as jnp
from jax import lax
from jax.experimental import pallas as pl
from jax.experimental.pallas import tpu as pltpu
from jax.sharding import PartitionSpec as P

ROW_GROUP = 16
BIG = -1e30
MIB = 1024 * 1024
VMEM = pl.BlockSpec(memory_space=pltpu.VMEM)
HBM = pl.BlockSpec(memory_space=pltpu.HBM)
ANY = pl.BlockSpec(memory_space=pl.ANY)


def params(rows):
    return pltpu.CompilerParams(vmem_limit_bytes=(14 if rows <= 512 else 48) * MIB)


def dot_rows(left, right):
    return lax.dot_general(left, right, (((1,), (0,)), ((), ())), preferred_element_type=jnp.float32)


def dot_lanes(left, right):
    return lax.dot_general(left, right, (((1,), (1,)), ((), ())), preferred_element_type=jnp.float32)


def rms_scale(values, gain_vec):
    mean_sq = jnp.mean(values * values, axis=-1, keepdims=True)
    return values * lax.rsqrt(mean_sq + 1e-05) * gain_vec


def iota(shape, dim):
    return lax.broadcasted_iota(jnp.int32, shape, dim)


def pick_kernel(count, wanted_ref, tiles_ref, after_ref, out_ref):
    for peer in range(count):
        out_ref[peer] = tiles_ref[wanted_ref[peer]]


def pick(tiles, wanted, after):
    count = wanted.shape[0]
    return pl.pallas_call(
        functools.partial(pick_kernel, count),
        out_shape=jax.ShapeDtypeStruct((count,) + tiles.shape[1:], tiles.dtype),
        in_specs=[pl.BlockSpec(memory_space=pltpu.SMEM), VMEM, ANY],
        out_specs=VMEM,
        compiler_params=params(0),
        cost_estimate=pl.CostEstimate(flops=0, bytes_accessed=2 * MIB, transcendentals=0),
        name="pick",
    )(wanted, tiles, after)


def front_kernel(groups, heads, head_size, chunk, cols, row_size, *refs):
    cell_refs, refs = refs[:groups], refs[groups:]
    (holder_ref, mask_ref, gain_col_ref, w_qkv_ref, w_out_ref, gain_tile_ref, w_query_ref,
     after_ref, resid_ref, asked_hbm, normed_ref, packed_ref, asked_ref, sem) = refs
    own_rows, width = cell_refs[0].shape
    steps = own_rows // chunk
    span = groups * chunk
    lanes_two = 2 * head_size
    for step in range(steps):
        for group in range(groups):
            cells = cell_refs[group][pl.ds(step * chunk, chunk), :].astype(jnp.float32)
            normed_ref[pl.ds(step * span + group * chunk, chunk), :] = rms_scale(cells, gain_col_ref[...]).astype(jnp.bfloat16)
    for part in range(3):
        packed_ref[part] = dot_rows(normed_ref[...], w_qkv_ref[:, pl.ds(part * width, width)]).astype(jnp.bfloat16)
    stacked = heads * span
    same_row = iota((stacked, span), 0) % chunk // cols == iota((stacked, span), 1) % chunk // cols
    lane_low = iota((span, lanes_two), 1) < head_size
    scale = head_size ** (-0.5)
    for step in range(steps):
        rows = pl.ds(step * span, span)
        scores = []
        for head in range(heads):
            lanes = pl.ds(head // 2 * lanes_two, lanes_two)
            query = packed_ref[0, rows, lanes]
            query = jnp.where(lane_low == (head % 2 == 0), query, jnp.zeros_like(query))
            scores.append(dot_lanes(query, packed_ref[1, rows, lanes]))
        scores = jnp.where(same_row, jnp.concatenate(scores, axis=0) * scale, BIG)
        expo = jnp.exp(scores - jnp.max(scores, axis=1, keepdims=True))
        weights = (expo / jnp.sum(expo, axis=1, keepdims=True)).astype(jnp.bfloat16)
        for pair in range(heads // 2):
            lanes = pl.ds(pair * lanes_two, lanes_two)
            start = 2 * pair * span
            mixed = dot_rows(weights[start:start + 2 * span], packed_ref[2, rows, lanes])
            normed_ref[rows, lanes] = jnp.where(lane_low, mixed[:span], mixed[span:]).astype(jnp.bfloat16)
    delta = dot_rows(normed_ref[...], w_out_ref[...])
    for step in range(steps):
        for group in range(groups):
            start = step * span + group * chunk
            resid = cell_refs[group][pl.ds(step * chunk, chunk), :].astype(jnp.float32) + delta[start:start + chunk]
            if group == 0:
                resid_ref[pl.ds(step * chunk, chunk), :] = resid
            normed_ref[pl.ds(start, chunk), :] = rms_scale(resid, gain_tile_ref[...]).astype(jnp.bfloat16)
    slots = mask_ref.shape[1]
    place = (holder_ref[...] + head_size == iota((slots, lanes_two), 1)).astype(jnp.bfloat16)
    live = dot_rows((mask_ref[...] > 0).astype(jnp.bfloat16), place)
    lane = iota(live.shape, 1)
    shut = jnp.where((lane >= head_size) & (lane < head_size + row_size) & (live < 0.5), 1.0, 0.0).astype(jnp.bfloat16)
    total = steps * span
    cell = iota((total, shut.shape[0]), 0)
    row_of = cell // span * (chunk // cols) + cell % chunk // cols
    spread = (row_of == iota((total, shut.shape[0]), 1)).astype(jnp.bfloat16)
    bias = dot_rows(spread, shut) * BIG
    asked = dot_rows(normed_ref[...], w_query_ref[...]).astype(jnp.bfloat16).astype(jnp.float32) * scale
    heads_here = asked.shape[1] // head_size
    low = iota((total, lanes_two), 1) < head_size
    for head in range(heads_here):
        if heads_here % 2 == 0:
            two = asked[:, head // 2 * lanes_two:(head // 2 + 1) * lanes_two]
            one = two if head % 2 == 0 else pltpu.roll(two, head_size, 1)
            query = jnp.where(low, one, bias)
        else:
            one = asked[:, head * head_size:(head + 1) * head_size]
            query = jnp.concatenate([one, bias[:, head_size:]], axis=1)
        asked_ref[head] = query.astype(jnp.bfloat16)
    copy = pltpu.make_async_copy(asked_ref, asked_hbm, sem)
    copy.start()
    copy.wait()


def front(cells, holder, key_mask, gain_col, w_qkv, w_out, gain_tile, w_query, heads, head_size, cols, row_size, after):
    groups = len(cells)
    own_rows, width = cells[0].shape
    total = groups * own_rows
    asked_shape = (w_query.shape[1] // head_size, total, 2 * head_size)
    return pl.pallas_call(
        functools.partial(front_kernel, groups, heads, head_size, ROW_GROUP * cols, cols, row_size),
        out_shape=(jax.ShapeDtypeStruct((own_rows, width), jnp.float32),
                   jax.ShapeDtypeStruct(asked_shape, jnp.bfloat16)),
        in_specs=[VMEM] * (groups + 7) + [ANY],
        out_specs=(VMEM, HBM),
        scratch_shapes=[pltpu.VMEM((total, width), jnp.bfloat16), pltpu.VMEM((3, total, width), jnp.bfloat16),
                        pltpu.VMEM(asked_shape, jnp.bfloat16), pltpu.SemaphoreType.DMA],
        compiler_params=params(total),
        cost_estimate=pl.CostEstimate(flops=2 * total * width * 5 * width, bytes_accessed=4 * MIB,
                                      transcendentals=total * heads * 128),
        name="front",
    )(*cells, holder, key_mask, gain_col.reshape(1, width), w_qkv, w_out, gain_tile.reshape(1, width), w_query, after)


def weigh(query, tiles, first_holder):
    slots, keys, lanes = tiles.shape
    half = lanes // 2
    lane = iota(tiles.shape, 2)
    slot = iota(tiles.shape, 0)
    marks = (lane == slot + (half + first_holder)).astype(tiles.dtype)
    key_part = jnp.where(lane < half, tiles, marks).reshape(slots * keys, lanes)
    val_part = jnp.where(lane < half, jnp.ones_like(tiles), tiles).reshape(slots * keys, lanes)
    scores = dot_lanes(query, key_part)
    top = jnp.max(scores, axis=1, keepdims=True)
    return top, dot_rows(jnp.exp(scores - top).astype(jnp.bfloat16), val_part)


def first_kernel(block, asked_hbm, tiles_ref, state_hbm, asked_ref, state_ref, sems):
    heads, rows_all, lanes = asked_hbm.shape
    lane = iota((block, lanes), 1)
    copies = [pltpu.make_async_copy(asked_hbm.at[head], asked_ref.at[head], sems.at[head]) for head in range(heads)]
    for copy in copies:
        copy.start()
    for step in range(rows_all // block):
        rows = pl.ds(step * block, block)
        tops = jnp.zeros((block, lanes), jnp.float32)
        for head in range(heads):
            if step == 0:
                copies[head].wait()
            top, state_ref[head, rows, :] = weigh(asked_ref[head, rows, :], tiles_ref[:, head], 0)
            tops = jnp.where(lane == head, top, tops)
        state_ref[heads, rows, :] = tops
    copy = pltpu.make_async_copy(state_ref, state_hbm, sems.at[heads])
    copy.start()
    copy.wait()


def first_tiles(asked, tiles):
    slots, heads, keys, lanes = tiles.shape
    rows = asked.shape[1]
    state_shape = (heads + 1, rows, lanes)
    return pl.pallas_call(
        functools.partial(first_kernel, rows if rows <= 512 else 128),
        out_shape=jax.ShapeDtypeStruct(state_shape, jnp.float32),
        in_specs=[HBM, VMEM],
        out_specs=HBM,
        scratch_shapes=[pltpu.VMEM(asked.shape, jnp.bfloat16), pltpu.VMEM(state_shape, jnp.float32),
                        pltpu.SemaphoreType.DMA((heads + 1,))],
        compiler_params=params(rows),
        cost_estimate=pl.CostEstimate(flops=4 * rows * heads * slots * keys * lanes, bytes_accessed=4 * MIB,
                                      transcendentals=rows * heads * slots * keys),
        name="first_tiles",
    )(asked, tiles)


def last_kernel(groups, first_holder, first_head, heads, chunk, asked_hbm, tiles_ref, state_hbm, *refs):
    out_refs, (asked_ref, state_ref, tops_ref, sems) = refs[:groups], refs[groups:]
    heads_here, rows_all, lanes = asked_hbm.shape
    half = lanes // 2
    span = groups * chunk
    block = rows_all if rows_all <= 512 else span
    lane_low = iota((block, lanes), 1) < half

    def put(step, values, lane, lane_count):
        for part in range(block // span):
            for group in range(groups):
                start = part * span + group * chunk
                place = pl.ds(step * (block // groups) + part * chunk, chunk)
                out_refs[group][place, pl.ds(lane, lane_count)] = values[start:start + chunk]

    copies = [pltpu.make_async_copy(asked_hbm.at[first_head + head], asked_ref.at[head], sems.at[head]) for head in range(heads)]
    copies.append(pltpu.make_async_copy(state_hbm.at[pl.ds(first_head, heads)], state_ref, sems.at[heads]))
    copies.append(pltpu.make_async_copy(state_hbm.at[heads_here], tops_ref, sems.at[heads + 1]))
    for copy in copies:
        copy.start()
    for step in range(rows_all // block):
        rows = pl.ds(step * block, block)
        low = None
        for head in range(heads):
            if step == 0:
                copies[head].wait()
            top, sums = weigh(asked_ref[head, rows, :], tiles_ref[:, head], first_holder)
            if step == 0 and head == 0:
                copies[heads].wait()
                copies[heads + 1].wait()
            old_top = tops_ref[rows, first_head + head:first_head + head + 1]
            new_top = jnp.maximum(top, old_top)
            sums = state_ref[head, rows, :] * jnp.exp(old_top - new_top) + sums * jnp.exp(top - new_top)
            turned = pltpu.roll(sums, half, 1)
            if head % 2:
                put(step, jnp.where(lane_low, low, sums / turned).astype(jnp.bfloat16), head // 2 * lanes, lanes)
            elif head + 1 < heads:
                low = turned / sums
            else:
                put(step, (turned / sums)[:, :half].astype(jnp.bfloat16), head * half, half)


def last_tiles(asked, tiles, state, first_holder, first_head, groups, cols):
    slots, heads, keys, lanes = tiles.shape
    rows = asked.shape[1]
    out = jax.ShapeDtypeStruct((rows // groups, heads * lanes // 2), jnp.bfloat16)
    return pl.pallas_call(
        functools.partial(last_kernel, groups, first_holder, first_head, heads, ROW_GROUP * cols),
        out_shape=(out,) * groups,
        in_specs=[HBM, VMEM, HBM],
        out_specs=(VMEM,) * groups,
        scratch_shapes=[pltpu.VMEM((heads, rows, lanes), jnp.bfloat16), pltpu.VMEM((heads, rows, lanes), jnp.float32),
                        pltpu.VMEM((rows, lanes), jnp.float32), pltpu.SemaphoreType.DMA((heads + 2,))],
        compiler_params=params(rows),
        cost_estimate=pl.CostEstimate(flops=4 * rows * heads * slots * keys * lanes, bytes_accessed=4 * MIB,
                                      transcendentals=rows * heads * slots * keys),
        name="last_tiles",
    )(asked, tiles, state)


def turn(size, step):
    return [(src, (src + step) % size) for src in range(size)]


def shards(row_size, col_size, fact_cells, gain_col, w_qkv, w_col_out, gain_tile, w_query, w_tile_out,
           tile_kv, tile_ids, key_mask):
    rows, cols, width = fact_cells.shape
    tiles_here, keys, heads_here, lanes = tile_kv.shape
    head_size = lanes // 2
    heads_all = width // head_size
    group_width = heads_here * head_size
    half = row_size // 2
    col_me = lax.axis_index("cols")
    my_half = lax.axis_index("rows") // half
    halves = [list(range(half)), list(range(half, row_size))]
    assert row_size <= head_size and row_size % 2 == 0

    def swap(value):
        return lax.all_to_all(value, "rows", split_axis=0, concat_axis=0, tiled=True, axis_index_groups=halves)

    parts = [(0, heads_here - 1), (heads_here - 1, heads_here)] if heads_here > 1 else [(0, 1)]
    heads_first = jnp.transpose(tile_kv, (0, 2, 1, 3))
    mirrored = [lax.ppermute(heads_first[:, low:high], "rows", turn(row_size, half)) for low, high in parts]

    listed = tile_ids[0] >= 0
    holder = jnp.where(listed, (tile_ids[0] // tiles_here + my_half * half) % row_size, -1)
    wanted = jnp.sum(jnp.where(holder[:, None] == jnp.arange(row_size)[None, :], (tile_ids[0] % tiles_here)[:, None], 0), axis=0)
    asked_of = jnp.broadcast_to(wanted.astype(jnp.int32).reshape(2, half).T[:, :, None], (half, 2, 128))
    asked_by = swap(asked_of)[:, :, 0]

    cells = [fact_cells.reshape(rows * cols, width)]
    for step in range(1, col_size):
        cells.append(lax.ppermute(cells[0], "cols", turn(col_size, -step)))

    near_by, far_by = asked_by[:, 0], asked_by[:, 1]
    sent = pick(heads_first, near_by, mirrored[0])
    near = swap(sent)
    far = []
    for arrived in mirrored:
        sent = pick(arrived, far_by, sent)
        far.append(swap(sent))
    query_here = lax.dynamic_slice_in_dim(w_query, col_me * group_width, group_width, 1)
    residual, asked = front(cells, holder[:, None], key_mask, gain_col, w_qkv, w_col_out, gain_tile, query_here,
                            heads_all, head_size, cols, row_size, sent)
    state = first_tiles(asked, near)

    final = residual
    for (low, high), tiles in zip(parts, far):
        answers = last_tiles(asked, tiles, state, half, low, col_size, cols)
        for step in range(col_size):
            answer = lax.ppermute(answers[step], "cols", turn(col_size, step)) if step else answers[0]
            start = (col_me - step) % col_size * group_width + low * head_size
            weight = lax.dynamic_slice_in_dim(w_tile_out, start, (high - low) * head_size, 0)
            final = final + dot_rows(answer, weight)
    return final.astype(jnp.bfloat16).reshape(rows, cols, width)


def solution(mesh):
    row_size, col_size = mesh.shape["rows"], mesh.shape["cols"]
    placed = (P("rows", "cols", None), P(), P(), P(), P(), P(), P(), P("rows", None, "cols", None),
              P("rows", None), P("rows", None))

    def body(*arrays):
        return shards(row_size, col_size, *arrays)

    return jax.shard_map(body, mesh=mesh, in_specs=placed, out_specs=P("rows", "cols", None), check_vma=False)
```

```python
import functools

import jax
import jax.numpy as jnp
from jax import lax
from jax.experimental import pallas as pl
from jax.experimental.pallas import tpu as pltpu
from jax.sharding import PartitionSpec as P

ROW_GROUP = 16
BIG = -1e30
MIB = 1024 * 1024
VMEM = pl.BlockSpec(memory_space=pltpu.VMEM)
ANY = pl.BlockSpec(memory_space=pl.ANY)


def params(rows):
    return pltpu.CompilerParams(vmem_limit_bytes=(20 if rows <= 512 else 48) * MIB)


def dot_rows(left, right):
    return lax.dot_general(left, right, (((1,), (0,)), ((), ())), preferred_element_type=jnp.float32)


def dot_lanes(left, right):
    return lax.dot_general(left, right, (((1,), (1,)), ((), ())), preferred_element_type=jnp.float32)


def rms_scale(values, gain_vec):
    mean_sq = jnp.mean(values * values, axis=-1, keepdims=True)
    return values * lax.rsqrt(mean_sq + 1e-05) * gain_vec


def iota(shape, dim):
    return lax.broadcasted_iota(jnp.int32, shape, dim)


def pick_kernel(parts, wanted_ref, *refs):
    tile_refs, out_ref = refs[:parts], refs[-1]
    for peer in range(out_ref.shape[0]):
        low = 0
        for tiles_ref in tile_refs:
            high = low + tiles_ref.shape[1]
            out_ref[peer, low:high] = tiles_ref[wanted_ref[peer]]
            low = high


def pick(tiles, wanted, after):
    count = wanted.shape[0]
    heads = sum(part.shape[1] for part in tiles)
    return pl.pallas_call(
        functools.partial(pick_kernel, len(tiles)),
        out_shape=jax.ShapeDtypeStruct((count, heads) + tiles[0].shape[2:], tiles[0].dtype),
        in_specs=[pl.BlockSpec(memory_space=pltpu.SMEM)] + [VMEM] * len(tiles) + [ANY] * len(after),
        out_specs=VMEM,
        compiler_params=params(0),
        cost_estimate=pl.CostEstimate(flops=0, bytes_accessed=2 * MIB, transcendentals=0),
        name="pick",
    )(wanted, *tiles, *after)


def pick_each_kernel(wanted_ref, me_ref, tiles_ref, *refs):
    out_refs = refs[-wanted_ref.shape[0]:]
    for step, out_ref in enumerate(out_refs):
        out_ref[...] = tiles_ref[wanted_ref[me_ref[0] ^ step]]


def pick_each(tiles, wanted, me, after):
    count = wanted.shape[0]
    smem = pl.BlockSpec(memory_space=pltpu.SMEM)
    return pl.pallas_call(
        pick_each_kernel,
        out_shape=(jax.ShapeDtypeStruct(tiles.shape[1:], tiles.dtype),) * count,
        in_specs=[smem, smem, VMEM] + [ANY] * len(after),
        out_specs=(VMEM,) * count,
        compiler_params=params(0),
        cost_estimate=pl.CostEstimate(flops=0, bytes_accessed=2 * MIB, transcendentals=0),
        name="pick_each",
    )(wanted, me, tiles, *after)


def front_kernel(groups, heads, head_size, chunk, cols, row_size, *refs):
    cell_refs, refs = refs[:groups], refs[groups:]
    (holder_ref, mask_ref, gain_col_ref, w_qkv_ref, w_out_ref, gain_tile_ref, w_query_ref,
     after_ref, resid_ref, asked_ref, normed_ref, packed_ref) = refs
    own_rows, width = cell_refs[0].shape
    steps = own_rows // chunk
    span = groups * chunk
    lanes_two = 2 * head_size
    for step in range(steps):
        for group in range(groups):
            cells = cell_refs[group][pl.ds(step * chunk, chunk), :].astype(jnp.float32)
            normed_ref[pl.ds(step * span + group * chunk, chunk), :] = rms_scale(cells, gain_col_ref[...]).astype(jnp.bfloat16)
    for part in range(3):
        packed_ref[part] = dot_rows(normed_ref[...], w_qkv_ref[:, pl.ds(part * width, width)]).astype(jnp.bfloat16)
    stacked = heads * span
    same_row = iota((stacked, span), 0) % chunk // cols == iota((stacked, span), 1) % chunk // cols
    lane_low = iota((span, lanes_two), 1) < head_size
    scale = head_size ** (-0.5)
    for step in range(steps):
        rows = pl.ds(step * span, span)
        scores = []
        for head in range(heads):
            lanes = pl.ds(head // 2 * lanes_two, lanes_two)
            query = packed_ref[0, rows, lanes]
            query = jnp.where(lane_low == (head % 2 == 0), query, jnp.zeros_like(query))
            scores.append(dot_lanes(query, packed_ref[1, rows, lanes]))
        scores = jnp.where(same_row, jnp.concatenate(scores, axis=0) * scale, BIG)
        expo = jnp.exp(scores - jnp.max(scores, axis=1, keepdims=True))
        weights = (expo / jnp.sum(expo, axis=1, keepdims=True)).astype(jnp.bfloat16)
        for pair in range(heads // 2):
            lanes = pl.ds(pair * lanes_two, lanes_two)
            start = 2 * pair * span
            mixed = dot_rows(weights[start:start + 2 * span], packed_ref[2, rows, lanes])
            normed_ref[rows, lanes] = jnp.where(lane_low, mixed[:span], mixed[span:]).astype(jnp.bfloat16)
    delta = dot_rows(normed_ref[...], w_out_ref[...])
    for step in range(steps):
        for group in range(groups):
            start = step * span + group * chunk
            resid = cell_refs[group][pl.ds(step * chunk, chunk), :].astype(jnp.float32) + delta[start:start + chunk]
            if group == 0:
                resid_ref[pl.ds(step * chunk, chunk), :] = resid
            normed_ref[pl.ds(start, chunk), :] = rms_scale(resid, gain_tile_ref[...]).astype(jnp.bfloat16)
    slots = mask_ref.shape[1]
    place = (holder_ref[...] + head_size == iota((slots, lanes_two), 1)).astype(jnp.bfloat16)
    live = dot_rows((mask_ref[...] > 0).astype(jnp.bfloat16), place)
    lane = iota(live.shape, 1)
    shut = jnp.where((lane >= head_size) & (lane < head_size + row_size) & (live < 0.5), 1.0, 0.0).astype(jnp.bfloat16)
    total = steps * span
    cell = iota((total, shut.shape[0]), 0)
    row_of = cell // span * (chunk // cols) + cell % chunk // cols
    spread = (row_of == iota((total, shut.shape[0]), 1)).astype(jnp.bfloat16)
    bias = dot_rows(spread, shut) * BIG
    asked = dot_rows(normed_ref[...], w_query_ref[...]).astype(jnp.bfloat16).astype(jnp.float32) * scale
    heads_here = asked.shape[1] // head_size
    low = iota((total, lanes_two), 1) < head_size
    for head in range(heads_here):
        if heads_here % 2 == 0:
            two = asked[:, head // 2 * lanes_two:(head // 2 + 1) * lanes_two]
            one = two if head % 2 == 0 else pltpu.roll(two, head_size, 1)
            query = jnp.where(low, one, bias)
        else:
            one = asked[:, head * head_size:(head + 1) * head_size]
            query = jnp.concatenate([one, bias[:, head_size:]], axis=1)
        asked_ref[head] = query.astype(jnp.bfloat16)


def front(cells, holder, key_mask, gain_col, w_qkv, w_out, gain_tile, w_query, heads, head_size, cols, row_size, after):
    groups = len(cells)
    own_rows, width = cells[0].shape
    total = groups * own_rows
    asked_shape = (w_query.shape[1] // head_size, total, 2 * head_size)
    return pl.pallas_call(
        functools.partial(front_kernel, groups, heads, head_size, ROW_GROUP * cols, cols, row_size),
        out_shape=(jax.ShapeDtypeStruct((own_rows, width), jnp.float32),
                   jax.ShapeDtypeStruct(asked_shape, jnp.bfloat16)),
        in_specs=[VMEM] * (groups + 7) + [ANY],
        out_specs=(VMEM, VMEM),
        scratch_shapes=[pltpu.VMEM((total, width), jnp.bfloat16), pltpu.VMEM((3, total, width), jnp.bfloat16)],
        compiler_params=params(total),
        cost_estimate=pl.CostEstimate(flops=2 * total * width * 5 * width, bytes_accessed=4 * MIB,
                                      transcendentals=total * heads * 128),
        name="front",
    )(*cells, holder, key_mask, gain_col.reshape(1, width), w_qkv, w_out, gain_tile.reshape(1, width), w_query, after)


def weigh(query, tiles):
    slots, keys, lanes = tiles.shape
    half = lanes // 2
    lane = iota(tiles.shape, 2)
    marks = (lane == iota(tiles.shape, 0) + half).astype(tiles.dtype)
    key_part = jnp.where(lane < half, tiles, marks).reshape(slots * keys, lanes)
    val_part = jnp.where(lane < half, jnp.ones_like(tiles), tiles).reshape(slots * keys, lanes)
    scores = dot_lanes(query, key_part)
    top = jnp.max(scores, axis=1, keepdims=True)
    return dot_rows(jnp.exp(scores - top).astype(jnp.bfloat16), val_part)


def attend_kernel(groups, tile_count, chunk, asked_ref, *refs):
    tile_refs, out_refs = refs[:tile_count], refs[tile_count:]
    heads, rows_all, lanes = asked_ref.shape
    half = lanes // 2
    span = groups * chunk
    block = rows_all if rows_all <= 512 else span
    lane_low = iota((block, lanes), 1) < half

    def put(step, values, lane, lane_count):
        for part in range(block // span):
            for group in range(groups):
                start = part * span + group * chunk
                place = pl.ds(step * (block // groups) + part * chunk, chunk)
                out_refs[group][place, pl.ds(lane, lane_count)] = values[start:start + chunk]

    for step in range(rows_all // block):
        low = None
        for head in range(heads):
            tiles = jnp.concatenate([ref[:, head] for ref in tile_refs], axis=0)
            sums = weigh(asked_ref[head, pl.ds(step * block, block), :], tiles)
            turned = pltpu.roll(sums, half, 1)
            if head % 2:
                put(step, jnp.where(lane_low, low, sums / turned).astype(jnp.bfloat16), head // 2 * lanes, lanes)
            elif head + 1 < heads:
                low = turned / sums
            else:
                put(step, (turned / sums)[:, :half].astype(jnp.bfloat16), head * half, half)


def attend(asked, tiles, groups, cols):
    heads, rows, lanes = asked.shape
    keys = sum(part.shape[0] * part.shape[2] for part in tiles)
    out = jax.ShapeDtypeStruct((rows // groups, heads * lanes // 2), jnp.bfloat16)
    return pl.pallas_call(
        functools.partial(attend_kernel, groups, len(tiles), ROW_GROUP * cols),
        out_shape=(out,) * groups,
        in_specs=[VMEM] * (1 + len(tiles)),
        out_specs=(VMEM,) * groups,
        compiler_params=params(rows),
        cost_estimate=pl.CostEstimate(flops=4 * rows * heads * keys * lanes, bytes_accessed=4 * MIB,
                                      transcendentals=rows * heads * keys),
        name="attend",
    )(asked, *tiles)


def turn(size, step):
    return [(src, (src + step) % size) for src in range(size)]


def shards(row_size, col_size, fact_cells, gain_col, w_qkv, w_col_out, gain_tile, w_query, w_tile_out,
           tile_kv, tile_ids, key_mask):
    rows, cols, width = fact_cells.shape
    tiles_here, keys, heads_here, lanes = tile_kv.shape
    head_size = lanes // 2
    heads_all = width // head_size
    group_width = heads_here * head_size
    half = row_size // 2
    col_me = lax.axis_index("cols")
    row_me = lax.axis_index("rows")
    my_half, my_place = row_me // half, row_me % half
    halves = [list(range(half)), list(range(half, row_size))]
    assert row_size <= head_size and row_size % 2 == 0

    def swap(value):
        return lax.all_to_all(value, "rows", split_axis=0, concat_axis=0, tiled=True, axis_index_groups=halves)

    middle = max(heads_here // 2, 1)
    heads_first = jnp.transpose(tile_kv, (0, 2, 1, 3))
    mirrored = [lax.ppermute(heads_first[:, low:low + middle], "rows", turn(row_size, half))
                for low in range(0, heads_here, middle)]

    listed = tile_ids[0] >= 0
    holder = jnp.where(listed, (tile_ids[0] // tiles_here + my_half * half) % row_size, -1)
    wanted = jnp.sum(jnp.where(holder[:, None] == jnp.arange(row_size)[None, :], (tile_ids[0] % tiles_here)[:, None], 0), axis=0)
    asked_of = jnp.broadcast_to(wanted.astype(jnp.int32).reshape(2, half).T[:, :, None], (half, 2, 128))
    asked_by = swap(asked_of)[:, :, 0]

    cells = [fact_cells.reshape(rows * cols, width)]
    for step in range(1, col_size):
        cells.append(lax.ppermute(cells[0], "cols", turn(col_size, -step)))

    near_by, far_by = asked_by[:, 0], asked_by[:, 1]
    if half <= 8 and half & (half - 1) == 0:
        sent = pick_each(heads_first, near_by, my_place.reshape(1), mirrored[:1])
        near = [sent[0][None]]
        for step in range(1, half):
            pairs = [(row, row // half * half + (row % half ^ step)) for row in range(row_size)]
            near.append(lax.ppermute(sent[step][None], "rows", pairs))
        holder = jnp.where((holder >= 0) & (holder < half), holder ^ my_place, holder)
    else:
        near = [swap(pick([heads_first], near_by, mirrored[:1]))]
    sent = pick(mirrored, far_by, near)
    far = swap(sent)
    query_here = lax.dynamic_slice_in_dim(w_query, col_me * group_width, group_width, 1)
    residual, asked = front(cells, holder[:, None], key_mask, gain_col, w_qkv, w_col_out, gain_tile, query_here,
                            heads_all, head_size, cols, row_size, sent)
    answers = attend(asked, near + [far], col_size, cols)

    final = residual
    for step in range(col_size):
        answer = lax.ppermute(answers[step], "cols", turn(col_size, step)) if step else answers[0]
        start = (col_me - step) % col_size * group_width
        final = final + dot_rows(answer, lax.dynamic_slice_in_dim(w_tile_out, start, group_width, 0))
    return final.astype(jnp.bfloat16).reshape(rows, cols, width)


def solution(mesh):
    row_size, col_size = mesh.shape["rows"], mesh.shape["cols"]
    placed = (P("rows", "cols", None), P(), P(), P(), P(), P(), P(), P("rows", None, "cols", None),
              P("rows", None), P("rows", None))

    def body(*arrays):
        return shards(row_size, col_size, *arrays)

    return jax.shard_map(body, mesh=mesh, in_specs=placed, out_specs=P("rows", "cols", None), check_vma=False)
```

```python
import functools

import jax
import jax.numpy as jnp
from jax import lax
from jax.experimental import pallas as pl
from jax.experimental.pallas import tpu as pltpu
from jax.sharding import PartitionSpec as P

ROW_GROUP = 16
BIG = -1e30
MIB = 1024 * 1024
VMEM = pl.BlockSpec(memory_space=pltpu.VMEM)
ANY = pl.BlockSpec(memory_space=pl.ANY)


def params(rows):
    return pltpu.CompilerParams(vmem_limit_bytes=(20 if rows <= 512 else 48) * MIB)


def dot_rows(left, right):
    return lax.dot_general(left, right, (((1,), (0,)), ((), ())), preferred_element_type=jnp.float32)


def dot_lanes(left, right):
    return lax.dot_general(left, right, (((1,), (1,)), ((), ())), preferred_element_type=jnp.float32)


def rms_scale(values, gain_vec):
    mean_sq = jnp.mean(values * values, axis=-1, keepdims=True)
    return values * lax.rsqrt(mean_sq + 1e-05) * gain_vec


def iota(shape, dim):
    return lax.broadcasted_iota(jnp.int32, shape, dim)


def pick_kernel(parts, wanted_ref, *refs):
    tile_refs, out_ref = refs[:parts], refs[-1]
    for peer in range(out_ref.shape[0]):
        low = 0
        for tiles_ref in tile_refs:
            high = low + tiles_ref.shape[1]
            out_ref[peer, low:high] = tiles_ref[wanted_ref[peer]]
            low = high


def pick(tiles, wanted, after):
    count = wanted.shape[0]
    heads = sum(part.shape[1] for part in tiles)
    return pl.pallas_call(
        functools.partial(pick_kernel, len(tiles)),
        out_shape=jax.ShapeDtypeStruct((count, heads) + tiles[0].shape[2:], tiles[0].dtype),
        in_specs=[pl.BlockSpec(memory_space=pltpu.SMEM)] + [VMEM] * len(tiles) + [ANY] * len(after),
        out_specs=VMEM,
        compiler_params=params(0),
        cost_estimate=pl.CostEstimate(flops=0, bytes_accessed=2 * MIB, transcendentals=0),
        name="pick",
    )(wanted, *tiles, *after)


def pick_each_kernel(parts, wanted_ref, me_ref, *refs):
    tile_refs, out_refs = refs[:parts], refs[-wanted_ref.shape[0]:]
    for step, out_ref in enumerate(out_refs):
        tile = wanted_ref[me_ref[0] ^ step]
        low = 0
        for tiles_ref in tile_refs:
            high = low + tiles_ref.shape[1]
            out_ref[0, low:high] = tiles_ref[tile]
            low = high


def pick_each(tiles, wanted, me, after):
    count = wanted.shape[0]
    heads = sum(part.shape[1] for part in tiles)
    smem = pl.BlockSpec(memory_space=pltpu.SMEM)
    return pl.pallas_call(
        functools.partial(pick_each_kernel, len(tiles)),
        out_shape=(jax.ShapeDtypeStruct((1, heads) + tiles[0].shape[2:], tiles[0].dtype),) * count,
        in_specs=[smem, smem] + [VMEM] * len(tiles) + [ANY] * len(after),
        out_specs=(VMEM,) * count,
        compiler_params=params(0),
        cost_estimate=pl.CostEstimate(flops=0, bytes_accessed=2 * MIB, transcendentals=0),
        name="pick_each",
    )(wanted, me, *tiles, *after)


def front_kernel(groups, heads, head_size, chunk, cols, row_size, *refs):
    cell_refs, refs = refs[:groups], refs[groups:]
    (holder_ref, mask_ref, gain_col_ref, w_qkv_ref, w_out_ref, gain_tile_ref, w_query_ref,
     after_ref, resid_ref, asked_ref, normed_ref, packed_ref) = refs
    own_rows, width = cell_refs[0].shape
    steps = own_rows // chunk
    span = groups * chunk
    lanes_two = 2 * head_size
    for step in range(steps):
        for group in range(groups):
            cells = cell_refs[group][pl.ds(step * chunk, chunk), :].astype(jnp.float32)
            normed_ref[pl.ds(step * span + group * chunk, chunk), :] = rms_scale(cells, gain_col_ref[...]).astype(jnp.bfloat16)
    for part in range(3):
        packed_ref[part] = dot_rows(normed_ref[...], w_qkv_ref[:, pl.ds(part * width, width)]).astype(jnp.bfloat16)
    stacked = heads * span
    same_row = iota((stacked, span), 0) % chunk // cols == iota((stacked, span), 1) % chunk // cols
    lane_low = iota((span, lanes_two), 1) < head_size
    scale = head_size ** (-0.5)
    for step in range(steps):
        rows = pl.ds(step * span, span)
        scores = []
        for head in range(heads):
            lanes = pl.ds(head // 2 * lanes_two, lanes_two)
            query = packed_ref[0, rows, lanes]
            query = jnp.where(lane_low == (head % 2 == 0), query, jnp.zeros_like(query))
            scores.append(dot_lanes(query, packed_ref[1, rows, lanes]))
        scores = jnp.where(same_row, jnp.concatenate(scores, axis=0) * scale, BIG)
        expo = jnp.exp(scores - jnp.max(scores, axis=1, keepdims=True))
        weights = (expo / jnp.sum(expo, axis=1, keepdims=True)).astype(jnp.bfloat16)
        for pair in range(heads // 2):
            lanes = pl.ds(pair * lanes_two, lanes_two)
            start = 2 * pair * span
            mixed = dot_rows(weights[start:start + 2 * span], packed_ref[2, rows, lanes])
            normed_ref[rows, lanes] = jnp.where(lane_low, mixed[:span], mixed[span:]).astype(jnp.bfloat16)
    delta = dot_rows(normed_ref[...], w_out_ref[...])
    for step in range(steps):
        for group in range(groups):
            start = step * span + group * chunk
            resid = cell_refs[group][pl.ds(step * chunk, chunk), :].astype(jnp.float32) + delta[start:start + chunk]
            if group == 0:
                resid_ref[pl.ds(step * chunk, chunk), :] = resid
            normed_ref[pl.ds(start, chunk), :] = rms_scale(resid, gain_tile_ref[...]).astype(jnp.bfloat16)
    slots = mask_ref.shape[1]
    place = (holder_ref[...] + head_size == iota((slots, lanes_two), 1)).astype(jnp.bfloat16)
    live = dot_rows((mask_ref[...] > 0).astype(jnp.bfloat16), place)
    lane = iota(live.shape, 1)
    shut = jnp.where((lane >= head_size) & (lane < head_size + row_size) & (live < 0.5), 1.0, 0.0).astype(jnp.bfloat16)
    total = steps * span
    cell = iota((total, shut.shape[0]), 0)
    row_of = cell // span * (chunk // cols) + cell % chunk // cols
    spread = (row_of == iota((total, shut.shape[0]), 1)).astype(jnp.bfloat16)
    bias = dot_rows(spread, shut) * BIG
    asked = dot_rows(normed_ref[...], w_query_ref[...]).astype(jnp.bfloat16).astype(jnp.float32) * scale
    heads_here = asked.shape[1] // head_size
    low = iota((total, lanes_two), 1) < head_size
    for head in range(heads_here):
        if heads_here % 2 == 0:
            two = asked[:, head // 2 * lanes_two:(head // 2 + 1) * lanes_two]
            one = two if head % 2 == 0 else pltpu.roll(two, head_size, 1)
            query = jnp.where(low, one, bias)
        else:
            one = asked[:, head * head_size:(head + 1) * head_size]
            query = jnp.concatenate([one, bias[:, head_size:]], axis=1)
        asked_ref[head] = query.astype(jnp.bfloat16)


def front(cells, holder, key_mask, gain_col, w_qkv, w_out, gain_tile, w_query, heads, head_size, cols, row_size, after):
    groups = len(cells)
    own_rows, width = cells[0].shape
    total = groups * own_rows
    asked_shape = (w_query.shape[1] // head_size, total, 2 * head_size)
    return pl.pallas_call(
        functools.partial(front_kernel, groups, heads, head_size, ROW_GROUP * cols, cols, row_size),
        out_shape=(jax.ShapeDtypeStruct((own_rows, width), jnp.float32),
                   jax.ShapeDtypeStruct(asked_shape, jnp.bfloat16)),
        in_specs=[VMEM] * (groups + 7) + [ANY],
        out_specs=(VMEM, VMEM),
        scratch_shapes=[pltpu.VMEM((total, width), jnp.bfloat16), pltpu.VMEM((3, total, width), jnp.bfloat16)],
        compiler_params=params(total),
        cost_estimate=pl.CostEstimate(flops=2 * total * width * 5 * width, bytes_accessed=4 * MIB,
                                      transcendentals=total * heads * 128),
        name="front",
    )(*cells, holder, key_mask, gain_col.reshape(1, width), w_qkv, w_out, gain_tile.reshape(1, width), w_query, after)


def weigh(query, tiles):
    slots, keys, lanes = tiles.shape
    half = lanes // 2
    lane = iota(tiles.shape, 2)
    marks = (lane == iota(tiles.shape, 0) + half).astype(tiles.dtype)
    key_part = jnp.where(lane < half, tiles, marks).reshape(slots * keys, lanes)
    val_part = jnp.where(lane < half, jnp.ones_like(tiles), tiles).reshape(slots * keys, lanes)
    scores = dot_lanes(query, key_part)
    top = jnp.max(scores, axis=1, keepdims=True)
    return dot_rows(jnp.exp(scores - top).astype(jnp.bfloat16), val_part)


def attend_kernel(groups, tile_count, chunk, asked_ref, *refs):
    tile_refs, out_refs = refs[:tile_count], refs[tile_count:]
    heads, rows_all, lanes = asked_ref.shape
    half = lanes // 2
    span = groups * chunk
    block = rows_all if rows_all <= 512 else span
    lane_low = iota((block, lanes), 1) < half

    def put(step, values, lane, lane_count):
        for part in range(block // span):
            for group in range(groups):
                start = part * span + group * chunk
                place = pl.ds(step * (block // groups) + part * chunk, chunk)
                out_refs[group][place, pl.ds(lane, lane_count)] = values[start:start + chunk]

    for step in range(rows_all // block):
        low = None
        for head in range(heads):
            tiles = jnp.concatenate([ref[:, head] for ref in tile_refs], axis=0)
            sums = weigh(asked_ref[head, pl.ds(step * block, block), :], tiles)
            turned = pltpu.roll(sums, half, 1)
            if head % 2:
                put(step, jnp.where(lane_low, low, sums / turned).astype(jnp.bfloat16), head // 2 * lanes, lanes)
            elif head + 1 < heads:
                low = turned / sums
            else:
                put(step, (turned / sums)[:, :half].astype(jnp.bfloat16), head * half, half)


def attend(asked, tiles, groups, cols):
    heads, rows, lanes = asked.shape
    keys = sum(part.shape[0] * part.shape[2] for part in tiles)
    out = jax.ShapeDtypeStruct((rows // groups, heads * lanes // 2), jnp.bfloat16)
    return pl.pallas_call(
        functools.partial(attend_kernel, groups, len(tiles), ROW_GROUP * cols),
        out_shape=(out,) * groups,
        in_specs=[VMEM] * (1 + len(tiles)),
        out_specs=(VMEM,) * groups,
        compiler_params=params(rows),
        cost_estimate=pl.CostEstimate(flops=4 * rows * heads * keys * lanes, bytes_accessed=4 * MIB,
                                      transcendentals=rows * heads * keys),
        name="attend",
    )(asked, *tiles)


def turn(size, step):
    return [(src, (src + step) % size) for src in range(size)]


def shards(row_size, col_size, fact_cells, gain_col, w_qkv, w_col_out, gain_tile, w_query, w_tile_out,
           tile_kv, tile_ids, key_mask):
    rows, cols, width = fact_cells.shape
    tiles_here, keys, heads_here, lanes = tile_kv.shape
    head_size = lanes // 2
    heads_all = width // head_size
    group_width = heads_here * head_size
    half = row_size // 2
    col_me = lax.axis_index("cols")
    row_me = lax.axis_index("rows")
    my_half, my_place = row_me // half, row_me % half
    halves = [list(range(half)), list(range(half, row_size))]
    assert row_size <= head_size and row_size % 2 == 0

    def swap(value):
        return lax.all_to_all(value, "rows", split_axis=0, concat_axis=0, tiled=True, axis_index_groups=halves)

    heads_first = jnp.transpose(tile_kv, (0, 2, 1, 3))
    parts = [(0, 1), (1, heads_here)] if heads_here > 1 else [(0, 1)]
    mirrored = [lax.ppermute(heads_first[:, low:high], "rows", turn(row_size, half)) for low, high in parts]

    listed = tile_ids[0] >= 0
    holder = jnp.where(listed, (tile_ids[0] // tiles_here + my_half * half) % row_size, -1)
    wanted = jnp.sum(jnp.where(holder[:, None] == jnp.arange(row_size)[None, :], (tile_ids[0] % tiles_here)[:, None], 0), axis=0)
    asked_of = jnp.broadcast_to(wanted.astype(jnp.int32).reshape(2, half).T[:, :, None], (half, 2, 128))
    asked_by = swap(asked_of)[:, :, 0]

    cells = [fact_cells.reshape(rows * cols, width)]
    for step in range(1, col_size):
        cells.append(lax.ppermute(cells[0], "cols", turn(col_size, -step)))

    near_by, far_by = asked_by[:, 0], asked_by[:, 1]
    if half <= 8 and half & (half - 1) == 0:
        holder = jnp.where(holder < 0, holder, holder ^ my_place)

        def spread(tiles, wanted, after):
            picked = pick_each(tiles, wanted, my_place.reshape(1), after)
            arrived = [picked[0]]
            for step in range(1, half):
                pairs = [(row, row // half * half + (row % half ^ step)) for row in range(row_size)]
                arrived.append(lax.ppermute(picked[step], "rows", pairs))
            return picked[0], arrived
    else:
        def spread(tiles, wanted, after):
            picked = pick(tiles, wanted, after)
            return picked, [swap(picked)]

    picked, near = spread([heads_first], near_by, mirrored[:1])
    picked, far = spread(mirrored, far_by, near)
    query_here = lax.dynamic_slice_in_dim(w_query, col_me * group_width, group_width, 1)
    residual, asked = front(cells, holder[:, None], key_mask, gain_col, w_qkv, w_col_out, gain_tile, query_here,
                            heads_all, head_size, cols, row_size, picked)
    answers = attend(asked, near + far, col_size, cols)

    final = residual
    for step in range(col_size):
        answer = lax.ppermute(answers[step], "cols", turn(col_size, step)) if step else answers[0]
        start = (col_me - step) % col_size * group_width
        final = final + dot_rows(answer, lax.dynamic_slice_in_dim(w_tile_out, start, group_width, 0))
    return final.astype(jnp.bfloat16).reshape(rows, cols, width)


def solution(mesh):
    row_size, col_size = mesh.shape["rows"], mesh.shape["cols"]
    placed = (P("rows", "cols", None), P(), P(), P(), P(), P(), P(), P("rows", None, "cols", None),
              P("rows", None), P("rows", None))

    def body(*arrays):
        return shards(row_size, col_size, *arrays)

    return jax.shard_map(body, mesh=mesh, in_specs=placed, out_specs=P("rows", "cols", None), check_vma=False)
```

```python
import functools

import jax
import jax.numpy as jnp
from jax import lax
from jax.experimental import pallas as pl
from jax.experimental.pallas import tpu as pltpu
from jax.sharding import PartitionSpec as P

ROW_GROUP = 16
BIG = -1e30
MIB = 1024 * 1024
VMEM = pl.BlockSpec(memory_space=pltpu.VMEM)
ANY = pl.BlockSpec(memory_space=pl.ANY)


def params(rows):
    return pltpu.CompilerParams(vmem_limit_bytes=(20 if rows <= 512 else 48) * MIB)


def dot_rows(left, right):
    return lax.dot_general(left, right, (((1,), (0,)), ((), ())), preferred_element_type=jnp.float32)


def dot_lanes(left, right):
    return lax.dot_general(left, right, (((1,), (1,)), ((), ())), preferred_element_type=jnp.float32)


def rms_scale(values, gain_vec):
    mean_sq = jnp.mean(values * values, axis=-1, keepdims=True)
    return values * lax.rsqrt(mean_sq + 1e-05) * gain_vec


def iota(shape, dim):
    return lax.broadcasted_iota(jnp.int32, shape, dim)


def pick_kernel(wanted_ref, tiles_ref, *refs):
    out_ref = refs[-1]
    for peer in range(out_ref.shape[0]):
        out_ref[peer] = tiles_ref[wanted_ref[peer]]


def pick(tiles, wanted, after):
    return pl.pallas_call(
        pick_kernel,
        out_shape=jax.ShapeDtypeStruct(wanted.shape + tiles.shape[1:], tiles.dtype),
        in_specs=[pl.BlockSpec(memory_space=pltpu.SMEM), VMEM] + [ANY] * len(after),
        out_specs=VMEM,
        compiler_params=params(0),
        cost_estimate=pl.CostEstimate(flops=0, bytes_accessed=2 * MIB, transcendentals=0),
        name="pick",
    )(wanted, tiles, *after)


def pick_each_kernel(wanted_ref, me_ref, tiles_ref, *refs):
    for step, out_ref in enumerate(refs[-wanted_ref.shape[0]:]):
        out_ref[0] = tiles_ref[wanted_ref[me_ref[0] ^ step]]


def pick_each(tiles, wanted, me, after):
    count = wanted.shape[0]
    smem = pl.BlockSpec(memory_space=pltpu.SMEM)
    return pl.pallas_call(
        pick_each_kernel,
        out_shape=(jax.ShapeDtypeStruct((1,) + tiles.shape[1:], tiles.dtype),) * count,
        in_specs=[smem, smem, VMEM] + [ANY] * len(after),
        out_specs=(VMEM,) * count,
        compiler_params=params(0),
        cost_estimate=pl.CostEstimate(flops=0, bytes_accessed=2 * MIB, transcendentals=0),
        name="pick_each",
    )(wanted, me, tiles, *after)


def front_kernel(groups, heads, head_size, chunk, cols, row_size, *refs):
    cell_refs, refs = refs[:groups], refs[groups:]
    (holder_ref, mask_ref, gain_col_ref, w_qkv_ref, w_out_ref, gain_tile_ref, w_query_ref,
     after_ref, resid_ref, asked_ref, normed_ref, packed_ref) = refs
    own_rows, width = cell_refs[0].shape
    steps = own_rows // chunk
    span = groups * chunk
    lanes_two = 2 * head_size
    for step in range(steps):
        for group in range(groups):
            cells = cell_refs[group][pl.ds(step * chunk, chunk), :].astype(jnp.float32)
            normed_ref[pl.ds(step * span + group * chunk, chunk), :] = rms_scale(cells, gain_col_ref[...]).astype(jnp.bfloat16)
    for part in range(3):
        packed_ref[part] = dot_rows(normed_ref[...], w_qkv_ref[:, pl.ds(part * width, width)]).astype(jnp.bfloat16)
    stacked = heads * span
    same_row = iota((stacked, span), 0) % chunk // cols == iota((stacked, span), 1) % chunk // cols
    lane_low = iota((span, lanes_two), 1) < head_size
    scale = head_size ** (-0.5)
    for step in range(steps):
        rows = pl.ds(step * span, span)
        scores = []
        for head in range(heads):
            lanes = pl.ds(head // 2 * lanes_two, lanes_two)
            query = packed_ref[0, rows, lanes]
            query = jnp.where(lane_low == (head % 2 == 0), query, jnp.zeros_like(query))
            scores.append(dot_lanes(query, packed_ref[1, rows, lanes]))
        scores = jnp.where(same_row, jnp.concatenate(scores, axis=0) * scale, BIG)
        expo = jnp.exp(scores - jnp.max(scores, axis=1, keepdims=True))
        weights = (expo / jnp.sum(expo, axis=1, keepdims=True)).astype(jnp.bfloat16)
        for pair in range(heads // 2):
            lanes = pl.ds(pair * lanes_two, lanes_two)
            start = 2 * pair * span
            mixed = dot_rows(weights[start:start + 2 * span], packed_ref[2, rows, lanes])
            normed_ref[rows, lanes] = jnp.where(lane_low, mixed[:span], mixed[span:]).astype(jnp.bfloat16)
    delta = dot_rows(normed_ref[...], w_out_ref[...])
    for step in range(steps):
        for group in range(groups):
            start = step * span + group * chunk
            resid = cell_refs[group][pl.ds(step * chunk, chunk), :].astype(jnp.float32) + delta[start:start + chunk]
            if group == 0:
                resid_ref[pl.ds(step * chunk, chunk), :] = resid
            normed_ref[pl.ds(start, chunk), :] = rms_scale(resid, gain_tile_ref[...]).astype(jnp.bfloat16)
    slots = mask_ref.shape[1]
    place = (holder_ref[...] + head_size == iota((slots, lanes_two), 1)).astype(jnp.bfloat16)
    live = dot_rows((mask_ref[...] > 0).astype(jnp.bfloat16), place)
    lane = iota(live.shape, 1)
    shut = jnp.where((lane >= head_size) & (lane < head_size + row_size) & (live < 0.5), 1.0, 0.0).astype(jnp.bfloat16)
    total = steps * span
    cell = iota((total, shut.shape[0]), 0)
    row_of = cell // span * (chunk // cols) + cell % chunk // cols
    spread = (row_of == iota((total, shut.shape[0]), 1)).astype(jnp.bfloat16)
    bias = dot_rows(spread, shut) * BIG
    asked = dot_rows(normed_ref[...], w_query_ref[...]).astype(jnp.bfloat16).astype(jnp.float32) * scale
    heads_here = asked.shape[1] // head_size
    low = iota((total, lanes_two), 1) < head_size
    for head in range(heads_here):
        if heads_here % 2 == 0:
            two = asked[:, head // 2 * lanes_two:(head // 2 + 1) * lanes_two]
            one = two if head % 2 == 0 else pltpu.roll(two, head_size, 1)
            query = jnp.where(low, one, bias)
        else:
            one = asked[:, head * head_size:(head + 1) * head_size]
            query = jnp.concatenate([one, bias[:, head_size:]], axis=1)
        asked_ref[head] = query.astype(jnp.bfloat16)


def front(cells, holder, key_mask, gain_col, w_qkv, w_out, gain_tile, w_query, heads, head_size, cols, row_size, after):
    groups = len(cells)
    own_rows, width = cells[0].shape
    total = groups * own_rows
    asked_shape = (w_query.shape[1] // head_size, total, 2 * head_size)
    return pl.pallas_call(
        functools.partial(front_kernel, groups, heads, head_size, ROW_GROUP * cols, cols, row_size),
        out_shape=(jax.ShapeDtypeStruct((own_rows, width), jnp.float32),
                   jax.ShapeDtypeStruct(asked_shape, jnp.bfloat16)),
        in_specs=[VMEM] * (groups + 7) + [ANY],
        out_specs=(VMEM, VMEM),
        scratch_shapes=[pltpu.VMEM((total, width), jnp.bfloat16), pltpu.VMEM((3, total, width), jnp.bfloat16)],
        compiler_params=params(total),
        cost_estimate=pl.CostEstimate(flops=2 * total * width * 5 * width, bytes_accessed=4 * MIB,
                                      transcendentals=total * heads * 128),
        name="front",
    )(*cells, holder, key_mask, gain_col.reshape(1, width), w_qkv, w_out, gain_tile.reshape(1, width), w_query, after)


def weigh(query, tile_refs, head, first_slot):
    tiles = jnp.concatenate([ref[:, head] for ref in tile_refs], axis=0)
    slots, keys, lanes = tiles.shape
    half = lanes // 2
    lane = iota(tiles.shape, 2)
    marks = (lane == iota(tiles.shape, 0) + (half + first_slot)).astype(tiles.dtype)
    key_part = jnp.where(lane < half, tiles, marks).reshape(slots * keys, lanes)
    val_part = jnp.where(lane < half, jnp.ones_like(tiles), tiles).reshape(slots * keys, lanes)
    scores = dot_lanes(query, key_part)
    top = jnp.max(scores, axis=1, keepdims=True)
    return top, dot_rows(jnp.exp(scores - top).astype(jnp.bfloat16), val_part)


def attention_cost(asked, tiles):
    heads, rows, lanes = asked.shape
    keys = sum(part.shape[0] * part.shape[2] for part in tiles)
    return pl.CostEstimate(flops=4 * rows * heads * keys * lanes, bytes_accessed=4 * MIB, transcendentals=rows * heads * keys)


def first_kernel(count, block, asked_ref, *refs):
    tile_refs, (sums_ref, tops_ref) = refs[:count], refs[count:]
    heads, rows_all, lanes = asked_ref.shape
    lane = iota((block, lanes), 1)
    for step in range(rows_all // block):
        rows = pl.ds(step * block, block)
        tops = jnp.zeros((block, lanes), jnp.float32)
        for head in range(heads):
            top, sums_ref[head, rows, :] = weigh(asked_ref[head, rows, :], tile_refs, head, 0)
            tops = jnp.where(lane == head, top, tops)
        tops_ref[rows, :] = tops


def first_tiles(asked, tiles):
    heads, rows, lanes = asked.shape
    return pl.pallas_call(
        functools.partial(first_kernel, len(tiles), rows if rows <= 512 else 128),
        out_shape=(jax.ShapeDtypeStruct((heads, rows, lanes), jnp.float32), jax.ShapeDtypeStruct((rows, lanes), jnp.float32)),
        in_specs=[VMEM] * (1 + len(tiles)),
        out_specs=(VMEM, VMEM),
        compiler_params=params(rows),
        cost_estimate=attention_cost(asked, tiles),
        name="first_tiles",
    )(asked, *tiles)


def last_kernel(groups, count, first_slot, chunk, asked_ref, sums_ref, tops_ref, *refs):
    tile_refs, out_refs = refs[:count], refs[count:]
    heads, rows_all, lanes = asked_ref.shape
    half = lanes // 2
    span = groups * chunk
    block = rows_all if rows_all <= 512 else span
    lane_low = iota((block, lanes), 1) < half

    def put(step, values, lane, lane_count):
        for part in range(block // span):
            for group in range(groups):
                start = part * span + group * chunk
                place = pl.ds(step * (block // groups) + part * chunk, chunk)
                out_refs[group][place, pl.ds(lane, lane_count)] = values[start:start + chunk]

    for step in range(rows_all // block):
        rows = pl.ds(step * block, block)
        low = None
        for head in range(heads):
            top, sums = weigh(asked_ref[head, rows, :], tile_refs, head, first_slot)
            old_top = tops_ref[rows, head:head + 1]
            new_top = jnp.maximum(top, old_top)
            sums = sums_ref[head, rows, :] * jnp.exp(old_top - new_top) + sums * jnp.exp(top - new_top)
            turned = pltpu.roll(sums, half, 1)
            if head % 2:
                put(step, jnp.where(lane_low, low, sums / turned).astype(jnp.bfloat16), head // 2 * lanes, lanes)
            elif head + 1 < heads:
                low = turned / sums
            else:
                put(step, (turned / sums)[:, :half].astype(jnp.bfloat16), head * half, half)


def last_tiles(asked, sums, tops, tiles, first_slot, groups, cols):
    heads, rows, lanes = asked.shape
    out = jax.ShapeDtypeStruct((rows // groups, heads * lanes // 2), jnp.bfloat16)
    return pl.pallas_call(
        functools.partial(last_kernel, groups, len(tiles), first_slot, ROW_GROUP * cols),
        out_shape=(out,) * groups,
        in_specs=[VMEM] * (3 + len(tiles)),
        out_specs=(VMEM,) * groups,
        compiler_params=params(rows),
        cost_estimate=attention_cost(asked, tiles),
        name="last_tiles",
    )(asked, sums, tops, *tiles)


def turn(size, step):
    return [(src, (src + step) % size) for src in range(size)]


def shards(row_size, col_size, fact_cells, gain_col, w_qkv, w_col_out, gain_tile, w_query, w_tile_out,
           tile_kv, tile_ids, key_mask):
    rows, cols, width = fact_cells.shape
    tiles_here, keys, heads_here, lanes = tile_kv.shape
    head_size = lanes // 2
    heads_all = width // head_size
    group_width = heads_here * head_size
    half = row_size // 2
    col_me = lax.axis_index("cols")
    row_me = lax.axis_index("rows")
    my_half, my_place = row_me // half, row_me % half
    halves = [list(range(half)), list(range(half, row_size))]
    assert row_size <= head_size and row_size % 2 == 0

    def swap(value):
        return lax.all_to_all(value, "rows", split_axis=0, concat_axis=0, tiled=True, axis_index_groups=halves)

    heads_first = jnp.transpose(tile_kv, (0, 2, 1, 3))
    mirrored = lax.ppermute(heads_first, "rows", turn(row_size, half))

    listed = tile_ids[0] >= 0
    holder = jnp.where(listed, (tile_ids[0] // tiles_here + my_half * half) % row_size, -1)
    wanted = jnp.sum(jnp.where(holder[:, None] == jnp.arange(row_size)[None, :], (tile_ids[0] % tiles_here)[:, None], 0), axis=0)
    asked_of = jnp.broadcast_to(wanted.astype(jnp.int32).reshape(2, half).T[:, :, None], (half, 2, 128))
    asked_by = swap(asked_of)[:, :, 0]

    cells = [fact_cells.reshape(rows * cols, width)]
    for step in range(1, col_size):
        cells.append(lax.ppermute(cells[0], "cols", turn(col_size, -step)))

    near_by, far_by = asked_by[:, 0], asked_by[:, 1]
    if half <= 8 and half & (half - 1) == 0:
        holder = jnp.where(holder < 0, holder, holder ^ my_place)

        def spread(tiles, wanted, after):
            picked = pick_each(tiles, wanted, my_place.reshape(1), after)
            arrived = [picked[0]]
            for step in range(1, half):
                pairs = [(row, row // half * half + (row % half ^ step)) for row in range(row_size)]
                arrived.append(lax.ppermute(picked[step], "rows", pairs))
            return picked[0], arrived
    else:
        def spread(tiles, wanted, after):
            picked = pick(tiles, wanted, after)
            return picked, [swap(picked)]

    picked, near = spread(heads_first, near_by, [])
    picked, far = spread(mirrored, far_by, near)
    query_here = lax.dynamic_slice_in_dim(w_query, col_me * group_width, group_width, 1)
    residual, asked = front(cells, holder[:, None], key_mask, gain_col, w_qkv, w_col_out, gain_tile, query_here,
                            heads_all, head_size, cols, row_size, picked)
    sums, tops = first_tiles(asked, near)
    answers = last_tiles(asked, sums, tops, far, half, col_size, cols)

    final = residual
    for step in range(col_size):
        answer = lax.ppermute(answers[step], "cols", turn(col_size, step)) if step else answers[0]
        start = (col_me - step) % col_size * group_width
        final = final + dot_rows(answer, lax.dynamic_slice_in_dim(w_tile_out, start, group_width, 0))
    return final.astype(jnp.bfloat16).reshape(rows, cols, width)


def solution(mesh):
    row_size, col_size = mesh.shape["rows"], mesh.shape["cols"]
    placed = (P("rows", "cols", None), P(), P(), P(), P(), P(), P(), P("rows", None, "cols", None),
              P("rows", None), P("rows", None))

    def body(*arrays):
        return shards(row_size, col_size, *arrays)

    return jax.shard_map(body, mesh=mesh, in_specs=placed, out_specs=P("rows", "cols", None), check_vma=False)
```

```python
import functools

import jax
import jax.numpy as jnp
from jax import lax
from jax.experimental import pallas as pl
from jax.experimental.pallas import tpu as pltpu
from jax.sharding import PartitionSpec as P

ROW_GROUP = 16
BIG = -1e30
MIB = 1024 * 1024
VMEM = pl.BlockSpec(memory_space=pltpu.VMEM)
SMEM = pl.BlockSpec(memory_space=pltpu.SMEM)
ANY = pl.BlockSpec(memory_space=pl.ANY)


def params(rows):
    return pltpu.CompilerParams(vmem_limit_bytes=(20 if rows <= 512 else 48) * MIB)


def dot_rows(left, right):
    return lax.dot_general(left, right, (((1,), (0,)), ((), ())), preferred_element_type=jnp.float32)


def dot_lanes(left, right):
    return lax.dot_general(left, right, (((1,), (1,)), ((), ())), preferred_element_type=jnp.float32)


def rms_scale(values, gain_vec):
    mean_sq = jnp.mean(values * values, axis=-1, keepdims=True)
    return values * lax.rsqrt(mean_sq + 1e-05) * gain_vec


def iota(shape, dim):
    return lax.broadcasted_iota(jnp.int32, shape, dim)


def slot_of(owner, row_me, row_size, paired):
    half = row_size // 2
    return owner ^ row_me if paired else lax.rem(owner + lax.div(row_me, half) * half, row_size)


def request_kernel(tiles_here, row_size, ids_ref, me_ref, out_ref):
    half = row_size // 2
    peer, which = iota(out_ref.shape, 0), iota(out_ref.shape, 1)
    wanted = jnp.zeros(out_ref.shape, jnp.int32)
    for slot in range(ids_ref.shape[1]):
        tile = ids_ref[0, slot]
        owner = lax.div(tile, tiles_here)
        far = jnp.where(lax.div(owner, half) == lax.div(me_ref[0], half), 0, 1)
        here = (peer == jnp.where(tile < 0, -1, lax.rem(owner, half))) & (which == far)
        wanted = jnp.where(here, lax.rem(tile, tiles_here), wanted)
    out_ref[...] = wanted


def request(ids, me, tiles_here, row_size):
    return pl.pallas_call(
        functools.partial(request_kernel, tiles_here, row_size),
        out_shape=jax.ShapeDtypeStruct((row_size // 2, 2, 128), jnp.int32),
        in_specs=[SMEM, SMEM],
        out_specs=VMEM,
        compiler_params=params(0),
        cost_estimate=pl.CostEstimate(flops=0, bytes_accessed=MIB // 4, transcendentals=0),
        name="request",
    )(ids, me)


def pick_kernel(which, wanted_ref, tiles_ref, *refs):
    out_ref = refs[-1]
    for peer in range(out_ref.shape[0]):
        out_ref[peer] = tiles_ref[wanted_ref[peer, which, 0]]


def pick(tiles, wanted, which, after):
    return pl.pallas_call(
        functools.partial(pick_kernel, which),
        out_shape=jax.ShapeDtypeStruct(wanted.shape[:1] + tiles.shape[1:], tiles.dtype),
        in_specs=[SMEM, VMEM] + [ANY] * len(after),
        out_specs=VMEM,
        compiler_params=params(0),
        cost_estimate=pl.CostEstimate(flops=0, bytes_accessed=2 * MIB, transcendentals=0),
        name="pick",
    )(wanted, tiles, *after)


def pick_each_kernel(which, wanted_ref, me_ref, tiles_ref, *refs):
    half = wanted_ref.shape[0]
    place = lax.rem(me_ref[0], half)
    for step, out_ref in enumerate(refs[-half:]):
        out_ref[0] = tiles_ref[wanted_ref[place ^ step, which, 0]]


def pick_each(tiles, wanted, which, me, after):
    count = wanted.shape[0]
    return pl.pallas_call(
        functools.partial(pick_each_kernel, which),
        out_shape=(jax.ShapeDtypeStruct((1,) + tiles.shape[1:], tiles.dtype),) * count,
        in_specs=[SMEM, SMEM, VMEM] + [ANY] * len(after),
        out_specs=(VMEM,) * count,
        compiler_params=params(0),
        cost_estimate=pl.CostEstimate(flops=0, bytes_accessed=2 * MIB, transcendentals=0),
        name="pick_each",
    )(wanted, me, tiles, *after)


def front_kernel(groups, heads, head_size, chunk, cols, heads_here, tiles_here, row_size, paired, *refs):
    cell_refs, refs = refs[:groups], refs[groups:]
    (ids_ref, me_ref, mask_ref, gain_col_ref, w_qkv_ref, w_out_ref, gain_tile_ref, w_query_ref,
     resid_ref, asked_ref, normed_ref, packed_ref) = refs
    own_rows, width = cell_refs[0].shape
    steps = own_rows // chunk
    span = groups * chunk
    lanes_two = 2 * head_size
    for step in range(steps):
        for group in range(groups):
            cells = cell_refs[group][pl.ds(step * chunk, chunk), :].astype(jnp.float32)
            normed_ref[pl.ds(step * span + group * chunk, chunk), :] = rms_scale(cells, gain_col_ref[...]).astype(jnp.bfloat16)
    for part in range(3):
        packed_ref[part] = dot_rows(normed_ref[...], w_qkv_ref[:, pl.ds(part * width, width)]).astype(jnp.bfloat16)
    stacked = heads * span
    same_row = iota((stacked, span), 0) % chunk // cols == iota((stacked, span), 1) % chunk // cols
    lane_low = iota((span, lanes_two), 1) < head_size
    scale = head_size ** (-0.5)
    for step in range(steps):
        rows = pl.ds(step * span, span)
        scores = []
        for head in range(heads):
            lanes = pl.ds(head // 2 * lanes_two, lanes_two)
            query = packed_ref[0, rows, lanes]
            query = jnp.where(lane_low == (head % 2 == 0), query, jnp.zeros_like(query))
            scores.append(dot_lanes(query, packed_ref[1, rows, lanes]))
        scores = jnp.where(same_row, jnp.concatenate(scores, axis=0) * scale, BIG)
        expo = jnp.exp(scores - jnp.max(scores, axis=1, keepdims=True))
        weights = (expo / jnp.sum(expo, axis=1, keepdims=True)).astype(jnp.bfloat16)
        for pair in range(heads // 2):
            lanes = pl.ds(pair * lanes_two, lanes_two)
            start = 2 * pair * span
            mixed = dot_rows(weights[start:start + 2 * span], packed_ref[2, rows, lanes])
            normed_ref[rows, lanes] = jnp.where(lane_low, mixed[:span], mixed[span:]).astype(jnp.bfloat16)
    delta = dot_rows(normed_ref[...], w_out_ref[...])
    for step in range(steps):
        for group in range(groups):
            start = step * span + group * chunk
            resid = cell_refs[group][pl.ds(step * chunk, chunk), :].astype(jnp.float32) + delta[start:start + chunk]
            if group == 0:
                resid_ref[pl.ds(step * chunk, chunk), :] = resid
            normed_ref[pl.ds(start, chunk), :] = rms_scale(resid, gain_tile_ref[...]).astype(jnp.bfloat16)
    slots = mask_ref.shape[0]
    slot, lane = iota((slots, lanes_two), 0), iota((slots, lanes_two), 1)
    place = jnp.zeros((slots, lanes_two), jnp.float32)
    for index in range(slots):
        tile = ids_ref[0, index]
        spot = jnp.where(tile < 0, -1, head_size + slot_of(lax.div(tile, tiles_here), me_ref[0], row_size, paired))
        place = jnp.where((slot == index) & (lane == spot), 1.0, place)
    live = lax.dot_general((mask_ref[...] > 0).astype(jnp.float32).astype(jnp.bfloat16), place.astype(jnp.bfloat16),
                           (((0,), (0,)), ((), ())), preferred_element_type=jnp.float32)
    lane = iota(live.shape, 1)
    shut = jnp.where((lane >= head_size) & (lane < head_size + row_size) & (live < 0.5), 1.0, 0.0).astype(jnp.bfloat16)
    total = steps * span
    cell = iota((total, shut.shape[0]), 0)
    row_of = cell // span * (chunk // cols) + cell % chunk // cols
    spread = (row_of == iota((total, shut.shape[0]), 1)).astype(jnp.bfloat16)
    bias = dot_rows(spread, shut) * BIG
    group_width = heads_here * head_size
    if w_query_ref.shape[1] == group_width:
        w_query = w_query_ref[...]
    else:
        w_query = w_query_ref[:, pl.ds(pl.multiple_of(me_ref[1] * group_width, group_width), group_width)]
    asked = dot_rows(normed_ref[...], w_query).astype(jnp.bfloat16).astype(jnp.float32) * scale
    low = iota((total, lanes_two), 1) < head_size
    for head in range(heads_here):
        if heads_here % 2 == 0:
            two = asked[:, head // 2 * lanes_two:(head // 2 + 1) * lanes_two]
            one = two if head % 2 == 0 else pltpu.roll(two, head_size, 1)
            query = jnp.where(low, one, bias)
        else:
            one = asked[:, head * head_size:(head + 1) * head_size]
            query = jnp.concatenate([one, bias[:, head_size:]], axis=1)
        asked_ref[head] = query.astype(jnp.bfloat16)


def front(cells, ids, me, key_mask, gain_col, w_qkv, w_out, gain_tile, w_query, heads, head_size, cols,
          heads_here, tiles_here, row_size, paired):
    groups = len(cells)
    own_rows, width = cells[0].shape
    total = groups * own_rows
    return pl.pallas_call(
        functools.partial(front_kernel, groups, heads, head_size, ROW_GROUP * cols, cols, heads_here, tiles_here, row_size, paired),
        out_shape=(jax.ShapeDtypeStruct((own_rows, width), jnp.float32),
                   jax.ShapeDtypeStruct((heads_here, total, 2 * head_size), jnp.bfloat16)),
        in_specs=[VMEM] * groups + [SMEM, SMEM] + [VMEM] * 6,
        out_specs=(VMEM, VMEM),
        scratch_shapes=[pltpu.VMEM((total, width), jnp.bfloat16), pltpu.VMEM((3, total, width), jnp.bfloat16)],
        compiler_params=params(total),
        cost_estimate=pl.CostEstimate(flops=2 * total * width * 5 * width, bytes_accessed=4 * MIB,
                                      transcendentals=total * heads * 128),
        name="front",
    )(*cells, ids, me, key_mask.T, gain_col.reshape(1, width), w_qkv, w_out, gain_tile.reshape(1, width), w_query)


def weigh(query, tile_refs, head, first_slot):
    tiles = jnp.concatenate([ref[:, head] for ref in tile_refs], axis=0)
    slots, keys, lanes = tiles.shape
    half = lanes // 2
    lane = iota(tiles.shape, 2)
    marks = (lane == iota(tiles.shape, 0) + (half + first_slot)).astype(tiles.dtype)
    key_part = jnp.where(lane < half, tiles, marks).reshape(slots * keys, lanes)
    val_part = jnp.where(lane < half, jnp.ones_like(tiles), tiles).reshape(slots * keys, lanes)
    scores = dot_lanes(query, key_part)
    top = jnp.max(scores, axis=1, keepdims=True)
    return top, dot_rows(jnp.exp(scores - top).astype(jnp.bfloat16), val_part)


def attention_cost(asked, tiles):
    heads, rows, lanes = asked.shape
    keys = sum(part.shape[0] * part.shape[2] for part in tiles)
    return pl.CostEstimate(flops=4 * rows * heads * keys * lanes, bytes_accessed=4 * MIB, transcendentals=rows * heads * keys)


def first_kernel(count, block, asked_ref, *refs):
    tile_refs, (sums_ref, tops_ref) = refs[:count], refs[count:]
    heads, rows_all, lanes = asked_ref.shape
    lane = iota((block, lanes), 1)
    for step in range(rows_all // block):
        rows = pl.ds(step * block, block)
        tops = jnp.zeros((block, lanes), jnp.float32)
        for head in range(heads):
            top, sums_ref[head, rows, :] = weigh(asked_ref[head, rows, :], tile_refs, head, 0)
            tops = jnp.where(lane == head, top, tops)
        tops_ref[rows, :] = tops


def first_tiles(asked, tiles):
    heads, rows, lanes = asked.shape
    return pl.pallas_call(
        functools.partial(first_kernel, len(tiles), rows if rows <= 512 else 128),
        out_shape=(jax.ShapeDtypeStruct((heads, rows, lanes), jnp.float32), jax.ShapeDtypeStruct((rows, lanes), jnp.float32)),
        in_specs=[VMEM] * (1 + len(tiles)),
        out_specs=(VMEM, VMEM),
        compiler_params=params(rows),
        cost_estimate=attention_cost(asked, tiles),
        name="first_tiles",
    )(asked, *tiles)


def last_kernel(groups, count, first_slot, chunk, asked_ref, sums_ref, tops_ref, *refs):
    tile_refs, out_refs = refs[:count], refs[count:]
    heads, rows_all, lanes = asked_ref.shape
    half = lanes // 2
    span = groups * chunk
    block = rows_all if rows_all <= 512 else span
    lane_low = iota((block, lanes), 1) < half

    def put(step, values, lane, lane_count):
        for part in range(block // span):
            for group in range(groups):
                start = part * span + group * chunk
                place = pl.ds(step * (block // groups) + part * chunk, chunk)
                out_refs[group][place, pl.ds(lane, lane_count)] = values[start:start + chunk]

    for step in range(rows_all // block):
        rows = pl.ds(step * block, block)
        low = None
        for head in range(heads):
            top, sums = weigh(asked_ref[head, rows, :], tile_refs, head, first_slot)
            old_top = tops_ref[rows, head:head + 1]
            new_top = jnp.maximum(top, old_top)
            sums = sums_ref[head, rows, :] * jnp.exp(old_top - new_top) + sums * jnp.exp(top - new_top)
            turned = pltpu.roll(sums, half, 1)
            if head % 2:
                put(step, jnp.where(lane_low, low, sums / turned).astype(jnp.bfloat16), head // 2 * lanes, lanes)
            elif head + 1 < heads:
                low = turned / sums
            else:
                put(step, (turned / sums)[:, :half].astype(jnp.bfloat16), head * half, half)


def last_tiles(asked, sums, tops, tiles, first_slot, groups, cols):
    heads, rows, lanes = asked.shape
    out = jax.ShapeDtypeStruct((rows // groups, heads * lanes // 2), jnp.bfloat16)
    return pl.pallas_call(
        functools.partial(last_kernel, groups, len(tiles), first_slot, ROW_GROUP * cols),
        out_shape=(out,) * groups,
        in_specs=[VMEM] * (3 + len(tiles)),
        out_specs=(VMEM,) * groups,
        compiler_params=params(rows),
        cost_estimate=attention_cost(asked, tiles),
        name="last_tiles",
    )(asked, sums, tops, *tiles)


def turn(size, step):
    return [(src, (src + step) % size) for src in range(size)]


def shards(row_size, col_size, fact_cells, gain_col, w_qkv, w_col_out, gain_tile, w_query, w_tile_out,
           tile_kv, tile_ids, key_mask):
    rows, cols, width = fact_cells.shape
    tiles_here, keys, heads_here, lanes = tile_kv.shape
    head_size = lanes // 2
    heads_all = width // head_size
    group_width = heads_here * head_size
    half = row_size // 2
    row_me, col_me = lax.axis_index("rows"), lax.axis_index("cols")
    me = jnp.stack([row_me, col_me]).astype(jnp.int32)
    halves = [list(range(half)), list(range(half, row_size))]
    paired = half <= 8 and half & (half - 1) == 0
    assert row_size <= head_size and row_size % 2 == 0

    def swap(value):
        return lax.all_to_all(value, "rows", split_axis=0, concat_axis=0, tiled=True, axis_index_groups=halves)

    heads_first = jnp.transpose(tile_kv, (0, 2, 1, 3))
    mirrored = lax.ppermute(heads_first, "rows", turn(row_size, half))
    asked_by = swap(request(tile_ids, me, tiles_here, row_size))

    cells = [fact_cells.reshape(rows * cols, width)]
    for step in range(1, col_size):
        cells.append(lax.ppermute(cells[0], "cols", turn(col_size, -step)))

    def spread(tiles, which, after):
        if not paired:
            return [swap(pick(tiles, asked_by, which, after))]
        picked = pick_each(tiles, asked_by, which, me, after)
        arrived = list(picked[:1]) + [None] * (half - 1)
        for step in sorted(range(1, half), key=lambda step: (-(step & half // 2), step & 1, -step)):
            pairs = [(row, row ^ step) for row in range(row_size)]
            arrived[step] = lax.ppermute(picked[step], "rows", pairs)
        return arrived

    near = spread(heads_first, 0, cells[:1])
    if group_width % 128:
        w_query = lax.dynamic_slice_in_dim(w_query, col_me * group_width, group_width, 1)
    residual, asked = front(cells, tile_ids, me, key_mask, gain_col, w_qkv, w_col_out, gain_tile, w_query,
                            heads_all, head_size, cols, heads_here, tiles_here, row_size, paired)
    far = spread(mirrored, 1, near + [asked])
    sums, tops = first_tiles(asked, near)
    answers = last_tiles(asked, sums, tops, far, half, col_size, cols)

    final = residual
    for step in range(col_size):
        answer = lax.ppermute(answers[step], "cols", turn(col_size, step)) if step else answers[0]
        start = (col_me - step) % col_size * group_width
        final = final + dot_rows(answer, lax.dynamic_slice_in_dim(w_tile_out, start, group_width, 0))
    return final.astype(jnp.bfloat16).reshape(rows, cols, width)


def solution(mesh):
    row_size, col_size = mesh.shape["rows"], mesh.shape["cols"]
    placed = (P("rows", "cols", None), P(), P(), P(), P(), P(), P(), P("rows", None, "cols", None),
              P("rows", None), P("rows", None))

    def body(*arrays):
        return shards(row_size, col_size, *arrays)

    return jax.shard_map(body, mesh=mesh, in_specs=placed, out_specs=P("rows", "cols", None), check_vma=False)
```

```python
import functools

import jax
import jax.numpy as jnp
from jax import lax
from jax.experimental import pallas as pl
from jax.experimental.pallas import tpu as pltpu
from jax.sharding import PartitionSpec as P

ROW_GROUP = 16
BIG = -1e30
MIB = 1024 * 1024
VMEM = pl.BlockSpec(memory_space=pltpu.VMEM)
SMEM = pl.BlockSpec(memory_space=pltpu.SMEM)
HBM = pl.BlockSpec(memory_space=pltpu.HBM)
ANY = pl.BlockSpec(memory_space=pl.ANY)


def params(rows):
    return pltpu.CompilerParams(vmem_limit_bytes=(20 if rows <= 512 else 48) * MIB)


def dot_rows(left, right):
    return lax.dot_general(left, right, (((1,), (0,)), ((), ())), preferred_element_type=jnp.float32)


def dot_lanes(left, right):
    return lax.dot_general(left, right, (((1,), (1,)), ((), ())), preferred_element_type=jnp.float32)


def rms_scale(values, gain_vec):
    mean_sq = jnp.mean(values * values, axis=-1, keepdims=True)
    return values * lax.rsqrt(mean_sq + 1e-05) * gain_vec


def iota(shape, dim):
    return lax.broadcasted_iota(jnp.int32, shape, dim)


def slot_of(owner, row_me, row_size, paired):
    half = row_size // 2
    return owner ^ row_me if paired else lax.rem(owner + lax.div(row_me, half) * half, row_size)


def request_kernel(tiles_here, row_size, ids_ref, me_ref, out_ref):
    half = row_size // 2
    peer, which = iota(out_ref.shape, 0), iota(out_ref.shape, 1)
    wanted = jnp.zeros(out_ref.shape, jnp.int32)
    for slot in range(ids_ref.shape[1]):
        tile = ids_ref[0, slot]
        owner = lax.div(tile, tiles_here)
        far = jnp.where(lax.div(owner, half) == lax.div(me_ref[0], half), 0, 1)
        here = (peer == jnp.where(tile < 0, -1, lax.rem(owner, half))) & (which == far)
        wanted = jnp.where(here, lax.rem(tile, tiles_here), wanted)
    out_ref[...] = wanted


def request(ids, me, tiles_here, row_size):
    return pl.pallas_call(
        functools.partial(request_kernel, tiles_here, row_size),
        out_shape=jax.ShapeDtypeStruct((row_size // 2, 2, 128), jnp.int32),
        in_specs=[SMEM, SMEM],
        out_specs=VMEM,
        compiler_params=params(0),
        cost_estimate=pl.CostEstimate(flops=0, bytes_accessed=MIB // 4, transcendentals=0),
        name="request",
    )(ids, me)


def pick_kernel(which, wanted_ref, tiles_ref, *refs):
    out_ref = refs[-1]
    for peer in range(out_ref.shape[0]):
        out_ref[peer] = tiles_ref[wanted_ref[peer, which, 0]]


def pick(tiles, wanted, which, after):
    return pl.pallas_call(
        functools.partial(pick_kernel, which),
        out_shape=jax.ShapeDtypeStruct(wanted.shape[:1] + tiles.shape[1:], tiles.dtype),
        in_specs=[SMEM, VMEM] + [ANY] * len(after),
        out_specs=VMEM,
        compiler_params=params(0),
        cost_estimate=pl.CostEstimate(flops=0, bytes_accessed=2 * MIB, transcendentals=0),
        name="pick",
    )(wanted, tiles, *after)


def pick_each_kernel(which, order, wanted_ref, me_ref, tiles_ref, *refs):
    place = lax.rem(me_ref[0], wanted_ref.shape[0])
    for step, out_ref in zip(order, refs[-len(order):]):
        out_ref[0] = tiles_ref[wanted_ref[place ^ step, which, 0]]


def pick_each(tiles, wanted, which, me, order, after):
    count = len(order)
    return pl.pallas_call(
        functools.partial(pick_each_kernel, which, order),
        out_shape=(jax.ShapeDtypeStruct((1,) + tiles.shape[1:], tiles.dtype),) * count,
        in_specs=[SMEM, SMEM, VMEM] + [ANY] * len(after),
        out_specs=(VMEM,) * count,
        compiler_params=params(0),
        cost_estimate=pl.CostEstimate(flops=0, bytes_accessed=2 * MIB, transcendentals=0),
        name="pick_each",
    )(wanted, me, tiles, *after)


def front_kernel(groups, heads, head_size, chunk, cols, heads_here, tiles_here, row_size, paired, *refs):
    cell_refs, refs = refs[:groups], refs[groups:]
    (ids_ref, me_ref, mask_ref, gain_col_ref, gain_tile_ref, w_qkv_hbm, w_out_hbm, w_query_hbm,
     resid_ref, asked_ref, normed_ref, packed_ref, w_qkv_ref, w_out_ref, w_query_ref, sems) = refs
    own_rows, width = resid_ref.shape
    steps = own_rows // chunk
    span = groups * chunk
    lanes_two = 2 * head_size
    group_width = heads_here * head_size
    if w_query_hbm.shape[1] != group_width:
        w_query_hbm = w_query_hbm.at[:, pl.ds(pl.multiple_of(me_ref[1] * group_width, group_width), group_width)]
    copies = [pltpu.make_async_copy(w_qkv_hbm.at[:, pl.ds(part * width, width)], w_qkv_ref.at[part], sems.at[part])
              for part in range(3)]
    copies.append(pltpu.make_async_copy(w_out_hbm, w_out_ref, sems.at[3]))
    copies.append(pltpu.make_async_copy(w_query_hbm, w_query_ref, sems.at[4]))
    for copy in copies:
        copy.start()

    def cells_of(group, step):
        cells = cell_refs[group][pl.ds(step * (chunk // cols), chunk // cols)].astype(jnp.float32)
        return cells.reshape(chunk, width)

    for step in range(steps):
        for group in range(groups):
            cells = cells_of(group, step)
            normed_ref[pl.ds(step * span + group * chunk, chunk), :] = rms_scale(cells, gain_col_ref[...]).astype(jnp.bfloat16)
    for part in range(3):
        copies[part].wait()
        packed_ref[part] = dot_rows(normed_ref[...], w_qkv_ref[part]).astype(jnp.bfloat16)
    stacked = heads * span
    same_row = iota((stacked, span), 0) % chunk // cols == iota((stacked, span), 1) % chunk // cols
    lane_low = iota((span, lanes_two), 1) < head_size
    scale = head_size ** (-0.5)
    for step in range(steps):
        rows = pl.ds(step * span, span)
        scores = []
        for head in range(heads):
            lanes = pl.ds(head // 2 * lanes_two, lanes_two)
            query = packed_ref[0, rows, lanes]
            query = jnp.where(lane_low == (head % 2 == 0), query, jnp.zeros_like(query))
            scores.append(dot_lanes(query, packed_ref[1, rows, lanes]))
        scores = jnp.where(same_row, jnp.concatenate(scores, axis=0) * scale, BIG)
        expo = jnp.exp(scores - jnp.max(scores, axis=1, keepdims=True))
        weights = (expo / jnp.sum(expo, axis=1, keepdims=True)).astype(jnp.bfloat16)
        for pair in range(heads // 2):
            lanes = pl.ds(pair * lanes_two, lanes_two)
            start = 2 * pair * span
            mixed = dot_rows(weights[start:start + 2 * span], packed_ref[2, rows, lanes])
            normed_ref[rows, lanes] = jnp.where(lane_low, mixed[:span], mixed[span:]).astype(jnp.bfloat16)
    copies[3].wait()
    delta = dot_rows(normed_ref[...], w_out_ref[...])
    for step in range(steps):
        for group in range(groups):
            start = step * span + group * chunk
            resid = cells_of(group, step) + delta[start:start + chunk]
            if group == 0:
                resid_ref[pl.ds(step * chunk, chunk), :] = resid
            normed_ref[pl.ds(start, chunk), :] = rms_scale(resid, gain_tile_ref[...]).astype(jnp.bfloat16)
    slots = mask_ref.shape[0]
    slot, lane = iota((slots, lanes_two), 0), iota((slots, lanes_two), 1)
    place = jnp.zeros((slots, lanes_two), jnp.float32)
    for index in range(slots):
        tile = ids_ref[0, index]
        spot = jnp.where(tile < 0, -1, head_size + slot_of(lax.div(tile, tiles_here), me_ref[0], row_size, paired))
        place = jnp.where((slot == index) & (lane == spot), 1.0, place)
    live = lax.dot_general((mask_ref[...] > 0).astype(jnp.float32).astype(jnp.bfloat16), place.astype(jnp.bfloat16),
                           (((0,), (0,)), ((), ())), preferred_element_type=jnp.float32)
    lane = iota(live.shape, 1)
    shut = jnp.where((lane >= head_size) & (lane < head_size + row_size) & (live < 0.5), 1.0, 0.0).astype(jnp.bfloat16)
    total = steps * span
    cell = iota((total, shut.shape[0]), 0)
    row_of = cell // span * (chunk // cols) + cell % chunk // cols
    spread = (row_of == iota((total, shut.shape[0]), 1)).astype(jnp.bfloat16)
    bias = dot_rows(spread, shut) * BIG
    copies[4].wait()
    asked = dot_rows(normed_ref[...], w_query_ref[...]).astype(jnp.bfloat16).astype(jnp.float32) * scale
    low = iota((total, lanes_two), 1) < head_size
    for head in range(heads_here):
        if heads_here % 2 == 0:
            two = asked[:, head // 2 * lanes_two:(head // 2 + 1) * lanes_two]
            one = two if head % 2 == 0 else pltpu.roll(two, head_size, 1)
            query = jnp.where(low, one, bias)
        else:
            one = asked[:, head * head_size:(head + 1) * head_size]
            query = jnp.concatenate([one, bias[:, head_size:]], axis=1)
        query = query.astype(jnp.bfloat16)
        for step in range(steps):
            for group in range(groups):
                start = step * span + group * chunk
                asked_ref[head, pl.ds(group * own_rows + step * chunk, chunk), :] = query[start:start + chunk]


def front(cells, ids, me, key_mask, gain_col, w_qkv, w_out, gain_tile, w_query, heads, head_size, cols,
          heads_here, tiles_here, row_size, paired):
    groups = len(cells)
    width = cells[0].shape[2]
    own_rows = cells[0].shape[0] * cols
    total = groups * own_rows
    weights = [(3, width, width), (width, width), (width, heads_here * head_size)]
    return pl.pallas_call(
        functools.partial(front_kernel, groups, heads, head_size, ROW_GROUP * cols, cols, heads_here, tiles_here, row_size, paired),
        out_shape=(jax.ShapeDtypeStruct((own_rows, width), jnp.float32),
                   jax.ShapeDtypeStruct((heads_here, total, 2 * head_size), jnp.bfloat16)),
        in_specs=[VMEM] * groups + [SMEM, SMEM] + [VMEM] * 3 + [HBM] * 3,
        out_specs=(VMEM, VMEM),
        scratch_shapes=[pltpu.VMEM((total, width), jnp.bfloat16), pltpu.VMEM((3, total, width), jnp.bfloat16)]
        + [pltpu.VMEM(shape, jnp.bfloat16) for shape in weights] + [pltpu.SemaphoreType.DMA((5,))],
        compiler_params=params(total),
        cost_estimate=pl.CostEstimate(flops=2 * total * width * 5 * width, bytes_accessed=4 * MIB,
                                      transcendentals=total * heads * 128),
        name="front",
    )(*cells, ids, me, key_mask.T, gain_col.reshape(1, width), gain_tile.reshape(1, width), w_qkv, w_out, w_query)


def weigh(query, tile_refs, head, slots):
    key_parts, val_parts = [], []
    for ref, slot in zip(tile_refs, slots):
        tiles = ref[:, head]
        count, keys, lanes = tiles.shape
        lane = iota(tiles.shape, 2)
        marks = (lane == iota(tiles.shape, 0) + (lanes // 2 + slot)).astype(tiles.dtype)
        key_parts.append(jnp.where(lane < lanes // 2, tiles, marks).reshape(count * keys, lanes))
        val_parts.append(jnp.where(lane < lanes // 2, jnp.ones_like(tiles), tiles).reshape(count * keys, lanes))
    scores = dot_lanes(query, jnp.concatenate(key_parts, axis=0))
    top = jnp.max(scores, axis=1, keepdims=True)
    return top, dot_rows(jnp.exp(scores - top).astype(jnp.bfloat16), jnp.concatenate(val_parts, axis=0))


def attention_cost(asked, tiles):
    heads, rows, lanes = asked.shape
    keys = sum(part.shape[0] * part.shape[2] for part in tiles)
    return pl.CostEstimate(flops=4 * rows * heads * keys * lanes, bytes_accessed=4 * MIB, transcendentals=rows * heads * keys)


def first_kernel(slots, block, asked_ref, *refs):
    tile_refs, (sums_ref, tops_ref) = refs[:len(slots)], refs[len(slots):]
    heads, rows_all, lanes = asked_ref.shape
    lane = iota((block, lanes), 1)
    for step in range(rows_all // block):
        rows = pl.ds(step * block, block)
        tops = jnp.zeros((block, lanes), jnp.float32)
        for head in range(heads):
            top, sums_ref[head, rows, :] = weigh(asked_ref[head, rows, :], tile_refs, head, slots)
            tops = jnp.where(lane == head, top, tops)
        tops_ref[rows, :] = tops


def first_tiles(asked, tiles, slots, own_rows):
    heads, rows, lanes = asked.shape
    return pl.pallas_call(
        functools.partial(first_kernel, slots, rows if rows <= 512 else own_rows),
        out_shape=(jax.ShapeDtypeStruct((heads, rows, lanes), jnp.float32), jax.ShapeDtypeStruct((rows, lanes), jnp.float32)),
        in_specs=[VMEM] * (1 + len(tiles)),
        out_specs=(VMEM, VMEM),
        compiler_params=params(rows),
        cost_estimate=attention_cost(asked, tiles),
        name="first_tiles",
    )(asked, *tiles)


def last_kernel(slots, groups, asked_ref, sums_ref, tops_ref, *refs):
    tile_refs, out_refs = refs[:len(slots)], refs[-len(groups):]
    heads, lanes = asked_ref.shape[0], asked_ref.shape[2]
    block = out_refs[0].shape[0]
    half = lanes // 2
    lane_low = iota((block, lanes), 1) < half
    for group, out_ref in zip(groups, out_refs):
        rows = pl.ds(group * block, block)
        low = None
        for head in range(heads):
            top, sums = weigh(asked_ref[head, rows, :], tile_refs, head, slots)
            old_top = tops_ref[rows, head:head + 1]
            new_top = jnp.maximum(top, old_top)
            sums = sums_ref[head, rows, :] * jnp.exp(old_top - new_top) + sums * jnp.exp(top - new_top)
            turned = pltpu.roll(sums, half, 1)
            if head % 2:
                out_ref[:, pl.ds(head // 2 * lanes, lanes)] = jnp.where(lane_low, low, sums / turned).astype(jnp.bfloat16)
            elif head + 1 < heads:
                low = turned / sums
            else:
                out_ref[:, pl.ds(head * half, half)] = (turned / sums)[:, :half].astype(jnp.bfloat16)


def last_tiles(asked, sums, tops, tiles, slots, groups, own_rows, after):
    heads, rows, lanes = asked.shape
    out = jax.ShapeDtypeStruct((own_rows, heads * lanes // 2), jnp.bfloat16)
    return pl.pallas_call(
        functools.partial(last_kernel, slots, groups),
        out_shape=(out,) * len(groups),
        in_specs=[VMEM] * (3 + len(tiles)) + [ANY] * len(after),
        out_specs=(VMEM,) * len(groups),
        compiler_params=params(rows),
        cost_estimate=attention_cost(asked[:, :own_rows * len(groups)], tiles),
        name="last_tiles",
    )(asked, sums, tops, *tiles, *after)


def finish_kernel(me_ref, weight_ref, resid_ref, *refs):
    answer_refs, out_ref = refs[:-1], refs[-1]
    group_width = answer_refs[0].shape[1]
    final = resid_ref[...]
    for step, answer_ref in enumerate(answer_refs):
        group = lax.rem(me_ref[1] - step + len(answer_refs), len(answer_refs))
        rows = pl.ds(pl.multiple_of(group * group_width, group_width), group_width)
        final = final + dot_rows(answer_ref[...], weight_ref[rows, :])
    out_ref[...] = final.reshape(out_ref.shape).astype(out_ref.dtype)


def finish(me, weight, residual, answers, shape):
    return pl.pallas_call(
        finish_kernel,
        out_shape=jax.ShapeDtypeStruct(shape, jnp.bfloat16),
        in_specs=[SMEM, VMEM, VMEM] + [VMEM] * len(answers),
        out_specs=VMEM,
        compiler_params=params(0),
        cost_estimate=pl.CostEstimate(flops=2 * residual.size * weight.shape[0], bytes_accessed=MIB, transcendentals=0),
        name="finish",
    )(me, weight, residual, *answers)


def turn(size, step):
    return [(src, (src + step) % size) for src in range(size)]


def shards(row_size, col_size, fact_cells, gain_col, w_qkv, w_col_out, gain_tile, w_query, w_tile_out,
           tile_kv, tile_ids, key_mask):
    rows, cols, width = fact_cells.shape
    tiles_here, keys, heads_here, lanes = tile_kv.shape
    head_size = lanes // 2
    heads_all = width // head_size
    group_width = heads_here * head_size
    half = row_size // 2
    row_me, col_me = lax.axis_index("rows"), lax.axis_index("cols")
    me = jnp.stack([row_me, col_me]).astype(jnp.int32)
    halves = [list(range(half)), list(range(half, row_size))]
    paired = half <= 8 and half & (half - 1) == 0
    assert row_size <= head_size and row_size % 2 == 0

    def swap(value):
        return lax.all_to_all(value, "rows", split_axis=0, concat_axis=0, tiled=True, axis_index_groups=halves)

    heads_first = jnp.transpose(tile_kv, (0, 2, 1, 3))
    mirrored = lax.ppermute(heads_first, "rows", turn(row_size, half))
    asked_by = swap(request(tile_ids, me, tiles_here, row_size))

    cells = [fact_cells]
    for step in range(1, col_size):
        cells.append(lax.ppermute(fact_cells, "cols", turn(col_size, -step)))

    order = [0] + sorted(range(1, half), key=lambda step: (-(step & half // 2), step & 1, -step))
    slots = order if paired else [0]

    def spread(tiles, which, after):
        if not paired:
            return [swap(pick(tiles, asked_by, which, after))]
        picked = pick_each(tiles, asked_by, which, me, order, after)
        return [tile if step == 0 else lax.ppermute(tile, "rows", [(row, row ^ step) for row in range(row_size)])
                for step, tile in zip(order, picked)]

    near = spread(heads_first, 0, cells[1:])
    if group_width % 128:
        w_query = lax.dynamic_slice_in_dim(w_query, col_me * group_width, group_width, 1)
    w_qkv, w_col_out, w_query = [pltpu.with_memory_space_constraint(weight, pltpu.HBM) for weight in (w_qkv, w_col_out, w_query)]
    residual, asked = front(cells, tile_ids, me, key_mask, gain_col, w_qkv, w_col_out, gain_tile, w_query,
                            heads_all, head_size, cols, heads_here, tiles_here, row_size, paired)
    far = spread(mirrored, 1, near + [asked])
    sums, tops = first_tiles(asked, near, slots, rows * cols)
    far_slots = [half + slot for slot in slots]
    others = last_tiles(asked, sums, tops, far, far_slots, list(range(1, col_size)), rows * cols, [])
    own = last_tiles(asked, sums, tops, far, far_slots, [0], rows * cols, others[:1])
    answers = list(own) + [lax.ppermute(other, "cols", turn(col_size, step + 1)) for step, other in enumerate(others)]
    return finish(me, w_tile_out, residual, answers, fact_cells.shape)


def solution(mesh):
    row_size, col_size = mesh.shape["rows"], mesh.shape["cols"]
    placed = (P("rows", "cols", None), P(), P(), P(), P(), P(), P(), P("rows", None, "cols", None),
              P("rows", None), P("rows", None))

    def body(*arrays):
        return shards(row_size, col_size, *arrays)

    return jax.shard_map(body, mesh=mesh, in_specs=placed, out_specs=P("rows", "cols", None), check_vma=False)
```

```python
import functools

import jax
import jax.numpy as jnp
from jax import lax
from jax.experimental import pallas as pl
from jax.experimental.pallas import tpu as pltpu
from jax.sharding import PartitionSpec as P

ROW_GROUP = 16
BIG = -1e30
MIB = 1024 * 1024
VMEM = pl.BlockSpec(memory_space=pltpu.VMEM)
SMEM = pl.BlockSpec(memory_space=pltpu.SMEM)
HBM = pl.BlockSpec(memory_space=pltpu.HBM)
ANY = pl.BlockSpec(memory_space=pl.ANY)


def params(rows):
    return pltpu.CompilerParams(vmem_limit_bytes=(20 if rows <= 512 else 48) * MIB)


def dot_rows(left, right):
    return lax.dot_general(left, right, (((1,), (0,)), ((), ())), preferred_element_type=jnp.float32)


def dot_lanes(left, right):
    return lax.dot_general(left, right, (((1,), (1,)), ((), ())), preferred_element_type=jnp.float32)


def rms_scale(values, gain_vec):
    mean_sq = jnp.mean(values * values, axis=-1, keepdims=True)
    return values * lax.rsqrt(mean_sq + 1e-05) * gain_vec


def iota(shape, dim):
    return lax.broadcasted_iota(jnp.int32, shape, dim)


def slot_of(owner, row_me, row_size, paired):
    half = row_size // 2
    return owner ^ row_me if paired else lax.rem(owner + lax.div(row_me, half) * half, row_size)


def request_kernel(tiles_here, row_size, ids_ref, me_ref, out_ref):
    half = row_size // 2
    peer, which = iota(out_ref.shape, 0), iota(out_ref.shape, 1)
    wanted = jnp.zeros(out_ref.shape, jnp.int32)
    for slot in range(ids_ref.shape[1]):
        tile = ids_ref[0, slot]
        owner = lax.div(tile, tiles_here)
        far = jnp.where(lax.div(owner, half) == lax.div(me_ref[0], half), 0, 1)
        here = (peer == jnp.where(tile < 0, -1, lax.rem(owner, half))) & (which == far)
        wanted = jnp.where(here, lax.rem(tile, tiles_here), wanted)
    out_ref[...] = wanted


def request(ids, me, tiles_here, row_size):
    return pl.pallas_call(
        functools.partial(request_kernel, tiles_here, row_size),
        out_shape=jax.ShapeDtypeStruct((row_size // 2, 2, 128), jnp.int32),
        in_specs=[SMEM, SMEM],
        out_specs=VMEM,
        compiler_params=params(0),
        cost_estimate=pl.CostEstimate(flops=0, bytes_accessed=MIB // 4, transcendentals=0),
        name="request",
    )(ids, me)


def pick_kernel(which, wanted_ref, tiles_ref, *refs):
    out_ref = refs[-1]
    for peer in range(out_ref.shape[0]):
        out_ref[peer] = tiles_ref[wanted_ref[peer, which, 0]]


def pick(tiles, wanted, which, after):
    return pl.pallas_call(
        functools.partial(pick_kernel, which),
        out_shape=jax.ShapeDtypeStruct(wanted.shape[:1] + tiles.shape[1:], tiles.dtype),
        in_specs=[SMEM, VMEM] + [ANY] * len(after),
        out_specs=VMEM,
        compiler_params=params(0),
        cost_estimate=pl.CostEstimate(flops=0, bytes_accessed=2 * MIB, transcendentals=0),
        name="pick",
    )(wanted, tiles, *after)


def pick_each_kernel(which, order, wanted_ref, me_ref, tiles_ref, *refs):
    place = lax.rem(me_ref[0], wanted_ref.shape[0])
    for step, out_ref in zip(order, refs[-len(order):]):
        out_ref[0] = tiles_ref[wanted_ref[place ^ step, which, 0]]


def pick_each(tiles, wanted, which, me, order, after):
    count = len(order)
    return pl.pallas_call(
        functools.partial(pick_each_kernel, which, order),
        out_shape=(jax.ShapeDtypeStruct((1,) + tiles.shape[1:], tiles.dtype),) * count,
        in_specs=[SMEM, SMEM, VMEM] + [ANY] * len(after),
        out_specs=(VMEM,) * count,
        compiler_params=params(0),
        cost_estimate=pl.CostEstimate(flops=0, bytes_accessed=2 * MIB, transcendentals=0),
        name="pick_each",
    )(wanted, me, tiles, *after)


def front_kernel(groups, heads, head_size, chunk, cols, heads_here, tiles_here, row_size, paired, *refs):
    cell_refs, refs = refs[:groups], refs[groups:]
    (ids_ref, me_ref, mask_ref, gain_col_ref, gain_tile_ref, w_qkv_hbm, w_out_hbm, w_query_hbm,
     resid_ref, asked_ref, normed_ref, packed_ref, w_qkv_ref, w_out_ref, w_query_ref, sems) = refs
    own_rows, width = resid_ref.shape
    steps = own_rows // chunk
    span = groups * chunk
    lanes_two = 2 * head_size
    group_width = heads_here * head_size
    if w_query_hbm.shape[1] != group_width:
        w_query_hbm = w_query_hbm.at[:, pl.ds(pl.multiple_of(me_ref[1] * group_width, group_width), group_width)]
    copies = [pltpu.make_async_copy(w_qkv_hbm.at[:, pl.ds(part * width, width)], w_qkv_ref.at[part], sems.at[part])
              for part in range(3)]
    copies.append(pltpu.make_async_copy(w_out_hbm, w_out_ref, sems.at[3]))
    copies.append(pltpu.make_async_copy(w_query_hbm, w_query_ref, sems.at[4]))
    for copy in copies:
        copy.start()

    def cells_of(group, step):
        cells = cell_refs[group][pl.ds(step * (chunk // cols), chunk // cols)].astype(jnp.float32)
        return cells.reshape(chunk, width)

    for step in range(steps):
        for group in range(groups):
            cells = cells_of(group, step)
            normed_ref[pl.ds(step * span + group * chunk, chunk), :] = rms_scale(cells, gain_col_ref[...]).astype(jnp.bfloat16)
    for part in range(3):
        copies[part].wait()
        packed_ref[part] = dot_rows(normed_ref[...], w_qkv_ref[part]).astype(jnp.bfloat16)
    stacked = heads * span
    same_row = iota((stacked, span), 0) % chunk // cols == iota((stacked, span), 1) % chunk // cols
    lane_low = iota((span, lanes_two), 1) < head_size
    scale = head_size ** (-0.5)
    for step in range(steps):
        rows = pl.ds(step * span, span)
        scores = []
        for head in range(heads):
            lanes = pl.ds(head // 2 * lanes_two, lanes_two)
            query = packed_ref[0, rows, lanes]
            query = jnp.where(lane_low == (head % 2 == 0), query, jnp.zeros_like(query))
            scores.append(dot_lanes(query, packed_ref[1, rows, lanes]))
        scores = jnp.where(same_row, jnp.concatenate(scores, axis=0) * scale, BIG)
        expo = jnp.exp(scores - jnp.max(scores, axis=1, keepdims=True))
        weights = (expo / jnp.sum(expo, axis=1, keepdims=True)).astype(jnp.bfloat16)
        for pair in range(heads // 2):
            lanes = pl.ds(pair * lanes_two, lanes_two)
            start = 2 * pair * span
            mixed = dot_rows(weights[start:start + 2 * span], packed_ref[2, rows, lanes])
            normed_ref[rows, lanes] = jnp.where(lane_low, mixed[:span], mixed[span:]).astype(jnp.bfloat16)
    copies[3].wait()
    delta = dot_rows(normed_ref[...], w_out_ref[...])
    for step in range(steps):
        for group in range(groups):
            start = step * span + group * chunk
            resid = cells_of(group, step) + delta[start:start + chunk]
            if group == 0:
                resid_ref[pl.ds(step * chunk, chunk), :] = resid
            normed_ref[pl.ds(start, chunk), :] = rms_scale(resid, gain_tile_ref[...]).astype(jnp.bfloat16)
    slots = mask_ref.shape[0]
    slot, lane = iota((slots, lanes_two), 0), iota((slots, lanes_two), 1)
    place = jnp.zeros((slots, lanes_two), jnp.float32)
    for index in range(slots):
        tile = ids_ref[0, index]
        spot = jnp.where(tile < 0, -1, head_size + slot_of(lax.div(tile, tiles_here), me_ref[0], row_size, paired))
        place = jnp.where((slot == index) & (lane == spot), 1.0, place)
    live = lax.dot_general((mask_ref[...] > 0).astype(jnp.float32).astype(jnp.bfloat16), place.astype(jnp.bfloat16),
                           (((0,), (0,)), ((), ())), preferred_element_type=jnp.float32)
    lane = iota(live.shape, 1)
    shut = jnp.where((lane >= head_size) & (lane < head_size + row_size) & (live < 0.5), 1.0, 0.0).astype(jnp.bfloat16)
    total = steps * span
    cell = iota((total, shut.shape[0]), 0)
    row_of = cell // span * (chunk // cols) + cell % chunk // cols
    spread = (row_of == iota((total, shut.shape[0]), 1)).astype(jnp.bfloat16)
    bias = dot_rows(spread, shut) * BIG
    copies[4].wait()
    asked = dot_rows(normed_ref[...], w_query_ref[...]).astype(jnp.bfloat16).astype(jnp.float32) * scale
    low = iota((total, lanes_two), 1) < head_size
    for head in range(heads_here):
        if heads_here % 2 == 0:
            two = asked[:, head // 2 * lanes_two:(head // 2 + 1) * lanes_two]
            one = two if head % 2 == 0 else pltpu.roll(two, head_size, 1)
            query = jnp.where(low, one, bias)
        else:
            one = asked[:, head * head_size:(head + 1) * head_size]
            query = jnp.concatenate([one, bias[:, head_size:]], axis=1)
        query = query.astype(jnp.bfloat16)
        for step in range(steps):
            for group in range(groups):
                start = step * span + group * chunk
                asked_ref[head, pl.ds(group * own_rows + step * chunk, chunk), :] = query[start:start + chunk]


def front(cells, ids, me, key_mask, gain_col, w_qkv, w_out, gain_tile, w_query, heads, head_size, cols,
          heads_here, tiles_here, row_size, paired):
    groups = len(cells)
    width = cells[0].shape[2]
    own_rows = cells[0].shape[0] * cols
    total = groups * own_rows
    weights = [(3, width, width), (width, width), (width, heads_here * head_size)]
    return pl.pallas_call(
        functools.partial(front_kernel, groups, heads, head_size, ROW_GROUP * cols, cols, heads_here, tiles_here, row_size, paired),
        out_shape=(jax.ShapeDtypeStruct((own_rows, width), jnp.float32),
                   jax.ShapeDtypeStruct((heads_here, total, 2 * head_size), jnp.bfloat16)),
        in_specs=[VMEM] * groups + [SMEM, SMEM] + [VMEM] * 3 + [HBM] * 3,
        out_specs=(VMEM, VMEM),
        scratch_shapes=[pltpu.VMEM((total, width), jnp.bfloat16), pltpu.VMEM((3, total, width), jnp.bfloat16)]
        + [pltpu.VMEM(shape, jnp.bfloat16) for shape in weights] + [pltpu.SemaphoreType.DMA((5,))],
        compiler_params=params(total),
        cost_estimate=pl.CostEstimate(flops=2 * total * width * 5 * width, bytes_accessed=4 * MIB,
                                      transcendentals=total * heads * 128),
        name="front",
    )(*cells, ids, me, key_mask.T, gain_col.reshape(1, width), gain_tile.reshape(1, width), w_qkv, w_out, w_query)


def weigh(query, tile_refs, head, slots):
    key_parts, val_parts = [], []
    for ref, slot in zip(tile_refs, slots):
        tiles = ref[:, head]
        count, keys, lanes = tiles.shape
        lane = iota(tiles.shape, 2)
        marks = (lane == iota(tiles.shape, 0) + (lanes // 2 + slot)).astype(tiles.dtype)
        key_parts.append(jnp.where(lane < lanes // 2, tiles, marks).reshape(count * keys, lanes))
        val_parts.append(jnp.where(lane < lanes // 2, jnp.ones_like(tiles), tiles).reshape(count * keys, lanes))
    scores = dot_lanes(query, jnp.concatenate(key_parts, axis=0))
    top = jnp.max(scores, axis=1, keepdims=True)
    return top, dot_rows(jnp.exp(scores - top).astype(jnp.bfloat16), jnp.concatenate(val_parts, axis=0))


def attention_cost(asked, tiles):
    heads, rows, lanes = asked.shape
    keys = sum(part.shape[0] * part.shape[2] for part in tiles)
    return pl.CostEstimate(flops=4 * rows * heads * keys * lanes, bytes_accessed=4 * MIB, transcendentals=rows * heads * keys)


def first_kernel(slots, block, asked_ref, *refs):
    tile_refs, (sums_ref, tops_ref) = refs[:len(slots)], refs[len(slots):]
    heads, rows_all, lanes = asked_ref.shape
    lane = iota((block, lanes), 1)
    for step in range(rows_all // block):
        rows = pl.ds(step * block, block)
        tops = jnp.zeros((block, lanes), jnp.float32)
        for head in range(heads):
            top, sums_ref[head, rows, :] = weigh(asked_ref[head, rows, :], tile_refs, head, slots)
            tops = jnp.where(lane == head, top, tops)
        tops_ref[rows, :] = tops


def first_tiles(asked, tiles, slots, own_rows):
    heads, rows, lanes = asked.shape
    return pl.pallas_call(
        functools.partial(first_kernel, slots, rows if rows <= 512 else own_rows),
        out_shape=(jax.ShapeDtypeStruct((heads, rows, lanes), jnp.float32), jax.ShapeDtypeStruct((rows, lanes), jnp.float32)),
        in_specs=[VMEM] * (1 + len(tiles)),
        out_specs=(VMEM, VMEM),
        compiler_params=params(rows),
        cost_estimate=attention_cost(asked, tiles),
        name="first_tiles",
    )(asked, *tiles)


def last_kernel(slots, groups, asked_ref, sums_ref, tops_ref, *refs):
    tile_refs, out_refs = refs[:len(slots)], refs[-len(groups):]
    heads, lanes = asked_ref.shape[0], asked_ref.shape[2]
    block = out_refs[0].shape[0]
    half = lanes // 2
    lane_low = iota((block, lanes), 1) < half
    for group, out_ref in zip(groups, out_refs):
        rows = pl.ds(group * block, block)
        low = None
        for head in range(heads):
            top, sums = weigh(asked_ref[head, rows, :], tile_refs, head, slots)
            old_top = tops_ref[rows, head:head + 1]
            new_top = jnp.maximum(top, old_top)
            sums = sums_ref[head, rows, :] * jnp.exp(old_top - new_top) + sums * jnp.exp(top - new_top)
            turned = pltpu.roll(sums, half, 1)
            if head % 2:
                out_ref[:, pl.ds(head // 2 * lanes, lanes)] = jnp.where(lane_low, low, sums / turned).astype(jnp.bfloat16)
            elif head + 1 < heads:
                low = turned / sums
            else:
                out_ref[:, pl.ds(head * half, half)] = (turned / sums)[:, :half].astype(jnp.bfloat16)


def last_tiles(asked, sums, tops, tiles, slots, groups, own_rows, after):
    heads, rows, lanes = asked.shape
    out = jax.ShapeDtypeStruct((own_rows, heads * lanes // 2), jnp.bfloat16)
    return pl.pallas_call(
        functools.partial(last_kernel, slots, groups),
        out_shape=(out,) * len(groups),
        in_specs=[VMEM] * (3 + len(tiles)) + [ANY] * len(after),
        out_specs=(VMEM,) * len(groups),
        compiler_params=params(rows),
        cost_estimate=attention_cost(asked[:, :own_rows * len(groups)], tiles),
        name="last_tiles",
    )(asked, sums, tops, *tiles, *after)


def finish_kernel(me_ref, weight_ref, resid_ref, *refs):
    answer_refs, out_ref = refs[:-1], refs[-1]
    group_width = answer_refs[0].shape[1]
    final = resid_ref[...]
    for step, answer_ref in enumerate(answer_refs):
        group = lax.rem(me_ref[1] - step + len(answer_refs), len(answer_refs))
        rows = pl.ds(pl.multiple_of(group * group_width, group_width), group_width)
        final = final + dot_rows(answer_ref[...], weight_ref[rows, :])
    out_ref[...] = final.reshape(out_ref.shape).astype(out_ref.dtype)


def finish(me, weight, residual, answers, shape):
    return pl.pallas_call(
        finish_kernel,
        out_shape=jax.ShapeDtypeStruct(shape, jnp.bfloat16),
        in_specs=[SMEM, VMEM, VMEM] + [VMEM] * len(answers),
        out_specs=VMEM,
        compiler_params=params(0),
        cost_estimate=pl.CostEstimate(flops=2 * residual.size * weight.shape[0], bytes_accessed=MIB, transcendentals=0),
        name="finish",
    )(me, weight, residual, *answers)


def turn(size, step):
    return [(src, (src + step) % size) for src in range(size)]


def shards(row_size, col_size, fact_cells, gain_col, w_qkv, w_col_out, gain_tile, w_query, w_tile_out,
           tile_kv, tile_ids, key_mask):
    rows, cols, width = fact_cells.shape
    tiles_here, keys, heads_here, lanes = tile_kv.shape
    head_size = lanes // 2
    heads_all = width // head_size
    group_width = heads_here * head_size
    half = row_size // 2
    row_me, col_me = lax.axis_index("rows"), lax.axis_index("cols")
    me = jnp.stack([row_me, col_me]).astype(jnp.int32)
    halves = [list(range(half)), list(range(half, row_size))]
    paired = half <= 8 and half & (half - 1) == 0
    assert row_size <= head_size and row_size % 2 == 0

    def swap(value):
        return lax.all_to_all(value, "rows", split_axis=0, concat_axis=0, tiled=True, axis_index_groups=halves)

    heads_first = jnp.transpose(tile_kv, (0, 2, 1, 3))
    mirrored = lax.ppermute(heads_first, "rows", turn(row_size, half))
    asked_by = swap(request(tile_ids, me, tiles_here, row_size))

    cells = [fact_cells]
    for step in range(1, col_size):
        cells.append(lax.ppermute(fact_cells, "cols", turn(col_size, -step)))

    near_order = [0] + sorted(range(1, half), key=lambda step: (step & half // 2, step & 1, step))
    far_order = [0, 1] + sorted(range(2, half), key=lambda step: (step != 2, not step & half // 2, step & 1, step))
    near_slots, far_slots = (near_order, [half + step for step in far_order]) if paired else ([0], [half])

    def spread(tiles, which, order, after):
        if not paired:
            return [swap(pick(tiles, asked_by, which, after))]
        picked = pick_each(tiles, asked_by, which, me, order, after)
        return [tile if step == 0 else lax.ppermute(tile, "rows", [(row, row ^ step) for row in range(row_size)])
                for step, tile in zip(order, picked)]

    if group_width % 128:
        w_query = lax.dynamic_slice_in_dim(w_query, col_me * group_width, group_width, 1)
    w_qkv, w_col_out, w_query = [pltpu.with_memory_space_constraint(weight, pltpu.HBM) for weight in (w_qkv, w_col_out, w_query)]
    residual, asked = front(cells, tile_ids, me, key_mask, gain_col, w_qkv, w_col_out, gain_tile, w_query,
                            heads_all, head_size, cols, heads_here, tiles_here, row_size, paired)
    near = spread(heads_first, 0, near_order, [asked])
    far = spread(mirrored, 1, far_order, near)
    sums, tops = first_tiles(asked, near, near_slots, rows * cols)
    others = last_tiles(asked, sums, tops, far, far_slots, list(range(1, col_size)), rows * cols, [])
    own = last_tiles(asked, sums, tops, far, far_slots, [0], rows * cols, others[:1])
    answers = list(own) + [lax.ppermute(other, "cols", turn(col_size, step + 1)) for step, other in enumerate(others)]
    return finish(me, w_tile_out, residual, answers, fact_cells.shape)


def solution(mesh):
    row_size, col_size = mesh.shape["rows"], mesh.shape["cols"]
    placed = (P("rows", "cols", None), P(), P(), P(), P(), P(), P(), P("rows", None, "cols", None),
              P("rows", None), P("rows", None))

    def body(*arrays):
        return shards(row_size, col_size, *arrays)

    return jax.shard_map(body, mesh=mesh, in_specs=placed, out_specs=P("rows", "cols", None), check_vma=False)
```

```python
import functools

import jax
import jax.numpy as jnp
from jax import lax
from jax.experimental import pallas as pl
from jax.experimental.pallas import tpu as pltpu
from jax.sharding import PartitionSpec as P

ROW_GROUP = 16
BIG = -1e30
MIB = 1024 * 1024
VMEM = pl.BlockSpec(memory_space=pltpu.VMEM)
SMEM = pl.BlockSpec(memory_space=pltpu.SMEM)
HBM = pl.BlockSpec(memory_space=pltpu.HBM)
ANY = pl.BlockSpec(memory_space=pl.ANY)


def params(rows):
    return pltpu.CompilerParams(vmem_limit_bytes=(20 if rows <= 512 else 48) * MIB)


def dot_rows(left, right):
    return lax.dot_general(left, right, (((1,), (0,)), ((), ())), preferred_element_type=jnp.float32)


def dot_lanes(left, right):
    return lax.dot_general(left, right, (((1,), (1,)), ((), ())), preferred_element_type=jnp.float32)


def rms_scale(values, gain_vec):
    mean_sq = jnp.mean(values * values, axis=-1, keepdims=True)
    return values * lax.rsqrt(mean_sq + 1e-05) * gain_vec


def iota(shape, dim):
    return lax.broadcasted_iota(jnp.int32, shape, dim)


def slot_of(owner, row_me, row_size, paired):
    half = row_size // 2
    return owner ^ row_me if paired else lax.rem(owner + lax.div(row_me, half) * half, row_size)


def tie_kernel(value_ref, after_ref, out_ref):
    pass


def tie(value, after):
    return pl.pallas_call(
        tie_kernel,
        out_shape=jax.ShapeDtypeStruct(value.shape, value.dtype),
        in_specs=[ANY, ANY],
        out_specs=ANY,
        input_output_aliases={0: 0},
        compiler_params=params(0),
        cost_estimate=pl.CostEstimate(flops=0, bytes_accessed=0, transcendentals=0),
        name="tie",
    )(value, after)


def request_kernel(tiles_here, row_size, ids_ref, me_ref, out_ref):
    half = row_size // 2
    peer, which = iota(out_ref.shape, 0), iota(out_ref.shape, 1)
    wanted = jnp.zeros(out_ref.shape, jnp.int32)
    for slot in range(ids_ref.shape[1]):
        tile = ids_ref[0, slot]
        owner = lax.div(tile, tiles_here)
        far = jnp.where(lax.div(owner, half) == lax.div(me_ref[0], half), 0, 1)
        here = (peer == jnp.where(tile < 0, -1, lax.rem(owner, half))) & (which == far)
        wanted = jnp.where(here, lax.rem(tile, tiles_here), wanted)
    out_ref[...] = wanted


def request(ids, me, tiles_here, row_size):
    return pl.pallas_call(
        functools.partial(request_kernel, tiles_here, row_size),
        out_shape=jax.ShapeDtypeStruct((row_size // 2, 2, 128), jnp.int32),
        in_specs=[SMEM, SMEM],
        out_specs=VMEM,
        compiler_params=params(0),
        cost_estimate=pl.CostEstimate(flops=0, bytes_accessed=MIB // 4, transcendentals=0),
        name="request",
    )(ids, me)


def pick_kernel(which, wanted_ref, tiles_ref, *refs):
    out_ref = refs[-1]
    for peer in range(out_ref.shape[0]):
        out_ref[peer] = tiles_ref[wanted_ref[peer, which, 0]]


def pick(tiles, wanted, which, after):
    return pl.pallas_call(
        functools.partial(pick_kernel, which),
        out_shape=jax.ShapeDtypeStruct(wanted.shape[:1] + tiles.shape[1:], tiles.dtype),
        in_specs=[SMEM, VMEM] + [ANY] * len(after),
        out_specs=VMEM,
        compiler_params=params(0),
        cost_estimate=pl.CostEstimate(flops=0, bytes_accessed=2 * MIB, transcendentals=0),
        name="pick",
    )(wanted, tiles, *after)


def pick_each_kernel(which, order, wanted_ref, me_ref, tiles_ref, *refs):
    place = lax.rem(me_ref[0], wanted_ref.shape[0])
    for step, out_ref in zip(order, refs[-len(order):]):
        out_ref[0] = tiles_ref[wanted_ref[place ^ step, which, 0]]


def pick_each(tiles, wanted, which, me, order, after):
    count = len(order)
    return pl.pallas_call(
        functools.partial(pick_each_kernel, which, order),
        out_shape=(jax.ShapeDtypeStruct((1,) + tiles.shape[1:], tiles.dtype),) * count,
        in_specs=[SMEM, SMEM, VMEM] + [ANY] * len(after),
        out_specs=(VMEM,) * count,
        compiler_params=params(0),
        cost_estimate=pl.CostEstimate(flops=0, bytes_accessed=2 * MIB, transcendentals=0),
        name="pick_each",
    )(wanted, me, tiles, *after)


def front_kernel(groups, heads, head_size, chunk, cols, heads_here, tiles_here, row_size, paired, *refs):
    cell_hbms, refs = refs[:groups], refs[groups:]
    (me_ref, ids_hbm, mask_hbm, gain_col_hbm, gain_tile_hbm, w_qkv_hbm, w_out_hbm, w_query_hbm, after_ref,
     resid_ref, asked_ref, normed_ref, packed_ref, w_qkv_ref, w_out_ref, w_query_ref, cell_refs,
     ids_ref, mask_ref, gain_col_ref, gain_tile_ref, sems) = refs
    own_rows, width = resid_ref.shape
    steps = own_rows // chunk
    span = groups * chunk
    lanes_two = 2 * head_size
    group_width = heads_here * head_size
    if w_query_hbm.shape[1] != group_width:
        w_query_hbm = w_query_hbm.at[:, pl.ds(pl.multiple_of(me_ref[1] * group_width, group_width), group_width)]
    pairs = [(hbm, cell_refs.at[group]) for group, hbm in enumerate(cell_hbms)]
    pairs += [(gain_col_hbm, gain_col_ref)]
    pairs += [(w_qkv_hbm.at[:, pl.ds(part * width, width)], w_qkv_ref.at[part]) for part in range(3)]
    pairs += [(w_out_hbm, w_out_ref), (gain_tile_hbm, gain_tile_ref), (w_query_hbm, w_query_ref), (ids_hbm, ids_ref), (mask_hbm, mask_ref)]
    copies = [pltpu.make_async_copy(*pair, sems.at[index]) for index, pair in enumerate(pairs)]
    for copy in copies:
        copy.start()
    for copy in copies[:groups + 1]:
        copy.wait()
    copies = copies[groups + 1:]

    def cells_of(group, step):
        cells = cell_refs[group, pl.ds(step * (chunk // cols), chunk // cols)].astype(jnp.float32)
        return cells.reshape(chunk, width)

    for step in range(steps):
        for group in range(groups):
            cells = cells_of(group, step)
            normed_ref[pl.ds(step * span + group * chunk, chunk), :] = rms_scale(cells, gain_col_ref[...]).astype(jnp.bfloat16)
    for part in range(3):
        copies[part].wait()
        packed_ref[part] = dot_rows(normed_ref[...], w_qkv_ref[part]).astype(jnp.bfloat16)
    stacked = heads * span
    same_row = iota((stacked, span), 0) % chunk // cols == iota((stacked, span), 1) % chunk // cols
    lane_low = iota((span, lanes_two), 1) < head_size
    scale = head_size ** (-0.5)
    for step in range(steps):
        rows = pl.ds(step * span, span)
        scores = []
        for head in range(heads):
            lanes = pl.ds(head // 2 * lanes_two, lanes_two)
            query = packed_ref[0, rows, lanes]
            query = jnp.where(lane_low == (head % 2 == 0), query, jnp.zeros_like(query))
            scores.append(dot_lanes(query, packed_ref[1, rows, lanes]))
        scores = jnp.where(same_row, jnp.concatenate(scores, axis=0) * scale, BIG)
        expo = jnp.exp(scores - jnp.max(scores, axis=1, keepdims=True))
        weights = (expo / jnp.sum(expo, axis=1, keepdims=True)).astype(jnp.bfloat16)
        for pair in range(heads // 2):
            lanes = pl.ds(pair * lanes_two, lanes_two)
            start = 2 * pair * span
            mixed = dot_rows(weights[start:start + 2 * span], packed_ref[2, rows, lanes])
            normed_ref[rows, lanes] = jnp.where(lane_low, mixed[:span], mixed[span:]).astype(jnp.bfloat16)
    for copy in copies[3:]:
        copy.wait()
    delta = dot_rows(normed_ref[...], w_out_ref[...])
    for step in range(steps):
        for group in range(groups):
            start = step * span + group * chunk
            resid = cells_of(group, step) + delta[start:start + chunk]
            if group == 0:
                resid_ref[pl.ds(step * chunk, chunk), :] = resid
            normed_ref[pl.ds(start, chunk), :] = rms_scale(resid, gain_tile_ref[...]).astype(jnp.bfloat16)
    slots = mask_ref.shape[0]
    slot, lane = iota((slots, lanes_two), 0), iota((slots, lanes_two), 1)
    place = jnp.zeros((slots, lanes_two), jnp.float32)
    for index in range(slots):
        tile = ids_ref[0, index]
        spot = jnp.where(tile < 0, -1, head_size + slot_of(lax.div(tile, tiles_here), me_ref[0], row_size, paired))
        place = jnp.where((slot == index) & (lane == spot), 1.0, place)
    live = lax.dot_general((mask_ref[...] > 0).astype(jnp.float32).astype(jnp.bfloat16), place.astype(jnp.bfloat16),
                           (((0,), (0,)), ((), ())), preferred_element_type=jnp.float32)
    lane = iota(live.shape, 1)
    shut = jnp.where((lane >= head_size) & (lane < head_size + row_size) & (live < 0.5), 1.0, 0.0).astype(jnp.bfloat16)
    total = steps * span
    cell = iota((total, shut.shape[0]), 0)
    row_of = cell // span * (chunk // cols) + cell % chunk // cols
    spread = (row_of == iota((total, shut.shape[0]), 1)).astype(jnp.bfloat16)
    bias = dot_rows(spread, shut) * BIG
    asked = dot_rows(normed_ref[...], w_query_ref[...]).astype(jnp.bfloat16).astype(jnp.float32) * scale
    low = iota((total, lanes_two), 1) < head_size
    for head in range(heads_here):
        if heads_here % 2 == 0:
            two = asked[:, head // 2 * lanes_two:(head // 2 + 1) * lanes_two]
            one = two if head % 2 == 0 else pltpu.roll(two, head_size, 1)
            query = jnp.where(low, one, bias)
        else:
            one = asked[:, head * head_size:(head + 1) * head_size]
            query = jnp.concatenate([one, bias[:, head_size:]], axis=1)
        query = query.astype(jnp.bfloat16)
        for step in range(steps):
            for group in range(groups):
                start = step * span + group * chunk
                asked_ref[head, pl.ds(group * own_rows + step * chunk, chunk), :] = query[start:start + chunk]


def front(cells, ids, me, key_mask, gain_col, w_qkv, w_out, gain_tile, w_query, heads, head_size, cols,
          heads_here, tiles_here, row_size, paired, after):
    groups = len(cells)
    width = cells[0].shape[2]
    own_rows = cells[0].shape[0] * cols
    total = groups * own_rows
    key_mask, gain_col, gain_tile = key_mask.T, gain_col.reshape(1, width), gain_tile.reshape(1, width)
    weights = [(3, width, width), (width, width), (width, heads_here * head_size), (groups,) + cells[0].shape]
    scratch = [pltpu.VMEM(shape, jnp.bfloat16) for shape in [(total, width), (3, total, width)] + weights]
    scratch += [pltpu.SMEM(ids.shape, jnp.int32), pltpu.VMEM(key_mask.shape, jnp.int32)]
    scratch += [pltpu.VMEM((1, width), jnp.float32)] * 2 + [pltpu.SemaphoreType.DMA((groups + 9,))]
    fetched = [pltpu.with_memory_space_constraint(value, pltpu.HBM)
               for value in (ids, key_mask, gain_col, gain_tile, w_qkv, w_out, w_query)]
    own = pltpu.with_memory_space_constraint(cells[0], pltpu.HBM)
    return pl.pallas_call(
        functools.partial(front_kernel, groups, heads, head_size, ROW_GROUP * cols, cols, heads_here, tiles_here, row_size, paired),
        out_shape=(jax.ShapeDtypeStruct((own_rows, width), jnp.float32),
                   jax.ShapeDtypeStruct((heads_here, total, 2 * head_size), jnp.bfloat16)),
        in_specs=[HBM] + [ANY] * (groups - 1) + [SMEM] + [HBM] * 7 + [ANY],
        out_specs=(VMEM, VMEM),
        scratch_shapes=scratch,
        compiler_params=params(total),
        cost_estimate=pl.CostEstimate(flops=2 * total * width * 5 * width, bytes_accessed=4 * MIB,
                                      transcendentals=total * heads * 128),
        name="front",
    )(own, *cells[1:], me, *fetched, after)


def weigh(query, tile_refs, head, slots):
    key_parts, val_parts = [], []
    for ref, slot in zip(tile_refs, slots):
        tiles = ref[:, head]
        count, keys, lanes = tiles.shape
        lane = iota(tiles.shape, 2)
        marks = (lane == iota(tiles.shape, 0) + (lanes // 2 + slot)).astype(tiles.dtype)
        key_parts.append(jnp.where(lane < lanes // 2, tiles, marks).reshape(count * keys, lanes))
        val_parts.append(jnp.where(lane < lanes // 2, jnp.ones_like(tiles), tiles).reshape(count * keys, lanes))
    scores = dot_lanes(query, jnp.concatenate(key_parts, axis=0))
    top = jnp.max(scores, axis=1, keepdims=True)
    return top, dot_rows(jnp.exp(scores - top).astype(jnp.bfloat16), jnp.concatenate(val_parts, axis=0))


def attention_cost(asked, tiles):
    heads, rows, lanes = asked.shape
    keys = sum(part.shape[0] * part.shape[2] for part in tiles)
    return pl.CostEstimate(flops=4 * rows * heads * keys * lanes, bytes_accessed=4 * MIB, transcendentals=rows * heads * keys)


def first_kernel(slots, block, asked_ref, *refs):
    tile_refs, (sums_ref, tops_ref) = refs[:len(slots)], refs[len(slots):]
    heads, rows_all, lanes = asked_ref.shape
    lane = iota((block, lanes), 1)
    for step in range(rows_all // block):
        rows = pl.ds(step * block, block)
        tops = jnp.zeros((block, lanes), jnp.float32)
        for head in range(heads):
            top, sums_ref[head, rows, :] = weigh(asked_ref[head, rows, :], tile_refs, head, slots)
            tops = jnp.where(lane == head, top, tops)
        tops_ref[rows, :] = tops


def first_tiles(asked, tiles, slots, own_rows):
    heads, rows, lanes = asked.shape
    return pl.pallas_call(
        functools.partial(first_kernel, slots, rows if rows <= 512 else own_rows),
        out_shape=(jax.ShapeDtypeStruct((heads, rows, lanes), jnp.float32), jax.ShapeDtypeStruct((rows, lanes), jnp.float32)),
        in_specs=[VMEM] * (1 + len(tiles)),
        out_specs=(VMEM, VMEM),
        compiler_params=params(rows),
        cost_estimate=attention_cost(asked, tiles),
        name="first_tiles",
    )(asked, *tiles)


def last_kernel(slots, groups, asked_ref, sums_ref, tops_ref, *refs):
    tile_refs, out_refs = refs[:len(slots)], refs[-len(groups):]
    heads, lanes = asked_ref.shape[0], asked_ref.shape[2]
    block = out_refs[0].shape[0]
    half = lanes // 2
    lane_low = iota((block, lanes), 1) < half
    for group, out_ref in zip(groups, out_refs):
        rows = pl.ds(group * block, block)
        low = None
        for head in range(heads):
            top, sums = weigh(asked_ref[head, rows, :], tile_refs, head, slots)
            old_top = tops_ref[rows, head:head + 1]
            new_top = jnp.maximum(top, old_top)
            sums = sums_ref[head, rows, :] * jnp.exp(old_top - new_top) + sums * jnp.exp(top - new_top)
            turned = pltpu.roll(sums, half, 1)
            if head % 2:
                out_ref[:, pl.ds(head // 2 * lanes, lanes)] = jnp.where(lane_low, low, sums / turned).astype(jnp.bfloat16)
            elif head + 1 < heads:
                low = turned / sums
            else:
                out_ref[:, pl.ds(head * half, half)] = (turned / sums)[:, :half].astype(jnp.bfloat16)


def last_tiles(asked, sums, tops, tiles, slots, groups, own_rows, after):
    heads, rows, lanes = asked.shape
    out = jax.ShapeDtypeStruct((own_rows, heads * lanes // 2), jnp.bfloat16)
    return pl.pallas_call(
        functools.partial(last_kernel, slots, groups),
        out_shape=(out,) * len(groups),
        in_specs=[VMEM] * (3 + len(tiles)) + [ANY] * len(after),
        out_specs=(VMEM,) * len(groups),
        compiler_params=params(rows),
        cost_estimate=attention_cost(asked[:, :own_rows * len(groups)], tiles),
        name="last_tiles",
    )(asked, sums, tops, *tiles, *after)


def finish_kernel(me_ref, weight_ref, resid_ref, *refs):
    answer_refs, out_ref = refs[:-1], refs[-1]
    group_width = answer_refs[0].shape[1]
    final = resid_ref[...]
    for step, answer_ref in enumerate(answer_refs):
        group = lax.rem(me_ref[1] - step + len(answer_refs), len(answer_refs))
        rows = pl.ds(pl.multiple_of(group * group_width, group_width), group_width)
        final = final + dot_rows(answer_ref[...], weight_ref[rows, :])
    out_ref[...] = final.reshape(out_ref.shape).astype(out_ref.dtype)


def finish(me, weight, residual, answers, shape):
    return pl.pallas_call(
        finish_kernel,
        out_shape=jax.ShapeDtypeStruct(shape, jnp.bfloat16),
        in_specs=[SMEM, VMEM, VMEM] + [VMEM] * len(answers),
        out_specs=VMEM,
        compiler_params=params(0),
        cost_estimate=pl.CostEstimate(flops=2 * residual.size * weight.shape[0], bytes_accessed=MIB, transcendentals=0),
        name="finish",
    )(me, weight, residual, *answers)


def turn(size, step):
    return [(src, (src + step) % size) for src in range(size)]


def shards(row_size, col_size, fact_cells, gain_col, w_qkv, w_col_out, gain_tile, w_query, w_tile_out,
           tile_kv, tile_ids, key_mask):
    rows, cols, width = fact_cells.shape
    tiles_here, keys, heads_here, lanes = tile_kv.shape
    head_size = lanes // 2
    heads_all = width // head_size
    group_width = heads_here * head_size
    half = row_size // 2
    row_me, col_me = lax.axis_index("rows"), lax.axis_index("cols")
    me = jnp.stack([row_me, col_me]).astype(jnp.int32)
    halves = [list(range(half)), list(range(half, row_size))]
    paired = half <= 8 and half & (half - 1) == 0
    assert row_size <= head_size and row_size % 2 == 0

    def swap(value):
        return lax.all_to_all(value, "rows", split_axis=0, concat_axis=0, tiled=True, axis_index_groups=halves)

    asked_of = request(tile_ids, me, tiles_here, row_size)
    asked_by = swap(asked_of)
    heads_first = tie(jnp.transpose(tile_kv, (0, 2, 1, 3)), asked_of)
    mirrored = lax.ppermute(heads_first, "rows", turn(row_size, half))

    cells = [fact_cells]
    for step in range(1, col_size):
        cells.append(lax.ppermute(fact_cells, "cols", turn(col_size, -step)))

    order = [0, 1] + sorted(range(2, half), key=lambda step: (step != 2, not step & half // 2, step & 1, step))
    near_slots, far_slots = (order, [half + step for step in order]) if paired else ([0], [half])

    def spread(tiles, which, after):
        if not paired:
            return [swap(pick(tiles, asked_by, which, after))]
        picked = pick_each(tiles, asked_by, which, me, order, after)
        return [tile if step == 0 else lax.ppermute(tile, "rows", [(row, row ^ step) for row in range(row_size)])
                for step, tile in zip(order, picked)]

    if group_width % 128:
        w_query = lax.dynamic_slice_in_dim(w_query, col_me * group_width, group_width, 1)
    near = spread(heads_first, 0, [])
    residual, asked = front(cells, tile_ids, me, key_mask, gain_col, w_qkv, w_col_out, gain_tile, w_query,
                            heads_all, head_size, cols, heads_here, tiles_here, row_size, paired, near[0])
    far = spread(mirrored, 1, [asked] + near[1:3])
    sums, tops = first_tiles(asked, near, near_slots, rows * cols)
    others = last_tiles(asked, sums, tops, far, far_slots, list(range(1, col_size)), rows * cols, [])
    own = last_tiles(asked, sums, tops, far, far_slots, [0], rows * cols, others[:1])
    answers = list(own) + [lax.ppermute(other, "cols", turn(col_size, step + 1)) for step, other in enumerate(others)]
    return finish(me, w_tile_out, residual, answers, fact_cells.shape)


def solution(mesh):
    row_size, col_size = mesh.shape["rows"], mesh.shape["cols"]
    placed = (P("rows", "cols", None), P(), P(), P(), P(), P(), P(), P("rows", None, "cols", None),
              P("rows", None), P("rows", None))

    def body(*arrays):
        return shards(row_size, col_size, *arrays)

    return jax.shard_map(body, mesh=mesh, in_specs=placed, out_specs=P("rows", "cols", None), check_vma=False)
```

```python
import functools

import jax
import jax.numpy as jnp
from jax import lax
from jax.experimental import pallas as pl
from jax.experimental.pallas import tpu as pltpu
from jax.sharding import PartitionSpec as P

ROW_GROUP = 16
BIG = -1e30
MIB = 1024 * 1024
VMEM = pl.BlockSpec(memory_space=pltpu.VMEM)
SMEM = pl.BlockSpec(memory_space=pltpu.SMEM)
HBM = pl.BlockSpec(memory_space=pltpu.HBM)
ANY = pl.BlockSpec(memory_space=pl.ANY)


def params(rows):
    return pltpu.CompilerParams(vmem_limit_bytes=(20 if rows <= 512 else 48) * MIB)


def dot_rows(left, right):
    return lax.dot_general(left, right, (((1,), (0,)), ((), ())), preferred_element_type=jnp.float32)


def dot_lanes(left, right):
    return lax.dot_general(left, right, (((1,), (1,)), ((), ())), preferred_element_type=jnp.float32)


def rms_scale(values, gain_vec):
    mean_sq = jnp.mean(values * values, axis=-1, keepdims=True)
    return values * lax.rsqrt(mean_sq + 1e-05) * gain_vec


def iota(shape, dim):
    return lax.broadcasted_iota(jnp.int32, shape, dim)


def slot_of(owner, row_me, row_size, paired):
    half = row_size // 2
    return owner ^ row_me if paired else lax.rem(owner + lax.div(row_me, half) * half, row_size)


def tie_kernel(value_ref, after_ref, out_ref):
    pass


def tie(value, after):
    return pl.pallas_call(
        tie_kernel,
        out_shape=jax.ShapeDtypeStruct(value.shape, value.dtype),
        in_specs=[ANY, ANY],
        out_specs=ANY,
        input_output_aliases={0: 0},
        compiler_params=params(0),
        cost_estimate=pl.CostEstimate(flops=0, bytes_accessed=0, transcendentals=0),
        name="tie",
    )(value, after)


def request_kernel(tiles_here, row_size, ids_ref, me_ref, out_ref):
    half = row_size // 2
    peer, which = iota(out_ref.shape, 0), iota(out_ref.shape, 1)
    wanted = jnp.zeros(out_ref.shape, jnp.int32)
    for slot in range(ids_ref.shape[1]):
        tile = ids_ref[0, slot]
        owner = lax.div(tile, tiles_here)
        far = jnp.where(lax.div(owner, half) == lax.div(me_ref[0], half), 0, 1)
        here = (peer == jnp.where(tile < 0, -1, lax.rem(owner, half))) & (which == far)
        wanted = jnp.where(here, lax.rem(tile, tiles_here), wanted)
    out_ref[...] = wanted


def request(ids, me, tiles_here, row_size):
    return pl.pallas_call(
        functools.partial(request_kernel, tiles_here, row_size),
        out_shape=jax.ShapeDtypeStruct((row_size // 2, 2, 128), jnp.int32),
        in_specs=[SMEM, SMEM],
        out_specs=VMEM,
        compiler_params=params(0),
        cost_estimate=pl.CostEstimate(flops=0, bytes_accessed=MIB // 4, transcendentals=0),
        name="request",
    )(ids, me)


def pick_kernel(which, wanted_ref, tiles_ref, *refs):
    out_ref = refs[-1]
    for peer in range(out_ref.shape[0]):
        out_ref[peer] = tiles_ref[wanted_ref[peer, which, 0]]


def pick(tiles, wanted, which, after):
    return pl.pallas_call(
        functools.partial(pick_kernel, which),
        out_shape=jax.ShapeDtypeStruct(wanted.shape[:1] + tiles.shape[1:], tiles.dtype),
        in_specs=[SMEM, VMEM] + [ANY] * len(after),
        out_specs=VMEM,
        compiler_params=params(0),
        cost_estimate=pl.CostEstimate(flops=0, bytes_accessed=2 * MIB, transcendentals=0),
        name="pick",
    )(wanted, tiles, *after)


def pick_each_kernel(which, order, wanted_ref, me_ref, tiles_ref, *refs):
    place = lax.rem(me_ref[0], wanted_ref.shape[0])
    for step, out_ref in zip(order, refs[-len(order):]):
        out_ref[0] = tiles_ref[wanted_ref[place ^ step, which, 0]]


def pick_each(tiles, wanted, which, me, order, after):
    count = len(order)
    return pl.pallas_call(
        functools.partial(pick_each_kernel, which, order),
        out_shape=(jax.ShapeDtypeStruct((1,) + tiles.shape[1:], tiles.dtype),) * count,
        in_specs=[SMEM, SMEM, VMEM] + [ANY] * len(after),
        out_specs=(VMEM,) * count,
        compiler_params=params(0),
        cost_estimate=pl.CostEstimate(flops=0, bytes_accessed=2 * MIB, transcendentals=0),
        name="pick_each",
    )(wanted, me, tiles, *after)


def front_kernel(groups, heads, head_size, chunk, cols, heads_here, tiles_here, row_size, paired, *refs):
    cell_hbms, refs = refs[:groups], refs[groups:]
    (me_ref, ids_hbm, mask_hbm, gain_col_hbm, gain_tile_hbm, w_qkv_hbm, w_out_hbm, w_query_hbm, after_ref,
     resid_ref, asked_ref, normed_ref, packed_ref, w_qkv_ref, w_out_ref, w_query_ref, cell_refs,
     ids_ref, mask_ref, gain_col_ref, gain_tile_ref, sems) = refs
    own_rows, width = resid_ref.shape
    steps = own_rows // chunk
    span = groups * chunk
    lanes_two = 2 * head_size
    group_width = heads_here * head_size
    if w_query_hbm.shape[1] != group_width:
        w_query_hbm = w_query_hbm.at[:, pl.ds(pl.multiple_of(me_ref[1] * group_width, group_width), group_width)]
    pairs = [(hbm, cell_refs.at[group]) for group, hbm in enumerate(cell_hbms)]
    pairs += [(gain_col_hbm, gain_col_ref)]
    pairs += [(w_qkv_hbm.at[:, pl.ds(part * width, width)], w_qkv_ref.at[part]) for part in range(3)]
    pairs += [(w_out_hbm, w_out_ref), (gain_tile_hbm, gain_tile_ref), (w_query_hbm, w_query_ref), (ids_hbm, ids_ref), (mask_hbm, mask_ref)]
    copies = [pltpu.make_async_copy(*pair, sems.at[index]) for index, pair in enumerate(pairs)]
    for copy in copies:
        copy.start()
    for copy in copies[:groups + 1]:
        copy.wait()
    copies = copies[groups + 1:]

    def cells_of(group, step):
        cells = cell_refs[group, pl.ds(step * (chunk // cols), chunk // cols)].astype(jnp.float32)
        return cells.reshape(chunk, width)

    for step in range(steps):
        for group in range(groups):
            cells = cells_of(group, step)
            normed_ref[pl.ds(step * span + group * chunk, chunk), :] = rms_scale(cells, gain_col_ref[...]).astype(jnp.bfloat16)
    for part in range(3):
        copies[part].wait()
        packed_ref[part] = dot_rows(normed_ref[...], w_qkv_ref[part]).astype(jnp.bfloat16)
    stacked = heads * span
    same_row = iota((stacked, span), 0) % chunk // cols == iota((stacked, span), 1) % chunk // cols
    lane_low = iota((span, lanes_two), 1) < head_size
    scale = head_size ** (-0.5)
    for step in range(steps):
        rows = pl.ds(step * span, span)
        scores = []
        for head in range(heads):
            lanes = pl.ds(head // 2 * lanes_two, lanes_two)
            query = packed_ref[0, rows, lanes]
            query = jnp.where(lane_low == (head % 2 == 0), query, jnp.zeros_like(query))
            scores.append(dot_lanes(query, packed_ref[1, rows, lanes]))
        scores = jnp.where(same_row, jnp.concatenate(scores, axis=0) * scale, BIG)
        expo = jnp.exp(scores - jnp.max(scores, axis=1, keepdims=True))
        weights = (expo / jnp.sum(expo, axis=1, keepdims=True)).astype(jnp.bfloat16)
        for pair in range(heads // 2):
            lanes = pl.ds(pair * lanes_two, lanes_two)
            start = 2 * pair * span
            mixed = dot_rows(weights[start:start + 2 * span], packed_ref[2, rows, lanes])
            normed_ref[rows, lanes] = jnp.where(lane_low, mixed[:span], mixed[span:]).astype(jnp.bfloat16)
    for copy in copies[3:]:
        copy.wait()
    delta = dot_rows(normed_ref[...], w_out_ref[...])
    for step in range(steps):
        for group in range(groups):
            start = step * span + group * chunk
            resid = cells_of(group, step) + delta[start:start + chunk]
            if group == 0:
                resid_ref[pl.ds(step * chunk, chunk), :] = resid
            normed_ref[pl.ds(start, chunk), :] = rms_scale(resid, gain_tile_ref[...]).astype(jnp.bfloat16)
    slots = mask_ref.shape[0]
    slot, lane = iota((slots, lanes_two), 0), iota((slots, lanes_two), 1)
    place = jnp.zeros((slots, lanes_two), jnp.float32)
    for index in range(slots):
        tile = ids_ref[0, index]
        spot = jnp.where(tile < 0, -1, head_size + slot_of(lax.div(tile, tiles_here), me_ref[0], row_size, paired))
        place = jnp.where((slot == index) & (lane == spot), 1.0, place)
    live = lax.dot_general((mask_ref[...] > 0).astype(jnp.float32).astype(jnp.bfloat16), place.astype(jnp.bfloat16),
                           (((0,), (0,)), ((), ())), preferred_element_type=jnp.float32)
    lane = iota(live.shape, 1)
    shut = jnp.where((lane >= head_size) & (lane < head_size + row_size) & (live < 0.5), 1.0, 0.0).astype(jnp.bfloat16)
    total = steps * span
    cell = iota((total, shut.shape[0]), 0)
    row_of = cell // span * (chunk // cols) + cell % chunk // cols
    spread = (row_of == iota((total, shut.shape[0]), 1)).astype(jnp.bfloat16)
    bias = dot_rows(spread, shut) * BIG
    asked = dot_rows(normed_ref[...], w_query_ref[...]).astype(jnp.bfloat16).astype(jnp.float32) * scale
    low = iota((total, lanes_two), 1) < head_size
    for head in range(heads_here):
        if heads_here % 2 == 0:
            two = asked[:, head // 2 * lanes_two:(head // 2 + 1) * lanes_two]
            one = two if head % 2 == 0 else pltpu.roll(two, head_size, 1)
            query = jnp.where(low, one, bias)
        else:
            one = asked[:, head * head_size:(head + 1) * head_size]
            query = jnp.concatenate([one, bias[:, head_size:]], axis=1)
        query = query.astype(jnp.bfloat16)
        for step in range(steps):
            for group in range(groups):
                start = step * span + group * chunk
                asked_ref[head, pl.ds(group * own_rows + step * chunk, chunk), :] = query[start:start + chunk]


def front(cells, ids, me, key_mask, gain_col, w_qkv, w_out, gain_tile, w_query, heads, head_size, cols,
          heads_here, tiles_here, row_size, paired, after):
    groups = len(cells)
    width = cells[0].shape[2]
    own_rows = cells[0].shape[0] * cols
    total = groups * own_rows
    key_mask, gain_col, gain_tile = key_mask.T, gain_col.reshape(1, width), gain_tile.reshape(1, width)
    weights = [(3, width, width), (width, width), (width, heads_here * head_size), (groups,) + cells[0].shape]
    scratch = [pltpu.VMEM(shape, jnp.bfloat16) for shape in [(total, width), (3, total, width)] + weights]
    scratch += [pltpu.SMEM(ids.shape, jnp.int32), pltpu.VMEM(key_mask.shape, jnp.int32)]
    scratch += [pltpu.VMEM((1, width), jnp.float32)] * 2 + [pltpu.SemaphoreType.DMA((groups + 9,))]
    fetched = [pltpu.with_memory_space_constraint(value, pltpu.HBM)
               for value in (ids, key_mask, gain_col, gain_tile, w_qkv, w_out, w_query)]
    own = pltpu.with_memory_space_constraint(cells[0], pltpu.HBM)
    return pl.pallas_call(
        functools.partial(front_kernel, groups, heads, head_size, ROW_GROUP * cols, cols, heads_here, tiles_here, row_size, paired),
        out_shape=(jax.ShapeDtypeStruct((own_rows, width), jnp.float32),
                   jax.ShapeDtypeStruct((heads_here, total, 2 * head_size), jnp.bfloat16)),
        in_specs=[HBM] + [ANY] * (groups - 1) + [SMEM] + [HBM] * 7 + [ANY],
        out_specs=(VMEM, VMEM),
        scratch_shapes=scratch,
        compiler_params=params(total),
        cost_estimate=pl.CostEstimate(flops=2 * total * width * 5 * width, bytes_accessed=4 * MIB,
                                      transcendentals=total * heads * 128),
        name="front",
    )(own, *cells[1:], me, *fetched, after)


def weigh(query, tile_refs, head, slots):
    key_parts, val_parts = [], []
    for ref, slot in zip(tile_refs, slots):
        tiles = ref[:, head]
        count, keys, lanes = tiles.shape
        lane = iota(tiles.shape, 2)
        marks = (lane == iota(tiles.shape, 0) + (lanes // 2 + slot)).astype(tiles.dtype)
        key_parts.append(jnp.where(lane < lanes // 2, tiles, marks).reshape(count * keys, lanes))
        val_parts.append(jnp.where(lane < lanes // 2, jnp.ones_like(tiles), tiles).reshape(count * keys, lanes))
    scores = dot_lanes(query, jnp.concatenate(key_parts, axis=0))
    top = jnp.max(scores, axis=1, keepdims=True)
    return top, dot_rows(jnp.exp(scores - top).astype(jnp.bfloat16), jnp.concatenate(val_parts, axis=0))


def attention_cost(asked, tiles):
    heads, rows, lanes = asked.shape
    keys = sum(part.shape[0] * part.shape[2] for part in tiles)
    return pl.CostEstimate(flops=4 * rows * heads * keys * lanes, bytes_accessed=4 * MIB, transcendentals=rows * heads * keys)


def first_kernel(slots, block, asked_ref, *refs):
    tile_refs, (sums_ref, tops_ref) = refs[:len(slots)], refs[len(slots):]
    heads, rows_all, lanes = asked_ref.shape
    lane = iota((block, lanes), 1)
    for step in range(rows_all // block):
        rows = pl.ds(step * block, block)
        tops = jnp.zeros((block, lanes), jnp.float32)
        for head in range(heads):
            top, sums_ref[head, rows, :] = weigh(asked_ref[head, rows, :], tile_refs, head, slots)
            tops = jnp.where(lane == head, top, tops)
        tops_ref[rows, :] = tops


def first_tiles(asked, tiles, slots, own_rows):
    heads, rows, lanes = asked.shape
    return pl.pallas_call(
        functools.partial(first_kernel, slots, rows if rows <= 512 else own_rows),
        out_shape=(jax.ShapeDtypeStruct((heads, rows, lanes), jnp.float32), jax.ShapeDtypeStruct((rows, lanes), jnp.float32)),
        in_specs=[VMEM] * (1 + len(tiles)),
        out_specs=(VMEM, VMEM),
        compiler_params=params(rows),
        cost_estimate=attention_cost(asked, tiles),
        name="first_tiles",
    )(asked, *tiles)


def merge(asked_ref, sums_ref, tops_ref, tile_refs, slots, head, rows):
    top, sums = weigh(asked_ref[head, rows, :], tile_refs, head, slots)
    old_top = tops_ref[rows, head:head + 1]
    new_top = jnp.maximum(top, old_top)
    return new_top, sums_ref[head, rows, :] * jnp.exp(old_top - new_top) + sums * jnp.exp(top - new_top)


def more_kernel(slots, block, asked_ref, old_sums_ref, old_tops_ref, *refs):
    tile_refs, (sums_ref, tops_ref) = refs[:len(slots)], refs[len(slots):]
    heads, rows_all, lanes = asked_ref.shape
    lane = iota((block, lanes), 1)
    for step in range(rows_all // block):
        rows = pl.ds(step * block, block)
        tops = jnp.zeros((block, lanes), jnp.float32)
        for head in range(heads):
            top, sums_ref[head, rows, :] = merge(asked_ref, old_sums_ref, old_tops_ref, tile_refs, slots, head, rows)
            tops = jnp.where(lane == head, top, tops)
        tops_ref[rows, :] = tops


def more_tiles(asked, sums, tops, tiles, slots, own_rows):
    rows = asked.shape[1]
    return pl.pallas_call(
        functools.partial(more_kernel, slots, rows if rows <= 512 else own_rows),
        out_shape=(jax.ShapeDtypeStruct(sums.shape, jnp.float32), jax.ShapeDtypeStruct(tops.shape, jnp.float32)),
        in_specs=[VMEM] * (3 + len(tiles)),
        out_specs=(VMEM, VMEM),
        compiler_params=params(rows),
        cost_estimate=attention_cost(asked, tiles),
        name="more_tiles",
    )(asked, sums, tops, *tiles)


def last_kernel(slots, groups, asked_ref, sums_ref, tops_ref, *refs):
    tile_refs, out_refs = refs[:len(slots)], refs[-len(groups):]
    heads, lanes = asked_ref.shape[0], asked_ref.shape[2]
    block = out_refs[0].shape[0]
    half = lanes // 2
    lane_low = iota((block, lanes), 1) < half
    for group, out_ref in zip(groups, out_refs):
        rows = pl.ds(group * block, block)
        low = None
        for head in range(heads):
            _, sums = merge(asked_ref, sums_ref, tops_ref, tile_refs, slots, head, rows)
            turned = pltpu.roll(sums, half, 1)
            if head % 2:
                out_ref[:, pl.ds(head // 2 * lanes, lanes)] = jnp.where(lane_low, low, sums / turned).astype(jnp.bfloat16)
            elif head + 1 < heads:
                low = turned / sums
            else:
                out_ref[:, pl.ds(head * half, half)] = (turned / sums)[:, :half].astype(jnp.bfloat16)


def last_tiles(asked, sums, tops, tiles, slots, groups, own_rows, after):
    heads, rows, lanes = asked.shape
    out = jax.ShapeDtypeStruct((own_rows, heads * lanes // 2), jnp.bfloat16)
    return pl.pallas_call(
        functools.partial(last_kernel, slots, groups),
        out_shape=(out,) * len(groups),
        in_specs=[VMEM] * (3 + len(tiles)) + [ANY] * len(after),
        out_specs=(VMEM,) * len(groups),
        compiler_params=params(rows),
        cost_estimate=attention_cost(asked[:, :own_rows * len(groups)], tiles),
        name="last_tiles",
    )(asked, sums, tops, *tiles, *after)


def finish_kernel(me_ref, weight_ref, resid_ref, *refs):
    answer_refs, out_ref = refs[:-1], refs[-1]
    group_width = answer_refs[0].shape[1]
    final = resid_ref[...]
    for step, answer_ref in enumerate(answer_refs):
        group = lax.rem(me_ref[1] - step + len(answer_refs), len(answer_refs))
        rows = pl.ds(pl.multiple_of(group * group_width, group_width), group_width)
        final = final + dot_rows(answer_ref[...], weight_ref[rows, :])
    out_ref[...] = final.reshape(out_ref.shape).astype(out_ref.dtype)


def finish(me, weight, residual, answers, shape):
    return pl.pallas_call(
        finish_kernel,
        out_shape=jax.ShapeDtypeStruct(shape, jnp.bfloat16),
        in_specs=[SMEM, VMEM, VMEM] + [VMEM] * len(answers),
        out_specs=VMEM,
        compiler_params=params(0),
        cost_estimate=pl.CostEstimate(flops=2 * residual.size * weight.shape[0], bytes_accessed=MIB, transcendentals=0),
        name="finish",
    )(me, weight, residual, *answers)


def turn(size, step):
    return [(src, (src + step) % size) for src in range(size)]


def shards(row_size, col_size, fact_cells, gain_col, w_qkv, w_col_out, gain_tile, w_query, w_tile_out,
           tile_kv, tile_ids, key_mask):
    rows, cols, width = fact_cells.shape
    tiles_here, keys, heads_here, lanes = tile_kv.shape
    head_size = lanes // 2
    heads_all = width // head_size
    group_width = heads_here * head_size
    half = row_size // 2
    row_me, col_me = lax.axis_index("rows"), lax.axis_index("cols")
    me = jnp.stack([row_me, col_me]).astype(jnp.int32)
    halves = [list(range(half)), list(range(half, row_size))]
    paired = half <= 8 and half & (half - 1) == 0
    assert row_size <= head_size and row_size % 2 == 0

    def swap(value):
        return lax.all_to_all(value, "rows", split_axis=0, concat_axis=0, tiled=True, axis_index_groups=halves)

    asked_of = request(tile_ids, me, tiles_here, row_size)
    asked_by = swap(asked_of)
    heads_first = tie(jnp.transpose(tile_kv, (0, 2, 1, 3)), asked_of)
    mirrored = lax.ppermute(heads_first, "rows", turn(row_size, half))

    cells = [fact_cells]
    for step in range(1, col_size):
        cells.append(lax.ppermute(fact_cells, "cols", turn(col_size, -step)))

    order = [0] + sorted(range(1, half), key=lambda step: (not step & half // 2, step & 1, -(step & 2) if step < half // 2 else step))
    near_slots, far_slots = (order, [half + step for step in order]) if paired else ([0], [half])

    def spread(tiles, which, after):
        if not paired:
            return [swap(pick(tiles, asked_by, which, after))]
        picked = pick_each(tiles, asked_by, which, me, order, after)
        return [tile if step == 0 else lax.ppermute(tile, "rows", [(row, row ^ step) for row in range(row_size)])
                for step, tile in zip(order, picked)]

    if group_width % 128:
        w_query = lax.dynamic_slice_in_dim(w_query, col_me * group_width, group_width, 1)
    near = spread(heads_first, 0, cells[1:])
    residual, asked = front(cells, tile_ids, me, key_mask, gain_col, w_qkv, w_col_out, gain_tile, w_query,
                            heads_all, head_size, cols, heads_here, tiles_here, row_size, paired, near[0])
    far = spread(mirrored, 1, [asked] + near[1:3])
    sums, tops = first_tiles(asked, near, near_slots, rows * cols)
    batch = len(far) // 2
    if batch:
        sums, tops = more_tiles(asked, sums, tops, far[:batch], far_slots[:batch], rows * cols)
    far, far_slots = far[batch:], far_slots[batch:]
    others = last_tiles(asked, sums, tops, far, far_slots, list(range(1, col_size)), rows * cols, [])
    own = last_tiles(asked, sums, tops, far, far_slots, [0], rows * cols, others[:1])
    answers = list(own) + [lax.ppermute(other, "cols", turn(col_size, step + 1)) for step, other in enumerate(others)]
    return finish(me, w_tile_out, residual, answers, fact_cells.shape)


def solution(mesh):
    row_size, col_size = mesh.shape["rows"], mesh.shape["cols"]
    placed = (P("rows", "cols", None), P(), P(), P(), P(), P(), P(), P("rows", None, "cols", None),
              P("rows", None), P("rows", None))

    def body(*arrays):
        return shards(row_size, col_size, *arrays)

    return jax.shard_map(body, mesh=mesh, in_specs=placed, out_specs=P("rows", "cols", None), check_vma=False)
```

```python
import functools

import jax
import jax.numpy as jnp
from jax import lax
from jax.experimental import pallas as pl
from jax.experimental.pallas import tpu as pltpu
from jax.sharding import PartitionSpec as P

ROW_GROUP = 16
BIG = -1e30
MIB = 1024 * 1024
VMEM = pl.BlockSpec(memory_space=pltpu.VMEM)
SMEM = pl.BlockSpec(memory_space=pltpu.SMEM)
HBM = pl.BlockSpec(memory_space=pltpu.HBM)
ANY = pl.BlockSpec(memory_space=pl.ANY)


def params(rows):
    return pltpu.CompilerParams(vmem_limit_bytes=(20 if rows <= 512 else 48) * MIB)


def dot_rows(left, right):
    return lax.dot_general(left, right, (((1,), (0,)), ((), ())), preferred_element_type=jnp.float32)


def dot_lanes(left, right):
    return lax.dot_general(left, right, (((1,), (1,)), ((), ())), preferred_element_type=jnp.float32)


def rms_scale(values, gain_vec):
    mean_sq = jnp.mean(values * values, axis=-1, keepdims=True)
    return values * lax.rsqrt(mean_sq + 1e-05) * gain_vec


def iota(shape, dim):
    return lax.broadcasted_iota(jnp.int32, shape, dim)


def slot_of(owner, row_me, row_size, paired):
    half = row_size // 2
    near = lax.div(owner, half) == lax.div(row_me, half)
    far_slot = half + (lax.rem(owner ^ row_me, half) if paired else lax.rem(owner, half))
    return jnp.where(near, lax.rem(owner, half), far_slot)


def tie_kernel(value_ref, after_ref, out_ref):
    pass


def tie(value, after):
    return pl.pallas_call(
        tie_kernel,
        out_shape=jax.ShapeDtypeStruct(value.shape, value.dtype),
        in_specs=[ANY, ANY],
        out_specs=ANY,
        input_output_aliases={0: 0},
        compiler_params=params(0),
        cost_estimate=pl.CostEstimate(flops=0, bytes_accessed=0, transcendentals=0),
        name="tie",
    )(value, after)


def request_kernel(tiles_here, row_size, ids_ref, me_ref, out_ref):
    half = row_size // 2
    peer, which = iota(out_ref.shape, 0), iota(out_ref.shape, 1)
    wanted = jnp.zeros(out_ref.shape, jnp.int32)
    for slot in range(ids_ref.shape[1]):
        tile = ids_ref[0, slot]
        owner = lax.div(tile, tiles_here)
        far = jnp.where(lax.div(owner, half) == lax.div(me_ref[0], half), 0, 1)
        here = (peer == jnp.where(tile < 0, -1, lax.rem(owner, half))) & (which == far)
        wanted = jnp.where(here, lax.rem(tile, tiles_here), wanted)
    out_ref[...] = wanted


def request(ids, me, tiles_here, row_size):
    return pl.pallas_call(
        functools.partial(request_kernel, tiles_here, row_size),
        out_shape=jax.ShapeDtypeStruct((row_size // 2, 2, 128), jnp.int32),
        in_specs=[SMEM, SMEM],
        out_specs=VMEM,
        compiler_params=params(0),
        cost_estimate=pl.CostEstimate(flops=0, bytes_accessed=MIB // 4, transcendentals=0),
        name="request",
    )(ids, me)


def pick_kernel(which, wanted_ref, tiles_ref, *refs):
    out_ref = refs[-1]
    for peer in range(out_ref.shape[0]):
        out_ref[peer] = tiles_ref[wanted_ref[peer, which, 0]]


def pick(tiles, wanted, which, after):
    return pl.pallas_call(
        functools.partial(pick_kernel, which),
        out_shape=jax.ShapeDtypeStruct(wanted.shape[:1] + tiles.shape[1:], tiles.dtype),
        in_specs=[SMEM, VMEM] + [ANY] * len(after),
        out_specs=VMEM,
        compiler_params=params(0),
        cost_estimate=pl.CostEstimate(flops=0, bytes_accessed=2 * MIB, transcendentals=0),
        name="pick",
    )(wanted, tiles, *after)


def pick_each_kernel(which, order, wanted_ref, me_ref, tiles_ref, *refs):
    place = lax.rem(me_ref[0], wanted_ref.shape[0])
    for step, out_ref in zip(order, refs[-len(order):]):
        out_ref[0] = tiles_ref[wanted_ref[place ^ step, which, 0]]


def pick_each(tiles, wanted, which, me, order, after):
    count = len(order)
    return pl.pallas_call(
        functools.partial(pick_each_kernel, which, order),
        out_shape=(jax.ShapeDtypeStruct((1,) + tiles.shape[1:], tiles.dtype),) * count,
        in_specs=[SMEM, SMEM, VMEM] + [ANY] * len(after),
        out_specs=(VMEM,) * count,
        compiler_params=params(0),
        cost_estimate=pl.CostEstimate(flops=0, bytes_accessed=2 * MIB, transcendentals=0),
        name="pick_each",
    )(wanted, me, tiles, *after)


def front_kernel(groups, heads, head_size, chunk, cols, heads_here, tiles_here, row_size, paired, *refs):
    cell_hbms, refs = refs[:groups], refs[groups:]
    (me_ref, ids_hbm, mask_hbm, gain_col_hbm, gain_tile_hbm, w_qkv_hbm, w_out_hbm, w_query_hbm, after_ref,
     resid_ref, asked_ref, normed_ref, packed_ref, w_qkv_ref, w_out_ref, w_query_ref, cell_refs,
     ids_ref, mask_ref, gain_col_ref, gain_tile_ref, sems) = refs
    own_rows, width = resid_ref.shape
    steps = own_rows // chunk
    span = groups * chunk
    lanes_two = 2 * head_size
    group_width = heads_here * head_size
    if w_query_hbm.shape[1] != group_width:
        w_query_hbm = w_query_hbm.at[:, pl.ds(pl.multiple_of(me_ref[1] * group_width, group_width), group_width)]
    pairs = [(hbm, cell_refs.at[group]) for group, hbm in enumerate(cell_hbms)]
    pairs += [(gain_col_hbm, gain_col_ref)]
    pairs += [(w_qkv_hbm.at[:, pl.ds(part * width, width)], w_qkv_ref.at[part]) for part in range(3)]
    pairs += [(w_out_hbm, w_out_ref), (gain_tile_hbm, gain_tile_ref), (w_query_hbm, w_query_ref), (ids_hbm, ids_ref), (mask_hbm, mask_ref)]
    copies = [pltpu.make_async_copy(*pair, sems.at[index]) for index, pair in enumerate(pairs)]
    for copy in copies:
        copy.start()
    for copy in copies[:groups + 1]:
        copy.wait()
    copies = copies[groups + 1:]

    def cells_of(group, step):
        cells = cell_refs[group, pl.ds(step * (chunk // cols), chunk // cols)].astype(jnp.float32)
        return cells.reshape(chunk, width)

    for step in range(steps):
        for group in range(groups):
            cells = cells_of(group, step)
            normed_ref[pl.ds(step * span + group * chunk, chunk), :] = rms_scale(cells, gain_col_ref[...]).astype(jnp.bfloat16)
    for part in range(3):
        copies[part].wait()
        packed_ref[part] = dot_rows(normed_ref[...], w_qkv_ref[part]).astype(jnp.bfloat16)
    stacked = heads * span
    same_row = iota((stacked, span), 0) % chunk // cols == iota((stacked, span), 1) % chunk // cols
    lane_low = iota((span, lanes_two), 1) < head_size
    scale = head_size ** (-0.5)
    for step in range(steps):
        rows = pl.ds(step * span, span)
        scores = []
        for head in range(heads):
            lanes = pl.ds(head // 2 * lanes_two, lanes_two)
            query = packed_ref[0, rows, lanes]
            query = jnp.where(lane_low == (head % 2 == 0), query, jnp.zeros_like(query))
            scores.append(dot_lanes(query, packed_ref[1, rows, lanes]))
        scores = jnp.where(same_row, jnp.concatenate(scores, axis=0) * scale, BIG)
        expo = jnp.exp(scores - jnp.max(scores, axis=1, keepdims=True))
        weights = (expo / jnp.sum(expo, axis=1, keepdims=True)).astype(jnp.bfloat16)
        for pair in range(heads // 2):
            lanes = pl.ds(pair * lanes_two, lanes_two)
            start = 2 * pair * span
            mixed = dot_rows(weights[start:start + 2 * span], packed_ref[2, rows, lanes])
            normed_ref[rows, lanes] = jnp.where(lane_low, mixed[:span], mixed[span:]).astype(jnp.bfloat16)
    for copy in copies[3:]:
        copy.wait()
    delta = dot_rows(normed_ref[...], w_out_ref[...])
    for step in range(steps):
        for group in range(groups):
            start = step * span + group * chunk
            resid = cells_of(group, step) + delta[start:start + chunk]
            if group == 0:
                resid_ref[pl.ds(step * chunk, chunk), :] = resid
            normed_ref[pl.ds(start, chunk), :] = rms_scale(resid, gain_tile_ref[...]).astype(jnp.bfloat16)
    slots = mask_ref.shape[0]
    slot, lane = iota((slots, lanes_two), 0), iota((slots, lanes_two), 1)
    place = jnp.zeros((slots, lanes_two), jnp.float32)
    for index in range(slots):
        tile = ids_ref[0, index]
        spot = jnp.where(tile < 0, -1, head_size + slot_of(lax.div(tile, tiles_here), me_ref[0], row_size, paired))
        place = jnp.where((slot == index) & (lane == spot), 1.0, place)
    live = lax.dot_general((mask_ref[...] > 0).astype(jnp.float32).astype(jnp.bfloat16), place.astype(jnp.bfloat16),
                           (((0,), (0,)), ((), ())), preferred_element_type=jnp.float32)
    lane = iota(live.shape, 1)
    shut = jnp.where((lane >= head_size) & (lane < head_size + row_size) & (live < 0.5), 1.0, 0.0).astype(jnp.bfloat16)
    total = steps * span
    cell = iota((total, shut.shape[0]), 0)
    row_of = cell // span * (chunk // cols) + cell % chunk // cols
    spread = (row_of == iota((total, shut.shape[0]), 1)).astype(jnp.bfloat16)
    bias = dot_rows(spread, shut) * BIG
    asked = dot_rows(normed_ref[...], w_query_ref[...]).astype(jnp.bfloat16).astype(jnp.float32) * scale
    low = iota((total, lanes_two), 1) < head_size
    for head in range(heads_here):
        if heads_here % 2 == 0:
            two = asked[:, head // 2 * lanes_two:(head // 2 + 1) * lanes_two]
            one = two if head % 2 == 0 else pltpu.roll(two, head_size, 1)
            query = jnp.where(low, one, bias)
        else:
            one = asked[:, head * head_size:(head + 1) * head_size]
            query = jnp.concatenate([one, bias[:, head_size:]], axis=1)
        query = query.astype(jnp.bfloat16)
        for step in range(steps):
            for group in range(groups):
                start = step * span + group * chunk
                asked_ref[head, pl.ds(group * own_rows + step * chunk, chunk), :] = query[start:start + chunk]


def front(cells, ids, me, key_mask, gain_col, w_qkv, w_out, gain_tile, w_query, heads, head_size, cols,
          heads_here, tiles_here, row_size, paired, after):
    groups = len(cells)
    width = cells[0].shape[2]
    own_rows = cells[0].shape[0] * cols
    total = groups * own_rows
    key_mask, gain_col, gain_tile = key_mask.T, gain_col.reshape(1, width), gain_tile.reshape(1, width)
    weights = [(3, width, width), (width, width), (width, heads_here * head_size), (groups,) + cells[0].shape]
    scratch = [pltpu.VMEM(shape, jnp.bfloat16) for shape in [(total, width), (3, total, width)] + weights]
    scratch += [pltpu.SMEM(ids.shape, jnp.int32), pltpu.VMEM(key_mask.shape, jnp.int32)]
    scratch += [pltpu.VMEM((1, width), jnp.float32)] * 2 + [pltpu.SemaphoreType.DMA((groups + 9,))]
    fetched = [pltpu.with_memory_space_constraint(value, pltpu.HBM)
               for value in (ids, key_mask, gain_col, gain_tile, w_qkv, w_out, w_query)]
    own = pltpu.with_memory_space_constraint(cells[0], pltpu.HBM)
    return pl.pallas_call(
        functools.partial(front_kernel, groups, heads, head_size, ROW_GROUP * cols, cols, heads_here, tiles_here, row_size, paired),
        out_shape=(jax.ShapeDtypeStruct((own_rows, width), jnp.float32),
                   jax.ShapeDtypeStruct((heads_here, total, 2 * head_size), jnp.bfloat16)),
        in_specs=[HBM] + [ANY] * (groups - 1) + [SMEM] + [HBM] * 7 + [ANY],
        out_specs=(VMEM, VMEM),
        scratch_shapes=scratch,
        compiler_params=params(total),
        cost_estimate=pl.CostEstimate(flops=2 * total * width * 5 * width, bytes_accessed=4 * MIB,
                                      transcendentals=total * heads * 128),
        name="front",
    )(own, *cells[1:], me, *fetched, after)


def weigh(query, tile_refs, head, slots):
    key_parts, val_parts = [], []
    for ref, slot in zip(tile_refs, slots):
        tiles = ref[:, head]
        count, keys, lanes = tiles.shape
        lane = iota(tiles.shape, 2)
        marks = (lane == iota(tiles.shape, 0) + (lanes // 2 + slot)).astype(tiles.dtype)
        key_parts.append(jnp.where(lane < lanes // 2, tiles, marks).reshape(count * keys, lanes))
        val_parts.append(jnp.where(lane < lanes // 2, jnp.ones_like(tiles), tiles).reshape(count * keys, lanes))
    scores = dot_lanes(query, jnp.concatenate(key_parts, axis=0))
    top = jnp.max(scores, axis=1, keepdims=True)
    return top, dot_rows(jnp.exp(scores - top).astype(jnp.bfloat16), jnp.concatenate(val_parts, axis=0))


def attention_cost(asked, tiles):
    heads, rows, lanes = asked.shape
    keys = sum(part.shape[0] * part.shape[2] for part in tiles)
    return pl.CostEstimate(flops=4 * rows * heads * keys * lanes, bytes_accessed=4 * MIB, transcendentals=rows * heads * keys)


def first_kernel(slots, block, asked_ref, *refs):
    tile_refs, (sums_ref, tops_ref) = refs[:len(slots)], refs[len(slots):]
    heads, rows_all, lanes = asked_ref.shape
    lane = iota((block, lanes), 1)
    for step in range(rows_all // block):
        rows = pl.ds(step * block, block)
        tops = jnp.zeros((block, lanes), jnp.float32)
        for head in range(heads):
            top, sums_ref[head, rows, :] = weigh(asked_ref[head, rows, :], tile_refs, head, slots)
            tops = jnp.where(lane == head, top, tops)
        tops_ref[rows, :] = tops


def first_tiles(asked, tiles, slots, own_rows):
    heads, rows, lanes = asked.shape
    return pl.pallas_call(
        functools.partial(first_kernel, slots, rows if rows <= 512 else own_rows),
        out_shape=(jax.ShapeDtypeStruct((heads, rows, lanes), jnp.float32), jax.ShapeDtypeStruct((rows, lanes), jnp.float32)),
        in_specs=[VMEM] * (1 + len(tiles)),
        out_specs=(VMEM, VMEM),
        compiler_params=params(rows),
        cost_estimate=attention_cost(asked, tiles),
        name="first_tiles",
    )(asked, *tiles)


def merge(asked_ref, sums_ref, tops_ref, tile_refs, slots, head, rows):
    top, sums = weigh(asked_ref[head, rows, :], tile_refs, head, slots)
    old_top = tops_ref[rows, head:head + 1]
    new_top = jnp.maximum(top, old_top)
    return new_top, sums_ref[head, rows, :] * jnp.exp(old_top - new_top) + sums * jnp.exp(top - new_top)


def more_kernel(slots, block, asked_ref, old_sums_ref, old_tops_ref, *refs):
    tile_refs, (sums_ref, tops_ref) = refs[:len(slots)], refs[len(slots):]
    heads, rows_all, lanes = asked_ref.shape
    lane = iota((block, lanes), 1)
    for step in range(rows_all // block):
        rows = pl.ds(step * block, block)
        tops = jnp.zeros((block, lanes), jnp.float32)
        for head in range(heads):
            top, sums_ref[head, rows, :] = merge(asked_ref, old_sums_ref, old_tops_ref, tile_refs, slots, head, rows)
            tops = jnp.where(lane == head, top, tops)
        tops_ref[rows, :] = tops


def more_tiles(asked, sums, tops, tiles, slots, own_rows):
    rows = asked.shape[1]
    return pl.pallas_call(
        functools.partial(more_kernel, slots, rows if rows <= 512 else own_rows),
        out_shape=(jax.ShapeDtypeStruct(sums.shape, jnp.float32), jax.ShapeDtypeStruct(tops.shape, jnp.float32)),
        in_specs=[VMEM] * (3 + len(tiles)),
        out_specs=(VMEM, VMEM),
        compiler_params=params(rows),
        cost_estimate=attention_cost(asked, tiles),
        name="more_tiles",
    )(asked, sums, tops, *tiles)


def last_kernel(slots, groups, asked_ref, sums_ref, tops_ref, *refs):
    tile_refs, out_refs = refs[:len(slots)], refs[-len(groups):]
    heads, lanes = asked_ref.shape[0], asked_ref.shape[2]
    block = out_refs[0].shape[0]
    half = lanes // 2
    lane_low = iota((block, lanes), 1) < half
    for group, out_ref in zip(groups, out_refs):
        rows = pl.ds(group * block, block)
        low = None
        for head in range(heads):
            _, sums = merge(asked_ref, sums_ref, tops_ref, tile_refs, slots, head, rows)
            turned = pltpu.roll(sums, half, 1)
            if head % 2:
                out_ref[:, pl.ds(head // 2 * lanes, lanes)] = jnp.where(lane_low, low, sums / turned).astype(jnp.bfloat16)
            elif head + 1 < heads:
                low = turned / sums
            else:
                out_ref[:, pl.ds(head * half, half)] = (turned / sums)[:, :half].astype(jnp.bfloat16)


def last_tiles(asked, sums, tops, tiles, slots, groups, own_rows, after):
    heads, rows, lanes = asked.shape
    out = jax.ShapeDtypeStruct((own_rows, heads * lanes // 2), jnp.bfloat16)
    return pl.pallas_call(
        functools.partial(last_kernel, slots, groups),
        out_shape=(out,) * len(groups),
        in_specs=[VMEM] * (3 + len(tiles)) + [ANY] * len(after),
        out_specs=(VMEM,) * len(groups),
        compiler_params=params(rows),
        cost_estimate=attention_cost(asked[:, :own_rows * len(groups)], tiles),
        name="last_tiles",
    )(asked, sums, tops, *tiles, *after)


def finish_kernel(me_ref, weight_ref, resid_ref, *refs):
    answer_refs, out_ref = refs[:-1], refs[-1]
    group_width = answer_refs[0].shape[1]
    final = resid_ref[...]
    for step, answer_ref in enumerate(answer_refs):
        group = lax.rem(me_ref[1] - step + len(answer_refs), len(answer_refs))
        rows = pl.ds(pl.multiple_of(group * group_width, group_width), group_width)
        final = final + dot_rows(answer_ref[...], weight_ref[rows, :])
    out_ref[...] = final.reshape(out_ref.shape).astype(out_ref.dtype)


def finish(me, weight, residual, answers, shape):
    return pl.pallas_call(
        finish_kernel,
        out_shape=jax.ShapeDtypeStruct(shape, jnp.bfloat16),
        in_specs=[SMEM, VMEM, VMEM] + [VMEM] * len(answers),
        out_specs=VMEM,
        compiler_params=params(0),
        cost_estimate=pl.CostEstimate(flops=2 * residual.size * weight.shape[0], bytes_accessed=MIB, transcendentals=0),
        name="finish",
    )(me, weight, residual, *answers)


def turn(size, step):
    return [(src, (src + step) % size) for src in range(size)]


def shards(row_size, col_size, fact_cells, gain_col, w_qkv, w_col_out, gain_tile, w_query, w_tile_out,
           tile_kv, tile_ids, key_mask):
    rows, cols, width = fact_cells.shape
    tiles_here, keys, heads_here, lanes = tile_kv.shape
    head_size = lanes // 2
    heads_all = width // head_size
    group_width = heads_here * head_size
    half = row_size // 2
    row_me, col_me = lax.axis_index("rows"), lax.axis_index("cols")
    me = jnp.stack([row_me, col_me]).astype(jnp.int32)
    halves = [list(range(half)), list(range(half, row_size))]
    paired = half <= 8 and half & (half - 1) == 0
    assert row_size <= head_size and row_size % 2 == 0

    def swap(value):
        return lax.all_to_all(value, "rows", split_axis=0, concat_axis=0, tiled=True, axis_index_groups=halves)

    asked_of = request(tile_ids, me, tiles_here, row_size)
    asked_by = swap(asked_of)
    heads_first = tie(jnp.transpose(tile_kv, (0, 2, 1, 3)), asked_of)
    mirrored = lax.ppermute(heads_first, "rows", turn(row_size, half))

    cells = [fact_cells]
    for step in range(1, col_size):
        cells.append(lax.ppermute(fact_cells, "cols", turn(col_size, -step)))

    order = [0] + sorted(range(1, half), key=lambda step: (not step & half // 2, step & 1, -(step & 2) if step < half // 2 else step))
    near_slots, far_slots = [0], [half + step for step in order] if paired else [half]
    if group_width % 128:
        w_query = lax.dynamic_slice_in_dim(w_query, col_me * group_width, group_width, 1)
    sent = pick(heads_first, asked_by, 0, cells[1:])
    near = [swap(sent)]
    residual, asked = front(cells, tile_ids, me, key_mask, gain_col, w_qkv, w_col_out, gain_tile, w_query,
                            heads_all, head_size, cols, heads_here, tiles_here, row_size, paired, sent)
    if paired:
        picked = pick_each(mirrored, asked_by, 1, me, order, [asked])
        far = [tile if step == 0 else lax.ppermute(tile, "rows", [(row, row ^ step) for row in range(row_size)])
               for step, tile in zip(order, picked)]
    else:
        far = [swap(pick(mirrored, asked_by, 1, [asked]))]
    sums, tops = first_tiles(asked, near, near_slots, rows * cols)
    batch = len(far) // 2
    if batch:
        sums, tops = more_tiles(asked, sums, tops, far[:batch], far_slots[:batch], rows * cols)
    far, far_slots = far[batch:], far_slots[batch:]
    others = last_tiles(asked, sums, tops, far, far_slots, list(range(1, col_size)), rows * cols, [])
    own = last_tiles(asked, sums, tops, far, far_slots, [0], rows * cols, others[:1])
    answers = list(own) + [lax.ppermute(other, "cols", turn(col_size, step + 1)) for step, other in enumerate(others)]
    return finish(me, w_tile_out, residual, answers, fact_cells.shape)


def solution(mesh):
    row_size, col_size = mesh.shape["rows"], mesh.shape["cols"]
    placed = (P("rows", "cols", None), P(), P(), P(), P(), P(), P(), P("rows", None, "cols", None),
              P("rows", None), P("rows", None))

    def body(*arrays):
        return shards(row_size, col_size, *arrays)

    return jax.shard_map(body, mesh=mesh, in_specs=placed, out_specs=P("rows", "cols", None), check_vma=False)
```

```python
import functools

import jax
import jax.numpy as jnp
from jax import lax
from jax.experimental import pallas as pl
from jax.experimental.pallas import tpu as pltpu
from jax.sharding import PartitionSpec as P

ROW_GROUP = 16
BIG = -1e30
MIB = 1024 * 1024
VMEM = pl.BlockSpec(memory_space=pltpu.VMEM)
SMEM = pl.BlockSpec(memory_space=pltpu.SMEM)
HBM = pl.BlockSpec(memory_space=pltpu.HBM)
ANY = pl.BlockSpec(memory_space=pl.ANY)


def params(rows):
    return pltpu.CompilerParams(vmem_limit_bytes=(20 if rows <= 512 else 48) * MIB)


def dot_rows(left, right):
    return lax.dot_general(left, right, (((1,), (0,)), ((), ())), preferred_element_type=jnp.float32)


def dot_lanes(left, right):
    return lax.dot_general(left, right, (((1,), (1,)), ((), ())), preferred_element_type=jnp.float32)


def rms_scale(values, gain_vec):
    mean_sq = jnp.mean(values * values, axis=-1, keepdims=True)
    return values * lax.rsqrt(mean_sq + 1e-05) * gain_vec


def iota(shape, dim):
    return lax.broadcasted_iota(jnp.int32, shape, dim)


def slot_of(owner, row_me, row_size, paired):
    half = row_size // 2
    return owner ^ row_me if paired else lax.rem(owner + lax.div(row_me, half) * half, row_size)


def tie_kernel(value_ref, after_ref, out_ref):
    pass


def tie(value, after):
    return pl.pallas_call(
        tie_kernel,
        out_shape=jax.ShapeDtypeStruct(value.shape, value.dtype),
        in_specs=[ANY, ANY],
        out_specs=ANY,
        input_output_aliases={0: 0},
        compiler_params=params(0),
        cost_estimate=pl.CostEstimate(flops=0, bytes_accessed=0, transcendentals=0),
        name="tie",
    )(value, after)


def request_kernel(tiles_here, row_size, ids_ref, me_ref, out_ref):
    half = row_size // 2
    peer, which = iota(out_ref.shape, 0), iota(out_ref.shape, 1)
    wanted = jnp.zeros(out_ref.shape, jnp.int32)
    for slot in range(ids_ref.shape[1]):
        tile = ids_ref[0, slot]
        owner = lax.div(tile, tiles_here)
        far = jnp.where(lax.div(owner, half) == lax.div(me_ref[0], half), 0, 1)
        here = (peer == jnp.where(tile < 0, -1, lax.rem(owner, half))) & (which == far)
        wanted = jnp.where(here, lax.rem(tile, tiles_here), wanted)
    out_ref[...] = wanted


def request(ids, me, tiles_here, row_size):
    return pl.pallas_call(
        functools.partial(request_kernel, tiles_here, row_size),
        out_shape=jax.ShapeDtypeStruct((row_size // 2, 2, 128), jnp.int32),
        in_specs=[SMEM, SMEM],
        out_specs=VMEM,
        compiler_params=params(0),
        cost_estimate=pl.CostEstimate(flops=0, bytes_accessed=MIB // 4, transcendentals=0),
        name="request",
    )(ids, me)


def pick_kernel(which, wanted_ref, tiles_ref, *refs):
    out_ref = refs[-1]
    for peer in range(out_ref.shape[0]):
        out_ref[peer] = tiles_ref[wanted_ref[peer, which, 0]]


def pick(tiles, wanted, which, after):
    return pl.pallas_call(
        functools.partial(pick_kernel, which),
        out_shape=jax.ShapeDtypeStruct(wanted.shape[:1] + tiles.shape[1:], tiles.dtype),
        in_specs=[SMEM, VMEM] + [ANY] * len(after),
        out_specs=VMEM,
        compiler_params=params(0),
        cost_estimate=pl.CostEstimate(flops=0, bytes_accessed=2 * MIB, transcendentals=0),
        name="pick",
    )(wanted, tiles, *after)


def pick_each_kernel(which, order, wanted_ref, me_ref, tiles_ref, *refs):
    place = lax.rem(me_ref[0], wanted_ref.shape[0])
    for step, out_ref in zip(order, refs[-len(order):]):
        out_ref[0] = tiles_ref[wanted_ref[place ^ step, which, 0]]


def pick_each(tiles, wanted, which, me, order, after):
    count = len(order)
    return pl.pallas_call(
        functools.partial(pick_each_kernel, which, order),
        out_shape=(jax.ShapeDtypeStruct((1,) + tiles.shape[1:], tiles.dtype),) * count,
        in_specs=[SMEM, SMEM, VMEM] + [ANY] * len(after),
        out_specs=(VMEM,) * count,
        compiler_params=params(0),
        cost_estimate=pl.CostEstimate(flops=0, bytes_accessed=2 * MIB, transcendentals=0),
        name="pick_each",
    )(wanted, me, tiles, *after)


def front_kernel(groups, heads, head_size, chunk, cols, heads_here, tiles_here, row_size, paired, waited, *refs):
    cell_hbms, refs = refs[:groups], refs[groups:]
    (me_ref, ids_hbm, mask_hbm, gain_col_hbm, gain_tile_hbm, w_qkv_hbm, w_out_hbm, w_query_hbm) = refs[:8]
    (resid_ref, asked_ref, normed_ref, packed_ref, w_qkv_ref, w_out_ref, w_query_ref, cell_refs,
     ids_ref, mask_ref, gain_col_ref, gain_tile_ref, sems) = refs[8 + waited:]
    own_rows, width = resid_ref.shape
    steps = own_rows // chunk
    span = groups * chunk
    lanes_two = 2 * head_size
    group_width = heads_here * head_size
    if w_query_hbm.shape[1] != group_width:
        w_query_hbm = w_query_hbm.at[:, pl.ds(pl.multiple_of(me_ref[1] * group_width, group_width), group_width)]
    pairs = [(hbm, cell_refs.at[group]) for group, hbm in enumerate(cell_hbms)]
    pairs += [(gain_col_hbm, gain_col_ref)]
    pairs += [(w_qkv_hbm.at[:, pl.ds(part * width, width)], w_qkv_ref.at[part]) for part in range(3)]
    pairs += [(w_out_hbm, w_out_ref), (gain_tile_hbm, gain_tile_ref), (w_query_hbm, w_query_ref), (ids_hbm, ids_ref), (mask_hbm, mask_ref)]
    copies = [pltpu.make_async_copy(*pair, sems.at[index]) for index, pair in enumerate(pairs)]
    for copy in copies:
        copy.start()
    for copy in copies[:groups + 1]:
        copy.wait()
    copies = copies[groups + 1:]

    def cells_of(group, step):
        cells = cell_refs[group, pl.ds(step * (chunk // cols), chunk // cols)].astype(jnp.float32)
        return cells.reshape(chunk, width)

    for step in range(steps):
        for group in range(groups):
            cells = cells_of(group, step)
            normed_ref[pl.ds(step * span + group * chunk, chunk), :] = rms_scale(cells, gain_col_ref[...]).astype(jnp.bfloat16)
    for part in range(3):
        copies[part].wait()
        packed_ref[part] = dot_rows(normed_ref[...], w_qkv_ref[part]).astype(jnp.bfloat16)
    stacked = heads * span
    same_row = iota((stacked, span), 0) % chunk // cols == iota((stacked, span), 1) % chunk // cols
    lane_low = iota((span, lanes_two), 1) < head_size
    scale = head_size ** (-0.5)
    for step in range(steps):
        rows = pl.ds(step * span, span)
        scores = []
        for head in range(heads):
            lanes = pl.ds(head // 2 * lanes_two, lanes_two)
            query = packed_ref[0, rows, lanes]
            query = jnp.where(lane_low == (head % 2 == 0), query, jnp.zeros_like(query))
            scores.append(dot_lanes(query, packed_ref[1, rows, lanes]))
        scores = jnp.where(same_row, jnp.concatenate(scores, axis=0) * scale, BIG)
        expo = jnp.exp(scores - jnp.max(scores, axis=1, keepdims=True))
        weights = (expo / jnp.sum(expo, axis=1, keepdims=True)).astype(jnp.bfloat16)
        for pair in range(heads // 2):
            lanes = pl.ds(pair * lanes_two, lanes_two)
            start = 2 * pair * span
            mixed = dot_rows(weights[start:start + 2 * span], packed_ref[2, rows, lanes])
            normed_ref[rows, lanes] = jnp.where(lane_low, mixed[:span], mixed[span:]).astype(jnp.bfloat16)
    for copy in copies[3:]:
        copy.wait()
    delta = dot_rows(normed_ref[...], w_out_ref[...])
    for step in range(steps):
        for group in range(groups):
            start = step * span + group * chunk
            resid = cells_of(group, step) + delta[start:start + chunk]
            if group == 0:
                resid_ref[pl.ds(step * chunk, chunk), :] = resid
            normed_ref[pl.ds(start, chunk), :] = rms_scale(resid, gain_tile_ref[...]).astype(jnp.bfloat16)
    slots = mask_ref.shape[0]
    slot, lane = iota((slots, lanes_two), 0), iota((slots, lanes_two), 1)
    place = jnp.zeros((slots, lanes_two), jnp.float32)
    for index in range(slots):
        tile = ids_ref[0, index]
        spot = jnp.where(tile < 0, -1, head_size + slot_of(lax.div(tile, tiles_here), me_ref[0], row_size, paired))
        place = jnp.where((slot == index) & (lane == spot), 1.0, place)
    live = lax.dot_general((mask_ref[...] > 0).astype(jnp.float32).astype(jnp.bfloat16), place.astype(jnp.bfloat16),
                           (((0,), (0,)), ((), ())), preferred_element_type=jnp.float32)
    lane = iota(live.shape, 1)
    shut = jnp.where((lane >= head_size) & (lane < head_size + row_size) & (live < 0.5), 1.0, 0.0).astype(jnp.bfloat16)
    total = steps * span
    cell = iota((total, shut.shape[0]), 0)
    row_of = cell // span * (chunk // cols) + cell % chunk // cols
    spread = (row_of == iota((total, shut.shape[0]), 1)).astype(jnp.bfloat16)
    bias = dot_rows(spread, shut) * BIG
    asked = dot_rows(normed_ref[...], w_query_ref[...]).astype(jnp.bfloat16).astype(jnp.float32) * scale
    low = iota((total, lanes_two), 1) < head_size
    for head in range(heads_here):
        if heads_here % 2 == 0:
            two = asked[:, head // 2 * lanes_two:(head // 2 + 1) * lanes_two]
            one = two if head % 2 == 0 else pltpu.roll(two, head_size, 1)
            query = jnp.where(low, one, bias)
        else:
            one = asked[:, head * head_size:(head + 1) * head_size]
            query = jnp.concatenate([one, bias[:, head_size:]], axis=1)
        query = query.astype(jnp.bfloat16)
        for step in range(steps):
            for group in range(groups):
                start = step * span + group * chunk
                asked_ref[head, pl.ds(group * own_rows + step * chunk, chunk), :] = query[start:start + chunk]


def front(cells, ids, me, key_mask, gain_col, w_qkv, w_out, gain_tile, w_query, heads, head_size, cols,
          heads_here, tiles_here, row_size, paired, after):
    groups = len(cells)
    width = cells[0].shape[2]
    own_rows = cells[0].shape[0] * cols
    total = groups * own_rows
    key_mask, gain_col, gain_tile = key_mask.T, gain_col.reshape(1, width), gain_tile.reshape(1, width)
    weights = [(3, width, width), (width, width), (width, heads_here * head_size), (groups,) + cells[0].shape]
    scratch = [pltpu.VMEM(shape, jnp.bfloat16) for shape in [(total, width), (3, total, width)] + weights]
    scratch += [pltpu.SMEM(ids.shape, jnp.int32), pltpu.VMEM(key_mask.shape, jnp.int32)]
    scratch += [pltpu.VMEM((1, width), jnp.float32)] * 2 + [pltpu.SemaphoreType.DMA((groups + 9,))]
    fetched = [pltpu.with_memory_space_constraint(value, pltpu.HBM)
               for value in (ids, key_mask, gain_col, gain_tile, w_qkv, w_out, w_query)]
    own = pltpu.with_memory_space_constraint(cells[0], pltpu.HBM)
    return pl.pallas_call(
        functools.partial(front_kernel, groups, heads, head_size, ROW_GROUP * cols, cols, heads_here, tiles_here, row_size, paired,
                          len(after)),
        out_shape=(jax.ShapeDtypeStruct((own_rows, width), jnp.float32),
                   jax.ShapeDtypeStruct((heads_here, total, 2 * head_size), jnp.bfloat16)),
        in_specs=[HBM] + [ANY] * (groups - 1) + [SMEM] + [HBM] * 7 + [ANY] * len(after),
        out_specs=(VMEM, VMEM),
        scratch_shapes=scratch,
        compiler_params=params(total),
        cost_estimate=pl.CostEstimate(flops=2 * total * width * 5 * width, bytes_accessed=4 * MIB,
                                      transcendentals=total * heads * 128),
        name="front",
    )(own, *cells[1:], me, *fetched, *after)


def weigh(query, tile_refs, head, slots):
    key_parts, val_parts = [], []
    for ref, slot in zip(tile_refs, slots):
        tiles = ref[:, head]
        count, keys, lanes = tiles.shape
        lane = iota(tiles.shape, 2)
        marks = (lane == iota(tiles.shape, 0) + (lanes // 2 + slot)).astype(tiles.dtype)
        key_parts.append(jnp.where(lane < lanes // 2, tiles, marks).reshape(count * keys, lanes))
        val_parts.append(jnp.where(lane < lanes // 2, jnp.ones_like(tiles), tiles).reshape(count * keys, lanes))
    scores = dot_lanes(query, jnp.concatenate(key_parts, axis=0))
    top = jnp.max(scores, axis=1, keepdims=True)
    return top, dot_rows(jnp.exp(scores - top).astype(jnp.bfloat16), jnp.concatenate(val_parts, axis=0))


def attention_cost(asked, tiles):
    heads, rows, lanes = asked.shape
    keys = sum(part.shape[0] * part.shape[2] for part in tiles)
    return pl.CostEstimate(flops=4 * rows * heads * keys * lanes, bytes_accessed=4 * MIB, transcendentals=rows * heads * keys)


def first_kernel(slots, block, asked_ref, *refs):
    tile_refs, (sums_ref, tops_ref) = refs[:len(slots)], refs[len(slots):]
    heads, rows_all, lanes = asked_ref.shape
    lane = iota((block, lanes), 1)
    for step in range(rows_all // block):
        rows = pl.ds(step * block, block)
        tops = jnp.zeros((block, lanes), jnp.float32)
        for head in range(heads):
            top, sums_ref[head, rows, :] = weigh(asked_ref[head, rows, :], tile_refs, head, slots)
            tops = jnp.where(lane == head, top, tops)
        tops_ref[rows, :] = tops


def first_tiles(asked, tiles, slots, own_rows):
    heads, rows, lanes = asked.shape
    return pl.pallas_call(
        functools.partial(first_kernel, slots, rows if rows <= 512 else own_rows),
        out_shape=(jax.ShapeDtypeStruct((heads, rows, lanes), jnp.float32), jax.ShapeDtypeStruct((rows, lanes), jnp.float32)),
        in_specs=[VMEM] * (1 + len(tiles)),
        out_specs=(VMEM, VMEM),
        compiler_params=params(rows),
        cost_estimate=attention_cost(asked, tiles),
        name="first_tiles",
    )(asked, *tiles)


def merge(asked_ref, sums_ref, tops_ref, tile_refs, slots, head, rows):
    top, sums = weigh(asked_ref[head, rows, :], tile_refs, head, slots)
    old_top = tops_ref[rows, head:head + 1]
    new_top = jnp.maximum(top, old_top)
    return new_top, sums_ref[head, rows, :] * jnp.exp(old_top - new_top) + sums * jnp.exp(top - new_top)


def more_kernel(slots, block, asked_ref, old_sums_ref, old_tops_ref, *refs):
    tile_refs, (sums_ref, tops_ref) = refs[:len(slots)], refs[len(slots):]
    heads, rows_all, lanes = asked_ref.shape
    lane = iota((block, lanes), 1)
    for step in range(rows_all // block):
        rows = pl.ds(step * block, block)
        tops = jnp.zeros((block, lanes), jnp.float32)
        for head in range(heads):
            top, sums_ref[head, rows, :] = merge(asked_ref, old_sums_ref, old_tops_ref, tile_refs, slots, head, rows)
            tops = jnp.where(lane == head, top, tops)
        tops_ref[rows, :] = tops


def more_tiles(asked, sums, tops, tiles, slots, own_rows):
    rows = asked.shape[1]
    return pl.pallas_call(
        functools.partial(more_kernel, slots, rows if rows <= 512 else own_rows),
        out_shape=(jax.ShapeDtypeStruct(sums.shape, jnp.float32), jax.ShapeDtypeStruct(tops.shape, jnp.float32)),
        in_specs=[VMEM] * (3 + len(tiles)),
        out_specs=(VMEM, VMEM),
        compiler_params=params(rows),
        cost_estimate=attention_cost(asked, tiles),
        name="more_tiles",
    )(asked, sums, tops, *tiles)


def last_kernel(slots, groups, asked_ref, sums_ref, tops_ref, *refs):
    tile_refs, out_refs = refs[:len(slots)], refs[-len(groups):]
    heads, lanes = asked_ref.shape[0], asked_ref.shape[2]
    block = out_refs[0].shape[0]
    half = lanes // 2
    lane_low = iota((block, lanes), 1) < half
    for group, out_ref in zip(groups, out_refs):
        rows = pl.ds(group * block, block)
        low = None
        for head in range(heads):
            _, sums = merge(asked_ref, sums_ref, tops_ref, tile_refs, slots, head, rows)
            turned = pltpu.roll(sums, half, 1)
            if head % 2:
                out_ref[:, pl.ds(head // 2 * lanes, lanes)] = jnp.where(lane_low, low, sums / turned).astype(jnp.bfloat16)
            elif head + 1 < heads:
                low = turned / sums
            else:
                out_ref[:, pl.ds(head * half, half)] = (turned / sums)[:, :half].astype(jnp.bfloat16)


def last_tiles(asked, sums, tops, tiles, slots, groups, own_rows, after):
    heads, rows, lanes = asked.shape
    out = jax.ShapeDtypeStruct((own_rows, heads * lanes // 2), jnp.bfloat16)
    return pl.pallas_call(
        functools.partial(last_kernel, slots, groups),
        out_shape=(out,) * len(groups),
        in_specs=[VMEM] * (3 + len(tiles)) + [ANY] * len(after),
        out_specs=(VMEM,) * len(groups),
        compiler_params=params(rows),
        cost_estimate=attention_cost(asked[:, :own_rows * len(groups)], tiles),
        name="last_tiles",
    )(asked, sums, tops, *tiles, *after)


def finish_kernel(me_ref, weight_ref, resid_ref, *refs):
    answer_refs, out_ref = refs[:-1], refs[-1]
    group_width = answer_refs[0].shape[1]
    final = resid_ref[...]
    for step, answer_ref in enumerate(answer_refs):
        group = lax.rem(me_ref[1] - step + len(answer_refs), len(answer_refs))
        rows = pl.ds(pl.multiple_of(group * group_width, group_width), group_width)
        final = final + dot_rows(answer_ref[...], weight_ref[rows, :])
    out_ref[...] = final.reshape(out_ref.shape).astype(out_ref.dtype)


def finish(me, weight, residual, answers, shape):
    return pl.pallas_call(
        finish_kernel,
        out_shape=jax.ShapeDtypeStruct(shape, jnp.bfloat16),
        in_specs=[SMEM, VMEM, VMEM] + [VMEM] * len(answers),
        out_specs=VMEM,
        compiler_params=params(0),
        cost_estimate=pl.CostEstimate(flops=2 * residual.size * weight.shape[0], bytes_accessed=MIB, transcendentals=0),
        name="finish",
    )(me, weight, residual, *answers)


def turn(size, step):
    return [(src, (src + step) % size) for src in range(size)]


def shards(row_size, col_size, fact_cells, gain_col, w_qkv, w_col_out, gain_tile, w_query, w_tile_out,
           tile_kv, tile_ids, key_mask):
    rows, cols, width = fact_cells.shape
    tiles_here, keys, heads_here, lanes = tile_kv.shape
    head_size = lanes // 2
    heads_all = width // head_size
    group_width = heads_here * head_size
    half = row_size // 2
    row_me, col_me = lax.axis_index("rows"), lax.axis_index("cols")
    me = jnp.stack([row_me, col_me]).astype(jnp.int32)
    halves = [list(range(half)), list(range(half, row_size))]
    paired = half <= 8 and half & (half - 1) == 0
    assert row_size <= head_size and row_size % 2 == 0

    def swap(value):
        return lax.all_to_all(value, "rows", split_axis=0, concat_axis=0, tiled=True, axis_index_groups=halves)

    asked_of = request(tile_ids, me, tiles_here, row_size)
    asked_by = swap(asked_of)
    heads_first = tie(jnp.transpose(tile_kv, (0, 2, 1, 3)), asked_of)
    mirrored = lax.ppermute(heads_first, "rows", turn(row_size, half))

    cells = [fact_cells]
    for step in range(1, col_size):
        cells.append(lax.ppermute(fact_cells, "cols", turn(col_size, -step)))

    across = half // 2
    near_order = [0, 1] + sorted(range(2, half), key=lambda step: (step != 2, not step & across, step & 1, step))
    far_order = [0, across] + sorted(set(range(1, half)) - {across}, key=lambda step: (step != 2, not step & across, step & 1, -step))
    near_slots, far_slots = (near_order, [half + step for step in far_order]) if paired else ([0], [half])

    def spread(tiles, which, order, after):
        if not paired:
            return [swap(pick(tiles, asked_by, which, after))]
        picked = pick_each(tiles, asked_by, which, me, order, after)
        return [tile if step == 0 else lax.ppermute(tile, "rows", [(row, row ^ step) for row in range(row_size)])
                for step, tile in zip(order, picked)]

    if group_width % 128:
        w_query = lax.dynamic_slice_in_dim(w_query, col_me * group_width, group_width, 1)
    near = spread(heads_first, 0, near_order, cells[1:])
    residual, asked = front(cells, tile_ids, me, key_mask, gain_col, w_qkv, w_col_out, gain_tile, w_query,
                            heads_all, head_size, cols, heads_here, tiles_here, row_size, paired, near[:3])
    far = spread(mirrored, 1, far_order, [asked])
    sums, tops = first_tiles(asked, near, near_slots, rows * cols)
    batch = len(far) // 2
    if batch:
        sums, tops = more_tiles(asked, sums, tops, far[:batch], far_slots[:batch], rows * cols)
    far, far_slots = far[batch:], far_slots[batch:]
    others = last_tiles(asked, sums, tops, far, far_slots, list(range(1, col_size)), rows * cols, [])
    own = last_tiles(asked, sums, tops, far, far_slots, [0], rows * cols, others[:1])
    answers = list(own) + [lax.ppermute(other, "cols", turn(col_size, step + 1)) for step, other in enumerate(others)]
    return finish(me, w_tile_out, residual, answers, fact_cells.shape)


def solution(mesh):
    row_size, col_size = mesh.shape["rows"], mesh.shape["cols"]
    placed = (P("rows", "cols", None), P(), P(), P(), P(), P(), P(), P("rows", None, "cols", None),
              P("rows", None), P("rows", None))

    def body(*arrays):
        return shards(row_size, col_size, *arrays)

    return jax.shard_map(body, mesh=mesh, in_specs=placed, out_specs=P("rows", "cols", None), check_vma=False)
```

```python
import functools

import jax
import jax.numpy as jnp
from jax import lax
from jax.experimental import pallas as pl
from jax.experimental.pallas import tpu as pltpu
from jax.sharding import PartitionSpec as P

ROW_GROUP = 16
BIG = -1e30
MIB = 1024 * 1024
VMEM = pl.BlockSpec(memory_space=pltpu.VMEM)
SMEM = pl.BlockSpec(memory_space=pltpu.SMEM)
HBM = pl.BlockSpec(memory_space=pltpu.HBM)
ANY = pl.BlockSpec(memory_space=pl.ANY)


def params(rows):
    return pltpu.CompilerParams(vmem_limit_bytes=(20 if rows <= 512 else 48) * MIB)


def dot_rows(left, right):
    return lax.dot_general(left, right, (((1,), (0,)), ((), ())), preferred_element_type=jnp.float32)


def dot_lanes(left, right):
    return lax.dot_general(left, right, (((1,), (1,)), ((), ())), preferred_element_type=jnp.float32)


def rms_scale(values, gain_vec):
    mean_sq = jnp.mean(values * values, axis=-1, keepdims=True)
    return values * lax.rsqrt(mean_sq + 1e-05) * gain_vec


def iota(shape, dim):
    return lax.broadcasted_iota(jnp.int32, shape, dim)


def slot_of(owner, row_me, row_size, paired):
    half = row_size // 2
    return owner ^ row_me if paired else lax.rem(owner + lax.div(row_me, half) * half, row_size)


def tie_kernel(value_ref, after_ref, out_ref):
    pass


def tie(value, after):
    return pl.pallas_call(
        tie_kernel,
        out_shape=jax.ShapeDtypeStruct(value.shape, value.dtype),
        in_specs=[ANY, ANY],
        out_specs=ANY,
        input_output_aliases={0: 0},
        compiler_params=params(0),
        cost_estimate=pl.CostEstimate(flops=0, bytes_accessed=0, transcendentals=0),
        name="tie",
    )(value, after)


def request_kernel(tiles_here, row_size, ids_ref, me_ref, out_ref):
    half = row_size // 2
    peer, which = iota(out_ref.shape, 0), iota(out_ref.shape, 1)
    wanted = jnp.zeros(out_ref.shape, jnp.int32)
    for slot in range(ids_ref.shape[1]):
        tile = ids_ref[0, slot]
        owner = lax.div(tile, tiles_here)
        far = jnp.where(lax.div(owner, half) == lax.div(me_ref[0], half), 0, 1)
        here = (peer == jnp.where(tile < 0, -1, lax.rem(owner, half))) & (which == far)
        wanted = jnp.where(here, lax.rem(tile, tiles_here), wanted)
    out_ref[...] = wanted


def request(ids, me, tiles_here, row_size):
    return pl.pallas_call(
        functools.partial(request_kernel, tiles_here, row_size),
        out_shape=jax.ShapeDtypeStruct((row_size // 2, 2, 128), jnp.int32),
        in_specs=[SMEM, SMEM],
        out_specs=VMEM,
        compiler_params=params(0),
        cost_estimate=pl.CostEstimate(flops=0, bytes_accessed=MIB // 4, transcendentals=0),
        name="request",
    )(ids, me)


def pick_kernel(which, wanted_ref, tiles_ref, *refs):
    out_ref = refs[-1]
    for peer in range(out_ref.shape[0]):
        out_ref[peer] = tiles_ref[wanted_ref[peer, which, 0]]


def pick(tiles, wanted, which, after):
    return pl.pallas_call(
        functools.partial(pick_kernel, which),
        out_shape=jax.ShapeDtypeStruct(wanted.shape[:1] + tiles.shape[1:], tiles.dtype),
        in_specs=[SMEM, VMEM] + [ANY] * len(after),
        out_specs=VMEM,
        compiler_params=params(0),
        cost_estimate=pl.CostEstimate(flops=0, bytes_accessed=2 * MIB, transcendentals=0),
        name="pick",
    )(wanted, tiles, *after)


def pick_each_kernel(which, order, wanted_ref, me_ref, tiles_ref, *refs):
    place = lax.rem(me_ref[0], wanted_ref.shape[0])
    for step, out_ref in zip(order, refs[-len(order):]):
        out_ref[0] = tiles_ref[wanted_ref[place ^ step, which, 0]]


def pick_each(tiles, wanted, which, me, order, after):
    count = len(order)
    return pl.pallas_call(
        functools.partial(pick_each_kernel, which, order),
        out_shape=(jax.ShapeDtypeStruct((1,) + tiles.shape[1:], tiles.dtype),) * count,
        in_specs=[SMEM, SMEM, VMEM] + [ANY] * len(after),
        out_specs=(VMEM,) * count,
        compiler_params=params(0),
        cost_estimate=pl.CostEstimate(flops=0, bytes_accessed=2 * MIB, transcendentals=0),
        name="pick_each",
    )(wanted, me, tiles, *after)


def front_kernel(groups, heads, head_size, chunk, cols, heads_here, tiles_here, row_size, paired, waited, *refs):
    cell_hbms, refs = refs[:groups], refs[groups:]
    (me_ref, ids_hbm, mask_hbm, gain_col_hbm, gain_tile_hbm, w_qkv_hbm, w_out_hbm, w_query_hbm) = refs[:8]
    (resid_ref, asked_ref, normed_ref, packed_ref, w_qkv_ref, w_out_ref, w_query_ref, cell_refs,
     ids_ref, mask_ref, gain_col_ref, gain_tile_ref, sems) = refs[8 + waited:]
    own_rows, width = resid_ref.shape
    steps = own_rows // chunk
    span = groups * chunk
    lanes_two = 2 * head_size
    group_width = heads_here * head_size
    if w_query_hbm.shape[1] != group_width:
        w_query_hbm = w_query_hbm.at[:, pl.ds(pl.multiple_of(me_ref[1] * group_width, group_width), group_width)]
    pairs = [(hbm, cell_refs.at[group]) for group, hbm in enumerate(cell_hbms)]
    pairs += [(gain_col_hbm, gain_col_ref)]
    pairs += [(w_qkv_hbm.at[:, pl.ds(part * width, width)], w_qkv_ref.at[part]) for part in range(3)]
    pairs += [(w_out_hbm, w_out_ref), (gain_tile_hbm, gain_tile_ref), (w_query_hbm, w_query_ref), (ids_hbm, ids_ref), (mask_hbm, mask_ref)]
    copies = [pltpu.make_async_copy(*pair, sems.at[index]) for index, pair in enumerate(pairs)]
    for copy in copies:
        copy.start()
    for copy in copies[:groups + 1]:
        copy.wait()
    copies = copies[groups + 1:]

    def cells_of(group, step):
        cells = cell_refs[group, pl.ds(step * (chunk // cols), chunk // cols)].astype(jnp.float32)
        return cells.reshape(chunk, width)

    for step in range(steps):
        for group in range(groups):
            cells = cells_of(group, step)
            normed_ref[pl.ds(step * span + group * chunk, chunk), :] = rms_scale(cells, gain_col_ref[...]).astype(jnp.bfloat16)
    for part in range(3):
        copies[part].wait()
        packed_ref[part] = dot_rows(normed_ref[...], w_qkv_ref[part]).astype(jnp.bfloat16)
    stacked = heads * span
    same_row = iota((stacked, span), 0) % chunk // cols == iota((stacked, span), 1) % chunk // cols
    lane_low = iota((span, lanes_two), 1) < head_size
    scale = head_size ** (-0.5)
    for step in range(steps):
        rows = pl.ds(step * span, span)
        scores = []
        for head in range(heads):
            lanes = pl.ds(head // 2 * lanes_two, lanes_two)
            query = packed_ref[0, rows, lanes]
            query = jnp.where(lane_low == (head % 2 == 0), query, jnp.zeros_like(query))
            scores.append(dot_lanes(query, packed_ref[1, rows, lanes]))
        scores = jnp.where(same_row, jnp.concatenate(scores, axis=0) * scale, BIG)
        expo = jnp.exp(scores - jnp.max(scores, axis=1, keepdims=True))
        weights = (expo / jnp.sum(expo, axis=1, keepdims=True)).astype(jnp.bfloat16)
        for pair in range(heads // 2):
            lanes = pl.ds(pair * lanes_two, lanes_two)
            start = 2 * pair * span
            mixed = dot_rows(weights[start:start + 2 * span], packed_ref[2, rows, lanes])
            normed_ref[rows, lanes] = jnp.where(lane_low, mixed[:span], mixed[span:]).astype(jnp.bfloat16)
    for copy in copies[3:]:
        copy.wait()
    delta = dot_rows(normed_ref[...], w_out_ref[...])
    for step in range(steps):
        for group in range(groups):
            start = step * span + group * chunk
            resid = cells_of(group, step) + delta[start:start + chunk]
            if group == 0:
                resid_ref[pl.ds(step * chunk, chunk), :] = resid
            normed_ref[pl.ds(start, chunk), :] = rms_scale(resid, gain_tile_ref[...]).astype(jnp.bfloat16)
    slots = mask_ref.shape[0]
    slot, lane = iota((slots, lanes_two), 0), iota((slots, lanes_two), 1)
    place = jnp.zeros((slots, lanes_two), jnp.float32)
    for index in range(slots):
        tile = ids_ref[0, index]
        spot = jnp.where(tile < 0, -1, head_size + slot_of(lax.div(tile, tiles_here), me_ref[0], row_size, paired))
        place = jnp.where((slot == index) & (lane == spot), 1.0, place)
    live = lax.dot_general((mask_ref[...] > 0).astype(jnp.float32).astype(jnp.bfloat16), place.astype(jnp.bfloat16),
                           (((0,), (0,)), ((), ())), preferred_element_type=jnp.float32)
    lane = iota(live.shape, 1)
    shut = jnp.where((lane >= head_size) & (lane < head_size + row_size) & (live < 0.5), 1.0, 0.0).astype(jnp.bfloat16)
    total = steps * span
    cell = iota((total, shut.shape[0]), 0)
    row_of = cell // span * (chunk // cols) + cell % chunk // cols
    spread = (row_of == iota((total, shut.shape[0]), 1)).astype(jnp.bfloat16)
    bias = dot_rows(spread, shut) * BIG
    asked = dot_rows(normed_ref[...], w_query_ref[...]).astype(jnp.bfloat16).astype(jnp.float32) * scale
    low = iota((total, lanes_two), 1) < head_size
    for head in range(heads_here):
        if heads_here % 2 == 0:
            two = asked[:, head // 2 * lanes_two:(head // 2 + 1) * lanes_two]
            one = two if head % 2 == 0 else pltpu.roll(two, head_size, 1)
            query = jnp.where(low, one, bias)
        else:
            one = asked[:, head * head_size:(head + 1) * head_size]
            query = jnp.concatenate([one, bias[:, head_size:]], axis=1)
        query = query.astype(jnp.bfloat16)
        for step in range(steps):
            for group in range(groups):
                start = step * span + group * chunk
                asked_ref[head, pl.ds(group * own_rows + step * chunk, chunk), :] = query[start:start + chunk]


def front(cells, ids, me, key_mask, gain_col, w_qkv, w_out, gain_tile, w_query, heads, head_size, cols,
          heads_here, tiles_here, row_size, paired, after):
    groups = len(cells)
    width = cells[0].shape[2]
    own_rows = cells[0].shape[0] * cols
    total = groups * own_rows
    key_mask, gain_col, gain_tile = key_mask.T, gain_col.reshape(1, width), gain_tile.reshape(1, width)
    weights = [(3, width, width), (width, width), (width, heads_here * head_size), (groups,) + cells[0].shape]
    scratch = [pltpu.VMEM(shape, jnp.bfloat16) for shape in [(total, width), (3, total, width)] + weights]
    scratch += [pltpu.SMEM(ids.shape, jnp.int32), pltpu.VMEM(key_mask.shape, jnp.int32)]
    scratch += [pltpu.VMEM((1, width), jnp.float32)] * 2 + [pltpu.SemaphoreType.DMA((groups + 9,))]
    fetched = [pltpu.with_memory_space_constraint(value, pltpu.HBM)
               for value in (ids, key_mask, gain_col, gain_tile, w_qkv, w_out, w_query)]
    own = pltpu.with_memory_space_constraint(cells[0], pltpu.HBM)
    return pl.pallas_call(
        functools.partial(front_kernel, groups, heads, head_size, ROW_GROUP * cols, cols, heads_here, tiles_here, row_size, paired,
                          len(after)),
        out_shape=(jax.ShapeDtypeStruct((own_rows, width), jnp.float32),
                   jax.ShapeDtypeStruct((heads_here, total, 2 * head_size), jnp.bfloat16)),
        in_specs=[HBM] + [ANY] * (groups - 1) + [SMEM] + [HBM] * 7 + [ANY] * len(after),
        out_specs=(VMEM, VMEM),
        scratch_shapes=scratch,
        compiler_params=params(total),
        cost_estimate=pl.CostEstimate(flops=2 * total * width * 5 * width, bytes_accessed=4 * MIB,
                                      transcendentals=total * heads * 128),
        name="front",
    )(own, *cells[1:], me, *fetched, *after)


def weigh(query, tile_refs, head, slots):
    key_parts, val_parts = [], []
    for ref, slot in zip(tile_refs, slots):
        tiles = ref[:, head]
        count, keys, lanes = tiles.shape
        lane = iota(tiles.shape, 2)
        marks = (lane == iota(tiles.shape, 0) + (lanes // 2 + slot)).astype(tiles.dtype)
        key_parts.append(jnp.where(lane < lanes // 2, tiles, marks).reshape(count * keys, lanes))
        val_parts.append(jnp.where(lane < lanes // 2, jnp.ones_like(tiles), tiles).reshape(count * keys, lanes))
    scores = dot_lanes(query, jnp.concatenate(key_parts, axis=0))
    top = jnp.max(scores, axis=1, keepdims=True)
    return top, dot_rows(jnp.exp(scores - top).astype(jnp.bfloat16), jnp.concatenate(val_parts, axis=0))


def attention_cost(asked, tiles):
    heads, rows, lanes = asked.shape
    keys = sum(part.shape[0] * part.shape[2] for part in tiles)
    return pl.CostEstimate(flops=4 * rows * heads * keys * lanes, bytes_accessed=4 * MIB, transcendentals=rows * heads * keys)


def first_kernel(slots, block, asked_ref, *refs):
    tile_refs, (sums_ref, tops_ref) = refs[:len(slots)], refs[len(slots):]
    heads, rows_all, lanes = asked_ref.shape
    lane = iota((block, lanes), 1)
    for step in range(rows_all // block):
        rows = pl.ds(step * block, block)
        tops = jnp.zeros((block, lanes), jnp.float32)
        for head in range(heads):
            top, sums_ref[head, rows, :] = weigh(asked_ref[head, rows, :], tile_refs, head, slots)
            tops = jnp.where(lane == head, top, tops)
        tops_ref[rows, :] = tops


def first_tiles(asked, tiles, slots, own_rows):
    heads, rows, lanes = asked.shape
    return pl.pallas_call(
        functools.partial(first_kernel, slots, rows if rows <= 512 else own_rows),
        out_shape=(jax.ShapeDtypeStruct((heads, rows, lanes), jnp.float32), jax.ShapeDtypeStruct((rows, lanes), jnp.float32)),
        in_specs=[VMEM] * (1 + len(tiles)),
        out_specs=(VMEM, VMEM),
        compiler_params=params(rows),
        cost_estimate=attention_cost(asked, tiles),
        name="first_tiles",
    )(asked, *tiles)


def merge(asked_ref, sums_ref, tops_ref, tile_refs, slots, head, rows):
    top, sums = weigh(asked_ref[head, rows, :], tile_refs, head, slots)
    old_top = tops_ref[rows, head:head + 1]
    new_top = jnp.maximum(top, old_top)
    return new_top, sums_ref[head, rows, :] * jnp.exp(old_top - new_top) + sums * jnp.exp(top - new_top)


def more_kernel(slots, block, asked_ref, old_sums_ref, old_tops_ref, *refs):
    tile_refs, (sums_ref, tops_ref) = refs[:len(slots)], refs[len(slots):]
    heads, rows_all, lanes = asked_ref.shape
    lane = iota((block, lanes), 1)
    for step in range(rows_all // block):
        rows = pl.ds(step * block, block)
        tops = jnp.zeros((block, lanes), jnp.float32)
        for head in range(heads):
            top, sums_ref[head, rows, :] = merge(asked_ref, old_sums_ref, old_tops_ref, tile_refs, slots, head, rows)
            tops = jnp.where(lane == head, top, tops)
        tops_ref[rows, :] = tops


def more_tiles(asked, sums, tops, tiles, slots, own_rows):
    rows = asked.shape[1]
    return pl.pallas_call(
        functools.partial(more_kernel, slots, rows if rows <= 512 else own_rows),
        out_shape=(jax.ShapeDtypeStruct(sums.shape, jnp.float32), jax.ShapeDtypeStruct(tops.shape, jnp.float32)),
        in_specs=[VMEM] * (3 + len(tiles)),
        out_specs=(VMEM, VMEM),
        compiler_params=params(rows),
        cost_estimate=attention_cost(asked, tiles),
        name="more_tiles",
    )(asked, sums, tops, *tiles)


def last_kernel(slots, groups, asked_ref, sums_ref, tops_ref, *refs):
    tile_refs, out_refs = refs[:len(slots)], refs[-len(groups):]
    heads, lanes = asked_ref.shape[0], asked_ref.shape[2]
    block = out_refs[0].shape[0]
    half = lanes // 2
    lane_low = iota((block, lanes), 1) < half
    for group, out_ref in zip(groups, out_refs):
        rows = pl.ds(group * block, block)
        low = None
        for head in range(heads):
            _, sums = merge(asked_ref, sums_ref, tops_ref, tile_refs, slots, head, rows)
            turned = pltpu.roll(sums, half, 1)
            if head % 2:
                out_ref[:, pl.ds(head // 2 * lanes, lanes)] = jnp.where(lane_low, low, sums / turned).astype(jnp.bfloat16)
            elif head + 1 < heads:
                low = turned / sums
            else:
                out_ref[:, pl.ds(head * half, half)] = (turned / sums)[:, :half].astype(jnp.bfloat16)


def last_tiles(asked, sums, tops, tiles, slots, groups, own_rows, after):
    heads, rows, lanes = asked.shape
    out = jax.ShapeDtypeStruct((own_rows, heads * lanes // 2), jnp.bfloat16)
    return pl.pallas_call(
        functools.partial(last_kernel, slots, groups),
        out_shape=(out,) * len(groups),
        in_specs=[VMEM] * (3 + len(tiles)) + [ANY] * len(after),
        out_specs=(VMEM,) * len(groups),
        compiler_params=params(rows),
        cost_estimate=attention_cost(asked[:, :own_rows * len(groups)], tiles),
        name="last_tiles",
    )(asked, sums, tops, *tiles, *after)


def finish_kernel(me_ref, weight_ref, resid_ref, *refs):
    answer_refs, out_ref = refs[:-1], refs[-1]
    group_width = answer_refs[0].shape[1]
    final = resid_ref[...]
    for step, answer_ref in enumerate(answer_refs):
        group = lax.rem(me_ref[1] - step + len(answer_refs), len(answer_refs))
        rows = pl.ds(pl.multiple_of(group * group_width, group_width), group_width)
        final = final + dot_rows(answer_ref[...], weight_ref[rows, :])
    out_ref[...] = final.reshape(out_ref.shape).astype(out_ref.dtype)


def finish(me, weight, residual, answers, shape):
    return pl.pallas_call(
        finish_kernel,
        out_shape=jax.ShapeDtypeStruct(shape, jnp.bfloat16),
        in_specs=[SMEM, VMEM, VMEM] + [VMEM] * len(answers),
        out_specs=VMEM,
        compiler_params=params(0),
        cost_estimate=pl.CostEstimate(flops=2 * residual.size * weight.shape[0], bytes_accessed=MIB, transcendentals=0),
        name="finish",
    )(me, weight, residual, *answers)


def turn(size, step):
    return [(src, (src + step) % size) for src in range(size)]


def shards(row_size, col_size, fact_cells, gain_col, w_qkv, w_col_out, gain_tile, w_query, w_tile_out,
           tile_kv, tile_ids, key_mask):
    rows, cols, width = fact_cells.shape
    tiles_here, keys, heads_here, lanes = tile_kv.shape
    head_size = lanes // 2
    heads_all = width // head_size
    group_width = heads_here * head_size
    half = row_size // 2
    row_me, col_me = lax.axis_index("rows"), lax.axis_index("cols")
    me = jnp.stack([row_me, col_me]).astype(jnp.int32)
    halves = [list(range(half)), list(range(half, row_size))]
    paired = half <= 8 and half & (half - 1) == 0
    assert row_size <= head_size and row_size % 2 == 0

    def swap(value):
        return lax.all_to_all(value, "rows", split_axis=0, concat_axis=0, tiled=True, axis_index_groups=halves)

    asked_of = request(tile_ids, me, tiles_here, row_size)
    asked_by = swap(asked_of)
    heads_first = tie(jnp.transpose(tile_kv, (0, 2, 1, 3)), asked_of)
    mirrored = lax.ppermute(heads_first, "rows", turn(row_size, half))

    cells = [fact_cells]
    for step in range(1, col_size):
        cells.append(lax.ppermute(fact_cells, "cols", turn(col_size, -step)))

    across = half // 2
    near_order = [0, 1] + sorted(range(2, half), key=lambda step: (step != 2, not step & across, step & 1, step))
    rest = sorted(set(range(2, half)) - {across}, key=lambda step: (not step & across, step & 1, -step))
    far_order = list(dict.fromkeys([0, across, 1] + rest[:1] + rest[-2:-1] + rest[1:-2] + rest[-1:]))
    near_slots, far_slots = (near_order, [half + step for step in far_order]) if paired else ([0], [half])

    def spread(tiles, which, order, after):
        if not paired:
            return [swap(pick(tiles, asked_by, which, after))]
        picked = pick_each(tiles, asked_by, which, me, order, after)
        return [tile if step == 0 else lax.ppermute(tile, "rows", [(row, row ^ step) for row in range(row_size)])
                for step, tile in zip(order, picked)]

    if group_width % 128:
        w_query = lax.dynamic_slice_in_dim(w_query, col_me * group_width, group_width, 1)
    residual, asked = front(cells, tile_ids, me, key_mask, gain_col, w_qkv, w_col_out, gain_tile, w_query,
                            heads_all, head_size, cols, heads_here, tiles_here, row_size, paired, [])
    near = spread(heads_first, 0, near_order, [asked])
    far = spread(mirrored, 1, far_order, near[1:3])
    sums, tops = first_tiles(asked, near, near_slots, rows * cols)
    batch = len(far) // 2
    if batch:
        sums, tops = more_tiles(asked, sums, tops, far[:batch], far_slots[:batch], rows * cols)
    far, far_slots = far[batch:], far_slots[batch:]
    others = last_tiles(asked, sums, tops, far, far_slots, list(range(1, col_size)), rows * cols, [])
    own = last_tiles(asked, sums, tops, far, far_slots, [0], rows * cols, others[:1])
    answers = list(own) + [lax.ppermute(other, "cols", turn(col_size, step + 1)) for step, other in enumerate(others)]
    return finish(me, w_tile_out, residual, answers, fact_cells.shape)


def solution(mesh):
    row_size, col_size = mesh.shape["rows"], mesh.shape["cols"]
    placed = (P("rows", "cols", None), P(), P(), P(), P(), P(), P(), P("rows", None, "cols", None),
              P("rows", None), P("rows", None))

    def body(*arrays):
        return shards(row_size, col_size, *arrays)

    return jax.shard_map(body, mesh=mesh, in_specs=placed, out_specs=P("rows", "cols", None), check_vma=False)
```

```python
import functools

import jax
import jax.numpy as jnp
from jax import lax
from jax.experimental import pallas as pl
from jax.experimental.pallas import tpu as pltpu
from jax.sharding import PartitionSpec as P

ROW_GROUP = 16
BIG = -1e30
MIB = 1024 * 1024
VMEM = pl.BlockSpec(memory_space=pltpu.VMEM)
SMEM = pl.BlockSpec(memory_space=pltpu.SMEM)
HBM = pl.BlockSpec(memory_space=pltpu.HBM)
ANY = pl.BlockSpec(memory_space=pl.ANY)


def params(rows):
    return pltpu.CompilerParams(vmem_limit_bytes=(20 if rows <= 512 else 48) * MIB)


def dot_rows(left, right):
    return lax.dot_general(left, right, (((1,), (0,)), ((), ())), preferred_element_type=jnp.float32)


def dot_lanes(left, right):
    return lax.dot_general(left, right, (((1,), (1,)), ((), ())), preferred_element_type=jnp.float32)


def rms_scale(values, gain_vec):
    mean_sq = jnp.mean(values * values, axis=-1, keepdims=True)
    return values * lax.rsqrt(mean_sq + 1e-05) * gain_vec


def iota(shape, dim):
    return lax.broadcasted_iota(jnp.int32, shape, dim)


def slot_of(owner, row_me, row_size, paired):
    half = row_size // 2
    return owner ^ row_me if paired else lax.rem(owner + lax.div(row_me, half) * half, row_size)


def tie_kernel(value_ref, after_ref, out_ref):
    pass


def tie(value, after):
    return pl.pallas_call(
        tie_kernel,
        out_shape=jax.ShapeDtypeStruct(value.shape, value.dtype),
        in_specs=[ANY, ANY],
        out_specs=ANY,
        input_output_aliases={0: 0},
        compiler_params=params(0),
        cost_estimate=pl.CostEstimate(flops=0, bytes_accessed=0, transcendentals=0),
        name="tie",
    )(value, after)


def request_kernel(tiles_here, row_size, ids_ref, me_ref, out_ref):
    peer, which = iota(out_ref.shape, 0), iota(out_ref.shape, 1)
    wanted = jnp.zeros(out_ref.shape, jnp.int32)
    for slot in range(ids_ref.shape[1]):
        tile = ids_ref[0, slot]
        owner = lax.div(tile, tiles_here)
        target = jnp.where(which == 0, owner, lax.rem(owner + row_size // 2, row_size))
        wanted = jnp.where((peer == target) & (tile >= 0), lax.rem(tile, tiles_here), wanted)
    out_ref[...] = wanted


def request(ids, me, tiles_here, row_size):
    return pl.pallas_call(
        functools.partial(request_kernel, tiles_here, row_size),
        out_shape=jax.ShapeDtypeStruct((row_size, 2, 128), jnp.int32),
        in_specs=[SMEM, SMEM],
        out_specs=VMEM,
        compiler_params=params(0),
        cost_estimate=pl.CostEstimate(flops=0, bytes_accessed=MIB // 4, transcendentals=0),
        name="request",
    )(ids, me)


def pick_kernel(which, wanted_ref, me_ref, tiles_ref, *refs):
    out_ref = refs[-1]
    half = out_ref.shape[0]
    for peer in range(half):
        out_ref[peer] = tiles_ref[wanted_ref[lax.div(me_ref[0], half) * half + peer, which, 0]]


def pick(tiles, wanted, which, me, after):
    return pl.pallas_call(
        functools.partial(pick_kernel, which),
        out_shape=jax.ShapeDtypeStruct((wanted.shape[0] // 2,) + tiles.shape[1:], tiles.dtype),
        in_specs=[SMEM, SMEM, VMEM] + [ANY] * len(after),
        out_specs=VMEM,
        compiler_params=params(0),
        cost_estimate=pl.CostEstimate(flops=0, bytes_accessed=2 * MIB, transcendentals=0),
        name="pick",
    )(wanted, me, tiles, *after)


def pick_each_kernel(which, order, wanted_ref, me_ref, tiles_ref, *refs):
    for step, out_ref in zip(order, refs[-len(order):]):
        out_ref[0] = tiles_ref[wanted_ref[me_ref[0] ^ step, which, 0]]


def pick_each(tiles, wanted, which, me, order, after):
    count = len(order)
    return pl.pallas_call(
        functools.partial(pick_each_kernel, which, order),
        out_shape=(jax.ShapeDtypeStruct((1,) + tiles.shape[1:], tiles.dtype),) * count,
        in_specs=[SMEM, SMEM, VMEM] + [ANY] * len(after),
        out_specs=(VMEM,) * count,
        compiler_params=params(0),
        cost_estimate=pl.CostEstimate(flops=0, bytes_accessed=2 * MIB, transcendentals=0),
        name="pick_each",
    )(wanted, me, tiles, *after)


def front_kernel(groups, heads, head_size, chunk, cols, heads_here, tiles_here, row_size, paired, waited, *refs):
    cell_hbms, refs = refs[:groups], refs[groups:]
    (me_ref, ids_hbm, mask_hbm, gain_col_hbm, gain_tile_hbm, w_qkv_hbm, w_out_hbm, w_query_hbm) = refs[:8]
    (resid_ref, asked_ref, normed_ref, packed_ref, w_qkv_ref, w_out_ref, w_query_ref, cell_refs,
     ids_ref, mask_ref, gain_col_ref, gain_tile_ref, sems) = refs[8 + waited:]
    own_rows, width = resid_ref.shape
    steps = own_rows // chunk
    span = groups * chunk
    lanes_two = 2 * head_size
    group_width = heads_here * head_size
    if w_query_hbm.shape[1] != group_width:
        w_query_hbm = w_query_hbm.at[:, pl.ds(pl.multiple_of(me_ref[1] * group_width, group_width), group_width)]
    pairs = [(hbm, cell_refs.at[group]) for group, hbm in enumerate(cell_hbms)]
    pairs += [(gain_col_hbm, gain_col_ref)]
    pairs += [(w_qkv_hbm.at[:, pl.ds(part * width, width)], w_qkv_ref.at[part]) for part in range(3)]
    pairs += [(w_out_hbm, w_out_ref), (gain_tile_hbm, gain_tile_ref), (w_query_hbm, w_query_ref), (ids_hbm, ids_ref), (mask_hbm, mask_ref)]
    copies = [pltpu.make_async_copy(*pair, sems.at[index]) for index, pair in enumerate(pairs)]
    for copy in copies:
        copy.start()
    for copy in copies[:groups + 1]:
        copy.wait()
    copies = copies[groups + 1:]

    def cells_of(group, step):
        cells = cell_refs[group, pl.ds(step * (chunk // cols), chunk // cols)].astype(jnp.float32)
        return cells.reshape(chunk, width)

    for step in range(steps):
        for group in range(groups):
            cells = cells_of(group, step)
            normed_ref[pl.ds(step * span + group * chunk, chunk), :] = rms_scale(cells, gain_col_ref[...]).astype(jnp.bfloat16)
    for part in range(3):
        copies[part].wait()
        packed_ref[part] = dot_rows(normed_ref[...], w_qkv_ref[part]).astype(jnp.bfloat16)
    stacked = heads * span
    same_row = iota((stacked, span), 0) % chunk // cols == iota((stacked, span), 1) % chunk // cols
    lane_low = iota((span, lanes_two), 1) < head_size
    scale = head_size ** (-0.5)
    for step in range(steps):
        rows = pl.ds(step * span, span)
        scores = []
        for head in range(heads):
            lanes = pl.ds(head // 2 * lanes_two, lanes_two)
            query = packed_ref[0, rows, lanes]
            query = jnp.where(lane_low == (head % 2 == 0), query, jnp.zeros_like(query))
            scores.append(dot_lanes(query, packed_ref[1, rows, lanes]))
        scores = jnp.where(same_row, jnp.concatenate(scores, axis=0) * scale, BIG)
        expo = jnp.exp(scores - jnp.max(scores, axis=1, keepdims=True))
        weights = (expo / jnp.sum(expo, axis=1, keepdims=True)).astype(jnp.bfloat16)
        for pair in range(heads // 2):
            lanes = pl.ds(pair * lanes_two, lanes_two)
            start = 2 * pair * span
            mixed = dot_rows(weights[start:start + 2 * span], packed_ref[2, rows, lanes])
            normed_ref[rows, lanes] = jnp.where(lane_low, mixed[:span], mixed[span:]).astype(jnp.bfloat16)
    for copy in copies[3:]:
        copy.wait()
    delta = dot_rows(normed_ref[...], w_out_ref[...])
    for step in range(steps):
        for group in range(groups):
            start = step * span + group * chunk
            resid = cells_of(group, step) + delta[start:start + chunk]
            if group == 0:
                resid_ref[pl.ds(step * chunk, chunk), :] = resid
            normed_ref[pl.ds(start, chunk), :] = rms_scale(resid, gain_tile_ref[...]).astype(jnp.bfloat16)
    slots = mask_ref.shape[0]
    slot, lane = iota((slots, lanes_two), 0), iota((slots, lanes_two), 1)
    place = jnp.zeros((slots, lanes_two), jnp.float32)
    for index in range(slots):
        tile = ids_ref[0, index]
        spot = jnp.where(tile < 0, -1, head_size + slot_of(lax.div(tile, tiles_here), me_ref[0], row_size, paired))
        place = jnp.where((slot == index) & (lane == spot), 1.0, place)
    live = lax.dot_general((mask_ref[...] > 0).astype(jnp.float32).astype(jnp.bfloat16), place.astype(jnp.bfloat16),
                           (((0,), (0,)), ((), ())), preferred_element_type=jnp.float32)
    lane = iota(live.shape, 1)
    shut = jnp.where((lane >= head_size) & (lane < head_size + row_size) & (live < 0.5), 1.0, 0.0).astype(jnp.bfloat16)
    total = steps * span
    cell = iota((total, shut.shape[0]), 0)
    row_of = cell // span * (chunk // cols) + cell % chunk // cols
    spread = (row_of == iota((total, shut.shape[0]), 1)).astype(jnp.bfloat16)
    bias = dot_rows(spread, shut) * BIG
    asked = dot_rows(normed_ref[...], w_query_ref[...]).astype(jnp.bfloat16).astype(jnp.float32) * scale
    low = iota((total, lanes_two), 1) < head_size
    for head in range(heads_here):
        if heads_here % 2 == 0:
            two = asked[:, head // 2 * lanes_two:(head // 2 + 1) * lanes_two]
            one = two if head % 2 == 0 else pltpu.roll(two, head_size, 1)
            query = jnp.where(low, one, bias)
        else:
            one = asked[:, head * head_size:(head + 1) * head_size]
            query = jnp.concatenate([one, bias[:, head_size:]], axis=1)
        query = query.astype(jnp.bfloat16)
        for step in range(steps):
            for group in range(groups):
                start = step * span + group * chunk
                asked_ref[head, pl.ds(group * own_rows + step * chunk, chunk), :] = query[start:start + chunk]


def front(cells, ids, me, key_mask, gain_col, w_qkv, w_out, gain_tile, w_query, heads, head_size, cols,
          heads_here, tiles_here, row_size, paired, after):
    groups = len(cells)
    width = cells[0].shape[2]
    own_rows = cells[0].shape[0] * cols
    total = groups * own_rows
    key_mask, gain_col, gain_tile = key_mask.T, gain_col.reshape(1, width), gain_tile.reshape(1, width)
    weights = [(3, width, width), (width, width), (width, heads_here * head_size), (groups,) + cells[0].shape]
    scratch = [pltpu.VMEM(shape, jnp.bfloat16) for shape in [(total, width), (3, total, width)] + weights]
    scratch += [pltpu.SMEM(ids.shape, jnp.int32), pltpu.VMEM(key_mask.shape, jnp.int32)]
    scratch += [pltpu.VMEM((1, width), jnp.float32)] * 2 + [pltpu.SemaphoreType.DMA((groups + 9,))]
    fetched = [pltpu.with_memory_space_constraint(value, pltpu.HBM)
               for value in (ids, key_mask, gain_col, gain_tile, w_qkv, w_out, w_query)]
    own = pltpu.with_memory_space_constraint(cells[0], pltpu.HBM)
    return pl.pallas_call(
        functools.partial(front_kernel, groups, heads, head_size, ROW_GROUP * cols, cols, heads_here, tiles_here, row_size, paired,
                          len(after)),
        out_shape=(jax.ShapeDtypeStruct((own_rows, width), jnp.float32),
                   jax.ShapeDtypeStruct((heads_here, total, 2 * head_size), jnp.bfloat16)),
        in_specs=[HBM] + [ANY] * (groups - 1) + [SMEM] + [HBM] * 7 + [ANY] * len(after),
        out_specs=(VMEM, VMEM),
        scratch_shapes=scratch,
        compiler_params=params(total),
        cost_estimate=pl.CostEstimate(flops=2 * total * width * 5 * width, bytes_accessed=4 * MIB,
                                      transcendentals=total * heads * 128),
        name="front",
    )(own, *cells[1:], me, *fetched, *after)


def weigh(query, tile_refs, head, slots):
    key_parts, val_parts = [], []
    for refs, slot in zip(tile_refs, slots):
        tiles = functools.reduce(jnp.add, [ref[:, head] for ref in refs])
        count, keys, lanes = tiles.shape
        lane = iota(tiles.shape, 2)
        marks = (lane == iota(tiles.shape, 0) + (lanes // 2 + slot)).astype(tiles.dtype)
        key_parts.append(jnp.where(lane < lanes // 2, tiles, marks).reshape(count * keys, lanes))
        val_parts.append(jnp.where(lane < lanes // 2, jnp.ones_like(tiles), tiles).reshape(count * keys, lanes))
    scores = dot_lanes(query, jnp.concatenate(key_parts, axis=0))
    top = jnp.max(scores, axis=1, keepdims=True)
    return top, dot_rows(jnp.exp(scores - top).astype(jnp.bfloat16), jnp.concatenate(val_parts, axis=0))


def attention_cost(asked, tiles):
    heads, rows, lanes = asked.shape
    keys = sum(part.shape[0] * part.shape[2] for part in tiles)
    return pl.CostEstimate(flops=4 * rows * heads * keys * lanes, bytes_accessed=4 * MIB, transcendentals=rows * heads * keys)


def first_kernel(slots, block, asked_ref, *refs):
    tile_refs, (sums_ref, tops_ref) = [[ref] for ref in refs[:len(slots)]], refs[len(slots):]
    heads, rows_all, lanes = asked_ref.shape
    lane = iota((block, lanes), 1)
    for step in range(rows_all // block):
        rows = pl.ds(step * block, block)
        tops = jnp.zeros((block, lanes), jnp.float32)
        for head in range(heads):
            top, sums_ref[head, rows, :] = weigh(asked_ref[head, rows, :], tile_refs, head, slots)
            tops = jnp.where(lane == head, top, tops)
        tops_ref[rows, :] = tops


def first_tiles(asked, tiles, slots, own_rows):
    heads, rows, lanes = asked.shape
    return pl.pallas_call(
        functools.partial(first_kernel, slots, rows if rows <= 512 else own_rows),
        out_shape=(jax.ShapeDtypeStruct((heads, rows, lanes), jnp.float32), jax.ShapeDtypeStruct((rows, lanes), jnp.float32)),
        in_specs=[VMEM] * (1 + len(tiles)),
        out_specs=(VMEM, VMEM),
        compiler_params=params(rows),
        cost_estimate=attention_cost(asked, tiles),
        name="first_tiles",
    )(asked, *tiles)


def merge(asked_ref, sums_ref, tops_ref, tile_refs, slots, head, rows):
    top, sums = weigh(asked_ref[head, rows, :], tile_refs, head, slots)
    old_top = tops_ref[rows, head:head + 1]
    new_top = jnp.maximum(top, old_top)
    return new_top, sums_ref[head, rows, :] * jnp.exp(old_top - new_top) + sums * jnp.exp(top - new_top)


def more_kernel(slots, block, asked_ref, old_sums_ref, old_tops_ref, *refs):
    tile_refs, (sums_ref, tops_ref) = [[ref] for ref in refs[:len(slots)]], refs[len(slots):]
    heads, rows_all, lanes = asked_ref.shape
    lane = iota((block, lanes), 1)
    for step in range(rows_all // block):
        rows = pl.ds(step * block, block)
        tops = jnp.zeros((block, lanes), jnp.float32)
        for head in range(heads):
            top, sums_ref[head, rows, :] = merge(asked_ref, old_sums_ref, old_tops_ref, tile_refs, slots, head, rows)
            tops = jnp.where(lane == head, top, tops)
        tops_ref[rows, :] = tops


def more_tiles(asked, sums, tops, tiles, slots, own_rows):
    rows = asked.shape[1]
    return pl.pallas_call(
        functools.partial(more_kernel, slots, rows if rows <= 512 else own_rows),
        out_shape=(jax.ShapeDtypeStruct(sums.shape, jnp.float32), jax.ShapeDtypeStruct(tops.shape, jnp.float32)),
        in_specs=[VMEM] * (3 + len(tiles)),
        out_specs=(VMEM, VMEM),
        compiler_params=params(rows),
        cost_estimate=attention_cost(asked, tiles),
        name="more_tiles",
    )(asked, sums, tops, *tiles)


def last_kernel(slots, ways, groups, asked_ref, sums_ref, tops_ref, *refs):
    out_refs = refs[-len(groups):]
    tile_refs = [refs[ways * index:ways * (index + 1)] for index in range(len(slots))]
    heads, lanes = asked_ref.shape[0], asked_ref.shape[2]
    block = out_refs[0].shape[0]
    half = lanes // 2
    lane_low = iota((block, lanes), 1) < half
    for group, out_ref in zip(groups, out_refs):
        rows = pl.ds(group * block, block)
        low = None
        for head in range(heads):
            _, sums = merge(asked_ref, sums_ref, tops_ref, tile_refs, slots, head, rows)
            turned = pltpu.roll(sums, half, 1)
            if head % 2:
                out_ref[:, pl.ds(head // 2 * lanes, lanes)] = jnp.where(lane_low, low, sums / turned).astype(jnp.bfloat16)
            elif head + 1 < heads:
                low = turned / sums
            else:
                out_ref[:, pl.ds(head * half, half)] = (turned / sums)[:, :half].astype(jnp.bfloat16)


def last_tiles(asked, sums, tops, tiles, slots, groups, own_rows, after):
    heads, rows, lanes = asked.shape
    out = jax.ShapeDtypeStruct((own_rows, heads * lanes // 2), jnp.bfloat16)
    return pl.pallas_call(
        functools.partial(last_kernel, slots, len(tiles) // len(slots), groups),
        out_shape=(out,) * len(groups),
        in_specs=[VMEM] * (3 + len(tiles)) + [ANY] * len(after),
        out_specs=(VMEM,) * len(groups),
        compiler_params=params(rows),
        cost_estimate=attention_cost(asked[:, :own_rows * len(groups)], tiles),
        name="last_tiles",
    )(asked, sums, tops, *tiles, *after)


def finish_kernel(me_ref, weight_ref, resid_ref, *refs):
    answer_refs, out_ref = refs[:-1], refs[-1]
    group_width = answer_refs[0].shape[1]
    final = resid_ref[...]
    for step, answer_ref in enumerate(answer_refs):
        group = lax.rem(me_ref[1] - step + len(answer_refs), len(answer_refs))
        rows = pl.ds(pl.multiple_of(group * group_width, group_width), group_width)
        final = final + dot_rows(answer_ref[...], weight_ref[rows, :])
    out_ref[...] = final.reshape(out_ref.shape).astype(out_ref.dtype)


def finish(me, weight, residual, answers, shape):
    return pl.pallas_call(
        finish_kernel,
        out_shape=jax.ShapeDtypeStruct(shape, jnp.bfloat16),
        in_specs=[SMEM, VMEM, VMEM] + [VMEM] * len(answers),
        out_specs=VMEM,
        compiler_params=params(0),
        cost_estimate=pl.CostEstimate(flops=2 * residual.size * weight.shape[0], bytes_accessed=MIB, transcendentals=0),
        name="finish",
    )(me, weight, residual, *answers)


def turn(size, step):
    return [(src, (src + step) % size) for src in range(size)]


def shards(row_size, col_size, fact_cells, gain_col, w_qkv, w_col_out, gain_tile, w_query, w_tile_out,
           tile_kv, tile_ids, key_mask):
    rows, cols, width = fact_cells.shape
    tiles_here, keys, heads_here, lanes = tile_kv.shape
    head_size = lanes // 2
    heads_all = width // head_size
    group_width = heads_here * head_size
    half = row_size // 2
    row_me, col_me = lax.axis_index("rows"), lax.axis_index("cols")
    me = jnp.stack([row_me, col_me]).astype(jnp.int32)
    halves = [list(range(half)), list(range(half, row_size))]
    paired = half <= 8 and half & (half - 1) == 0
    assert row_size <= head_size and row_size % 2 == 0

    def swap(value):
        return lax.all_to_all(value, "rows", split_axis=0, concat_axis=0, tiled=True, axis_index_groups=halves)

    asked_of = request(tile_ids, me, tiles_here, row_size)
    asked_by = lax.all_to_all(asked_of, "rows", split_axis=0, concat_axis=0, tiled=True)
    heads_first = tie(jnp.transpose(tile_kv, (0, 2, 1, 3)), asked_of)
    mirrored = lax.ppermute(heads_first, "rows", turn(row_size, half))

    cells = [fact_cells]
    for step in range(1, col_size):
        cells.append(lax.ppermute(fact_cells, "cols", turn(col_size, -step)))

    across = half // 2

    def send(tile, step, some=False):
        inner = [row for row in range(row_size) if not some or bool(row & half) != bool(row & across)]
        return lax.ppermute(tile, "rows", [(row, row ^ step) for row in inner])

    if group_width % 128:
        w_query = lax.dynamic_slice_in_dim(w_query, col_me * group_width, group_width, 1)
    residual, asked = front(cells, tile_ids, me, key_mask, gain_col, w_qkv, w_col_out, gain_tile, w_query,
                            heads_all, head_size, cols, heads_here, tiles_here, row_size, paired, [])
    if paired:
        aside = list(range(1, across))
        over = sorted(range(across, half), key=lambda step: (step & 1, step))
        near_order = sorted(aside, key=lambda step: step != 1)[:2] + over + aside[2:]
        picked = pick_each(heads_first, asked_by, 0, me, [0] + near_order + [half + step for step in over], [asked])
        near = list(picked[:1]) + [send(tile, step) for step, tile in zip(near_order, picked[1:])]
        straight = [send(tile, half + step, True) for step, tile in zip(over, picked[half:])]
        mirror_picked = pick_each(mirrored, asked_by, 1, me, [0] + aside + over, near[1:3])
        far = list(mirror_picked[:1]) + [send(tile, step) for step, tile in zip(aside, mirror_picked[1:])]
        outward = [send(tile, step, True) for step, tile in zip(over, mirror_picked[across:])]
        sums, tops = first_tiles(asked, near, [0] + near_order, rows * cols)
        sums, tops = more_tiles(asked, sums, tops, far, [half + step for step in [0] + aside], rows * cols)
        far = [way for ways in zip(straight, outward) for way in ways]
        far_slots = [half + step for step in over]
    else:
        near = [swap(pick(heads_first, asked_by, 0, me, [asked]))]
        far, far_slots = [swap(pick(mirrored, asked_by, 1, me, near))], [half]
        sums, tops = first_tiles(asked, near, [0], rows * cols)
    others = last_tiles(asked, sums, tops, far, far_slots, list(range(1, col_size)), rows * cols, [])
    own = last_tiles(asked, sums, tops, far, far_slots, [0], rows * cols, others[:1])
    answers = list(own) + [lax.ppermute(other, "cols", turn(col_size, step + 1)) for step, other in enumerate(others)]
    return finish(me, w_tile_out, residual, answers, fact_cells.shape)


def solution(mesh):
    row_size, col_size = mesh.shape["rows"], mesh.shape["cols"]
    placed = (P("rows", "cols", None), P(), P(), P(), P(), P(), P(), P("rows", None, "cols", None),
              P("rows", None), P("rows", None))

    def body(*arrays):
        return shards(row_size, col_size, *arrays)

    return jax.shard_map(body, mesh=mesh, in_specs=placed, out_specs=P("rows", "cols", None), check_vma=False)
```

```python
import functools

import jax
import jax.numpy as jnp
from jax import lax
from jax.experimental import pallas as pl
from jax.experimental.pallas import tpu as pltpu
from jax.sharding import PartitionSpec as P

ROW_GROUP = 16
BIG = -1e30
MIB = 1024 * 1024
VMEM = pl.BlockSpec(memory_space=pltpu.VMEM)
SMEM = pl.BlockSpec(memory_space=pltpu.SMEM)
HBM = pl.BlockSpec(memory_space=pltpu.HBM)
ANY = pl.BlockSpec(memory_space=pl.ANY)


def params(rows):
    return pltpu.CompilerParams(vmem_limit_bytes=(20 if rows <= 512 else 48) * MIB)


def dot_rows(left, right):
    return lax.dot_general(left, right, (((1,), (0,)), ((), ())), preferred_element_type=jnp.float32)


def dot_lanes(left, right):
    return lax.dot_general(left, right, (((1,), (1,)), ((), ())), preferred_element_type=jnp.float32)


def rms_scale(values, gain_vec):
    mean_sq = jnp.mean(values * values, axis=-1, keepdims=True)
    return values * lax.rsqrt(mean_sq + 1e-05) * gain_vec


def iota(shape, dim):
    return lax.broadcasted_iota(jnp.int32, shape, dim)


def slot_of(owner, row_me, row_size, paired):
    half = row_size // 2
    return owner ^ row_me if paired else lax.rem(owner + lax.div(row_me, half) * half, row_size)


def tie_kernel(value_ref, after_ref, out_ref):
    pass


def tie(value, after):
    return pl.pallas_call(
        tie_kernel,
        out_shape=jax.ShapeDtypeStruct(value.shape, value.dtype),
        in_specs=[ANY, ANY],
        out_specs=ANY,
        input_output_aliases={0: 0},
        compiler_params=params(0),
        cost_estimate=pl.CostEstimate(flops=0, bytes_accessed=0, transcendentals=0),
        name="tie",
    )(value, after)


def request_kernel(tiles_here, row_size, ids_ref, me_ref, out_ref):
    half = row_size // 2
    peer, which = iota(out_ref.shape, 0), iota(out_ref.shape, 1)
    wanted = jnp.zeros(out_ref.shape, jnp.int32)
    for slot in range(ids_ref.shape[1]):
        tile = ids_ref[0, slot]
        owner = lax.div(tile, tiles_here)
        far = jnp.where(lax.div(owner, half) == lax.div(me_ref[0], half), 0, 1)
        here = (peer == jnp.where(tile < 0, -1, lax.rem(owner, half))) & (which == far)
        wanted = jnp.where(here, lax.rem(tile, tiles_here), wanted)
    out_ref[...] = wanted


def request(ids, me, tiles_here, row_size):
    return pl.pallas_call(
        functools.partial(request_kernel, tiles_here, row_size),
        out_shape=jax.ShapeDtypeStruct((row_size // 2, 2, 128), jnp.int32),
        in_specs=[SMEM, SMEM],
        out_specs=VMEM,
        compiler_params=params(0),
        cost_estimate=pl.CostEstimate(flops=0, bytes_accessed=MIB // 4, transcendentals=0),
        name="request",
    )(ids, me)


def pick_kernel(which, wanted_ref, tiles_ref, *refs):
    out_ref = refs[-1]
    for peer in range(out_ref.shape[0]):
        out_ref[peer] = tiles_ref[wanted_ref[peer, which, 0]]


def pick(tiles, wanted, which, after):
    return pl.pallas_call(
        functools.partial(pick_kernel, which),
        out_shape=jax.ShapeDtypeStruct(wanted.shape[:1] + tiles.shape[1:], tiles.dtype),
        in_specs=[SMEM, VMEM] + [ANY] * len(after),
        out_specs=VMEM,
        compiler_params=params(0),
        cost_estimate=pl.CostEstimate(flops=0, bytes_accessed=2 * MIB, transcendentals=0),
        name="pick",
    )(wanted, tiles, *after)


def pick_each_kernel(which, order, wanted_ref, me_ref, tiles_ref, *refs):
    place = lax.rem(me_ref[0], wanted_ref.shape[0])
    for step, out_ref in zip(order, refs[-len(order):]):
        out_ref[0] = tiles_ref[wanted_ref[place ^ step, which, 0]]


def pick_each(tiles, wanted, which, me, order, after):
    count = len(order)
    return pl.pallas_call(
        functools.partial(pick_each_kernel, which, order),
        out_shape=(jax.ShapeDtypeStruct((1,) + tiles.shape[1:], tiles.dtype),) * count,
        in_specs=[SMEM, SMEM, VMEM] + [ANY] * len(after),
        out_specs=(VMEM,) * count,
        compiler_params=params(0),
        cost_estimate=pl.CostEstimate(flops=0, bytes_accessed=2 * MIB, transcendentals=0),
        name="pick_each",
    )(wanted, me, tiles, *after)


def front_kernel(groups, heads, head_size, chunk, cols, heads_here, tiles_here, row_size, paired, waited, *refs):
    cell_hbms, refs = refs[:groups], refs[groups:]
    (me_ref, ids_hbm, mask_hbm, gain_col_hbm, gain_tile_hbm, w_qkv_hbm, w_out_hbm, w_query_hbm) = refs[:8]
    (resid_ref, asked_ref, normed_ref, packed_ref, w_qkv_ref, w_out_ref, w_query_ref, cell_refs,
     ids_ref, mask_ref, gain_col_ref, gain_tile_ref, sems) = refs[8 + waited:]
    own_rows, width = resid_ref.shape
    steps = own_rows // chunk
    span = groups * chunk
    lanes_two = 2 * head_size
    group_width = heads_here * head_size
    if w_query_hbm.shape[1] != group_width:
        w_query_hbm = w_query_hbm.at[:, pl.ds(pl.multiple_of(me_ref[1] * group_width, group_width), group_width)]
    pairs = [(hbm, cell_refs.at[group]) for group, hbm in enumerate(cell_hbms)]
    pairs += [(gain_col_hbm, gain_col_ref)]
    pairs += [(w_qkv_hbm.at[:, pl.ds(part * width, width)], w_qkv_ref.at[part]) for part in range(3)]
    pairs += [(w_out_hbm, w_out_ref), (gain_tile_hbm, gain_tile_ref), (w_query_hbm, w_query_ref), (ids_hbm, ids_ref), (mask_hbm, mask_ref)]
    copies = [pltpu.make_async_copy(*pair, sems.at[index]) for index, pair in enumerate(pairs)]
    for copy in copies:
        copy.start()
    for copy in copies[:groups + 1]:
        copy.wait()
    copies = copies[groups + 1:]

    def cells_of(group, step):
        cells = cell_refs[group, pl.ds(step * (chunk // cols), chunk // cols)].astype(jnp.float32)
        return cells.reshape(chunk, width)

    for step in range(steps):
        for group in range(groups):
            cells = cells_of(group, step)
            normed_ref[pl.ds(step * span + group * chunk, chunk), :] = rms_scale(cells, gain_col_ref[...]).astype(jnp.bfloat16)
    for part in range(3):
        copies[part].wait()
        packed_ref[part] = dot_rows(normed_ref[...], w_qkv_ref[part]).astype(jnp.bfloat16)
    stacked = heads * span
    same_row = iota((stacked, span), 0) % chunk // cols == iota((stacked, span), 1) % chunk // cols
    lane_low = iota((span, lanes_two), 1) < head_size
    scale = head_size ** (-0.5)
    for step in range(steps):
        rows = pl.ds(step * span, span)
        scores = []
        for head in range(heads):
            lanes = pl.ds(head // 2 * lanes_two, lanes_two)
            query = packed_ref[0, rows, lanes]
            query = jnp.where(lane_low == (head % 2 == 0), query, jnp.zeros_like(query))
            scores.append(dot_lanes(query, packed_ref[1, rows, lanes]))
        scores = jnp.where(same_row, jnp.concatenate(scores, axis=0) * scale, BIG)
        expo = jnp.exp(scores - jnp.max(scores, axis=1, keepdims=True))
        weights = (expo / jnp.sum(expo, axis=1, keepdims=True)).astype(jnp.bfloat16)
        for pair in range(heads // 2):
            lanes = pl.ds(pair * lanes_two, lanes_two)
            start = 2 * pair * span
            mixed = dot_rows(weights[start:start + 2 * span], packed_ref[2, rows, lanes])
            normed_ref[rows, lanes] = jnp.where(lane_low, mixed[:span], mixed[span:]).astype(jnp.bfloat16)
    for copy in copies[3:]:
        copy.wait()
    delta = dot_rows(normed_ref[...], w_out_ref[...])
    for step in range(steps):
        for group in range(groups):
            start = step * span + group * chunk
            resid = cells_of(group, step) + delta[start:start + chunk]
            if group == 0:
                resid_ref[pl.ds(step * chunk, chunk), :] = resid
            normed_ref[pl.ds(start, chunk), :] = rms_scale(resid, gain_tile_ref[...]).astype(jnp.bfloat16)
    slots = mask_ref.shape[0]
    slot, lane = iota((slots, lanes_two), 0), iota((slots, lanes_two), 1)
    place = jnp.zeros((slots, lanes_two), jnp.float32)
    for index in range(slots):
        tile = ids_ref[0, index]
        spot = jnp.where(tile < 0, -1, head_size + slot_of(lax.div(tile, tiles_here), me_ref[0], row_size, paired))
        place = jnp.where((slot == index) & (lane == spot), 1.0, place)
    live = lax.dot_general((mask_ref[...] > 0).astype(jnp.float32).astype(jnp.bfloat16), place.astype(jnp.bfloat16),
                           (((0,), (0,)), ((), ())), preferred_element_type=jnp.float32)
    lane = iota(live.shape, 1)
    shut = jnp.where((lane >= head_size) & (lane < head_size + row_size) & (live < 0.5), 1.0, 0.0).astype(jnp.bfloat16)
    total = steps * span
    cell = iota((total, shut.shape[0]), 0)
    row_of = cell // span * (chunk // cols) + cell % chunk // cols
    spread = (row_of == iota((total, shut.shape[0]), 1)).astype(jnp.bfloat16)
    bias = dot_rows(spread, shut) * BIG
    asked = dot_rows(normed_ref[...], w_query_ref[...]).astype(jnp.bfloat16).astype(jnp.float32) * scale
    low = iota((total, lanes_two), 1) < head_size
    for head in range(heads_here):
        if heads_here % 2 == 0:
            two = asked[:, head // 2 * lanes_two:(head // 2 + 1) * lanes_two]
            one = two if head % 2 == 0 else pltpu.roll(two, head_size, 1)
            query = jnp.where(low, one, bias)
        else:
            one = asked[:, head * head_size:(head + 1) * head_size]
            query = jnp.concatenate([one, bias[:, head_size:]], axis=1)
        query = query.astype(jnp.bfloat16)
        for step in range(steps):
            for group in range(groups):
                start = step * span + group * chunk
                asked_ref[head, pl.ds(group * own_rows + step * chunk, chunk), :] = query[start:start + chunk]


def front(cells, ids, me, key_mask, gain_col, w_qkv, w_out, gain_tile, w_query, heads, head_size, cols,
          heads_here, tiles_here, row_size, paired, after):
    groups = len(cells)
    width = cells[0].shape[2]
    own_rows = cells[0].shape[0] * cols
    total = groups * own_rows
    key_mask, gain_col, gain_tile = key_mask.T, gain_col.reshape(1, width), gain_tile.reshape(1, width)
    weights = [(3, width, width), (width, width), (width, heads_here * head_size), (groups,) + cells[0].shape]
    scratch = [pltpu.VMEM(shape, jnp.bfloat16) for shape in [(total, width), (3, total, width)] + weights]
    scratch += [pltpu.SMEM(ids.shape, jnp.int32), pltpu.VMEM(key_mask.shape, jnp.int32)]
    scratch += [pltpu.VMEM((1, width), jnp.float32)] * 2 + [pltpu.SemaphoreType.DMA((groups + 9,))]
    fetched = [pltpu.with_memory_space_constraint(value, pltpu.HBM)
               for value in (ids, key_mask, gain_col, gain_tile, w_qkv, w_out, w_query)]
    own = pltpu.with_memory_space_constraint(cells[0], pltpu.HBM)
    return pl.pallas_call(
        functools.partial(front_kernel, groups, heads, head_size, ROW_GROUP * cols, cols, heads_here, tiles_here, row_size, paired,
                          len(after)),
        out_shape=(jax.ShapeDtypeStruct((own_rows, width), jnp.float32),
                   jax.ShapeDtypeStruct((heads_here, total, 2 * head_size), jnp.bfloat16)),
        in_specs=[HBM] + [ANY] * (groups - 1) + [SMEM] + [HBM] * 7 + [ANY] * len(after),
        out_specs=(VMEM, VMEM),
        scratch_shapes=scratch,
        compiler_params=params(total),
        cost_estimate=pl.CostEstimate(flops=2 * total * width * 5 * width, bytes_accessed=4 * MIB,
                                      transcendentals=total * heads * 128),
        name="front",
    )(own, *cells[1:], me, *fetched, *after)


def weigh(query, tile_refs, head, slots):
    key_parts, val_parts = [], []
    for ref, slot in zip(tile_refs, slots):
        tiles = ref[:, head]
        count, keys, lanes = tiles.shape
        lane = iota(tiles.shape, 2)
        marks = (lane == iota(tiles.shape, 0) + (lanes // 2 + slot)).astype(tiles.dtype)
        key_parts.append(jnp.where(lane < lanes // 2, tiles, marks).reshape(count * keys, lanes))
        val_parts.append(jnp.where(lane < lanes // 2, jnp.ones_like(tiles), tiles).reshape(count * keys, lanes))
    scores = dot_lanes(query, jnp.concatenate(key_parts, axis=0))
    top = jnp.max(scores, axis=1, keepdims=True)
    return top, dot_rows(jnp.exp(scores - top).astype(jnp.bfloat16), jnp.concatenate(val_parts, axis=0))


def attention_cost(asked, tiles):
    heads, rows, lanes = asked.shape
    keys = sum(part.shape[0] * part.shape[2] for part in tiles)
    return pl.CostEstimate(flops=4 * rows * heads * keys * lanes, bytes_accessed=4 * MIB, transcendentals=rows * heads * keys)


def first_kernel(slots, block, asked_ref, *refs):
    tile_refs, (sums_ref, tops_ref) = refs[:len(slots)], refs[len(slots):]
    heads, rows_all, lanes = asked_ref.shape
    lane = iota((block, lanes), 1)
    for step in range(rows_all // block):
        rows = pl.ds(step * block, block)
        tops = jnp.zeros((block, lanes), jnp.float32)
        for head in range(heads):
            top, sums_ref[head, rows, :] = weigh(asked_ref[head, rows, :], tile_refs, head, slots)
            tops = jnp.where(lane == head, top, tops)
        tops_ref[rows, :] = tops


def first_tiles(asked, tiles, slots, own_rows):
    heads, rows, lanes = asked.shape
    return pl.pallas_call(
        functools.partial(first_kernel, slots, rows if rows <= 512 else own_rows),
        out_shape=(jax.ShapeDtypeStruct((heads, rows, lanes), jnp.float32), jax.ShapeDtypeStruct((rows, lanes), jnp.float32)),
        in_specs=[VMEM] * (1 + len(tiles)),
        out_specs=(VMEM, VMEM),
        compiler_params=params(rows),
        cost_estimate=attention_cost(asked, tiles),
        name="first_tiles",
    )(asked, *tiles)


def merge(asked_ref, sums_ref, tops_ref, tile_refs, slots, head, rows):
    top, sums = weigh(asked_ref[head, rows, :], tile_refs, head, slots)
    old_top = tops_ref[rows, head:head + 1]
    new_top = jnp.maximum(top, old_top)
    return new_top, sums_ref[head, rows, :] * jnp.exp(old_top - new_top) + sums * jnp.exp(top - new_top)


def more_kernel(slots, block, asked_ref, old_sums_ref, old_tops_ref, *refs):
    tile_refs, (sums_ref, tops_ref) = refs[:len(slots)], refs[len(slots):]
    heads, rows_all, lanes = asked_ref.shape
    lane = iota((block, lanes), 1)
    for step in range(rows_all // block):
        rows = pl.ds(step * block, block)
        tops = jnp.zeros((block, lanes), jnp.float32)
        for head in range(heads):
            top, sums_ref[head, rows, :] = merge(asked_ref, old_sums_ref, old_tops_ref, tile_refs, slots, head, rows)
            tops = jnp.where(lane == head, top, tops)
        tops_ref[rows, :] = tops


def more_tiles(asked, sums, tops, tiles, slots, own_rows):
    rows = asked.shape[1]
    return pl.pallas_call(
        functools.partial(more_kernel, slots, rows if rows <= 512 else own_rows),
        out_shape=(jax.ShapeDtypeStruct(sums.shape, jnp.float32), jax.ShapeDtypeStruct(tops.shape, jnp.float32)),
        in_specs=[VMEM] * (3 + len(tiles)),
        out_specs=(VMEM, VMEM),
        compiler_params=params(rows),
        cost_estimate=attention_cost(asked, tiles),
        name="more_tiles",
    )(asked, sums, tops, *tiles)


def last_kernel(slots, groups, asked_ref, sums_ref, tops_ref, *refs):
    tile_refs, out_refs = refs[:len(slots)], refs[-len(groups):]
    heads, lanes = asked_ref.shape[0], asked_ref.shape[2]
    block = out_refs[0].shape[0]
    half = lanes // 2
    lane_low = iota((block, lanes), 1) < half
    for group, out_ref in zip(groups, out_refs):
        rows = pl.ds(group * block, block)
        low = None
        for head in range(heads):
            _, sums = merge(asked_ref, sums_ref, tops_ref, tile_refs, slots, head, rows)
            turned = pltpu.roll(sums, half, 1)
            if head % 2:
                out_ref[:, pl.ds(head // 2 * lanes, lanes)] = jnp.where(lane_low, low, sums / turned).astype(jnp.bfloat16)
            elif head + 1 < heads:
                low = turned / sums
            else:
                out_ref[:, pl.ds(head * half, half)] = (turned / sums)[:, :half].astype(jnp.bfloat16)


def last_tiles(asked, sums, tops, tiles, slots, groups, own_rows, after):
    heads, rows, lanes = asked.shape
    out = jax.ShapeDtypeStruct((own_rows, heads * lanes // 2), jnp.bfloat16)
    return pl.pallas_call(
        functools.partial(last_kernel, slots, groups),
        out_shape=(out,) * len(groups),
        in_specs=[VMEM] * (3 + len(tiles)) + [ANY] * len(after),
        out_specs=(VMEM,) * len(groups),
        compiler_params=params(rows),
        cost_estimate=attention_cost(asked[:, :own_rows * len(groups)], tiles),
        name="last_tiles",
    )(asked, sums, tops, *tiles, *after)


def own_kernel(me_ref, weight_ref, resid_ref, answer_ref, partial_ref, *part_refs):
    groups, group_width = len(part_refs) + 1, answer_ref.shape[1]

    def rows(step):
        group = lax.rem(me_ref[1] - step + groups, groups)
        return weight_ref[pl.ds(pl.multiple_of(group * group_width, group_width), group_width), :]

    partial_ref[...] = resid_ref[...] + dot_rows(answer_ref[...], rows(0))
    for step, part_ref in enumerate(part_refs):
        part_ref[...] = rows(step + 1)


def own_part(me, weight, residual, answer, groups):
    part = jax.ShapeDtypeStruct((answer.shape[1], weight.shape[1]), weight.dtype)
    return pl.pallas_call(
        own_kernel,
        out_shape=(jax.ShapeDtypeStruct(residual.shape, jnp.float32),) + (part,) * (groups - 1),
        in_specs=[SMEM, VMEM, VMEM, VMEM],
        out_specs=(VMEM,) * groups,
        compiler_params=params(0),
        cost_estimate=pl.CostEstimate(flops=2 * residual.size * answer.shape[1], bytes_accessed=MIB, transcendentals=0),
        name="own_part",
    )(me, weight, residual, answer)


def turn(size, step):
    return [(src, (src + step) % size) for src in range(size)]


def shards(row_size, col_size, fact_cells, gain_col, w_qkv, w_col_out, gain_tile, w_query, w_tile_out,
           tile_kv, tile_ids, key_mask):
    rows, cols, width = fact_cells.shape
    tiles_here, keys, heads_here, lanes = tile_kv.shape
    head_size = lanes // 2
    heads_all = width // head_size
    group_width = heads_here * head_size
    half = row_size // 2
    row_me, col_me = lax.axis_index("rows"), lax.axis_index("cols")
    me = jnp.stack([row_me, col_me]).astype(jnp.int32)
    halves = [list(range(half)), list(range(half, row_size))]
    paired = half <= 8 and half & (half - 1) == 0
    assert row_size <= head_size and row_size % 2 == 0

    def swap(value):
        return lax.all_to_all(value, "rows", split_axis=0, concat_axis=0, tiled=True, axis_index_groups=halves)

    asked_of = request(tile_ids, me, tiles_here, row_size)
    asked_by = swap(asked_of)
    heads_first = tie(jnp.transpose(tile_kv, (0, 2, 1, 3)), asked_of)
    mirrored = lax.ppermute(heads_first, "rows", turn(row_size, half))

    cells = [fact_cells]
    for step in range(1, col_size):
        cells.append(lax.ppermute(fact_cells, "cols", turn(col_size, -step)))

    across = half // 2
    near_order = [0, 1] + sorted(range(2, half), key=lambda step: (step != 2, not step & across, step & 1, step))
    rest = sorted(set(range(2, half)) - {across}, key=lambda step: (step != 2, not step & across, step & 1, -step))
    far_order = list(dict.fromkeys([0, across] + rest + [1]))
    near_slots, far_slots = (near_order, [half + step for step in far_order]) if paired else ([0], [half])

    def spread(tiles, which, order, after):
        if not order:
            return []
        if not paired:
            return [swap(pick(tiles, asked_by, which, after))]
        picked = pick_each(tiles, asked_by, which, me, order, after)
        return [tile if step == 0 else lax.ppermute(tile, "rows", [(row, row ^ step) for row in range(row_size)])
                for step, tile in zip(order, picked)]

    if group_width % 128:
        w_query = lax.dynamic_slice_in_dim(w_query, col_me * group_width, group_width, 1)
    residual, asked = front(cells, tile_ids, me, key_mask, gain_col, w_qkv, w_col_out, gain_tile, w_query,
                            heads_all, head_size, cols, heads_here, tiles_here, row_size, paired, [])
    near = spread(heads_first, 0, near_order, [asked])
    far = spread(mirrored, 1, far_order[:-1] if paired else far_order, near[1:3])
    sums, tops = first_tiles(asked, near, near_slots, rows * cols)
    far += spread(mirrored, 1, far_order[-1:] if paired else [], [tops])
    batch = len(far) // 2
    if batch:
        sums, tops = more_tiles(asked, sums, tops, far[:batch], far_slots[:batch], rows * cols)
    far, far_slots = far[batch:], far_slots[batch:]
    others = last_tiles(asked, sums, tops, far, far_slots, list(range(1, col_size)), rows * cols, [])
    own = last_tiles(asked, sums, tops, far, far_slots, [0], rows * cols, others[:1])
    final, *weights = own_part(me, w_tile_out, residual, own[0], col_size)
    for step, (other, weight) in enumerate(zip(others, weights)):
        final = final + dot_rows(lax.ppermute(other, "cols", turn(col_size, step + 1)), weight)
    return final.astype(jnp.bfloat16).reshape(rows, cols, width)


def solution(mesh):
    row_size, col_size = mesh.shape["rows"], mesh.shape["cols"]
    placed = (P("rows", "cols", None), P(), P(), P(), P(), P(), P(), P("rows", None, "cols", None),
              P("rows", None), P("rows", None))

    def body(*arrays):
        return shards(row_size, col_size, *arrays)

    return jax.shard_map(body, mesh=mesh, in_specs=placed, out_specs=P("rows", "cols", None), check_vma=False)
```

```python
import functools

import jax
import jax.numpy as jnp
from jax import lax
from jax.experimental import pallas as pl
from jax.experimental.pallas import tpu as pltpu
from jax.sharding import PartitionSpec as P

ROW_GROUP = 16
BIG = -1e30
MIB = 1024 * 1024
VMEM = pl.BlockSpec(memory_space=pltpu.VMEM)
SMEM = pl.BlockSpec(memory_space=pltpu.SMEM)
HBM = pl.BlockSpec(memory_space=pltpu.HBM)
ANY = pl.BlockSpec(memory_space=pl.ANY)


def params(rows):
    return pltpu.CompilerParams(vmem_limit_bytes=(20 if rows <= 512 else 48) * MIB)


def dot_rows(left, right):
    return lax.dot_general(left, right, (((1,), (0,)), ((), ())), preferred_element_type=jnp.float32)


def dot_lanes(left, right):
    return lax.dot_general(left, right, (((1,), (1,)), ((), ())), preferred_element_type=jnp.float32)


def rms_scale(values, gain_vec):
    mean_sq = jnp.mean(values * values, axis=-1, keepdims=True)
    return values * lax.rsqrt(mean_sq + 1e-05) * gain_vec


def iota(shape, dim):
    return lax.broadcasted_iota(jnp.int32, shape, dim)


def slot_of(owner, row_me, row_size, paired):
    half = row_size // 2
    return owner ^ row_me if paired else lax.rem(owner + lax.div(row_me, half) * half, row_size)


def tie_kernel(value_ref, after_ref, out_ref):
    pass


def tie(value, after):
    return pl.pallas_call(
        tie_kernel,
        out_shape=jax.ShapeDtypeStruct(value.shape, value.dtype),
        in_specs=[ANY, ANY],
        out_specs=ANY,
        input_output_aliases={0: 0},
        compiler_params=params(0),
        cost_estimate=pl.CostEstimate(flops=0, bytes_accessed=0, transcendentals=0),
        name="tie",
    )(value, after)


def request_kernel(tiles_here, row_size, ids_ref, me_ref, out_ref):
    half = row_size // 2
    peer, which = iota(out_ref.shape, 0), iota(out_ref.shape, 1)
    wanted = jnp.zeros(out_ref.shape, jnp.int32)
    for slot in range(ids_ref.shape[1]):
        tile = ids_ref[0, slot]
        owner = lax.div(tile, tiles_here)
        far = jnp.where(lax.div(owner, half) == lax.div(me_ref[0], half), 0, 1)
        here = (peer == jnp.where(tile < 0, -1, lax.rem(owner, half))) & (which == far)
        wanted = jnp.where(here, lax.rem(tile, tiles_here), wanted)
    out_ref[...] = wanted


def request(ids, me, tiles_here, row_size):
    return pl.pallas_call(
        functools.partial(request_kernel, tiles_here, row_size),
        out_shape=jax.ShapeDtypeStruct((row_size // 2, 2, 128), jnp.int32),
        in_specs=[SMEM, SMEM],
        out_specs=VMEM,
        compiler_params=params(0),
        cost_estimate=pl.CostEstimate(flops=0, bytes_accessed=MIB // 4, transcendentals=0),
        name="request",
    )(ids, me)


def pick_kernel(which, wanted_ref, tiles_ref, *refs):
    out_ref = refs[-1]
    for peer in range(out_ref.shape[0]):
        out_ref[peer] = tiles_ref[wanted_ref[peer, which, 0]]


def pick(tiles, wanted, which, after):
    return pl.pallas_call(
        functools.partial(pick_kernel, which),
        out_shape=jax.ShapeDtypeStruct(wanted.shape[:1] + tiles.shape[1:], tiles.dtype),
        in_specs=[SMEM, VMEM] + [ANY] * len(after),
        out_specs=VMEM,
        compiler_params=params(0),
        cost_estimate=pl.CostEstimate(flops=0, bytes_accessed=2 * MIB, transcendentals=0),
        name="pick",
    )(wanted, tiles, *after)


def pick_each_kernel(which, order, wanted_ref, me_ref, tiles_ref, *refs):
    place = lax.rem(me_ref[0], wanted_ref.shape[0])
    for step, out_ref in zip(order, refs[-len(order):]):
        out_ref[0] = tiles_ref[wanted_ref[place ^ step, which, 0]]


def pick_each(tiles, wanted, which, me, order, after):
    count = len(order)
    return pl.pallas_call(
        functools.partial(pick_each_kernel, which, order),
        out_shape=(jax.ShapeDtypeStruct((1,) + tiles.shape[1:], tiles.dtype),) * count,
        in_specs=[SMEM, SMEM, VMEM] + [ANY] * len(after),
        out_specs=(VMEM,) * count,
        compiler_params=params(0),
        cost_estimate=pl.CostEstimate(flops=0, bytes_accessed=2 * MIB, transcendentals=0),
        name="pick_each",
    )(wanted, me, tiles, *after)


def front_kernel(groups, heads, head_size, chunk, cols, heads_here, tiles_here, row_size, paired, waited, *refs):
    cell_hbms, refs = refs[:groups], refs[groups:]
    (me_ref, ids_hbm, mask_hbm, gain_col_hbm, gain_tile_hbm, w_qkv_hbm, w_out_hbm, w_query_hbm) = refs[:8]
    (resid_ref, asked_ref, normed_ref, packed_ref, w_qkv_ref, w_out_ref, w_query_ref, cell_refs,
     ids_ref, mask_ref, gain_col_ref, gain_tile_ref, sems) = refs[8 + waited:]
    own_rows, width = resid_ref.shape
    steps = own_rows // chunk
    span = groups * chunk
    lanes_two = 2 * head_size
    group_width = heads_here * head_size
    if w_query_hbm.shape[1] != group_width:
        w_query_hbm = w_query_hbm.at[:, pl.ds(pl.multiple_of(me_ref[1] * group_width, group_width), group_width)]
    pairs = [(hbm, cell_refs.at[group]) for group, hbm in enumerate(cell_hbms)]
    pairs += [(gain_col_hbm, gain_col_ref)]
    pairs += [(w_qkv_hbm.at[:, pl.ds(part * width, width)], w_qkv_ref.at[part]) for part in range(3)]
    pairs += [(w_out_hbm, w_out_ref), (gain_tile_hbm, gain_tile_ref), (w_query_hbm, w_query_ref), (ids_hbm, ids_ref), (mask_hbm, mask_ref)]
    copies = [pltpu.make_async_copy(*pair, sems.at[index]) for index, pair in enumerate(pairs)]
    for copy in copies:
        copy.start()
    for copy in copies[:groups + 1]:
        copy.wait()
    copies = copies[groups + 1:]

    def cells_of(group, step):
        cells = cell_refs[group, pl.ds(step * (chunk // cols), chunk // cols)].astype(jnp.float32)
        return cells.reshape(chunk, width)

    for step in range(steps):
        for group in range(groups):
            cells = cells_of(group, step)
            normed_ref[pl.ds(step * span + group * chunk, chunk), :] = rms_scale(cells, gain_col_ref[...]).astype(jnp.bfloat16)
    for part in range(3):
        copies[part].wait()
        packed_ref[part] = dot_rows(normed_ref[...], w_qkv_ref[part]).astype(jnp.bfloat16)
    stacked = heads * span
    same_row = iota((stacked, span), 0) % chunk // cols == iota((stacked, span), 1) % chunk // cols
    lane_low = iota((span, lanes_two), 1) < head_size
    scale = head_size ** (-0.5)
    for step in range(steps):
        rows = pl.ds(step * span, span)
        scores = []
        for head in range(heads):
            lanes = pl.ds(head // 2 * lanes_two, lanes_two)
            query = packed_ref[0, rows, lanes]
            query = jnp.where(lane_low == (head % 2 == 0), query, jnp.zeros_like(query))
            scores.append(dot_lanes(query, packed_ref[1, rows, lanes]))
        scores = jnp.where(same_row, jnp.concatenate(scores, axis=0) * scale, BIG)
        expo = jnp.exp(scores - jnp.max(scores, axis=1, keepdims=True))
        weights = (expo / jnp.sum(expo, axis=1, keepdims=True)).astype(jnp.bfloat16)
        for pair in range(heads // 2):
            lanes = pl.ds(pair * lanes_two, lanes_two)
            start = 2 * pair * span
            mixed = dot_rows(weights[start:start + 2 * span], packed_ref[2, rows, lanes])
            normed_ref[rows, lanes] = jnp.where(lane_low, mixed[:span], mixed[span:]).astype(jnp.bfloat16)
    for copy in copies[3:]:
        copy.wait()
    delta = dot_rows(normed_ref[...], w_out_ref[...])
    for step in range(steps):
        for group in range(groups):
            start = step * span + group * chunk
            resid = cells_of(group, step) + delta[start:start + chunk]
            if group == 0:
                resid_ref[pl.ds(step * chunk, chunk), :] = resid
            normed_ref[pl.ds(start, chunk), :] = rms_scale(resid, gain_tile_ref[...]).astype(jnp.bfloat16)
    slots = mask_ref.shape[0]
    slot, lane = iota((slots, lanes_two), 0), iota((slots, lanes_two), 1)
    place = jnp.zeros((slots, lanes_two), jnp.float32)
    for index in range(slots):
        tile = ids_ref[0, index]
        spot = jnp.where(tile < 0, -1, head_size + slot_of(lax.div(tile, tiles_here), me_ref[0], row_size, paired))
        place = jnp.where((slot == index) & (lane == spot), 1.0, place)
    live = lax.dot_general((mask_ref[...] > 0).astype(jnp.float32).astype(jnp.bfloat16), place.astype(jnp.bfloat16),
                           (((0,), (0,)), ((), ())), preferred_element_type=jnp.float32)
    lane = iota(live.shape, 1)
    shut = jnp.where((lane >= head_size) & (lane < head_size + row_size) & (live < 0.5), 1.0, 0.0).astype(jnp.bfloat16)
    total = steps * span
    cell = iota((total, shut.shape[0]), 0)
    row_of = cell // span * (chunk // cols) + cell % chunk // cols
    spread = (row_of == iota((total, shut.shape[0]), 1)).astype(jnp.bfloat16)
    bias = dot_rows(spread, shut) * BIG
    asked = dot_rows(normed_ref[...], w_query_ref[...]).astype(jnp.bfloat16).astype(jnp.float32) * scale
    low = iota((total, lanes_two), 1) < head_size
    for head in range(heads_here):
        if heads_here % 2 == 0:
            two = asked[:, head // 2 * lanes_two:(head // 2 + 1) * lanes_two]
            one = two if head % 2 == 0 else pltpu.roll(two, head_size, 1)
            query = jnp.where(low, one, bias)
        else:
            one = asked[:, head * head_size:(head + 1) * head_size]
            query = jnp.concatenate([one, bias[:, head_size:]], axis=1)
        query = query.astype(jnp.bfloat16)
        for step in range(steps):
            for group in range(groups):
                start = step * span + group * chunk
                asked_ref[head, pl.ds(group * own_rows + step * chunk, chunk), :] = query[start:start + chunk]


def front(cells, ids, me, key_mask, gain_col, w_qkv, w_out, gain_tile, w_query, heads, head_size, cols,
          heads_here, tiles_here, row_size, paired, after):
    groups = len(cells)
    width = cells[0].shape[2]
    own_rows = cells[0].shape[0] * cols
    total = groups * own_rows
    key_mask, gain_col, gain_tile = key_mask.T, gain_col.reshape(1, width), gain_tile.reshape(1, width)
    weights = [(3, width, width), (width, width), (width, heads_here * head_size), (groups,) + cells[0].shape]
    scratch = [pltpu.VMEM(shape, jnp.bfloat16) for shape in [(total, width), (3, total, width)] + weights]
    scratch += [pltpu.SMEM(ids.shape, jnp.int32), pltpu.VMEM(key_mask.shape, jnp.int32)]
    scratch += [pltpu.VMEM((1, width), jnp.float32)] * 2 + [pltpu.SemaphoreType.DMA((groups + 9,))]
    fetched = [pltpu.with_memory_space_constraint(value, pltpu.HBM)
               for value in (ids, key_mask, gain_col, gain_tile, w_qkv, w_out, w_query)]
    own = pltpu.with_memory_space_constraint(cells[0], pltpu.HBM)
    return pl.pallas_call(
        functools.partial(front_kernel, groups, heads, head_size, ROW_GROUP * cols, cols, heads_here, tiles_here, row_size, paired,
                          len(after)),
        out_shape=(jax.ShapeDtypeStruct((own_rows, width), jnp.float32),
                   jax.ShapeDtypeStruct((heads_here, total, 2 * head_size), jnp.bfloat16)),
        in_specs=[HBM] + [ANY] * (groups - 1) + [SMEM] + [HBM] * 7 + [ANY] * len(after),
        out_specs=(VMEM, VMEM),
        scratch_shapes=scratch,
        compiler_params=params(total),
        cost_estimate=pl.CostEstimate(flops=2 * total * width * 5 * width, bytes_accessed=4 * MIB,
                                      transcendentals=total * heads * 128),
        name="front",
    )(own, *cells[1:], me, *fetched, *after)


def weigh(query, tile_refs, head, slots):
    key_parts, val_parts = [], []
    for ref, slot in zip(tile_refs, slots):
        tiles = ref[:, head]
        count, keys, lanes = tiles.shape
        lane = iota(tiles.shape, 2)
        marks = (lane == iota(tiles.shape, 0) + (lanes // 2 + slot)).astype(tiles.dtype)
        key_parts.append(jnp.where(lane < lanes // 2, tiles, marks).reshape(count * keys, lanes))
        val_parts.append(jnp.where(lane < lanes // 2, jnp.ones_like(tiles), tiles).reshape(count * keys, lanes))
    scores = dot_lanes(query, jnp.concatenate(key_parts, axis=0))
    top = jnp.max(scores, axis=1, keepdims=True)
    return top, dot_rows(jnp.exp(scores - top).astype(jnp.bfloat16), jnp.concatenate(val_parts, axis=0))


def attention_cost(asked, tiles):
    heads, rows, lanes = asked.shape
    keys = sum(part.shape[0] * part.shape[2] for part in tiles)
    return pl.CostEstimate(flops=4 * rows * heads * keys * lanes, bytes_accessed=4 * MIB, transcendentals=rows * heads * keys)


def first_kernel(slots, block, asked_ref, *refs):
    tile_refs, (sums_ref, tops_ref) = refs[:len(slots)], refs[-2:]
    heads, rows_all, lanes = asked_ref.shape
    lane = iota((block, lanes), 1)
    for step in range(rows_all // block):
        rows = pl.ds(step * block, block)
        tops = jnp.zeros((block, lanes), jnp.float32)
        for head in range(heads):
            top, sums_ref[head, rows, :] = weigh(asked_ref[head, rows, :], tile_refs, head, slots)
            tops = jnp.where(lane == head, top, tops)
        tops_ref[rows, :] = tops


def first_tiles(asked, tiles, slots, own_rows, after):
    heads, rows, lanes = asked.shape
    return pl.pallas_call(
        functools.partial(first_kernel, slots, rows if rows <= 512 else own_rows),
        out_shape=(jax.ShapeDtypeStruct((heads, rows, lanes), jnp.float32), jax.ShapeDtypeStruct((rows, lanes), jnp.float32)),
        in_specs=[VMEM] * (1 + len(tiles)) + [ANY] * len(after),
        out_specs=(VMEM, VMEM),
        compiler_params=params(rows),
        cost_estimate=attention_cost(asked, tiles),
        name="first_tiles",
    )(asked, *tiles, *after)


def merge(asked_ref, sums_ref, tops_ref, tile_refs, slots, head, rows):
    top, sums = weigh(asked_ref[head, rows, :], tile_refs, head, slots)
    old_top = tops_ref[rows, head:head + 1]
    new_top = jnp.maximum(top, old_top)
    return new_top, sums_ref[head, rows, :] * jnp.exp(old_top - new_top) + sums * jnp.exp(top - new_top)


def more_kernel(slots, block, asked_ref, old_sums_ref, old_tops_ref, *refs):
    tile_refs, (sums_ref, tops_ref) = refs[:len(slots)], refs[len(slots):]
    heads, rows_all, lanes = asked_ref.shape
    lane = iota((block, lanes), 1)
    for step in range(rows_all // block):
        rows = pl.ds(step * block, block)
        tops = jnp.zeros((block, lanes), jnp.float32)
        for head in range(heads):
            top, sums_ref[head, rows, :] = merge(asked_ref, old_sums_ref, old_tops_ref, tile_refs, slots, head, rows)
            tops = jnp.where(lane == head, top, tops)
        tops_ref[rows, :] = tops


def more_tiles(asked, sums, tops, tiles, slots, own_rows):
    rows = asked.shape[1]
    return pl.pallas_call(
        functools.partial(more_kernel, slots, rows if rows <= 512 else own_rows),
        out_shape=(jax.ShapeDtypeStruct(sums.shape, jnp.float32), jax.ShapeDtypeStruct(tops.shape, jnp.float32)),
        in_specs=[VMEM] * (3 + len(tiles)),
        out_specs=(VMEM, VMEM),
        compiler_params=params(rows),
        cost_estimate=attention_cost(asked, tiles),
        name="more_tiles",
    )(asked, sums, tops, *tiles)


def last_kernel(slots, groups, asked_ref, sums_ref, tops_ref, *refs):
    tile_refs, out_refs = refs[:len(slots)], refs[-len(groups):]
    heads, lanes = asked_ref.shape[0], asked_ref.shape[2]
    block = out_refs[0].shape[0]
    half = lanes // 2
    lane_low = iota((block, lanes), 1) < half
    for group, out_ref in zip(groups, out_refs):
        rows = pl.ds(group * block, block)
        low = None
        for head in range(heads):
            _, sums = merge(asked_ref, sums_ref, tops_ref, tile_refs, slots, head, rows)
            turned = pltpu.roll(sums, half, 1)
            if head % 2:
                out_ref[:, pl.ds(head // 2 * lanes, lanes)] = jnp.where(lane_low, low, sums / turned).astype(jnp.bfloat16)
            elif head + 1 < heads:
                low = turned / sums
            else:
                out_ref[:, pl.ds(head * half, half)] = (turned / sums)[:, :half].astype(jnp.bfloat16)


def last_tiles(asked, sums, tops, tiles, slots, groups, own_rows, after):
    heads, rows, lanes = asked.shape
    out = jax.ShapeDtypeStruct((own_rows, heads * lanes // 2), jnp.bfloat16)
    return pl.pallas_call(
        functools.partial(last_kernel, slots, groups),
        out_shape=(out,) * len(groups),
        in_specs=[VMEM] * (3 + len(tiles)) + [ANY] * len(after),
        out_specs=(VMEM,) * len(groups),
        compiler_params=params(rows),
        cost_estimate=attention_cost(asked[:, :own_rows * len(groups)], tiles),
        name="last_tiles",
    )(asked, sums, tops, *tiles, *after)


def own_kernel(me_ref, weight_ref, resid_ref, answer_ref, partial_ref, *part_refs):
    groups, group_width = len(part_refs) + 1, answer_ref.shape[1]

    def rows(step):
        group = lax.rem(me_ref[1] - step + groups, groups)
        return weight_ref[pl.ds(pl.multiple_of(group * group_width, group_width), group_width), :]

    partial_ref[...] = resid_ref[...] + dot_rows(answer_ref[...], rows(0))
    for step, part_ref in enumerate(part_refs):
        part_ref[...] = rows(step + 1)


def own_part(me, weight, residual, answer, groups):
    part = jax.ShapeDtypeStruct((answer.shape[1], weight.shape[1]), weight.dtype)
    return pl.pallas_call(
        own_kernel,
        out_shape=(jax.ShapeDtypeStruct(residual.shape, jnp.float32),) + (part,) * (groups - 1),
        in_specs=[SMEM, VMEM, VMEM, VMEM],
        out_specs=(VMEM,) * groups,
        compiler_params=params(0),
        cost_estimate=pl.CostEstimate(flops=2 * residual.size * answer.shape[1], bytes_accessed=MIB, transcendentals=0),
        name="own_part",
    )(me, weight, residual, answer)


def turn(size, step):
    return [(src, (src + step) % size) for src in range(size)]


def shards(row_size, col_size, fact_cells, gain_col, w_qkv, w_col_out, gain_tile, w_query, w_tile_out,
           tile_kv, tile_ids, key_mask):
    rows, cols, width = fact_cells.shape
    tiles_here, keys, heads_here, lanes = tile_kv.shape
    head_size = lanes // 2
    heads_all = width // head_size
    group_width = heads_here * head_size
    half = row_size // 2
    row_me, col_me = lax.axis_index("rows"), lax.axis_index("cols")
    me = jnp.stack([row_me, col_me]).astype(jnp.int32)
    halves = [list(range(half)), list(range(half, row_size))]
    paired = half <= 8 and half & (half - 1) == 0
    assert row_size <= head_size and row_size % 2 == 0

    def swap(value):
        return lax.all_to_all(value, "rows", split_axis=0, concat_axis=0, tiled=True, axis_index_groups=halves)

    asked_of = request(tile_ids, me, tiles_here, row_size)
    asked_by = swap(asked_of)
    heads_first = tie(jnp.transpose(tile_kv, (0, 2, 1, 3)), asked_of)
    mirrored = lax.ppermute(heads_first, "rows", turn(row_size, half))

    cells = [fact_cells]
    for step in range(1, col_size):
        cells.append(lax.ppermute(fact_cells, "cols", turn(col_size, -step)))

    across = half // 2
    near_order = [0, 1] + sorted(range(2, half), key=lambda step: (step != 2, not step & across, step & 1, step))
    rest = sorted(set(range(2, half)) - {across}, key=lambda step: (step != 2, not step & across, step & 1, -step))
    far_order = list(dict.fromkeys([0, across] + rest + [1]))
    near_slots, far_slots = (near_order, [half + step for step in far_order]) if paired else ([0], [half])

    def spread(tiles, which, order, after):
        if not order:
            return []
        if not paired:
            return [swap(pick(tiles, asked_by, which, after))]
        picked = pick_each(tiles, asked_by, which, me, order, after)
        return [tile if step == 0 else lax.ppermute(tile, "rows", [(row, row ^ step) for row in range(row_size)])
                for step, tile in zip(order, picked)]

    if group_width % 128:
        w_query = lax.dynamic_slice_in_dim(w_query, col_me * group_width, group_width, 1)
    residual, asked = front(cells, tile_ids, me, key_mask, gain_col, w_qkv, w_col_out, gain_tile, w_query,
                            heads_all, head_size, cols, heads_here, tiles_here, row_size, paired, [])
    near = spread(heads_first, 0, near_order, [asked])
    far = spread(mirrored, 1, far_order[:-1] if paired else far_order, near[1:3])
    sums, tops = first_tiles(asked, near, near_slots, rows * cols, far[1:2])
    far += spread(mirrored, 1, far_order[-1:] if paired else [], [tops])
    batch = len(far) // 2
    if batch:
        sums, tops = more_tiles(asked, sums, tops, far[:batch], far_slots[:batch], rows * cols)
    far, far_slots = far[batch:], far_slots[batch:]
    others = last_tiles(asked, sums, tops, far, far_slots, list(range(1, col_size)), rows * cols, [])
    own = last_tiles(asked, sums, tops, far, far_slots, [0], rows * cols, others[:1])
    final, *weights = own_part(me, w_tile_out, residual, own[0], col_size)
    for step, (other, weight) in enumerate(zip(others, weights)):
        final = final + dot_rows(lax.ppermute(other, "cols", turn(col_size, step + 1)), weight)
    return final.astype(jnp.bfloat16).reshape(rows, cols, width)


def solution(mesh):
    row_size, col_size = mesh.shape["rows"], mesh.shape["cols"]
    placed = (P("rows", "cols", None), P(), P(), P(), P(), P(), P(), P("rows", None, "cols", None),
              P("rows", None), P("rows", None))

    def body(*arrays):
        return shards(row_size, col_size, *arrays)

    return jax.shard_map(body, mesh=mesh, in_specs=placed, out_specs=P("rows", "cols", None), check_vma=False)
```

```python
import functools

import jax
import jax.numpy as jnp
from jax import lax
from jax.experimental import pallas as pl
from jax.experimental.pallas import tpu as pltpu
from jax.sharding import PartitionSpec as P

ROW_GROUP = 16
BIG = -1e30
MIB = 1024 * 1024
VMEM = pl.BlockSpec(memory_space=pltpu.VMEM)
SMEM = pl.BlockSpec(memory_space=pltpu.SMEM)
HBM = pl.BlockSpec(memory_space=pltpu.HBM)
ANY = pl.BlockSpec(memory_space=pl.ANY)


def params(rows):
    return pltpu.CompilerParams(vmem_limit_bytes=(20 if rows <= 512 else 48) * MIB)


def dot_rows(left, right):
    return lax.dot_general(left, right, (((1,), (0,)), ((), ())), preferred_element_type=jnp.float32)


def dot_lanes(left, right):
    return lax.dot_general(left, right, (((1,), (1,)), ((), ())), preferred_element_type=jnp.float32)


def rms_scale(values, gain_vec):
    mean_sq = jnp.mean(values * values, axis=-1, keepdims=True)
    return values * lax.rsqrt(mean_sq + 1e-05) * gain_vec


def iota(shape, dim):
    return lax.broadcasted_iota(jnp.int32, shape, dim)


def slot_of(owner, row_me, row_size, paired):
    half = row_size // 2
    return owner ^ row_me if paired else lax.rem(owner + lax.div(row_me, half) * half, row_size)


def request_kernel(tiles_here, row_size, ids_ref, me_ref, out_ref):
    half = row_size // 2
    peer, which = iota(out_ref.shape, 0), iota(out_ref.shape, 1)
    wanted = jnp.zeros(out_ref.shape, jnp.int32)
    for slot in range(ids_ref.shape[1]):
        tile = ids_ref[0, slot]
        owner = lax.div(tile, tiles_here)
        far = jnp.where(lax.div(owner, half) == lax.div(me_ref[0], half), 0, 1)
        here = (peer == jnp.where(tile < 0, -1, lax.rem(owner, half))) & (which == far)
        wanted = jnp.where(here, lax.rem(tile, tiles_here), wanted)
    out_ref[...] = wanted


def request(ids, me, tiles_here, row_size):
    return pl.pallas_call(
        functools.partial(request_kernel, tiles_here, row_size),
        out_shape=jax.ShapeDtypeStruct((row_size // 2, 2, 128), jnp.int32),
        in_specs=[SMEM, SMEM],
        out_specs=VMEM,
        compiler_params=params(0),
        cost_estimate=pl.CostEstimate(flops=0, bytes_accessed=MIB // 4, transcendentals=0),
        name="request",
    )(ids, me)


def pick_kernel(which, wanted_ref, tiles_ref, *refs):
    out_ref = refs[-1]
    for peer in range(out_ref.shape[0]):
        out_ref[peer] = tiles_ref[wanted_ref[peer, which, 0]]


def pick(tiles, wanted, which, after):
    return pl.pallas_call(
        functools.partial(pick_kernel, which),
        out_shape=jax.ShapeDtypeStruct(wanted.shape[:1] + tiles.shape[1:], tiles.dtype),
        in_specs=[SMEM, VMEM] + [ANY] * len(after),
        out_specs=VMEM,
        compiler_params=params(0),
        cost_estimate=pl.CostEstimate(flops=0, bytes_accessed=2 * MIB, transcendentals=0),
        name="pick",
    )(wanted, tiles, *after)


def pick_each_kernel(which, order, wanted_ref, me_ref, tiles_ref, *refs):
    place = lax.rem(me_ref[0], wanted_ref.shape[0])
    for step, out_ref in zip(order, refs[-len(order):]):
        out_ref[0] = tiles_ref[wanted_ref[place ^ step, which, 0]]


def pick_each(tiles, wanted, which, me, order, after):
    count = len(order)
    return pl.pallas_call(
        functools.partial(pick_each_kernel, which, order),
        out_shape=(jax.ShapeDtypeStruct((1,) + tiles.shape[1:], tiles.dtype),) * count,
        in_specs=[SMEM, SMEM, VMEM] + [ANY] * len(after),
        out_specs=(VMEM,) * count,
        compiler_params=params(0),
        cost_estimate=pl.CostEstimate(flops=0, bytes_accessed=2 * MIB, transcendentals=0),
        name="pick_each",
    )(wanted, me, tiles, *after)


def front_kernel(groups, heads, head_size, chunk, cols, heads_here, tiles_here, row_size, paired, waited, *refs):
    cell_hbms, refs = refs[:groups], refs[groups:]
    (me_ref, ids_hbm, mask_hbm, gain_col_hbm, gain_tile_hbm, w_qkv_hbm, w_out_hbm, w_query_hbm) = refs[:8]
    (resid_ref, asked_ref, normed_ref, packed_ref, w_qkv_ref, w_out_ref, w_query_ref, cell_refs,
     ids_ref, mask_ref, gain_col_ref, gain_tile_ref, sems) = refs[8 + waited:]
    own_rows, width = resid_ref.shape
    steps = own_rows // chunk
    span = groups * chunk
    lanes_two = 2 * head_size
    group_width = heads_here * head_size
    if w_query_hbm.shape[1] != group_width:
        w_query_hbm = w_query_hbm.at[:, pl.ds(pl.multiple_of(me_ref[1] * group_width, group_width), group_width)]
    pairs = [(hbm, cell_refs.at[group]) for group, hbm in enumerate(cell_hbms)]
    pairs += [(gain_col_hbm, gain_col_ref)]
    pairs += [(w_qkv_hbm.at[:, pl.ds(part * width, width)], w_qkv_ref.at[part]) for part in range(3)]
    pairs += [(w_out_hbm, w_out_ref), (gain_tile_hbm, gain_tile_ref), (w_query_hbm, w_query_ref), (ids_hbm, ids_ref), (mask_hbm, mask_ref)]
    copies = [pltpu.make_async_copy(*pair, sems.at[index]) for index, pair in enumerate(pairs)]
    for copy in copies:
        copy.start()
    for copy in copies[:groups + 1]:
        copy.wait()
    copies = copies[groups + 1:]

    def cells_of(group, step):
        cells = cell_refs[group, pl.ds(step * (chunk // cols), chunk // cols)].astype(jnp.float32)
        return cells.reshape(chunk, width)

    for step in range(steps):
        for group in range(groups):
            cells = cells_of(group, step)
            normed_ref[pl.ds(step * span + group * chunk, chunk), :] = rms_scale(cells, gain_col_ref[...]).astype(jnp.bfloat16)
    for part in range(3):
        copies[part].wait()
        packed_ref[part] = dot_rows(normed_ref[...], w_qkv_ref[part]).astype(jnp.bfloat16)
    stacked = heads * span
    same_row = iota((stacked, span), 0) % chunk // cols == iota((stacked, span), 1) % chunk // cols
    lane_low = iota((span, lanes_two), 1) < head_size
    scale = head_size ** (-0.5)
    for step in range(steps):
        rows = pl.ds(step * span, span)
        scores = []
        for head in range(heads):
            lanes = pl.ds(head // 2 * lanes_two, lanes_two)
            query = packed_ref[0, rows, lanes]
            query = jnp.where(lane_low == (head % 2 == 0), query, jnp.zeros_like(query))
            scores.append(dot_lanes(query, packed_ref[1, rows, lanes]))
        scores = jnp.where(same_row, jnp.concatenate(scores, axis=0) * scale, BIG)
        expo = jnp.exp(scores - jnp.max(scores, axis=1, keepdims=True))
        weights = (expo / jnp.sum(expo, axis=1, keepdims=True)).astype(jnp.bfloat16)
        for pair in range(heads // 2):
            lanes = pl.ds(pair * lanes_two, lanes_two)
            start = 2 * pair * span
            mixed = dot_rows(weights[start:start + 2 * span], packed_ref[2, rows, lanes])
            normed_ref[rows, lanes] = jnp.where(lane_low, mixed[:span], mixed[span:]).astype(jnp.bfloat16)
    for copy in copies[3:]:
        copy.wait()
    delta = dot_rows(normed_ref[...], w_out_ref[...])
    for step in range(steps):
        for group in range(groups):
            start = step * span + group * chunk
            resid = cells_of(group, step) + delta[start:start + chunk]
            if group == 0:
                resid_ref[pl.ds(step * chunk, chunk), :] = resid
            normed_ref[pl.ds(start, chunk), :] = rms_scale(resid, gain_tile_ref[...]).astype(jnp.bfloat16)
    slots = mask_ref.shape[0]
    slot, lane = iota((slots, lanes_two), 0), iota((slots, lanes_two), 1)
    place = jnp.zeros((slots, lanes_two), jnp.float32)
    for index in range(slots):
        tile = ids_ref[0, index]
        spot = jnp.where(tile < 0, -1, head_size + slot_of(lax.div(tile, tiles_here), me_ref[0], row_size, paired))
        place = jnp.where((slot == index) & (lane == spot), 1.0, place)
    live = lax.dot_general((mask_ref[...] > 0).astype(jnp.float32).astype(jnp.bfloat16), place.astype(jnp.bfloat16),
                           (((0,), (0,)), ((), ())), preferred_element_type=jnp.float32)
    lane = iota(live.shape, 1)
    shut = jnp.where((lane >= head_size) & (lane < head_size + row_size) & (live < 0.5), 1.0, 0.0).astype(jnp.bfloat16)
    total = steps * span
    cell = iota((total, shut.shape[0]), 0)
    row_of = cell // span * (chunk // cols) + cell % chunk // cols
    spread = (row_of == iota((total, shut.shape[0]), 1)).astype(jnp.bfloat16)
    bias = dot_rows(spread, shut) * BIG
    asked = dot_rows(normed_ref[...], w_query_ref[...]).astype(jnp.bfloat16).astype(jnp.float32) * scale
    low = iota((total, lanes_two), 1) < head_size
    for head in range(heads_here):
        if heads_here % 2 == 0:
            two = asked[:, head // 2 * lanes_two:(head // 2 + 1) * lanes_two]
            one = two if head % 2 == 0 else pltpu.roll(two, head_size, 1)
            query = jnp.where(low, one, bias)
        else:
            one = asked[:, head * head_size:(head + 1) * head_size]
            query = jnp.concatenate([one, bias[:, head_size:]], axis=1)
        query = query.astype(jnp.bfloat16)
        for step in range(steps):
            for group in range(groups):
                start = step * span + group * chunk
                asked_ref[head, pl.ds(group * own_rows + step * chunk, chunk), :] = query[start:start + chunk]


def front(cells, ids, me, key_mask, gain_col, w_qkv, w_out, gain_tile, w_query, heads, head_size, cols,
          heads_here, tiles_here, row_size, paired, after):
    groups = len(cells)
    width = cells[0].shape[2]
    own_rows = cells[0].shape[0] * cols
    total = groups * own_rows
    key_mask, gain_col, gain_tile = key_mask.T, gain_col.reshape(1, width), gain_tile.reshape(1, width)
    weights = [(3, width, width), (width, width), (width, heads_here * head_size), (groups,) + cells[0].shape]
    scratch = [pltpu.VMEM(shape, jnp.bfloat16) for shape in [(total, width), (3, total, width)] + weights]
    scratch += [pltpu.SMEM(ids.shape, jnp.int32), pltpu.VMEM(key_mask.shape, jnp.int32)]
    scratch += [pltpu.VMEM((1, width), jnp.float32)] * 2 + [pltpu.SemaphoreType.DMA((groups + 9,))]
    fetched = [pltpu.with_memory_space_constraint(value, pltpu.HBM)
               for value in (ids, key_mask, gain_col, gain_tile, w_qkv, w_out, w_query)]
    own = pltpu.with_memory_space_constraint(cells[0], pltpu.HBM)
    return pl.pallas_call(
        functools.partial(front_kernel, groups, heads, head_size, ROW_GROUP * cols, cols, heads_here, tiles_here, row_size, paired,
                          len(after)),
        out_shape=(jax.ShapeDtypeStruct((own_rows, width), jnp.float32),
                   jax.ShapeDtypeStruct((heads_here, total, 2 * head_size), jnp.bfloat16)),
        in_specs=[HBM] + [ANY] * (groups - 1) + [SMEM] + [HBM] * 7 + [ANY] * len(after),
        out_specs=(VMEM, VMEM),
        scratch_shapes=scratch,
        compiler_params=params(total),
        cost_estimate=pl.CostEstimate(flops=2 * total * width * 5 * width, bytes_accessed=4 * MIB,
                                      transcendentals=total * heads * 128),
        name="front",
    )(own, *cells[1:], me, *fetched, *after)


def weigh(query, tile_refs, head, slots):
    key_parts, val_parts = [], []
    for ref, slot in zip(tile_refs, slots):
        tiles = ref[:, head]
        count, keys, lanes = tiles.shape
        lane = iota(tiles.shape, 2)
        marks = (lane == iota(tiles.shape, 0) + (lanes // 2 + slot)).astype(tiles.dtype)
        key_parts.append(jnp.where(lane < lanes // 2, tiles, marks).reshape(count * keys, lanes))
        val_parts.append(jnp.where(lane < lanes // 2, jnp.ones_like(tiles), tiles).reshape(count * keys, lanes))
    scores = dot_lanes(query, jnp.concatenate(key_parts, axis=0))
    top = jnp.max(scores, axis=1, keepdims=True)
    return top, dot_rows(jnp.exp(scores - top).astype(jnp.bfloat16), jnp.concatenate(val_parts, axis=0))


def attention_cost(asked, tiles):
    heads, rows, lanes = asked.shape
    keys = sum(part.shape[0] * part.shape[2] for part in tiles)
    return pl.CostEstimate(flops=4 * rows * heads * keys * lanes, bytes_accessed=4 * MIB, transcendentals=rows * heads * keys)


def first_kernel(slots, block, asked_ref, *refs):
    tile_refs, (sums_ref, tops_ref) = refs[:len(slots)], refs[-2:]
    heads, rows_all, lanes = asked_ref.shape
    lane = iota((block, lanes), 1)
    for step in range(rows_all // block):
        rows = pl.ds(step * block, block)
        tops = jnp.zeros((block, lanes), jnp.float32)
        for head in range(heads):
            top, sums_ref[head, rows, :] = weigh(asked_ref[head, rows, :], tile_refs, head, slots)
            tops = jnp.where(lane == head, top, tops)
        tops_ref[rows, :] = tops


def first_tiles(asked, tiles, slots, own_rows, after):
    heads, rows, lanes = asked.shape
    return pl.pallas_call(
        functools.partial(first_kernel, slots, rows if rows <= 512 else own_rows),
        out_shape=(jax.ShapeDtypeStruct((heads, rows, lanes), jnp.float32), jax.ShapeDtypeStruct((rows, lanes), jnp.float32)),
        in_specs=[VMEM] * (1 + len(tiles)) + [ANY] * len(after),
        out_specs=(VMEM, VMEM),
        compiler_params=params(rows),
        cost_estimate=attention_cost(asked, tiles),
        name="first_tiles",
    )(asked, *tiles, *after)


def merge(asked_ref, sums_ref, tops_ref, tile_refs, slots, head, rows):
    top, sums = weigh(asked_ref[head, rows, :], tile_refs, head, slots)
    old_top = tops_ref[rows, head:head + 1]
    new_top = jnp.maximum(top, old_top)
    return new_top, sums_ref[head, rows, :] * jnp.exp(old_top - new_top) + sums * jnp.exp(top - new_top)


def more_kernel(slots, block, asked_ref, old_sums_ref, old_tops_ref, *refs):
    tile_refs, (sums_ref, tops_ref) = refs[:len(slots)], refs[len(slots):]
    heads, rows_all, lanes = asked_ref.shape
    lane = iota((block, lanes), 1)
    for step in range(rows_all // block):
        rows = pl.ds(step * block, block)
        tops = jnp.zeros((block, lanes), jnp.float32)
        for head in range(heads):
            top, sums_ref[head, rows, :] = merge(asked_ref, old_sums_ref, old_tops_ref, tile_refs, slots, head, rows)
            tops = jnp.where(lane == head, top, tops)
        tops_ref[rows, :] = tops


def more_tiles(asked, sums, tops, tiles, slots, own_rows):
    rows = asked.shape[1]
    return pl.pallas_call(
        functools.partial(more_kernel, slots, rows if rows <= 512 else own_rows),
        out_shape=(jax.ShapeDtypeStruct(sums.shape, jnp.float32), jax.ShapeDtypeStruct(tops.shape, jnp.float32)),
        in_specs=[VMEM] * (3 + len(tiles)),
        out_specs=(VMEM, VMEM),
        compiler_params=params(rows),
        cost_estimate=attention_cost(asked, tiles),
        name="more_tiles",
    )(asked, sums, tops, *tiles)


def last_kernel(slots, groups, asked_ref, sums_ref, tops_ref, *refs):
    tile_refs, out_refs = refs[:len(slots)], refs[-len(groups):]
    heads, lanes = asked_ref.shape[0], asked_ref.shape[2]
    block = out_refs[0].shape[0]
    half = lanes // 2
    lane_low = iota((block, lanes), 1) < half
    for group, out_ref in zip(groups, out_refs):
        rows = pl.ds(group * block, block)
        low = None
        for head in range(heads):
            _, sums = merge(asked_ref, sums_ref, tops_ref, tile_refs, slots, head, rows)
            turned = pltpu.roll(sums, half, 1)
            if head % 2:
                out_ref[:, pl.ds(head // 2 * lanes, lanes)] = jnp.where(lane_low, low, sums / turned).astype(jnp.bfloat16)
            elif head + 1 < heads:
                low = turned / sums
            else:
                out_ref[:, pl.ds(head * half, half)] = (turned / sums)[:, :half].astype(jnp.bfloat16)


def last_tiles(asked, sums, tops, tiles, slots, groups, own_rows, after):
    heads, rows, lanes = asked.shape
    out = jax.ShapeDtypeStruct((own_rows, heads * lanes // 2), jnp.bfloat16)
    return pl.pallas_call(
        functools.partial(last_kernel, slots, groups),
        out_shape=(out,) * len(groups),
        in_specs=[VMEM] * (3 + len(tiles)) + [ANY] * len(after),
        out_specs=(VMEM,) * len(groups),
        compiler_params=params(rows),
        cost_estimate=attention_cost(asked[:, :own_rows * len(groups)], tiles),
        name="last_tiles",
    )(asked, sums, tops, *tiles, *after)


def own_kernel(me_ref, weight_ref, resid_ref, answer_ref, partial_ref, *part_refs):
    groups, group_width = len(part_refs) + 1, answer_ref.shape[1]

    def rows(step):
        group = lax.rem(me_ref[1] - step + groups, groups)
        return weight_ref[pl.ds(pl.multiple_of(group * group_width, group_width), group_width), :]

    partial_ref[...] = resid_ref[...] + dot_rows(answer_ref[...], rows(0))
    for step, part_ref in enumerate(part_refs):
        part_ref[...] = rows(step + 1)


def own_part(me, weight, residual, answer, groups):
    part = jax.ShapeDtypeStruct((answer.shape[1], weight.shape[1]), weight.dtype)
    return pl.pallas_call(
        own_kernel,
        out_shape=(jax.ShapeDtypeStruct(residual.shape, jnp.float32),) + (part,) * (groups - 1),
        in_specs=[SMEM, VMEM, VMEM, VMEM],
        out_specs=(VMEM,) * groups,
        compiler_params=params(0),
        cost_estimate=pl.CostEstimate(flops=2 * residual.size * answer.shape[1], bytes_accessed=MIB, transcendentals=0),
        name="own_part",
    )(me, weight, residual, answer)


def turn(size, step):
    return [(src, (src + step) % size) for src in range(size)]


def shards(row_size, col_size, fact_cells, gain_col, w_qkv, w_col_out, gain_tile, w_query, w_tile_out,
           tile_kv, tile_ids, key_mask):
    rows, cols, width = fact_cells.shape
    tiles_here, keys, heads_here, lanes = tile_kv.shape
    head_size = lanes // 2
    heads_all = width // head_size
    group_width = heads_here * head_size
    half = row_size // 2
    row_me, col_me = lax.axis_index("rows"), lax.axis_index("cols")
    me = jnp.stack([row_me, col_me]).astype(jnp.int32)
    halves = [list(range(half)), list(range(half, row_size))]
    paired = half <= 8 and half & (half - 1) == 0
    assert row_size <= head_size and row_size % 2 == 0

    def swap(value):
        return lax.all_to_all(value, "rows", split_axis=0, concat_axis=0, tiled=True, axis_index_groups=halves)

    asked_of = request(tile_ids, me, tiles_here, row_size)
    asked_by = swap(asked_of)
    heads_first = jnp.transpose(tile_kv, (0, 2, 1, 3))
    mirrored = lax.ppermute(heads_first, "rows", turn(row_size, half))

    cells = [fact_cells]
    for step in range(1, col_size):
        cells.append(lax.ppermute(fact_cells, "cols", turn(col_size, -step)))

    across = half // 2
    near_order = [0, 1] + sorted(range(2, half), key=lambda step: (step != 2, not step & across, step & 1, step))
    rest = sorted(set(range(2, half)) - {across}, key=lambda step: (step != 2, not step & across, step & 1, -step))
    far_order = list(dict.fromkeys([0, across] + rest + [1]))
    near_slots, far_slots = (near_order, [half + step for step in far_order]) if paired else ([0], [half])

    def spread(tiles, which, order, after):
        if not order:
            return []
        if not paired:
            return [swap(pick(tiles, asked_by, which, after))]
        picked = pick_each(tiles, asked_by, which, me, order, after)
        return [tile if step == 0 else lax.ppermute(tile, "rows", [(row, row ^ step) for row in range(row_size)])
                for step, tile in zip(order, picked)]

    if group_width % 128:
        w_query = lax.dynamic_slice_in_dim(w_query, col_me * group_width, group_width, 1)
    residual, asked = front(cells, tile_ids, me, key_mask, gain_col, w_qkv, w_col_out, gain_tile, w_query,
                            heads_all, head_size, cols, heads_here, tiles_here, row_size, paired, [])
    near = spread(heads_first, 0, near_order, [asked])
    far = spread(mirrored, 1, far_order[:-1] if paired else far_order, near[1:3])
    sums, tops = first_tiles(asked, near, near_slots, rows * cols, far[1:2])
    far += spread(mirrored, 1, far_order[-1:] if paired else [], [tops])
    batch = (len(far) + 2) // 2 if paired else 0
    if batch:
        sums, tops = more_tiles(asked, sums, tops, far[:batch], far_slots[:batch], rows * cols)
    far, far_slots = far[batch:], far_slots[batch:]
    others = last_tiles(asked, sums, tops, far, far_slots, list(range(1, col_size)), rows * cols, [])
    own = last_tiles(asked, sums, tops, far, far_slots, [0], rows * cols, others[:1])
    final, *weights = own_part(me, w_tile_out, residual, own[0], col_size)
    for step, (other, weight) in enumerate(zip(others, weights)):
        final = final + dot_rows(lax.ppermute(other, "cols", turn(col_size, step + 1)), weight)
    return final.astype(jnp.bfloat16).reshape(rows, cols, width)


def solution(mesh):
    row_size, col_size = mesh.shape["rows"], mesh.shape["cols"]
    placed = (P("rows", "cols", None), P(), P(), P(), P(), P(), P(), P("rows", None, "cols", None),
              P("rows", None), P("rows", None))

    def body(*arrays):
        return shards(row_size, col_size, *arrays)

    return jax.shard_map(body, mesh=mesh, in_specs=placed, out_specs=P("rows", "cols", None), check_vma=False)
```

```python
import functools

import jax
import jax.numpy as jnp
from jax import lax
from jax.experimental import pallas as pl
from jax.experimental.pallas import tpu as pltpu
from jax.sharding import PartitionSpec as P

ROW_GROUP = 16
BIG = -1e30
MIB = 1024 * 1024
VMEM = pl.BlockSpec(memory_space=pltpu.VMEM)
SMEM = pl.BlockSpec(memory_space=pltpu.SMEM)
HBM = pl.BlockSpec(memory_space=pltpu.HBM)
ANY = pl.BlockSpec(memory_space=pl.ANY)


def params(rows):
    return pltpu.CompilerParams(vmem_limit_bytes=(20 if rows <= 512 else 48) * MIB)


def dot_rows(left, right):
    return lax.dot_general(left, right, (((1,), (0,)), ((), ())), preferred_element_type=jnp.float32)


def dot_lanes(left, right):
    return lax.dot_general(left, right, (((1,), (1,)), ((), ())), preferred_element_type=jnp.float32)


def rms_scale(values, gain_vec):
    mean_sq = jnp.mean(values * values, axis=-1, keepdims=True)
    return values * lax.rsqrt(mean_sq + 1e-05) * gain_vec


def iota(shape, dim):
    return lax.broadcasted_iota(jnp.int32, shape, dim)


def slot_of(owner, row_me, row_size, paired):
    half = row_size // 2
    return owner ^ row_me if paired else lax.rem(owner + lax.div(row_me, half) * half, row_size)


def request_kernel(tiles_here, row_size, ids_ref, me_ref, out_ref):
    half = row_size // 2
    peer, which = iota(out_ref.shape, 0), iota(out_ref.shape, 1)
    wanted = jnp.zeros(out_ref.shape, jnp.int32)
    for slot in range(ids_ref.shape[1]):
        tile = ids_ref[0, slot]
        owner = lax.div(tile, tiles_here)
        far = jnp.where(lax.div(owner, half) == lax.div(me_ref[0], half), 0, 1)
        here = (peer == jnp.where(tile < 0, -1, lax.rem(owner, half))) & (which == far)
        wanted = jnp.where(here, lax.rem(tile, tiles_here), wanted)
    out_ref[...] = wanted


def request(ids, me, tiles_here, row_size):
    return pl.pallas_call(
        functools.partial(request_kernel, tiles_here, row_size),
        out_shape=jax.ShapeDtypeStruct((row_size // 2, 2, 128), jnp.int32),
        in_specs=[SMEM, SMEM],
        out_specs=VMEM,
        compiler_params=params(0),
        cost_estimate=pl.CostEstimate(flops=0, bytes_accessed=MIB // 4, transcendentals=0),
        name="request",
    )(ids, me)


def pick_kernel(which, wanted_ref, tiles_ref, *refs):
    out_ref = refs[-1]
    for peer in range(out_ref.shape[0]):
        out_ref[peer] = tiles_ref[wanted_ref[peer, which, 0]]


def pick(tiles, wanted, which, after):
    return pl.pallas_call(
        functools.partial(pick_kernel, which),
        out_shape=jax.ShapeDtypeStruct(wanted.shape[:1] + tiles.shape[1:], tiles.dtype),
        in_specs=[SMEM, VMEM] + [ANY] * len(after),
        out_specs=VMEM,
        compiler_params=params(0),
        cost_estimate=pl.CostEstimate(flops=0, bytes_accessed=2 * MIB, transcendentals=0),
        name="pick",
    )(wanted, tiles, *after)


def pick_each_kernel(which, order, wanted_ref, me_ref, tiles_ref, *refs):
    place = lax.rem(me_ref[0], wanted_ref.shape[0])
    for step, out_ref in zip(order, refs[-len(order):]):
        out_ref[0] = tiles_ref[wanted_ref[place ^ step, which, 0]]


def pick_each(tiles, wanted, which, me, order, after):
    count = len(order)
    return pl.pallas_call(
        functools.partial(pick_each_kernel, which, order),
        out_shape=(jax.ShapeDtypeStruct((1,) + tiles.shape[1:], tiles.dtype),) * count,
        in_specs=[SMEM, SMEM, VMEM] + [ANY] * len(after),
        out_specs=(VMEM,) * count,
        compiler_params=params(0),
        cost_estimate=pl.CostEstimate(flops=0, bytes_accessed=2 * MIB, transcendentals=0),
        name="pick_each",
    )(wanted, me, tiles, *after)


def front_kernel(groups, heads, head_size, chunk, cols, heads_here, tiles_here, row_size, paired, waited, *refs):
    cell_hbms, refs = refs[:groups], refs[groups:]
    (me_ref, ids_hbm, mask_hbm, gain_col_hbm, gain_tile_hbm, w_qkv_hbm, w_out_hbm, w_query_hbm) = refs[:8]
    (resid_ref, asked_ref, normed_ref, packed_ref, w_qkv_ref, w_out_ref, w_query_ref, cell_refs,
     ids_ref, mask_ref, gain_col_ref, gain_tile_ref, sems) = refs[8 + waited:]
    own_rows, width = resid_ref.shape
    steps = own_rows // chunk
    span = groups * chunk
    lanes_two = 2 * head_size
    group_width = heads_here * head_size
    if w_query_hbm.shape[1] != group_width:
        w_query_hbm = w_query_hbm.at[:, pl.ds(pl.multiple_of(me_ref[1] * group_width, group_width), group_width)]
    pairs = [(hbm, cell_refs.at[group]) for group, hbm in enumerate(cell_hbms)]
    pairs += [(gain_col_hbm, gain_col_ref)]
    pairs += [(w_qkv_hbm.at[:, pl.ds(part * width, width)], w_qkv_ref.at[part]) for part in range(3)]
    pairs += [(w_out_hbm, w_out_ref), (gain_tile_hbm, gain_tile_ref), (w_query_hbm, w_query_ref), (ids_hbm, ids_ref), (mask_hbm, mask_ref)]
    copies = [pltpu.make_async_copy(*pair, sems.at[index]) for index, pair in enumerate(pairs)]
    for copy in copies:
        copy.start()
    for copy in copies[:groups + 1]:
        copy.wait()
    copies = copies[groups + 1:]

    def cells_of(group, step):
        cells = cell_refs[group, pl.ds(step * (chunk // cols), chunk // cols)].astype(jnp.float32)
        return cells.reshape(chunk, width)

    for step in range(steps):
        for group in range(groups):
            cells = cells_of(group, step)
            normed_ref[pl.ds(step * span + group * chunk, chunk), :] = rms_scale(cells, gain_col_ref[...]).astype(jnp.bfloat16)
    for part in range(3):
        copies[part].wait()
        packed_ref[part] = dot_rows(normed_ref[...], w_qkv_ref[part]).astype(jnp.bfloat16)
    stacked = heads * span
    same_row = iota((stacked, span), 0) % chunk // cols == iota((stacked, span), 1) % chunk // cols
    lane_low = iota((span, lanes_two), 1) < head_size
    scale = head_size ** (-0.5)
    for step in range(steps):
        rows = pl.ds(step * span, span)
        scores = []
        for head in range(heads):
            lanes = pl.ds(head // 2 * lanes_two, lanes_two)
            query = packed_ref[0, rows, lanes]
            query = jnp.where(lane_low == (head % 2 == 0), query, jnp.zeros_like(query))
            scores.append(dot_lanes(query, packed_ref[1, rows, lanes]))
        scores = jnp.where(same_row, jnp.concatenate(scores, axis=0) * scale, BIG)
        expo = jnp.exp(scores - jnp.max(scores, axis=1, keepdims=True))
        weights = (expo / jnp.sum(expo, axis=1, keepdims=True)).astype(jnp.bfloat16)
        for pair in range(heads // 2):
            lanes = pl.ds(pair * lanes_two, lanes_two)
            start = 2 * pair * span
            mixed = dot_rows(weights[start:start + 2 * span], packed_ref[2, rows, lanes])
            normed_ref[rows, lanes] = jnp.where(lane_low, mixed[:span], mixed[span:]).astype(jnp.bfloat16)
    for copy in copies[3:]:
        copy.wait()
    delta = dot_rows(normed_ref[...], w_out_ref[...])
    for step in range(steps):
        for group in range(groups):
            start = step * span + group * chunk
            resid = cells_of(group, step) + delta[start:start + chunk]
            if group == 0:
                resid_ref[pl.ds(step * chunk, chunk), :] = resid
            normed_ref[pl.ds(start, chunk), :] = rms_scale(resid, gain_tile_ref[...]).astype(jnp.bfloat16)
    slots = mask_ref.shape[0]
    slot, lane = iota((slots, lanes_two), 0), iota((slots, lanes_two), 1)
    place = jnp.zeros((slots, lanes_two), jnp.float32)
    for index in range(slots):
        tile = ids_ref[0, index]
        spot = jnp.where(tile < 0, -1, head_size + slot_of(lax.div(tile, tiles_here), me_ref[0], row_size, paired))
        place = jnp.where((slot == index) & (lane == spot), 1.0, place)
    live = lax.dot_general((mask_ref[...] > 0).astype(jnp.float32).astype(jnp.bfloat16), place.astype(jnp.bfloat16),
                           (((0,), (0,)), ((), ())), preferred_element_type=jnp.float32)
    lane = iota(live.shape, 1)
    shut = jnp.where((lane >= head_size) & (lane < head_size + row_size) & (live < 0.5), 1.0, 0.0).astype(jnp.bfloat16)
    total = steps * span
    cell = iota((total, shut.shape[0]), 0)
    row_of = cell // span * (chunk // cols) + cell % chunk // cols
    spread = (row_of == iota((total, shut.shape[0]), 1)).astype(jnp.bfloat16)
    bias = dot_rows(spread, shut) * BIG
    asked = dot_rows(normed_ref[...], w_query_ref[...]).astype(jnp.bfloat16).astype(jnp.float32) * scale
    low = iota((total, lanes_two), 1) < head_size
    for head in range(heads_here):
        if heads_here % 2 == 0:
            two = asked[:, head // 2 * lanes_two:(head // 2 + 1) * lanes_two]
            one = two if head % 2 == 0 else pltpu.roll(two, head_size, 1)
            query = jnp.where(low, one, bias)
        else:
            one = asked[:, head * head_size:(head + 1) * head_size]
            query = jnp.concatenate([one, bias[:, head_size:]], axis=1)
        query = query.astype(jnp.bfloat16)
        for step in range(steps):
            for group in range(groups):
                start = step * span + group * chunk
                asked_ref[head, pl.ds(group * own_rows + step * chunk, chunk), :] = query[start:start + chunk]


def front(cells, ids, me, key_mask, gain_col, w_qkv, w_out, gain_tile, w_query, heads, head_size, cols,
          heads_here, tiles_here, row_size, paired, after):
    groups = len(cells)
    width = cells[0].shape[2]
    own_rows = cells[0].shape[0] * cols
    total = groups * own_rows
    key_mask, gain_col, gain_tile = key_mask.T, gain_col.reshape(1, width), gain_tile.reshape(1, width)
    weights = [(3, width, width), (width, width), (width, heads_here * head_size), (groups,) + cells[0].shape]
    scratch = [pltpu.VMEM(shape, jnp.bfloat16) for shape in [(total, width), (3, total, width)] + weights]
    scratch += [pltpu.SMEM(ids.shape, jnp.int32), pltpu.VMEM(key_mask.shape, jnp.int32)]
    scratch += [pltpu.VMEM((1, width), jnp.float32)] * 2 + [pltpu.SemaphoreType.DMA((groups + 9,))]
    fetched = [pltpu.with_memory_space_constraint(value, pltpu.HBM)
               for value in (ids, key_mask, gain_col, gain_tile, w_qkv, w_out, w_query)]
    own = pltpu.with_memory_space_constraint(cells[0], pltpu.HBM)
    return pl.pallas_call(
        functools.partial(front_kernel, groups, heads, head_size, ROW_GROUP * cols, cols, heads_here, tiles_here, row_size, paired,
                          len(after)),
        out_shape=(jax.ShapeDtypeStruct((own_rows, width), jnp.float32),
                   jax.ShapeDtypeStruct((heads_here, total, 2 * head_size), jnp.bfloat16)),
        in_specs=[HBM] + [ANY] * (groups - 1) + [SMEM] + [HBM] * 7 + [ANY] * len(after),
        out_specs=(VMEM, VMEM),
        scratch_shapes=scratch,
        compiler_params=params(total),
        cost_estimate=pl.CostEstimate(flops=2 * total * width * 5 * width, bytes_accessed=4 * MIB,
                                      transcendentals=total * heads * 128),
        name="front",
    )(own, *cells[1:], me, *fetched, *after)


def weigh(query, tile_refs, head, slots):
    key_parts, val_parts = [], []
    for ref, slot in zip(tile_refs, slots):
        tiles = ref[:, head]
        count, keys, lanes = tiles.shape
        lane = iota(tiles.shape, 2)
        marks = (lane == iota(tiles.shape, 0) + (lanes // 2 + slot)).astype(tiles.dtype)
        key_parts.append(jnp.where(lane < lanes // 2, tiles, marks).reshape(count * keys, lanes))
        val_parts.append(jnp.where(lane < lanes // 2, jnp.ones_like(tiles), tiles).reshape(count * keys, lanes))
    scores = dot_lanes(query, jnp.concatenate(key_parts, axis=0))
    top = jnp.max(scores, axis=1, keepdims=True)
    return top, dot_rows(jnp.exp(scores - top).astype(jnp.bfloat16), jnp.concatenate(val_parts, axis=0))


def attention_cost(asked, tiles):
    heads, rows, lanes = asked.shape
    keys = sum(part.shape[0] * part.shape[2] for part in tiles)
    return pl.CostEstimate(flops=4 * rows * heads * keys * lanes, bytes_accessed=4 * MIB, transcendentals=rows * heads * keys)


def first_kernel(slots, block, asked_ref, *refs):
    tile_refs, (sums_ref, tops_ref) = refs[:len(slots)], refs[-2:]
    heads, rows_all, lanes = asked_ref.shape
    lane = iota((block, lanes), 1)
    for step in range(rows_all // block):
        rows = pl.ds(step * block, block)
        tops = jnp.zeros((block, lanes), jnp.float32)
        for head in range(heads):
            top, sums_ref[head, rows, :] = weigh(asked_ref[head, rows, :], tile_refs, head, slots)
            tops = jnp.where(lane == head, top, tops)
        tops_ref[rows, :] = tops


def first_tiles(asked, tiles, slots, own_rows, after):
    heads, rows, lanes = asked.shape
    return pl.pallas_call(
        functools.partial(first_kernel, slots, rows if rows <= 512 else own_rows),
        out_shape=(jax.ShapeDtypeStruct((heads, rows, lanes), jnp.float32), jax.ShapeDtypeStruct((rows, lanes), jnp.float32)),
        in_specs=[VMEM] * (1 + len(tiles)) + [ANY] * len(after),
        out_specs=(VMEM, VMEM),
        compiler_params=params(rows),
        cost_estimate=attention_cost(asked, tiles),
        name="first_tiles",
    )(asked, *tiles, *after)


def merge(asked_ref, sums_ref, tops_ref, tile_refs, slots, head, rows):
    top, sums = weigh(asked_ref[head, rows, :], tile_refs, head, slots)
    old_top = tops_ref[rows, head:head + 1]
    new_top = jnp.maximum(top, old_top)
    return new_top, sums_ref[head, rows, :] * jnp.exp(old_top - new_top) + sums * jnp.exp(top - new_top)


def more_kernel(slots, block, asked_ref, old_sums_ref, old_tops_ref, *refs):
    tile_refs, (sums_ref, tops_ref) = refs[:len(slots)], refs[len(slots):]
    heads, rows_all, lanes = asked_ref.shape
    lane = iota((block, lanes), 1)
    for step in range(rows_all // block):
        rows = pl.ds(step * block, block)
        tops = jnp.zeros((block, lanes), jnp.float32)
        for head in range(heads):
            top, sums_ref[head, rows, :] = merge(asked_ref, old_sums_ref, old_tops_ref, tile_refs, slots, head, rows)
            tops = jnp.where(lane == head, top, tops)
        tops_ref[rows, :] = tops


def more_tiles(asked, sums, tops, tiles, slots, own_rows):
    rows = asked.shape[1]
    return pl.pallas_call(
        functools.partial(more_kernel, slots, rows if rows <= 512 else own_rows),
        out_shape=(jax.ShapeDtypeStruct(sums.shape, jnp.float32), jax.ShapeDtypeStruct(tops.shape, jnp.float32)),
        in_specs=[VMEM] * (3 + len(tiles)),
        out_specs=(VMEM, VMEM),
        compiler_params=params(rows),
        cost_estimate=attention_cost(asked, tiles),
        name="more_tiles",
    )(asked, sums, tops, *tiles)


def last_kernel(slots, groups, asked_ref, sums_ref, tops_ref, *refs):
    tile_refs, out_refs = refs[:len(slots)], refs[-len(groups):]
    heads, lanes = asked_ref.shape[0], asked_ref.shape[2]
    block = out_refs[0].shape[0]
    half = lanes // 2
    lane_low = iota((block, lanes), 1) < half
    for group, out_ref in zip(groups, out_refs):
        rows = pl.ds(group * block, block)
        low = None
        for head in range(heads):
            _, sums = merge(asked_ref, sums_ref, tops_ref, tile_refs, slots, head, rows)
            turned = pltpu.roll(sums, half, 1)
            if head % 2:
                out_ref[:, pl.ds(head // 2 * lanes, lanes)] = jnp.where(lane_low, low, sums / turned).astype(jnp.bfloat16)
            elif head + 1 < heads:
                low = turned / sums
            else:
                out_ref[:, pl.ds(head * half, half)] = (turned / sums)[:, :half].astype(jnp.bfloat16)


def last_tiles(asked, sums, tops, tiles, slots, groups, own_rows, after):
    heads, rows, lanes = asked.shape
    out = jax.ShapeDtypeStruct((own_rows, heads * lanes // 2), jnp.bfloat16)
    return pl.pallas_call(
        functools.partial(last_kernel, slots, groups),
        out_shape=(out,) * len(groups),
        in_specs=[VMEM] * (3 + len(tiles)) + [ANY] * len(after),
        out_specs=(VMEM,) * len(groups),
        compiler_params=params(rows),
        cost_estimate=attention_cost(asked[:, :own_rows * len(groups)], tiles),
        name="last_tiles",
    )(asked, sums, tops, *tiles, *after)


def own_kernel(me_ref, weight_ref, resid_ref, answer_ref, partial_ref, *part_refs):
    groups, group_width = len(part_refs) + 1, answer_ref.shape[1]

    def rows(step):
        group = lax.rem(me_ref[1] - step + groups, groups)
        return weight_ref[pl.ds(pl.multiple_of(group * group_width, group_width), group_width), :]

    partial_ref[...] = resid_ref[...] + dot_rows(answer_ref[...], rows(0))
    for step, part_ref in enumerate(part_refs):
        part_ref[...] = rows(step + 1)


def own_part(me, weight, residual, answer, groups):
    part = jax.ShapeDtypeStruct((answer.shape[1], weight.shape[1]), weight.dtype)
    return pl.pallas_call(
        own_kernel,
        out_shape=(jax.ShapeDtypeStruct(residual.shape, jnp.float32),) + (part,) * (groups - 1),
        in_specs=[SMEM, VMEM, VMEM, VMEM],
        out_specs=(VMEM,) * groups,
        compiler_params=params(0),
        cost_estimate=pl.CostEstimate(flops=2 * residual.size * answer.shape[1], bytes_accessed=MIB, transcendentals=0),
        name="own_part",
    )(me, weight, residual, answer)


def turn(size, step):
    return [(src, (src + step) % size) for src in range(size)]


def shards(row_size, col_size, fact_cells, gain_col, w_qkv, w_col_out, gain_tile, w_query, w_tile_out,
           tile_kv, tile_ids, key_mask):
    rows, cols, width = fact_cells.shape
    tiles_here, keys, heads_here, lanes = tile_kv.shape
    head_size = lanes // 2
    heads_all = width // head_size
    group_width = heads_here * head_size
    half = row_size // 2
    row_me, col_me = lax.axis_index("rows"), lax.axis_index("cols")
    me = jnp.stack([row_me, col_me]).astype(jnp.int32)
    halves = [list(range(half)), list(range(half, row_size))]
    paired = half <= 8 and half & (half - 1) == 0
    assert row_size <= head_size and row_size % 2 == 0

    def swap(value):
        return lax.all_to_all(value, "rows", split_axis=0, concat_axis=0, tiled=True, axis_index_groups=halves)

    asked_of = request(tile_ids, me, tiles_here, row_size)
    asked_by = swap(asked_of)
    heads_first = jnp.transpose(tile_kv, (0, 2, 1, 3))
    mirrored = lax.ppermute(heads_first, "rows", turn(row_size, half))

    cells = [fact_cells]
    for step in range(1, col_size):
        cells.append(lax.ppermute(fact_cells, "cols", turn(col_size, -step)))

    across = half // 2

    def turns(step):
        return bool(step & across) and bool(step & (across - 1) & ~1)

    near_order = [0, 1] + sorted(range(2, half), key=lambda step: (turns(step), step != 2, not step & across, step))
    far_order = [0] + sorted(range(2, half), key=lambda step: (turns(step), step & 1, not step & across, step)) + [1]
    near_slots, far_slots = (near_order, [half + step for step in far_order]) if paired else ([0], [half])

    def spread(tiles, which, order, after):
        if not order:
            return []
        if not paired:
            return [swap(pick(tiles, asked_by, which, after))]
        picked = pick_each(tiles, asked_by, which, me, order, after)
        return [tile if step == 0 else lax.ppermute(tile, "rows", [(row, row ^ step) for row in range(row_size)])
                for step, tile in zip(order, picked)]

    if group_width % 128:
        w_query = lax.dynamic_slice_in_dim(w_query, col_me * group_width, group_width, 1)
    residual, asked = front(cells, tile_ids, me, key_mask, gain_col, w_qkv, w_col_out, gain_tile, w_query,
                            heads_all, head_size, cols, heads_here, tiles_here, row_size, paired, [])
    near = spread(heads_first, 0, near_order, [asked])
    far = spread(mirrored, 1, far_order[:-1] if paired else far_order, near[1:3])
    sums, tops = first_tiles(asked, near, near_slots, rows * cols, far[1:2])
    far += spread(mirrored, 1, far_order[-1:] if paired else [], [tops])
    batch = len(far) // 2
    if batch:
        sums, tops = more_tiles(asked, sums, tops, far[:batch], far_slots[:batch], rows * cols)
    far, far_slots = far[batch:], far_slots[batch:]
    others = last_tiles(asked, sums, tops, far, far_slots, list(range(1, col_size)), rows * cols, [])
    own = last_tiles(asked, sums, tops, far, far_slots, [0], rows * cols, others[:1])
    final, *weights = own_part(me, w_tile_out, residual, own[0], col_size)
    for step, (other, weight) in enumerate(zip(others, weights)):
        final = final + dot_rows(lax.ppermute(other, "cols", turn(col_size, step + 1)), weight)
    return final.astype(jnp.bfloat16).reshape(rows, cols, width)


def solution(mesh):
    row_size, col_size = mesh.shape["rows"], mesh.shape["cols"]
    placed = (P("rows", "cols", None), P(), P(), P(), P(), P(), P(), P("rows", None, "cols", None),
              P("rows", None), P("rows", None))

    def body(*arrays):
        return shards(row_size, col_size, *arrays)

    return jax.shard_map(body, mesh=mesh, in_specs=placed, out_specs=P("rows", "cols", None), check_vma=False)
```

```python
import functools

import jax
import jax.numpy as jnp
from jax import lax
from jax.experimental import pallas as pl
from jax.experimental.pallas import tpu as pltpu
from jax.sharding import PartitionSpec as P

ROW_GROUP = 16
BIG = -1e30
MIB = 1024 * 1024
VMEM = pl.BlockSpec(memory_space=pltpu.VMEM)
SMEM = pl.BlockSpec(memory_space=pltpu.SMEM)
HBM = pl.BlockSpec(memory_space=pltpu.HBM)
ANY = pl.BlockSpec(memory_space=pl.ANY)


def params(rows):
    return pltpu.CompilerParams(vmem_limit_bytes=(20 if rows <= 512 else 48) * MIB)


def dot_rows(left, right):
    return lax.dot_general(left, right, (((1,), (0,)), ((), ())), preferred_element_type=jnp.float32)


def dot_lanes(left, right):
    return lax.dot_general(left, right, (((1,), (1,)), ((), ())), preferred_element_type=jnp.float32)


def rms_scale(values, gain_vec):
    mean_sq = jnp.mean(values * values, axis=-1, keepdims=True)
    return values * lax.rsqrt(mean_sq + 1e-05) * gain_vec


def iota(shape, dim):
    return lax.broadcasted_iota(jnp.int32, shape, dim)


def slot_of(owner, row_me, row_size, paired):
    half = row_size // 2
    return owner ^ row_me if paired else lax.rem(owner + lax.div(row_me, half) * half, row_size)


def request_kernel(tiles_here, row_size, ids_ref, me_ref, out_ref):
    half = row_size // 2
    peer, which = iota(out_ref.shape, 0), iota(out_ref.shape, 1)
    wanted = jnp.zeros(out_ref.shape, jnp.int32)
    for slot in range(ids_ref.shape[1]):
        tile = ids_ref[0, slot]
        owner = lax.div(tile, tiles_here)
        far = jnp.where(lax.div(owner, half) == lax.div(me_ref[0], half), 0, 1)
        here = (peer == jnp.where(tile < 0, -1, lax.rem(owner, half))) & (which == far)
        wanted = jnp.where(here, lax.rem(tile, tiles_here), wanted)
    out_ref[...] = wanted


def request(ids, me, tiles_here, row_size):
    return pl.pallas_call(
        functools.partial(request_kernel, tiles_here, row_size),
        out_shape=jax.ShapeDtypeStruct((row_size // 2, 2, 128), jnp.int32),
        in_specs=[SMEM, SMEM],
        out_specs=VMEM,
        compiler_params=params(0),
        cost_estimate=pl.CostEstimate(flops=0, bytes_accessed=MIB // 4, transcendentals=0),
        name="request",
    )(ids, me)


def pick_kernel(which, wanted_ref, tiles_ref, *refs):
    out_ref = refs[-1]
    for peer in range(out_ref.shape[0]):
        out_ref[peer] = tiles_ref[wanted_ref[peer, which, 0]]


def pick(tiles, wanted, which, after):
    return pl.pallas_call(
        functools.partial(pick_kernel, which),
        out_shape=jax.ShapeDtypeStruct(wanted.shape[:1] + tiles.shape[1:], tiles.dtype),
        in_specs=[SMEM, VMEM] + [ANY] * len(after),
        out_specs=VMEM,
        compiler_params=params(0),
        cost_estimate=pl.CostEstimate(flops=0, bytes_accessed=2 * MIB, transcendentals=0),
        name="pick",
    )(wanted, tiles, *after)


def pick_each_kernel(which, order, wanted_ref, me_ref, tiles_ref, *refs):
    place = lax.rem(me_ref[0], wanted_ref.shape[0])
    for step, out_ref in zip(order, refs[-len(order):]):
        out_ref[0] = tiles_ref[wanted_ref[place ^ step, which, 0]]


def pick_each(tiles, wanted, which, me, order, after):
    count = len(order)
    return pl.pallas_call(
        functools.partial(pick_each_kernel, which, order),
        out_shape=(jax.ShapeDtypeStruct((1,) + tiles.shape[1:], tiles.dtype),) * count,
        in_specs=[SMEM, SMEM, VMEM] + [ANY] * len(after),
        out_specs=(VMEM,) * count,
        compiler_params=params(0),
        cost_estimate=pl.CostEstimate(flops=0, bytes_accessed=2 * MIB, transcendentals=0),
        name="pick_each",
    )(wanted, me, tiles, *after)


def front_kernel(groups, heads, head_size, chunk, cols, heads_here, tiles_here, row_size, paired, waited, *refs):
    cell_hbms, refs = refs[:groups], refs[groups:]
    (me_ref, ids_hbm, mask_hbm, gain_col_hbm, gain_tile_hbm, w_qkv_hbm, w_out_hbm, w_query_hbm) = refs[:8]
    (resid_ref, asked_ref, normed_ref, packed_ref, w_qkv_ref, w_out_ref, w_query_ref, cell_refs,
     ids_ref, mask_ref, gain_col_ref, gain_tile_ref, sems) = refs[8 + waited:]
    own_rows, width = resid_ref.shape
    steps = own_rows // chunk
    span = groups * chunk
    lanes_two = 2 * head_size
    group_width = heads_here * head_size
    if w_query_hbm.shape[1] != group_width:
        w_query_hbm = w_query_hbm.at[:, pl.ds(pl.multiple_of(me_ref[1] * group_width, group_width), group_width)]
    pairs = [(hbm, cell_refs.at[group]) for group, hbm in enumerate(cell_hbms)]
    pairs += [(gain_col_hbm, gain_col_ref)]
    pairs += [(w_qkv_hbm.at[:, pl.ds(part * width, width)], w_qkv_ref.at[part]) for part in range(3)]
    pairs += [(w_out_hbm, w_out_ref), (gain_tile_hbm, gain_tile_ref), (w_query_hbm, w_query_ref), (ids_hbm, ids_ref), (mask_hbm, mask_ref)]
    copies = [pltpu.make_async_copy(*pair, sems.at[index]) for index, pair in enumerate(pairs)]
    for copy in copies:
        copy.start()
    for copy in copies[:groups + 1]:
        copy.wait()
    copies = copies[groups + 1:]

    def cells_of(group, step):
        cells = cell_refs[group, pl.ds(step * (chunk // cols), chunk // cols)].astype(jnp.float32)
        return cells.reshape(chunk, width)

    for step in range(steps):
        for group in range(groups):
            cells = cells_of(group, step)
            normed_ref[pl.ds(step * span + group * chunk, chunk), :] = rms_scale(cells, gain_col_ref[...]).astype(jnp.bfloat16)
    for part in range(3):
        copies[part].wait()
        packed_ref[part] = dot_rows(normed_ref[...], w_qkv_ref[part]).astype(jnp.bfloat16)
    stacked = heads * span
    same_row = iota((stacked, span), 0) % chunk // cols == iota((stacked, span), 1) % chunk // cols
    lane_low = iota((span, lanes_two), 1) < head_size
    scale = head_size ** (-0.5)
    for step in range(steps):
        rows = pl.ds(step * span, span)
        scores = []
        for head in range(heads):
            lanes = pl.ds(head // 2 * lanes_two, lanes_two)
            query = packed_ref[0, rows, lanes]
            query = jnp.where(lane_low == (head % 2 == 0), query, jnp.zeros_like(query))
            scores.append(dot_lanes(query, packed_ref[1, rows, lanes]))
        scores = jnp.where(same_row, jnp.concatenate(scores, axis=0) * scale, BIG)
        expo = jnp.exp(scores - jnp.max(scores, axis=1, keepdims=True))
        weights = (expo / jnp.sum(expo, axis=1, keepdims=True)).astype(jnp.bfloat16)
        for pair in range(heads // 2):
            lanes = pl.ds(pair * lanes_two, lanes_two)
            start = 2 * pair * span
            mixed = dot_rows(weights[start:start + 2 * span], packed_ref[2, rows, lanes])
            normed_ref[rows, lanes] = jnp.where(lane_low, mixed[:span], mixed[span:]).astype(jnp.bfloat16)
    for copy in copies[3:]:
        copy.wait()
    delta = dot_rows(normed_ref[...], w_out_ref[...])
    for step in range(steps):
        for group in range(groups):
            start = step * span + group * chunk
            resid = cells_of(group, step) + delta[start:start + chunk]
            if group == 0:
                resid_ref[pl.ds(step * chunk, chunk), :] = resid
            normed_ref[pl.ds(start, chunk), :] = rms_scale(resid, gain_tile_ref[...]).astype(jnp.bfloat16)
    slots = mask_ref.shape[0]
    slot, lane = iota((slots, lanes_two), 0), iota((slots, lanes_two), 1)
    place = jnp.zeros((slots, lanes_two), jnp.float32)
    for index in range(slots):
        tile = ids_ref[0, index]
        spot = jnp.where(tile < 0, -1, head_size + slot_of(lax.div(tile, tiles_here), me_ref[0], row_size, paired))
        place = jnp.where((slot == index) & (lane == spot), 1.0, place)
    live = lax.dot_general((mask_ref[...] > 0).astype(jnp.float32).astype(jnp.bfloat16), place.astype(jnp.bfloat16),
                           (((0,), (0,)), ((), ())), preferred_element_type=jnp.float32)
    lane = iota(live.shape, 1)
    shut = jnp.where((lane >= head_size) & (lane < head_size + row_size) & (live < 0.5), 1.0, 0.0).astype(jnp.bfloat16)
    total = steps * span
    cell = iota((total, shut.shape[0]), 0)
    row_of = cell // span * (chunk // cols) + cell % chunk // cols
    spread = (row_of == iota((total, shut.shape[0]), 1)).astype(jnp.bfloat16)
    bias = dot_rows(spread, shut) * BIG
    asked = dot_rows(normed_ref[...], w_query_ref[...]).astype(jnp.bfloat16).astype(jnp.float32) * scale
    low = iota((total, lanes_two), 1) < head_size
    for head in range(heads_here):
        if heads_here % 2 == 0:
            two = asked[:, head // 2 * lanes_two:(head // 2 + 1) * lanes_two]
            one = two if head % 2 == 0 else pltpu.roll(two, head_size, 1)
            query = jnp.where(low, one, bias)
        else:
            one = asked[:, head * head_size:(head + 1) * head_size]
            query = jnp.concatenate([one, bias[:, head_size:]], axis=1)
        query = query.astype(jnp.bfloat16)
        for step in range(steps):
            for group in range(groups):
                start = step * span + group * chunk
                asked_ref[head, pl.ds(group * own_rows + step * chunk, chunk), :] = query[start:start + chunk]


def front(cells, ids, me, key_mask, gain_col, w_qkv, w_out, gain_tile, w_query, heads, head_size, cols,
          heads_here, tiles_here, row_size, paired, after):
    groups = len(cells)
    width = cells[0].shape[2]
    own_rows = cells[0].shape[0] * cols
    total = groups * own_rows
    key_mask, gain_col, gain_tile = key_mask.T, gain_col.reshape(1, width), gain_tile.reshape(1, width)
    weights = [(3, width, width), (width, width), (width, heads_here * head_size), (groups,) + cells[0].shape]
    scratch = [pltpu.VMEM(shape, jnp.bfloat16) for shape in [(total, width), (3, total, width)] + weights]
    scratch += [pltpu.SMEM(ids.shape, jnp.int32), pltpu.VMEM(key_mask.shape, jnp.int32)]
    scratch += [pltpu.VMEM((1, width), jnp.float32)] * 2 + [pltpu.SemaphoreType.DMA((groups + 9,))]
    fetched = [pltpu.with_memory_space_constraint(value, pltpu.HBM)
               for value in (ids, key_mask, gain_col, gain_tile, w_qkv, w_out, w_query)]
    own = pltpu.with_memory_space_constraint(cells[0], pltpu.HBM)
    return pl.pallas_call(
        functools.partial(front_kernel, groups, heads, head_size, ROW_GROUP * cols, cols, heads_here, tiles_here, row_size, paired,
                          len(after)),
        out_shape=(jax.ShapeDtypeStruct((own_rows, width), jnp.float32),
                   jax.ShapeDtypeStruct((heads_here, total, 2 * head_size), jnp.bfloat16)),
        in_specs=[HBM] + [ANY] * (groups - 1) + [SMEM] + [HBM] * 7 + [ANY] * len(after),
        out_specs=(VMEM, VMEM),
        scratch_shapes=scratch,
        compiler_params=params(total),
        cost_estimate=pl.CostEstimate(flops=2 * total * width * 5 * width, bytes_accessed=4 * MIB,
                                      transcendentals=total * heads * 128),
        name="front",
    )(own, *cells[1:], me, *fetched, *after)


def weigh(query, tile_refs, head, slots):
    key_parts, val_parts = [], []
    for ref, slot in zip(tile_refs, slots):
        tiles = ref[:, head]
        count, keys, lanes = tiles.shape
        lane = iota(tiles.shape, 2)
        marks = (lane == iota(tiles.shape, 0) + (lanes // 2 + slot)).astype(tiles.dtype)
        key_parts.append(jnp.where(lane < lanes // 2, tiles, marks).reshape(count * keys, lanes))
        val_parts.append(jnp.where(lane < lanes // 2, jnp.ones_like(tiles), tiles).reshape(count * keys, lanes))
    scores = dot_lanes(query, jnp.concatenate(key_parts, axis=0))
    top = jnp.max(scores, axis=1, keepdims=True)
    return top, dot_rows(jnp.exp(scores - top).astype(jnp.bfloat16), jnp.concatenate(val_parts, axis=0))


def attention_cost(asked, tiles):
    heads, rows, lanes = asked.shape
    keys = sum(part.shape[0] * part.shape[2] for part in tiles)
    return pl.CostEstimate(flops=4 * rows * heads * keys * lanes, bytes_accessed=4 * MIB, transcendentals=rows * heads * keys)


def first_kernel(slots, block, asked_ref, *refs):
    tile_refs, (sums_ref, tops_ref) = refs[:len(slots)], refs[-2:]
    heads, rows_all, lanes = asked_ref.shape
    lane = iota((block, lanes), 1)
    for step in range(rows_all // block):
        rows = pl.ds(step * block, block)
        tops = jnp.zeros((block, lanes), jnp.float32)
        for head in range(heads):
            top, sums_ref[head, rows, :] = weigh(asked_ref[head, rows, :], tile_refs, head, slots)
            tops = jnp.where(lane == head, top, tops)
        tops_ref[rows, :] = tops


def first_tiles(asked, tiles, slots, own_rows, after):
    heads, rows, lanes = asked.shape
    return pl.pallas_call(
        functools.partial(first_kernel, slots, rows if rows <= 512 else own_rows),
        out_shape=(jax.ShapeDtypeStruct((heads, rows, lanes), jnp.float32), jax.ShapeDtypeStruct((rows, lanes), jnp.float32)),
        in_specs=[VMEM] * (1 + len(tiles)) + [ANY] * len(after),
        out_specs=(VMEM, VMEM),
        compiler_params=params(rows),
        cost_estimate=attention_cost(asked, tiles),
        name="first_tiles",
    )(asked, *tiles, *after)


def merge(asked_ref, sums_ref, tops_ref, tile_refs, slots, head, rows):
    top, sums = weigh(asked_ref[head, rows, :], tile_refs, head, slots)
    old_top = tops_ref[rows, head:head + 1]
    new_top = jnp.maximum(top, old_top)
    return new_top, sums_ref[head, rows, :] * jnp.exp(old_top - new_top) + sums * jnp.exp(top - new_top)


def more_kernel(slots, block, asked_ref, old_sums_ref, old_tops_ref, *refs):
    tile_refs, (sums_ref, tops_ref) = refs[:len(slots)], refs[len(slots):]
    heads, rows_all, lanes = asked_ref.shape
    lane = iota((block, lanes), 1)
    for step in range(rows_all // block):
        rows = pl.ds(step * block, block)
        tops = jnp.zeros((block, lanes), jnp.float32)
        for head in range(heads):
            top, sums_ref[head, rows, :] = merge(asked_ref, old_sums_ref, old_tops_ref, tile_refs, slots, head, rows)
            tops = jnp.where(lane == head, top, tops)
        tops_ref[rows, :] = tops


def more_tiles(asked, sums, tops, tiles, slots, own_rows):
    rows = asked.shape[1]
    return pl.pallas_call(
        functools.partial(more_kernel, slots, rows if rows <= 512 else own_rows),
        out_shape=(jax.ShapeDtypeStruct(sums.shape, jnp.float32), jax.ShapeDtypeStruct(tops.shape, jnp.float32)),
        in_specs=[VMEM] * (3 + len(tiles)),
        out_specs=(VMEM, VMEM),
        compiler_params=params(rows),
        cost_estimate=attention_cost(asked, tiles),
        name="more_tiles",
    )(asked, sums, tops, *tiles)


def last_kernel(slots, groups, asked_ref, sums_ref, tops_ref, *refs):
    tile_refs, out_refs = refs[:len(slots)], refs[-len(groups):]
    heads, lanes = asked_ref.shape[0], asked_ref.shape[2]
    block = out_refs[0].shape[0]
    half = lanes // 2
    lane_low = iota((block, lanes), 1) < half
    for group, out_ref in zip(groups, out_refs):
        rows = pl.ds(group * block, block)
        low = None
        for head in range(heads):
            _, sums = merge(asked_ref, sums_ref, tops_ref, tile_refs, slots, head, rows)
            turned = pltpu.roll(sums, half, 1)
            if head % 2:
                out_ref[:, pl.ds(head // 2 * lanes, lanes)] = jnp.where(lane_low, low, sums / turned).astype(jnp.bfloat16)
            elif head + 1 < heads:
                low = turned / sums
            else:
                out_ref[:, pl.ds(head * half, half)] = (turned / sums)[:, :half].astype(jnp.bfloat16)


def last_tiles(asked, sums, tops, tiles, slots, groups, own_rows, after):
    heads, rows, lanes = asked.shape
    out = jax.ShapeDtypeStruct((own_rows, heads * lanes // 2), jnp.bfloat16)
    return pl.pallas_call(
        functools.partial(last_kernel, slots, groups),
        out_shape=(out,) * len(groups),
        in_specs=[VMEM] * (3 + len(tiles)) + [ANY] * len(after),
        out_specs=(VMEM,) * len(groups),
        compiler_params=params(rows),
        cost_estimate=attention_cost(asked[:, :own_rows * len(groups)], tiles),
        name="last_tiles",
    )(asked, sums, tops, *tiles, *after)


def own_kernel(me_ref, weight_ref, resid_ref, answer_ref, partial_ref, *part_refs):
    groups, group_width = len(part_refs) + 1, answer_ref.shape[1]

    def rows(step):
        group = lax.rem(me_ref[1] - step + groups, groups)
        return weight_ref[pl.ds(pl.multiple_of(group * group_width, group_width), group_width), :]

    partial_ref[...] = resid_ref[...] + dot_rows(answer_ref[...], rows(0))
    for step, part_ref in enumerate(part_refs):
        part_ref[...] = rows(step + 1)


def own_part(me, weight, residual, answer, groups):
    part = jax.ShapeDtypeStruct((answer.shape[1], weight.shape[1]), weight.dtype)
    return pl.pallas_call(
        own_kernel,
        out_shape=(jax.ShapeDtypeStruct(residual.shape, jnp.float32),) + (part,) * (groups - 1),
        in_specs=[SMEM, VMEM, VMEM, VMEM],
        out_specs=(VMEM,) * groups,
        compiler_params=params(0),
        cost_estimate=pl.CostEstimate(flops=2 * residual.size * answer.shape[1], bytes_accessed=MIB, transcendentals=0),
        name="own_part",
    )(me, weight, residual, answer)


def turn(size, step):
    return [(src, (src + step) % size) for src in range(size)]


def shards(row_size, col_size, fact_cells, gain_col, w_qkv, w_col_out, gain_tile, w_query, w_tile_out,
           tile_kv, tile_ids, key_mask):
    rows, cols, width = fact_cells.shape
    tiles_here, keys, heads_here, lanes = tile_kv.shape
    head_size = lanes // 2
    heads_all = width // head_size
    group_width = heads_here * head_size
    half = row_size // 2
    row_me, col_me = lax.axis_index("rows"), lax.axis_index("cols")
    me = jnp.stack([row_me, col_me]).astype(jnp.int32)
    halves = [list(range(half)), list(range(half, row_size))]
    paired = half <= 8 and half & (half - 1) == 0
    assert row_size <= head_size and row_size % 2 == 0

    def swap(value):
        return lax.all_to_all(value, "rows", split_axis=0, concat_axis=0, tiled=True, axis_index_groups=halves)

    asked_of = request(tile_ids, me, tiles_here, row_size)
    asked_by = swap(asked_of)
    heads_first = jnp.transpose(tile_kv, (0, 2, 1, 3))
    mirrored = lax.ppermute(heads_first, "rows", turn(row_size, half))

    cells = [fact_cells]
    for step in range(1, col_size):
        cells.append(lax.ppermute(fact_cells, "cols", turn(col_size, -step)))

    across = half // 2

    def turns(step):
        return bool(step & across) and bool(step & (across - 1) & ~1)

    near_order = [0, 1] + sorted(range(2, half), key=lambda step: (turns(step), step != 2, not step & across, step))
    far_order = [0] + sorted(range(2, half), key=lambda step: (turns(step), step & 1, step)) + [1]
    near_slots, far_slots = (near_order, [half + step for step in far_order]) if paired else ([0], [half])

    def spread(tiles, which, order, after):
        if not order:
            return []
        if not paired:
            return [swap(pick(tiles, asked_by, which, after))]
        picked = pick_each(tiles, asked_by, which, me, order, after)
        return [tile if step == 0 else lax.ppermute(tile, "rows", [(row, row ^ step) for row in range(row_size)])
                for step, tile in zip(order, picked)]

    if group_width % 128:
        w_query = lax.dynamic_slice_in_dim(w_query, col_me * group_width, group_width, 1)
    residual, asked = front(cells, tile_ids, me, key_mask, gain_col, w_qkv, w_col_out, gain_tile, w_query,
                            heads_all, head_size, cols, heads_here, tiles_here, row_size, paired, [])
    near = spread(heads_first, 0, near_order, [asked])
    far = spread(mirrored, 1, far_order[:-1] if paired else far_order, near[1:3])
    sums, tops = first_tiles(asked, near, near_slots, rows * cols, far[1:2])
    far += spread(mirrored, 1, far_order[-1:] if paired else [], [tops])
    batch = len(far) // 2
    if batch:
        sums, tops = more_tiles(asked, sums, tops, far[:batch], far_slots[:batch], rows * cols)
    far, far_slots = far[batch:], far_slots[batch:]
    others = last_tiles(asked, sums, tops, far, far_slots, list(range(1, col_size)), rows * cols, [])
    own = last_tiles(asked, sums, tops, far, far_slots, [0], rows * cols, others[:1])
    final, *weights = own_part(me, w_tile_out, residual, own[0], col_size)
    for step, (other, weight) in enumerate(zip(others, weights)):
        final = final + dot_rows(lax.ppermute(other, "cols", turn(col_size, step + 1)), weight)
    return final.astype(jnp.bfloat16).reshape(rows, cols, width)


def solution(mesh):
    row_size, col_size = mesh.shape["rows"], mesh.shape["cols"]
    placed = (P("rows", "cols", None), P(), P(), P(), P(), P(), P(), P("rows", None, "cols", None),
              P("rows", None), P("rows", None))

    def body(*arrays):
        return shards(row_size, col_size, *arrays)

    return jax.shard_map(body, mesh=mesh, in_specs=placed, out_specs=P("rows", "cols", None), check_vma=False)
```

```python
import functools

import jax
import jax.numpy as jnp
from jax import lax
from jax.experimental import pallas as pl
from jax.experimental.pallas import tpu as pltpu
from jax.sharding import PartitionSpec as P

ROW_GROUP = 16
BIG = -1e30
MIB = 1024 * 1024
VMEM = pl.BlockSpec(memory_space=pltpu.VMEM)
SMEM = pl.BlockSpec(memory_space=pltpu.SMEM)
HBM = pl.BlockSpec(memory_space=pltpu.HBM)
ANY = pl.BlockSpec(memory_space=pl.ANY)


def params(rows):
    return pltpu.CompilerParams(vmem_limit_bytes=(20 if rows <= 512 else 48) * MIB)


def dot_rows(left, right):
    return lax.dot_general(left, right, (((1,), (0,)), ((), ())), preferred_element_type=jnp.float32)


def dot_lanes(left, right):
    return lax.dot_general(left, right, (((1,), (1,)), ((), ())), preferred_element_type=jnp.float32)


def rms_scale(values, gain_vec):
    mean_sq = jnp.mean(values * values, axis=-1, keepdims=True)
    return values * lax.rsqrt(mean_sq + 1e-05) * gain_vec


def iota(shape, dim):
    return lax.broadcasted_iota(jnp.int32, shape, dim)


def slot_of(owner, row_me, row_size, paired):
    half = row_size // 2
    return owner ^ row_me if paired else lax.rem(owner + lax.div(row_me, half) * half, row_size)


def request_kernel(tiles_here, row_size, ids_ref, me_ref, out_ref):
    half = row_size // 2
    peer, which = iota(out_ref.shape, 0), iota(out_ref.shape, 1)
    wanted = jnp.zeros(out_ref.shape, jnp.int32)
    for slot in range(ids_ref.shape[1]):
        tile = ids_ref[0, slot]
        owner = lax.div(tile, tiles_here)
        far = jnp.where(lax.div(owner, half) == lax.div(me_ref[0], half), 0, 1)
        here = (peer == jnp.where(tile < 0, -1, lax.rem(owner, half))) & (which == far)
        wanted = jnp.where(here, lax.rem(tile, tiles_here), wanted)
    out_ref[...] = wanted


def request(ids, me, tiles_here, row_size):
    return pl.pallas_call(
        functools.partial(request_kernel, tiles_here, row_size),
        out_shape=jax.ShapeDtypeStruct((row_size // 2, 2, 128), jnp.int32),
        in_specs=[SMEM, SMEM],
        out_specs=VMEM,
        compiler_params=params(0),
        cost_estimate=pl.CostEstimate(flops=0, bytes_accessed=MIB // 4, transcendentals=0),
        name="request",
    )(ids, me)


def pick_kernel(which, wanted_ref, tiles_ref, *refs):
    out_ref = refs[-1]
    for peer in range(out_ref.shape[0]):
        out_ref[peer] = tiles_ref[wanted_ref[peer, which, 0]]


def pick(tiles, wanted, which, after):
    return pl.pallas_call(
        functools.partial(pick_kernel, which),
        out_shape=jax.ShapeDtypeStruct(wanted.shape[:1] + tiles.shape[1:], tiles.dtype),
        in_specs=[SMEM, VMEM] + [ANY] * len(after),
        out_specs=VMEM,
        compiler_params=params(0),
        cost_estimate=pl.CostEstimate(flops=0, bytes_accessed=2 * MIB, transcendentals=0),
        name="pick",
    )(wanted, tiles, *after)


def pick_each_kernel(which, order, wanted_ref, me_ref, tiles_ref, *refs):
    place = lax.rem(me_ref[0], wanted_ref.shape[0])
    for step, out_ref in zip(order, refs[-len(order):]):
        out_ref[0] = tiles_ref[wanted_ref[place ^ step, which, 0]]


def pick_each(tiles, wanted, which, me, order, after):
    count = len(order)
    return pl.pallas_call(
        functools.partial(pick_each_kernel, which, order),
        out_shape=(jax.ShapeDtypeStruct((1,) + tiles.shape[1:], tiles.dtype),) * count,
        in_specs=[SMEM, SMEM, VMEM] + [ANY] * len(after),
        out_specs=(VMEM,) * count,
        compiler_params=params(0),
        cost_estimate=pl.CostEstimate(flops=0, bytes_accessed=2 * MIB, transcendentals=0),
        name="pick_each",
    )(wanted, me, tiles, *after)


def front_kernel(groups, heads, head_size, chunk, cols, heads_here, tiles_here, row_size, paired, waited, *refs):
    cell_hbms, refs = refs[:groups], refs[groups:]
    (me_ref, ids_hbm, mask_hbm, gain_col_hbm, gain_tile_hbm, w_qkv_hbm, w_out_hbm, w_query_hbm) = refs[:8]
    (resid_ref, asked_ref, normed_ref, packed_ref, w_qkv_ref, w_out_ref, w_query_ref, cell_refs,
     ids_ref, mask_ref, gain_col_ref, gain_tile_ref, sems) = refs[8 + waited:]
    own_rows, width = resid_ref.shape
    steps = own_rows // chunk
    span = groups * chunk
    lanes_two = 2 * head_size
    group_width = heads_here * head_size
    if w_query_hbm.shape[1] != group_width:
        w_query_hbm = w_query_hbm.at[:, pl.ds(pl.multiple_of(me_ref[1] * group_width, group_width), group_width)]
    pairs = [(hbm, cell_refs.at[group]) for group, hbm in enumerate(cell_hbms)]
    pairs += [(gain_col_hbm, gain_col_ref)]
    pairs += [(w_qkv_hbm.at[:, pl.ds(part * width, width)], w_qkv_ref.at[part]) for part in range(3)]
    pairs += [(w_out_hbm, w_out_ref), (gain_tile_hbm, gain_tile_ref), (w_query_hbm, w_query_ref), (ids_hbm, ids_ref), (mask_hbm, mask_ref)]
    copies = [pltpu.make_async_copy(*pair, sems.at[index]) for index, pair in enumerate(pairs)]
    for copy in copies:
        copy.start()
    for copy in copies[:groups + 1]:
        copy.wait()
    copies = copies[groups + 1:]

    def cells_of(group, step):
        cells = cell_refs[group, pl.ds(step * (chunk // cols), chunk // cols)].astype(jnp.float32)
        return cells.reshape(chunk, width)

    for step in range(steps):
        for group in range(groups):
            cells = cells_of(group, step)
            normed_ref[pl.ds(step * span + group * chunk, chunk), :] = rms_scale(cells, gain_col_ref[...]).astype(jnp.bfloat16)
    for part in range(3):
        copies[part].wait()
        packed_ref[part] = dot_rows(normed_ref[...], w_qkv_ref[part]).astype(jnp.bfloat16)
    stacked = heads * span
    same_row = iota((stacked, span), 0) % chunk // cols == iota((stacked, span), 1) % chunk // cols
    lane_low = iota((span, lanes_two), 1) < head_size
    scale = head_size ** (-0.5)
    for step in range(steps):
        rows = pl.ds(step * span, span)
        scores = []
        for head in range(heads):
            lanes = pl.ds(head // 2 * lanes_two, lanes_two)
            query = packed_ref[0, rows, lanes]
            query = jnp.where(lane_low == (head % 2 == 0), query, jnp.zeros_like(query))
            scores.append(dot_lanes(query, packed_ref[1, rows, lanes]))
        scores = jnp.where(same_row, jnp.concatenate(scores, axis=0) * scale, BIG)
        expo = jnp.exp(scores - jnp.max(scores, axis=1, keepdims=True))
        weights = (expo / jnp.sum(expo, axis=1, keepdims=True)).astype(jnp.bfloat16)
        for pair in range(heads // 2):
            lanes = pl.ds(pair * lanes_two, lanes_two)
            start = 2 * pair * span
            mixed = dot_rows(weights[start:start + 2 * span], packed_ref[2, rows, lanes])
            normed_ref[rows, lanes] = jnp.where(lane_low, mixed[:span], mixed[span:]).astype(jnp.bfloat16)
    for copy in copies[3:]:
        copy.wait()
    delta = dot_rows(normed_ref[...], w_out_ref[...])
    for step in range(steps):
        for group in range(groups):
            start = step * span + group * chunk
            resid = cells_of(group, step) + delta[start:start + chunk]
            if group == 0:
                resid_ref[pl.ds(step * chunk, chunk), :] = resid
            normed_ref[pl.ds(start, chunk), :] = rms_scale(resid, gain_tile_ref[...]).astype(jnp.bfloat16)
    slots = mask_ref.shape[0]
    slot, lane = iota((slots, lanes_two), 0), iota((slots, lanes_two), 1)
    place = jnp.zeros((slots, lanes_two), jnp.float32)
    for index in range(slots):
        tile = ids_ref[0, index]
        spot = jnp.where(tile < 0, -1, head_size + slot_of(lax.div(tile, tiles_here), me_ref[0], row_size, paired))
        place = jnp.where((slot == index) & (lane == spot), 1.0, place)
    live = lax.dot_general((mask_ref[...] > 0).astype(jnp.float32).astype(jnp.bfloat16), place.astype(jnp.bfloat16),
                           (((0,), (0,)), ((), ())), preferred_element_type=jnp.float32)
    lane = iota(live.shape, 1)
    shut = jnp.where((lane >= head_size) & (lane < head_size + row_size) & (live < 0.5), 1.0, 0.0).astype(jnp.bfloat16)
    total = steps * span
    cell = iota((total, shut.shape[0]), 0)
    row_of = cell // span * (chunk // cols) + cell % chunk // cols
    spread = (row_of == iota((total, shut.shape[0]), 1)).astype(jnp.bfloat16)
    bias = dot_rows(spread, shut) * BIG
    asked = dot_rows(normed_ref[...], w_query_ref[...]).astype(jnp.bfloat16).astype(jnp.float32) * scale
    low = iota((total, lanes_two), 1) < head_size
    for head in range(heads_here):
        if heads_here % 2 == 0:
            two = asked[:, head // 2 * lanes_two:(head // 2 + 1) * lanes_two]
            one = two if head % 2 == 0 else pltpu.roll(two, head_size, 1)
            query = jnp.where(low, one, bias)
        else:
            one = asked[:, head * head_size:(head + 1) * head_size]
            query = jnp.concatenate([one, bias[:, head_size:]], axis=1)
        query = query.astype(jnp.bfloat16)
        for step in range(steps):
            for group in range(groups):
                start = step * span + group * chunk
                asked_ref[head, pl.ds(group * own_rows + step * chunk, chunk), :] = query[start:start + chunk]


def front(cells, ids, me, key_mask, gain_col, w_qkv, w_out, gain_tile, w_query, heads, head_size, cols,
          heads_here, tiles_here, row_size, paired, after):
    groups = len(cells)
    width = cells[0].shape[2]
    own_rows = cells[0].shape[0] * cols
    total = groups * own_rows
    key_mask, gain_col, gain_tile = key_mask.T, gain_col.reshape(1, width), gain_tile.reshape(1, width)
    weights = [(3, width, width), (width, width), (width, heads_here * head_size), (groups,) + cells[0].shape]
    scratch = [pltpu.VMEM(shape, jnp.bfloat16) for shape in [(total, width), (3, total, width)] + weights]
    scratch += [pltpu.SMEM(ids.shape, jnp.int32), pltpu.VMEM(key_mask.shape, jnp.int32)]
    scratch += [pltpu.VMEM((1, width), jnp.float32)] * 2 + [pltpu.SemaphoreType.DMA((groups + 9,))]
    fetched = [pltpu.with_memory_space_constraint(value, pltpu.HBM)
               for value in (ids, key_mask, gain_col, gain_tile, w_qkv, w_out, w_query)]
    own = pltpu.with_memory_space_constraint(cells[0], pltpu.HBM)
    return pl.pallas_call(
        functools.partial(front_kernel, groups, heads, head_size, ROW_GROUP * cols, cols, heads_here, tiles_here, row_size, paired,
                          len(after)),
        out_shape=(jax.ShapeDtypeStruct((own_rows, width), jnp.float32),
                   jax.ShapeDtypeStruct((heads_here, total, 2 * head_size), jnp.bfloat16)),
        in_specs=[HBM] + [ANY] * (groups - 1) + [SMEM] + [HBM] * 7 + [ANY] * len(after),
        out_specs=(VMEM, VMEM),
        scratch_shapes=scratch,
        compiler_params=params(total),
        cost_estimate=pl.CostEstimate(flops=2 * total * width * 5 * width, bytes_accessed=4 * MIB,
                                      transcendentals=total * heads * 128),
        name="front",
    )(own, *cells[1:], me, *fetched, *after)


def weigh(query, tile_refs, head, slots):
    key_parts, val_parts = [], []
    for ref, slot in zip(tile_refs, slots):
        tiles = ref[:, head]
        count, keys, lanes = tiles.shape
        lane = iota(tiles.shape, 2)
        marks = (lane == iota(tiles.shape, 0) + (lanes // 2 + slot)).astype(tiles.dtype)
        key_parts.append(jnp.where(lane < lanes // 2, tiles, marks).reshape(count * keys, lanes))
        val_parts.append(jnp.where(lane < lanes // 2, jnp.ones_like(tiles), tiles).reshape(count * keys, lanes))
    scores = dot_lanes(query, jnp.concatenate(key_parts, axis=0))
    top = jnp.max(scores, axis=1, keepdims=True)
    return top, dot_rows(jnp.exp(scores - top).astype(jnp.bfloat16), jnp.concatenate(val_parts, axis=0))


def attention_cost(asked, tiles):
    heads, rows, lanes = asked.shape
    keys = sum(part.shape[0] * part.shape[2] for part in tiles)
    return pl.CostEstimate(flops=4 * rows * heads * keys * lanes, bytes_accessed=4 * MIB, transcendentals=rows * heads * keys)


def first_kernel(slots, block, asked_ref, *refs):
    tile_refs, (sums_ref, tops_ref) = refs[:len(slots)], refs[-2:]
    heads, rows_all, lanes = asked_ref.shape
    lane = iota((block, lanes), 1)
    for step in range(rows_all // block):
        rows = pl.ds(step * block, block)
        tops = jnp.zeros((block, lanes), jnp.float32)
        for head in range(heads):
            top, sums_ref[head, rows, :] = weigh(asked_ref[head, rows, :], tile_refs, head, slots)
            tops = jnp.where(lane == head, top, tops)
        tops_ref[rows, :] = tops


def first_tiles(asked, tiles, slots, own_rows, after):
    heads, rows, lanes = asked.shape
    return pl.pallas_call(
        functools.partial(first_kernel, slots, rows if rows <= 512 else own_rows),
        out_shape=(jax.ShapeDtypeStruct((heads, rows, lanes), jnp.float32), jax.ShapeDtypeStruct((rows, lanes), jnp.float32)),
        in_specs=[VMEM] * (1 + len(tiles)) + [ANY] * len(after),
        out_specs=(VMEM, VMEM),
        compiler_params=params(rows),
        cost_estimate=attention_cost(asked, tiles),
        name="first_tiles",
    )(asked, *tiles, *after)


def merge(asked_ref, sums_ref, tops_ref, tile_refs, slots, head, rows):
    top, sums = weigh(asked_ref[head, rows, :], tile_refs, head, slots)
    old_top = tops_ref[rows, head:head + 1]
    new_top = jnp.maximum(top, old_top)
    return new_top, sums_ref[head, rows, :] * jnp.exp(old_top - new_top) + sums * jnp.exp(top - new_top)


def more_kernel(slots, block, asked_ref, old_sums_ref, old_tops_ref, *refs):
    tile_refs, (sums_ref, tops_ref) = refs[:len(slots)], refs[len(slots):]
    heads, rows_all, lanes = asked_ref.shape
    lane = iota((block, lanes), 1)
    for step in range(rows_all // block):
        rows = pl.ds(step * block, block)
        tops = jnp.zeros((block, lanes), jnp.float32)
        for head in range(heads):
            top, sums_ref[head, rows, :] = merge(asked_ref, old_sums_ref, old_tops_ref, tile_refs, slots, head, rows)
            tops = jnp.where(lane == head, top, tops)
        tops_ref[rows, :] = tops


def more_tiles(asked, sums, tops, tiles, slots, own_rows):
    rows = asked.shape[1]
    return pl.pallas_call(
        functools.partial(more_kernel, slots, rows if rows <= 512 else own_rows),
        out_shape=(jax.ShapeDtypeStruct(sums.shape, jnp.float32), jax.ShapeDtypeStruct(tops.shape, jnp.float32)),
        in_specs=[VMEM] * (3 + len(tiles)),
        out_specs=(VMEM, VMEM),
        compiler_params=params(rows),
        cost_estimate=attention_cost(asked, tiles),
        name="more_tiles",
    )(asked, sums, tops, *tiles)


def last_kernel(slots, groups, asked_ref, sums_ref, tops_ref, *refs):
    tile_refs, out_refs = refs[:len(slots)], refs[-len(groups):]
    heads, lanes = asked_ref.shape[0], asked_ref.shape[2]
    block = out_refs[0].shape[0]
    half = lanes // 2
    lane_low = iota((block, lanes), 1) < half
    for group, out_ref in zip(groups, out_refs):
        rows = pl.ds(group * block, block)
        low = None
        for head in range(heads):
            _, sums = merge(asked_ref, sums_ref, tops_ref, tile_refs, slots, head, rows)
            turned = pltpu.roll(sums, half, 1)
            if head % 2:
                out_ref[:, pl.ds(head // 2 * lanes, lanes)] = jnp.where(lane_low, low, sums / turned).astype(jnp.bfloat16)
            elif head + 1 < heads:
                low = turned / sums
            else:
                out_ref[:, pl.ds(head * half, half)] = (turned / sums)[:, :half].astype(jnp.bfloat16)


def last_tiles(asked, sums, tops, tiles, slots, groups, own_rows, after):
    heads, rows, lanes = asked.shape
    out = jax.ShapeDtypeStruct((own_rows, heads * lanes // 2), jnp.bfloat16)
    return pl.pallas_call(
        functools.partial(last_kernel, slots, groups),
        out_shape=(out,) * len(groups),
        in_specs=[VMEM] * (3 + len(tiles)) + [ANY] * len(after),
        out_specs=(VMEM,) * len(groups),
        compiler_params=params(rows),
        cost_estimate=attention_cost(asked[:, :own_rows * len(groups)], tiles),
        name="last_tiles",
    )(asked, sums, tops, *tiles, *after)


def own_kernel(me_ref, weight_ref, resid_ref, answer_ref, partial_ref, *part_refs):
    groups, group_width = len(part_refs) + 1, answer_ref.shape[1]

    def rows(step):
        group = lax.rem(me_ref[1] - step + groups, groups)
        return weight_ref[pl.ds(pl.multiple_of(group * group_width, group_width), group_width), :]

    partial_ref[...] = resid_ref[...] + dot_rows(answer_ref[...], rows(0))
    for step, part_ref in enumerate(part_refs):
        part_ref[...] = rows(step + 1)


def own_part(me, weight, residual, answer, groups):
    part = jax.ShapeDtypeStruct((answer.shape[1], weight.shape[1]), weight.dtype)
    return pl.pallas_call(
        own_kernel,
        out_shape=(jax.ShapeDtypeStruct(residual.shape, jnp.float32),) + (part,) * (groups - 1),
        in_specs=[SMEM, VMEM, VMEM, VMEM],
        out_specs=(VMEM,) * groups,
        compiler_params=params(0),
        cost_estimate=pl.CostEstimate(flops=2 * residual.size * answer.shape[1], bytes_accessed=MIB, transcendentals=0),
        name="own_part",
    )(me, weight, residual, answer)


def turn(size, step):
    return [(src, (src + step) % size) for src in range(size)]


def shards(row_size, col_size, fact_cells, gain_col, w_qkv, w_col_out, gain_tile, w_query, w_tile_out,
           tile_kv, tile_ids, key_mask):
    rows, cols, width = fact_cells.shape
    tiles_here, keys, heads_here, lanes = tile_kv.shape
    head_size = lanes // 2
    heads_all = width // head_size
    group_width = heads_here * head_size
    half = row_size // 2
    row_me, col_me = lax.axis_index("rows"), lax.axis_index("cols")
    me = jnp.stack([row_me, col_me]).astype(jnp.int32)
    halves = [list(range(half)), list(range(half, row_size))]
    paired = half <= 8 and half & (half - 1) == 0
    assert row_size <= head_size and row_size % 2 == 0

    def swap(value):
        return lax.all_to_all(value, "rows", split_axis=0, concat_axis=0, tiled=True, axis_index_groups=halves)

    asked_of = request(tile_ids, me, tiles_here, row_size)
    asked_by = swap(asked_of)
    heads_first = jnp.transpose(tile_kv, (0, 2, 1, 3))
    mirrored = lax.ppermute(heads_first, "rows", turn(row_size, half))

    cells = [fact_cells]
    for step in range(1, col_size):
        cells.append(lax.ppermute(fact_cells, "cols", turn(col_size, -step)))

    across = half // 2

    def turns(step):
        return bool(step & across) and bool(step & (across - 1) & ~1)

    near_order = [0, 1] + sorted(range(2, half), key=lambda step: (turns(step), step != 2, not step & across, step))
    far_order = [0] + sorted(range(2, half), key=lambda step: (turns(step), step & 1, not step & across, step)) + [1]
    near_slots, far_slots = (near_order, [half + step for step in far_order]) if paired else ([0], [half])

    def spread(tiles, which, order, after):
        if not order:
            return []
        if not paired:
            return [swap(pick(tiles, asked_by, which, after))]
        picked = pick_each(tiles, asked_by, which, me, order, after)
        return [tile if step == 0 else lax.ppermute(tile, "rows", [(row, row ^ step) for row in range(row_size)])
                for step, tile in zip(order, picked)]

    if group_width % 128:
        w_query = lax.dynamic_slice_in_dim(w_query, col_me * group_width, group_width, 1)
    residual, asked = front(cells, tile_ids, me, key_mask, gain_col, w_qkv, w_col_out, gain_tile, w_query,
                            heads_all, head_size, cols, heads_here, tiles_here, row_size, paired, [])
    near = spread(heads_first, 0, near_order, [asked])
    far = spread(mirrored, 1, far_order[:-1] if paired else far_order, near[1:3])
    sums, tops = first_tiles(asked, near, near_slots, rows * cols, far[1:2])
    far += spread(mirrored, 1, far_order[-1:] if paired else [], [tops])
    for batch in (len(far) // 2, len(far) // 4):
        if batch:
            sums, tops = more_tiles(asked, sums, tops, far[:batch], far_slots[:batch], rows * cols)
        far, far_slots = far[batch:], far_slots[batch:]
    others = last_tiles(asked, sums, tops, far, far_slots, list(range(1, col_size)), rows * cols, [])
    own = last_tiles(asked, sums, tops, far, far_slots, [0], rows * cols, others[:1])
    final, *weights = own_part(me, w_tile_out, residual, own[0], col_size)
    for step, (other, weight) in enumerate(zip(others, weights)):
        final = final + dot_rows(lax.ppermute(other, "cols", turn(col_size, step + 1)), weight)
    return final.astype(jnp.bfloat16).reshape(rows, cols, width)


def solution(mesh):
    row_size, col_size = mesh.shape["rows"], mesh.shape["cols"]
    placed = (P("rows", "cols", None), P(), P(), P(), P(), P(), P(), P("rows", None, "cols", None),
              P("rows", None), P("rows", None))

    def body(*arrays):
        return shards(row_size, col_size, *arrays)

    return jax.shard_map(body, mesh=mesh, in_specs=placed, out_specs=P("rows", "cols", None), check_vma=False)
```

```python
import functools

import jax
import jax.numpy as jnp
from jax import lax
from jax.experimental import pallas as pl
from jax.experimental.pallas import tpu as pltpu
from jax.sharding import PartitionSpec as P

ROW_GROUP = 16
BIG = -1e30
MIB = 1024 * 1024
VMEM = pl.BlockSpec(memory_space=pltpu.VMEM)
SMEM = pl.BlockSpec(memory_space=pltpu.SMEM)
HBM = pl.BlockSpec(memory_space=pltpu.HBM)
ANY = pl.BlockSpec(memory_space=pl.ANY)


def params(rows):
    return pltpu.CompilerParams(vmem_limit_bytes=(20 if rows <= 512 else 48) * MIB)


def dot_rows(left, right):
    return lax.dot_general(left, right, (((1,), (0,)), ((), ())), preferred_element_type=jnp.float32)


def dot_lanes(left, right):
    return lax.dot_general(left, right, (((1,), (1,)), ((), ())), preferred_element_type=jnp.float32)


def rms_scale(values, gain_vec):
    mean_sq = jnp.mean(values * values, axis=-1, keepdims=True)
    return values * lax.rsqrt(mean_sq + 1e-05) * gain_vec


def iota(shape, dim):
    return lax.broadcasted_iota(jnp.int32, shape, dim)


def slot_of(owner, row_me, row_size, paired):
    half = row_size // 2
    return owner ^ row_me if paired else lax.rem(owner + lax.div(row_me, half) * half, row_size)


def request_kernel(tiles_here, row_size, ids_ref, me_ref, out_ref):
    half = row_size // 2
    peer, which = iota(out_ref.shape, 0), iota(out_ref.shape, 1)
    wanted = jnp.zeros(out_ref.shape, jnp.int32)
    for slot in range(ids_ref.shape[1]):
        tile = ids_ref[0, slot]
        owner = lax.div(tile, tiles_here)
        far = jnp.where(lax.div(owner, half) == lax.div(me_ref[0], half), 0, 1)
        here = (peer == jnp.where(tile < 0, -1, lax.rem(owner, half))) & (which == far)
        wanted = jnp.where(here, lax.rem(tile, tiles_here), wanted)
    out_ref[...] = wanted


def request(ids, me, tiles_here, row_size):
    return pl.pallas_call(
        functools.partial(request_kernel, tiles_here, row_size),
        out_shape=jax.ShapeDtypeStruct((row_size // 2, 2, 128), jnp.int32),
        in_specs=[SMEM, SMEM],
        out_specs=VMEM,
        compiler_params=params(0),
        cost_estimate=pl.CostEstimate(flops=0, bytes_accessed=MIB // 4, transcendentals=0),
        name="request",
    )(ids, me)


def pick_kernel(which, wanted_ref, tiles_ref, *refs):
    out_ref = refs[-1]
    for peer in range(out_ref.shape[0]):
        out_ref[peer] = tiles_ref[wanted_ref[peer, which, 0]]


def pick(tiles, wanted, which, after):
    return pl.pallas_call(
        functools.partial(pick_kernel, which),
        out_shape=jax.ShapeDtypeStruct(wanted.shape[:1] + tiles.shape[1:], tiles.dtype),
        in_specs=[SMEM, VMEM] + [ANY] * len(after),
        out_specs=VMEM,
        compiler_params=params(0),
        cost_estimate=pl.CostEstimate(flops=0, bytes_accessed=2 * MIB, transcendentals=0),
        name="pick",
    )(wanted, tiles, *after)


def pick_each_kernel(which, order, wanted_ref, me_ref, tiles_ref, *refs):
    place = lax.rem(me_ref[0], wanted_ref.shape[0])
    for step, out_ref in zip(order, refs[-len(order):]):
        out_ref[0] = tiles_ref[wanted_ref[place ^ step, which, 0]]


def pick_each(tiles, wanted, which, me, order, after):
    count = len(order)
    return pl.pallas_call(
        functools.partial(pick_each_kernel, which, order),
        out_shape=(jax.ShapeDtypeStruct((1,) + tiles.shape[1:], tiles.dtype),) * count,
        in_specs=[SMEM, SMEM, VMEM] + [ANY] * len(after),
        out_specs=(VMEM,) * count,
        compiler_params=params(0),
        cost_estimate=pl.CostEstimate(flops=0, bytes_accessed=2 * MIB, transcendentals=0),
        name="pick_each",
    )(wanted, me, tiles, *after)


def front_kernel(groups, heads, head_size, chunk, cols, heads_here, tiles_here, row_size, paired, waited, *refs):
    cell_hbms, refs = refs[:groups], refs[groups:]
    (me_ref, ids_hbm, mask_hbm, gain_col_hbm, gain_tile_hbm, w_qkv_hbm, w_out_hbm, w_query_hbm) = refs[:8]
    (resid_ref, asked_ref, normed_ref, packed_ref, w_qkv_ref, w_out_ref, w_query_ref, cell_refs,
     ids_ref, mask_ref, gain_col_ref, gain_tile_ref, sems) = refs[8 + waited:]
    own_rows, width = resid_ref.shape
    steps = own_rows // chunk
    span = groups * chunk
    lanes_two = 2 * head_size
    group_width = heads_here * head_size
    if w_query_hbm.shape[1] != group_width:
        w_query_hbm = w_query_hbm.at[:, pl.ds(pl.multiple_of(me_ref[1] * group_width, group_width), group_width)]
    pairs = [(hbm, cell_refs.at[group]) for group, hbm in enumerate(cell_hbms)]
    pairs += [(gain_col_hbm, gain_col_ref)]
    pairs += [(w_qkv_hbm.at[:, pl.ds(part * width, width)], w_qkv_ref.at[part]) for part in range(3)]
    pairs += [(w_out_hbm, w_out_ref), (gain_tile_hbm, gain_tile_ref), (w_query_hbm, w_query_ref), (ids_hbm, ids_ref), (mask_hbm, mask_ref)]
    copies = [pltpu.make_async_copy(*pair, sems.at[index]) for index, pair in enumerate(pairs)]
    for copy in copies:
        copy.start()
    for copy in copies[:groups + 1]:
        copy.wait()
    copies = copies[groups + 1:]

    def cells_of(group, step):
        cells = cell_refs[group, pl.ds(step * (chunk // cols), chunk // cols)].astype(jnp.float32)
        return cells.reshape(chunk, width)

    for step in range(steps):
        for group in range(groups):
            cells = cells_of(group, step)
            normed_ref[pl.ds(step * span + group * chunk, chunk), :] = rms_scale(cells, gain_col_ref[...]).astype(jnp.bfloat16)
    for part in range(3):
        copies[part].wait()
        packed_ref[part] = dot_rows(normed_ref[...], w_qkv_ref[part]).astype(jnp.bfloat16)
    stacked = heads * span
    same_row = iota((stacked, span), 0) % chunk // cols == iota((stacked, span), 1) % chunk // cols
    lane_low = iota((span, lanes_two), 1) < head_size
    scale = head_size ** (-0.5)
    for step in range(steps):
        rows = pl.ds(step * span, span)
        scores = []
        for head in range(heads):
            lanes = pl.ds(head // 2 * lanes_two, lanes_two)
            query = packed_ref[0, rows, lanes]
            query = jnp.where(lane_low == (head % 2 == 0), query, jnp.zeros_like(query))
            scores.append(dot_lanes(query, packed_ref[1, rows, lanes]))
        scores = jnp.where(same_row, jnp.concatenate(scores, axis=0) * scale, BIG)
        expo = jnp.exp(scores - jnp.max(scores, axis=1, keepdims=True))
        weights = (expo / jnp.sum(expo, axis=1, keepdims=True)).astype(jnp.bfloat16)
        for pair in range(heads // 2):
            lanes = pl.ds(pair * lanes_two, lanes_two)
            start = 2 * pair * span
            mixed = dot_rows(weights[start:start + 2 * span], packed_ref[2, rows, lanes])
            normed_ref[rows, lanes] = jnp.where(lane_low, mixed[:span], mixed[span:]).astype(jnp.bfloat16)
    for copy in copies[3:]:
        copy.wait()
    delta = dot_rows(normed_ref[...], w_out_ref[...])
    for step in range(steps):
        for group in range(groups):
            start = step * span + group * chunk
            resid = cells_of(group, step) + delta[start:start + chunk]
            if group == 0:
                resid_ref[pl.ds(step * chunk, chunk), :] = resid
            normed_ref[pl.ds(start, chunk), :] = rms_scale(resid, gain_tile_ref[...]).astype(jnp.bfloat16)
    slots = mask_ref.shape[0]
    slot, lane = iota((slots, lanes_two), 0), iota((slots, lanes_two), 1)
    place = jnp.zeros((slots, lanes_two), jnp.float32)
    for index in range(slots):
        tile = ids_ref[0, index]
        spot = jnp.where(tile < 0, -1, head_size + slot_of(lax.div(tile, tiles_here), me_ref[0], row_size, paired))
        place = jnp.where((slot == index) & (lane == spot), 1.0, place)
    live = lax.dot_general((mask_ref[...] > 0).astype(jnp.float32).astype(jnp.bfloat16), place.astype(jnp.bfloat16),
                           (((0,), (0,)), ((), ())), preferred_element_type=jnp.float32)
    lane = iota(live.shape, 1)
    shut = jnp.where((lane >= head_size) & (lane < head_size + row_size) & (live < 0.5), 1.0, 0.0).astype(jnp.bfloat16)
    total = steps * span
    cell = iota((total, shut.shape[0]), 0)
    row_of = cell // span * (chunk // cols) + cell % chunk // cols
    spread = (row_of == iota((total, shut.shape[0]), 1)).astype(jnp.bfloat16)
    bias = dot_rows(spread, shut) * BIG
    asked = dot_rows(normed_ref[...], w_query_ref[...]).astype(jnp.bfloat16).astype(jnp.float32) * scale
    low = iota((total, lanes_two), 1) < head_size
    for head in range(heads_here):
        if heads_here % 2 == 0:
            two = asked[:, head // 2 * lanes_two:(head // 2 + 1) * lanes_two]
            one = two if head % 2 == 0 else pltpu.roll(two, head_size, 1)
            query = jnp.where(low, one, bias)
        else:
            one = asked[:, head * head_size:(head + 1) * head_size]
            query = jnp.concatenate([one, bias[:, head_size:]], axis=1)
        query = query.astype(jnp.bfloat16)
        for step in range(steps):
            for group in range(groups):
                start = step * span + group * chunk
                asked_ref[head, pl.ds(group * own_rows + step * chunk, chunk), :] = query[start:start + chunk]


def front(cells, ids, me, key_mask, gain_col, w_qkv, w_out, gain_tile, w_query, heads, head_size, cols,
          heads_here, tiles_here, row_size, paired, after):
    groups = len(cells)
    width = cells[0].shape[2]
    own_rows = cells[0].shape[0] * cols
    total = groups * own_rows
    key_mask, gain_col, gain_tile = key_mask.T, gain_col.reshape(1, width), gain_tile.reshape(1, width)
    weights = [(3, width, width), (width, width), (width, heads_here * head_size), (groups,) + cells[0].shape]
    scratch = [pltpu.VMEM(shape, jnp.bfloat16) for shape in [(total, width), (3, total, width)] + weights]
    scratch += [pltpu.SMEM(ids.shape, jnp.int32), pltpu.VMEM(key_mask.shape, jnp.int32)]
    scratch += [pltpu.VMEM((1, width), jnp.float32)] * 2 + [pltpu.SemaphoreType.DMA((groups + 9,))]
    fetched = [pltpu.with_memory_space_constraint(value, pltpu.HBM)
               for value in (ids, key_mask, gain_col, gain_tile, w_qkv, w_out, w_query)]
    own = pltpu.with_memory_space_constraint(cells[0], pltpu.HBM)
    return pl.pallas_call(
        functools.partial(front_kernel, groups, heads, head_size, ROW_GROUP * cols, cols, heads_here, tiles_here, row_size, paired,
                          len(after)),
        out_shape=(jax.ShapeDtypeStruct((own_rows, width), jnp.float32),
                   jax.ShapeDtypeStruct((heads_here, total, 2 * head_size), jnp.bfloat16)),
        in_specs=[HBM] + [ANY] * (groups - 1) + [SMEM] + [HBM] * 7 + [ANY] * len(after),
        out_specs=(VMEM, VMEM),
        scratch_shapes=scratch,
        compiler_params=params(total),
        cost_estimate=pl.CostEstimate(flops=2 * total * width * 5 * width, bytes_accessed=4 * MIB,
                                      transcendentals=total * heads * 128),
        name="front",
    )(own, *cells[1:], me, *fetched, *after)


def weigh(query, tile_refs, head, slots):
    key_parts, val_parts = [], []
    for ref, slot in zip(tile_refs, slots):
        tiles = ref[:, head]
        count, keys, lanes = tiles.shape
        lane = iota(tiles.shape, 2)
        marks = (lane == iota(tiles.shape, 0) + (lanes // 2 + slot)).astype(tiles.dtype)
        key_parts.append(jnp.where(lane < lanes // 2, tiles, marks).reshape(count * keys, lanes))
        val_parts.append(jnp.where(lane < lanes // 2, jnp.ones_like(tiles), tiles).reshape(count * keys, lanes))
    scores = dot_lanes(query, jnp.concatenate(key_parts, axis=0))
    top = jnp.max(scores, axis=1, keepdims=True)
    return top, dot_rows(jnp.exp(scores - top).astype(jnp.bfloat16), jnp.concatenate(val_parts, axis=0))


def attention_cost(asked, tiles):
    heads, rows, lanes = asked.shape
    keys = sum(part.shape[0] * part.shape[2] for part in tiles)
    return pl.CostEstimate(flops=4 * rows * heads * keys * lanes, bytes_accessed=4 * MIB, transcendentals=rows * heads * keys)


def first_kernel(slots, block, asked_ref, *refs):
    tile_refs, (sums_ref, tops_ref) = refs[:len(slots)], refs[-2:]
    heads, rows_all, lanes = asked_ref.shape
    lane = iota((block, lanes), 1)
    for step in range(rows_all // block):
        rows = pl.ds(step * block, block)
        tops = jnp.zeros((block, lanes), jnp.float32)
        for head in range(heads):
            top, sums_ref[head, rows, :] = weigh(asked_ref[head, rows, :], tile_refs, head, slots)
            tops = jnp.where(lane == head, top, tops)
        tops_ref[rows, :] = tops


def first_tiles(asked, tiles, slots, own_rows, after):
    heads, rows, lanes = asked.shape
    return pl.pallas_call(
        functools.partial(first_kernel, slots, rows if rows <= 512 else own_rows),
        out_shape=(jax.ShapeDtypeStruct((heads, rows, lanes), jnp.float32), jax.ShapeDtypeStruct((rows, lanes), jnp.float32)),
        in_specs=[VMEM] * (1 + len(tiles)) + [ANY] * len(after),
        out_specs=(VMEM, VMEM),
        compiler_params=params(rows),
        cost_estimate=attention_cost(asked, tiles),
        name="first_tiles",
    )(asked, *tiles, *after)


def merge(asked_ref, sums_ref, tops_ref, tile_refs, slots, head, rows):
    top, sums = weigh(asked_ref[head, rows, :], tile_refs, head, slots)
    old_top = tops_ref[rows, head:head + 1]
    new_top = jnp.maximum(top, old_top)
    return new_top, sums_ref[head, rows, :] * jnp.exp(old_top - new_top) + sums * jnp.exp(top - new_top)


def more_kernel(slots, block, asked_ref, old_sums_ref, old_tops_ref, *refs):
    tile_refs, (sums_ref, tops_ref) = refs[:len(slots)], refs[len(slots):]
    heads, rows_all, lanes = asked_ref.shape
    lane = iota((block, lanes), 1)
    for step in range(rows_all // block):
        rows = pl.ds(step * block, block)
        tops = jnp.zeros((block, lanes), jnp.float32)
        for head in range(heads):
            top, sums_ref[head, rows, :] = merge(asked_ref, old_sums_ref, old_tops_ref, tile_refs, slots, head, rows)
            tops = jnp.where(lane == head, top, tops)
        tops_ref[rows, :] = tops


def more_tiles(asked, sums, tops, tiles, slots, own_rows):
    rows = asked.shape[1]
    return pl.pallas_call(
        functools.partial(more_kernel, slots, rows if rows <= 512 else own_rows),
        out_shape=(jax.ShapeDtypeStruct(sums.shape, jnp.float32), jax.ShapeDtypeStruct(tops.shape, jnp.float32)),
        in_specs=[VMEM] * (3 + len(tiles)),
        out_specs=(VMEM, VMEM),
        compiler_params=params(rows),
        cost_estimate=attention_cost(asked, tiles),
        name="more_tiles",
    )(asked, sums, tops, *tiles)


def last_kernel(slots, groups, asked_ref, sums_ref, tops_ref, *refs):
    tile_refs, out_refs = refs[:len(slots)], refs[-len(groups):]
    heads, lanes = asked_ref.shape[0], asked_ref.shape[2]
    block = out_refs[0].shape[0]
    half = lanes // 2
    lane_low = iota((block, lanes), 1) < half
    for group, out_ref in zip(groups, out_refs):
        rows = pl.ds(group * block, block)
        low = None
        for head in range(heads):
            _, sums = merge(asked_ref, sums_ref, tops_ref, tile_refs, slots, head, rows)
            turned = pltpu.roll(sums, half, 1)
            if head % 2:
                out_ref[:, pl.ds(head // 2 * lanes, lanes)] = jnp.where(lane_low, low, sums / turned).astype(jnp.bfloat16)
            elif head + 1 < heads:
                low = turned / sums
            else:
                out_ref[:, pl.ds(head * half, half)] = (turned / sums)[:, :half].astype(jnp.bfloat16)


def last_tiles(asked, sums, tops, tiles, slots, groups, own_rows, after):
    heads, rows, lanes = asked.shape
    out = jax.ShapeDtypeStruct((own_rows, heads * lanes // 2), jnp.bfloat16)
    return pl.pallas_call(
        functools.partial(last_kernel, slots, groups),
        out_shape=(out,) * len(groups),
        in_specs=[VMEM] * (3 + len(tiles)) + [ANY] * len(after),
        out_specs=(VMEM,) * len(groups),
        compiler_params=params(rows),
        cost_estimate=attention_cost(asked[:, :own_rows * len(groups)], tiles),
        name="last_tiles",
    )(asked, sums, tops, *tiles, *after)


def own_kernel(me_ref, weight_ref, resid_ref, answer_ref, partial_ref, *part_refs):
    groups, group_width = len(part_refs) + 1, answer_ref.shape[1]

    def rows(step):
        group = lax.rem(me_ref[1] - step + groups, groups)
        return weight_ref[pl.ds(pl.multiple_of(group * group_width, group_width), group_width), :]

    partial_ref[...] = resid_ref[...] + dot_rows(answer_ref[...], rows(0))
    for step, part_ref in enumerate(part_refs):
        part_ref[...] = rows(step + 1)


def own_part(me, weight, residual, answer, groups):
    part = jax.ShapeDtypeStruct((answer.shape[1], weight.shape[1]), weight.dtype)
    return pl.pallas_call(
        own_kernel,
        out_shape=(jax.ShapeDtypeStruct(residual.shape, jnp.float32),) + (part,) * (groups - 1),
        in_specs=[SMEM, VMEM, VMEM, VMEM],
        out_specs=(VMEM,) * groups,
        compiler_params=params(0),
        cost_estimate=pl.CostEstimate(flops=2 * residual.size * answer.shape[1], bytes_accessed=MIB, transcendentals=0),
        name="own_part",
    )(me, weight, residual, answer)


def turn(size, step):
    return [(src, (src + step) % size) for src in range(size)]


def shards(row_size, col_size, fact_cells, gain_col, w_qkv, w_col_out, gain_tile, w_query, w_tile_out,
           tile_kv, tile_ids, key_mask):
    rows, cols, width = fact_cells.shape
    tiles_here, keys, heads_here, lanes = tile_kv.shape
    head_size = lanes // 2
    heads_all = width // head_size
    group_width = heads_here * head_size
    half = row_size // 2
    row_me, col_me = lax.axis_index("rows"), lax.axis_index("cols")
    me = jnp.stack([row_me, col_me]).astype(jnp.int32)
    halves = [list(range(half)), list(range(half, row_size))]
    paired = half <= 8 and half & (half - 1) == 0
    assert row_size <= head_size and row_size % 2 == 0

    def swap(value):
        return lax.all_to_all(value, "rows", split_axis=0, concat_axis=0, tiled=True, axis_index_groups=halves)

    asked_of = request(tile_ids, me, tiles_here, row_size)
    asked_by = swap(asked_of)
    heads_first = jnp.transpose(tile_kv, (0, 2, 1, 3))
    mirrored = lax.ppermute(heads_first, "rows", turn(row_size, half))

    cells = [fact_cells]
    for step in range(1, col_size):
        cells.append(lax.ppermute(fact_cells, "cols", turn(col_size, -step)))

    across = half // 2

    def turns(step):
        return bool(step & across) and bool(step & (across - 1) & ~1)

    near_order = [0, 1] + sorted(range(2, half), key=lambda step: (turns(step), step != 2, not step & across, step))
    far_order = [0] + sorted(range(2, half), key=lambda step: (turns(step), not step & across, step)) + [1]
    near_slots, far_slots = (near_order, [half + step for step in far_order]) if paired else ([0], [half])

    def spread(tiles, which, order, after):
        if not order:
            return []
        if not paired:
            return [swap(pick(tiles, asked_by, which, after))]
        picked = pick_each(tiles, asked_by, which, me, order, after)
        return [tile if step == 0 else lax.ppermute(tile, "rows", [(row, row ^ step) for row in range(row_size)])
                for step, tile in zip(order, picked)]

    if group_width % 128:
        w_query = lax.dynamic_slice_in_dim(w_query, col_me * group_width, group_width, 1)
    residual, asked = front(cells, tile_ids, me, key_mask, gain_col, w_qkv, w_col_out, gain_tile, w_query,
                            heads_all, head_size, cols, heads_here, tiles_here, row_size, paired, [])
    near = spread(heads_first, 0, near_order, [asked])
    far = spread(mirrored, 1, far_order[:-1] if paired else far_order, near[1:3])
    sums, tops = first_tiles(asked, near, near_slots, rows * cols, far[1:2])
    far += spread(mirrored, 1, far_order[-1:] if paired else [], [tops])
    batch = len(far) // 2
    if batch:
        sums, tops = more_tiles(asked, sums, tops, far[:batch], far_slots[:batch], rows * cols)
    far, far_slots = far[batch:], far_slots[batch:]
    others = last_tiles(asked, sums, tops, far, far_slots, list(range(1, col_size)), rows * cols, [])
    own = last_tiles(asked, sums, tops, far, far_slots, [0], rows * cols, others[:1])
    final, *weights = own_part(me, w_tile_out, residual, own[0], col_size)
    for step, (other, weight) in enumerate(zip(others, weights)):
        final = final + dot_rows(lax.ppermute(other, "cols", turn(col_size, step + 1)), weight)
    return final.astype(jnp.bfloat16).reshape(rows, cols, width)


def solution(mesh):
    row_size, col_size = mesh.shape["rows"], mesh.shape["cols"]
    placed = (P("rows", "cols", None), P(), P(), P(), P(), P(), P(), P("rows", None, "cols", None),
              P("rows", None), P("rows", None))

    def body(*arrays):
        return shards(row_size, col_size, *arrays)

    return jax.shard_map(body, mesh=mesh, in_specs=placed, out_specs=P("rows", "cols", None), check_vma=False)
```
